32 devices in a mesh: dp: 8 (over z, core), fsdp: 4 (over y, x).
Axes of the slice: x: 2, y: 2, z: 4, core: 2. Of those that a mesh axis runs over, the one named last changes fastest.
Arguments:
- inputs: bfloat16 [12288, 2048], P(('dp', 'fsdp')), may hold values from -6 to 6
- cotangent: bfloat16 [12288, 2048], P(('dp', 'fsdp')), may hold values from -6 to 6
- segments: int32 [32, 384], P(('dp', 'fsdp')), may hold values from 0 to 2, as said below
- qkv_weight: float32 [2048, 2560], P(('dp', 'fsdp')), may hold values from -0.125 to 0.125
- out_weight: float32 [2048, 2048], P(('dp', 'fsdp')), may hold values from -0.625 to 0.625
- mlp_weight: float32 [2048, 11264], P(('dp', 'fsdp')), may hold values from -0.125 to 0.125
- down_weight: float32 [5632, 2048], P(('dp', 'fsdp')), may hold values from -0.078125 to 0.078125
- norm_gains: float32 [2, 2048], P(None, ('dp', 'fsdp')), may hold values from 0.25 to 3
- qkv_first: float32 [2048, 2560], P(('dp', 'fsdp')), may hold values from -0.00024414062 to 0.00024414062
- out_first: float32 [2048, 2048], P(('dp', 'fsdp')), may hold values from -0.00024414062 to 0.00024414062
- mlp_first: float32 [2048, 11264], P(('dp', 'fsdp')), may hold values from -0.00024414062 to 0.00024414062
- down_first: float32 [5632, 2048], P(('dp', 'fsdp')), may hold values from -0.00024414062 to 0.00024414062
- gains_first: float32 [2, 2048], P(None, ('dp', 'fsdp')), may hold values from -0.00024414062 to 0.00024414062
- qkv_second: float32 [2048, 2560], P(('dp', 'fsdp')), may hold values from 1.1942525e-09 to 4.7679283e-09
- out_second: float32 [2048, 2048], P(('dp', 'fsdp')), may hold values from 1.1942525e-09 to 4.7679283e-09
- mlp_second: float32 [2048, 11264], P(('dp', 'fsdp')), may hold values from 1.1942525e-09 to 4.7679283e-09
- down_second: float32 [5632, 2048], P(('dp', 'fsdp')), may hold values from 1.1942525e-09 to 4.7679283e-09
- gains_second: float32 [2, 2048], P(None, ('dp', 'fsdp')), may hold values from 1.1942525e-09 to 4.7679283e-09
Outputs:
- layer_out: bfloat16 [12288, 2048], P(('dp', 'fsdp'))
- input_grad: bfloat16 [12288, 2048], P(('dp', 'fsdp'))
- grad_norm: float32 [], replicated
- qkv_new: float32 [2048, 2560], P(('dp', 'fsdp'))
- out_new: float32 [2048, 2048], P(('dp', 'fsdp'))
- mlp_new: float32 [2048, 11264], P(('dp', 'fsdp'))
- down_new: float32 [5632, 2048], P(('dp', 'fsdp'))
- gains_new: float32 [2, 2048], P(None, ('dp', 'fsdp'))
- qkv_first_new: float32 [2048, 2560], P(('dp', 'fsdp'))
- out_first_new: float32 [2048, 2048], P(('dp', 'fsdp'))
- mlp_first_new: float32 [2048, 11264], P(('dp', 'fsdp'))
- down_first_new: float32 [5632, 2048], P(('dp', 'fsdp'))
- gains_first_new: float32 [2, 2048], P(None, ('dp', 'fsdp'))
- qkv_second_new: float32 [2048, 2560], P(('dp', 'fsdp'))
- out_second_new: float32 [2048, 2048], P(('dp', 'fsdp'))
- mlp_second_new: float32 [2048, 11264], P(('dp', 'fsdp'))
- down_second_new: float32 [5632, 2048], P(('dp', 'fsdp'))
- gains_second_new: float32 [2, 2048], P(None, ('dp', 'fsdp'))
The draws below stay inside these ranges and needn't reach their ends.
Inputs may be any that keep to these rules, and one draw needn't show every extreme that they name: `segments`: along each row of 384 tokens the document numbers never fall; the first token of a row is in document 0 and the last in document 2, so a row holds two or three documents.
All inputs are finite; a program needn't handle non-finite values.
Results may differ from the reference program's by a relative error of at most 0.015.
The reference program's roundings to bfloat16 on the way count: a program that leaves them out, or rounds other values in their place, can miss the bound.
Values may be sent and summed in bfloat16 or wider, within the bound.
A program may use at most 384 MiB of HBM per device.

```python
import math
import jax
import jax.numpy as jnp
from jax import lax

D = 2048
HEADS = 32
KVH = 4
HD = 64
FF = 5632
TOK_DEV = 384
STEP = 10
QKV = 2560
ROWS = 32
TOKENS = 12288
PARAMS = 44044288
N_DP = 8
N_FSDP = 4
DEVICES = 32


def draw_segments(key, part):
    key = jax.random.fold_in(key, 3)
    cuts = jax.random.randint(key, (ROWS, 2), 1, TOK_DEV, dtype=jnp.int32)
    token_index = jnp.arange(TOK_DEV, dtype=jnp.int32)
    first_cut = (token_index[None, :] >= cuts[:, :1]).astype(jnp.int32)
    second_cut = (token_index[None, :] >= cuts[:, 1:]).astype(jnp.int32)
    return first_cut + second_cut


def draw_norm_gains(key, part):
    key = jax.random.fold_in(key, 7)
    column = jnp.arange(D, dtype=jnp.int32) // (D // DEVICES)
    wide_part = (column // N_FSDP).astype(jnp.float32) / max(N_DP - 1, 1)
    narrow = (column % N_FSDP).astype(jnp.float32) / max(N_FSDP - 1, 1)
    bottom = 0.75
    growth = 0.55
    profile = (bottom + growth * wide_part) * (bottom + growth * narrow)
    jitter = jax.random.uniform(key, (2, D), jnp.float32, 0.8, 1.25)
    return profile[None, :] * jitter


def block_scale(own_key, extent, shards, low, largest):
    gain = 1.0
    for dim, blocks in shards:
        heights = jax.random.uniform(jax.random.fold_in(jax.random.fold_in(own_key, 6), dim), (blocks,), jnp.float32, low / len(shards), largest / len(shards))
        gain = gain * jnp.repeat(jnp.exp(heights), extent[dim] // blocks).reshape((-1,) + (1,) * (len(extent) - 1 - dim))
    return gain


def scatter_about(stream_key, shape, width, reach, cuts=(), held_as=jnp.bfloat16):
    gain = block_scale(stream_key, shape, cuts, -0.22, 0.18) if cuts else 1.0
    drawn = jax.random.normal(stream_key, shape, jnp.float32) * width * gain
    return jnp.minimum(jnp.maximum(drawn, -reach), reach).astype(held_as)


def setup_inputs(seed: int = 0) -> dict:
    key_list = jax.random.split(jax.random.key(seed), 19)
    inputs = scatter_about(key_list[0], (TOKENS, D), 1.0, 6.0, ((0, 32),))
    cotangent = scatter_about(key_list[1], (TOKENS, D), 1.0, 6.0, ((0, 32),))
    segments = draw_segments(jax.random.fold_in(key_list[18], 71), 0)
    qkv_weight = scatter_about(key_list[3], (D, QKV), D ** -0.5, 0.125, ((0, 32),), jnp.float32)
    out_weight = scatter_about(key_list[4], (D, D), (D * 16 // TOK_DEV) ** -0.5, 0.625, ((0, 32),), jnp.float32)
    mlp_weight = scatter_about(key_list[5], (D, 2 * FF), D ** -0.5, 0.125, ((0, 32),), jnp.float32)
    down_weight = scatter_about(key_list[6], (FF, D), FF ** -0.5, 0.078125, ((0, 32),), jnp.float32)
    norm_gains = draw_norm_gains(jax.random.fold_in(key_list[18], 71), 0)
    qkv_first = scatter_about(key_list[8], (D, QKV), (0.111 * PARAMS ** -0.5), 0.00024414062, ((0, 32),), jnp.float32)
    out_first = scatter_about(key_list[9], (D, D), (0.111 * PARAMS ** -0.5), 0.00024414062, ((0, 32),), jnp.float32)
    mlp_first = scatter_about(key_list[10], (D, 2 * FF), (0.111 * PARAMS ** -0.5), 0.00024414062, ((0, 32),), jnp.float32)
    down_first = scatter_about(key_list[11], (FF, D), (0.111 * PARAMS ** -0.5), 0.00024414062, ((0, 32),), jnp.float32)
    gains_first = scatter_about(key_list[12], (2, D), (0.111 * PARAMS ** -0.5), 0.00024414062, ((1, 32),), jnp.float32)
    qkv_second = jnp.clip(jnp.exp(math.log(4.767928274418409e-09) - 1.3843914 * jax.random.uniform(key_list[13], (D, QKV), jnp.float32) ** block_scale(key_list[13], (D, QKV), ((0, 32),), -0.2, 0.2)), 1.1942524746899608e-09, 4.767928274418409e-09)
    out_second = jnp.clip(jnp.exp(math.log(4.767928274418409e-09) - 1.3843914 * jax.random.uniform(key_list[14], (D, D), jnp.float32) ** block_scale(key_list[14], (D, D), ((0, 32),), -0.2, 0.2)), 1.1942524746899608e-09, 4.767928274418409e-09)
    mlp_second = jnp.clip(jnp.exp(math.log(4.767928274418409e-09) - 1.3843914 * jax.random.uniform(key_list[15], (D, 2 * FF), jnp.float32) ** block_scale(key_list[15], (D, 2 * FF), ((0, 32),), -0.2, 0.2)), 1.1942524746899608e-09, 4.767928274418409e-09)
    down_second = jnp.clip(jnp.exp(math.log(4.767928274418409e-09) - 1.3843914 * jax.random.uniform(key_list[16], (FF, D), jnp.float32) ** block_scale(key_list[16], (FF, D), ((0, 32),), -0.2, 0.2)), 1.1942524746899608e-09, 4.767928274418409e-09)
    gains_second = jnp.clip(jnp.exp(math.log(4.767928274418409e-09) - 1.3843914 * jax.random.uniform(key_list[17], (2, D), jnp.float32) ** block_scale(key_list[17], (2, D), ((1, 32),), -0.2, 0.2)), 1.1942524746899608e-09, 4.767928274418409e-09)
    return dict(inputs=inputs, cotangent=cotangent, segments=segments, qkv_weight=qkv_weight, out_weight=out_weight, mlp_weight=mlp_weight, down_weight=down_weight, norm_gains=norm_gains, qkv_first=qkv_first, out_first=out_first, mlp_first=mlp_first, down_first=down_first, gains_first=gains_first, qkv_second=qkv_second, out_second=out_second, mlp_second=mlp_second, down_second=down_second, gains_second=gains_second)


norm_eps = 1e-05
rope_base = 10000.0
beta_one = 0.9
beta_two = 0.95
adam_eps = 1e-08
weight_decay = 0.1
matrix_rate = 0.04
gain_rate = 0.8
clip_norm = 1.0
highest = lax.Precision.HIGHEST

@jax.custom_vjp
def low(v):
    return lax.optimization_barrier(v.astype(jnp.bfloat16)).astype(jnp.float32)

@jax.custom_vjp
def low_back(v):
    return v

def low_keep(v):
    return (low(v), None)

def low_pass(kept, grad):
    return (grad,)

def back_keep(v):
    return (v, None)

def back_low(kept, grad):
    return (low(grad),)
low.defvjp(low_keep, low_pass)
low_back.defvjp(back_keep, back_low)

def tables(segment_row):
    length = segment_row.shape[0]
    token_index = jnp.arange(length, dtype=jnp.int32)
    previous = jnp.concatenate([segment_row[:1] - 1, segment_row[:-1]])
    starts = lax.cummax(jnp.where(segment_row != previous, token_index, 0), axis=0)
    position = (token_index - starts).astype(jnp.float32)
    frequency = rope_base ** (-(jnp.arange(HD // 2, dtype=jnp.float32) * 2.0 / HD))
    angles = position[:, None] * frequency[None, :]
    angles = jnp.concatenate([angles, angles], axis=-1)
    allowed = (segment_row[:, None] == segment_row[None, :]) & (token_index[:, None] >= token_index[None, :])
    return (jnp.cos(angles)[:, None, :], jnp.sin(angles)[:, None, :], allowed)

def rotate(heads_in, cosine, sine):
    half_width = heads_in.shape[-1] // 2
    turned = jnp.concatenate([-heads_in[..., half_width:], heads_in[..., :half_width]], axis=-1)
    return heads_in * cosine + turned * sine

def norm_rows(tokens_in):
    return tokens_in * lax.rsqrt(lax.optimization_barrier(jnp.mean(tokens_in * tokens_in, axis=-1, keepdims=True)) + norm_eps)

def layer_row(tokens_in, segment_row, qkv_w, out_w, mlp_w, down_w, gain_w):
    length = tokens_in.shape[0]
    groups = HEADS // KVH
    key_width = KVH * HD
    cosine, sine, allowed = tables(segment_row)
    normed_one = low(norm_rows(tokens_in) * gain_w[0])
    projected = low_back(jnp.dot(normed_one, qkv_w, precision=highest))
    queries = projected[:, :D].reshape(length, HEADS, HD)
    key_heads = projected[:, D:D + key_width].reshape(length, KVH, HD)
    values = low(projected[:, D + key_width:].reshape(length, KVH, HD))
    queries = low(rotate(queries, cosine, sine)).reshape(length, KVH, groups, HD)
    key_heads = low(rotate(key_heads, cosine, sine))
    scores = low_back(jnp.einsum('tkgh,skh->kgts', queries, key_heads, precision=highest)) * HD ** (-0.5)
    scores = jnp.where(allowed[None, None], scores, -1e+30)
    row_max = lax.optimization_barrier(jnp.max(scores, axis=-1, keepdims=True))
    exp_scores = jnp.exp(scores - row_max)
    attn_probs = low(exp_scores / lax.optimization_barrier(jnp.sum(exp_scores, axis=-1, keepdims=True)))
    context = jnp.einsum('kgts,skh->tkgh', attn_probs, values, precision=highest).reshape(length, D)
    attended = low(low_back(context))
    middle = tokens_in + low_back(jnp.dot(attended, out_w, precision=highest))
    normed_two = low(norm_rows(middle) * gain_w[1])
    hidden = low_back(jnp.dot(normed_two, mlp_w, precision=highest))
    activated = low(jax.nn.silu(hidden[:, :FF]) * hidden[:, FF:])
    return middle + low_back(jnp.dot(activated, down_w, precision=highest))

def adam_update(weight, gradient, first, second, rate, decay):
    first = beta_one * first + (1.0 - beta_one) * gradient
    second = beta_two * second + (1.0 - beta_two) * gradient * gradient
    first_hat = first / (1.0 - beta_one ** STEP)
    second_hat = second / (1.0 - beta_two ** STEP)
    weight = weight - rate * (first_hat / (jnp.sqrt(second_hat) + adam_eps) + decay * weight)
    return (weight, first, second)

def reference(inputs, cotangent, segments, qkv_weight, out_weight, mlp_weight, down_weight, norm_gains, qkv_first, out_first, mlp_first, down_first, gains_first, qkv_second, out_second, mlp_second, down_second, gains_second):

    def forward(tokens_in, qkv_w, out_w, mlp_w, down_w, gain_w):
        qkv_low = low(qkv_w)
        out_low = low(out_w)
        mlp_low = low(mlp_w)
        down_low = low(down_w)
        gain_low = low(gain_w)

        def one_row(row_tokens, segment_row):
            return layer_row(row_tokens, segment_row, qkv_low, out_low, mlp_low, down_low, gain_low)
        checked = jax.checkpoint(one_row)

        def scan_step(carry, row_pair):
            return (carry, checked(row_pair[0], row_pair[1]))
        _, result = lax.scan(scan_step, jnp.zeros((), jnp.float32), (tokens_in.reshape(ROWS, TOK_DEV, D), segments))
        return result.reshape(TOKENS, D)
    output, pullback = jax.vjp(forward, inputs.astype(jnp.float32), qkv_weight, out_weight, mlp_weight, down_weight, norm_gains)
    grad_inputs, grad_qkv, grad_out, grad_mlp, grad_down, grad_gains = pullback(cotangent.astype(jnp.float32))
    squares = jnp.sum(grad_qkv * grad_qkv) + jnp.sum(grad_out * grad_out) + jnp.sum(grad_mlp * grad_mlp)
    squares = squares + jnp.sum(grad_down * grad_down) + jnp.sum(grad_gains * grad_gains)
    grad_norm = jnp.sqrt(squares)
    clip_scale = clip_norm / jnp.maximum(grad_norm, clip_norm)
    qkv_new, qkv_first_new, qkv_second_new = adam_update(qkv_weight, grad_qkv * clip_scale, qkv_first, qkv_second, matrix_rate, weight_decay)
    out_new, out_first_new, out_second_new = adam_update(out_weight, grad_out * clip_scale, out_first, out_second, matrix_rate, weight_decay)
    mlp_new, mlp_first_new, mlp_second_new = adam_update(mlp_weight, grad_mlp * clip_scale, mlp_first, mlp_second, matrix_rate, weight_decay)
    down_new, down_first_new, down_second_new = adam_update(down_weight, grad_down * clip_scale, down_first, down_second, matrix_rate, weight_decay)
    gains_new, gains_first_new, gains_second_new = adam_update(norm_gains, grad_gains * clip_scale, gains_first, gains_second, gain_rate, 0.0)
    return (output.astype(jnp.bfloat16), grad_inputs.astype(jnp.bfloat16), grad_norm, qkv_new, out_new, mlp_new, down_new, gains_new, qkv_first_new, out_first_new, mlp_first_new, down_first_new, gains_first_new, qkv_second_new, out_second_new, mlp_second_new, down_second_new, gains_second_new)
```

```python
import functools

import jax
import jax.numpy as jnp
from jax import lax
from jax.experimental import pallas as pl
from jax.experimental.pallas import tpu as pltpu
from jax.sharding import PartitionSpec as P

D = 2048
HEADS = 32
KVH = 4
HD = 64
FF = 5632
STEP = 10
KW = KVH * HD
GROUP = HEADS // KVH


norm_eps = 1e-05
rope_base = 10000.0
beta_one = 0.9
beta_two = 0.95
adam_eps = 1e-08
weight_decay = 0.1
matrix_rate = 0.04
gain_rate = 0.8
clip_norm = 1.0

f32 = jnp.float32
bf16 = jnp.bfloat16


def tables(segment_row):
    length = segment_row.shape[0]
    token_index = jnp.arange(length, dtype=jnp.int32)
    previous = jnp.concatenate([segment_row[:1] - 1, segment_row[:-1]])
    starts = lax.cummax(jnp.where(segment_row != previous, token_index, 0), axis=0)
    position = (token_index - starts).astype(f32)
    frequency = rope_base ** (-(jnp.arange(HD // 2, dtype=f32) * 2.0 / HD))
    angles = position[:, None] * frequency[None, :]
    cosine, sine = jnp.cos(angles), jnp.sin(angles)
    cosine = jnp.concatenate([cosine] * 4, axis=-1)
    signed = jnp.concatenate([-sine, sine] * 2, axis=-1)
    return cosine, signed


def halves_swapped(pair):
    lane = lax.broadcasted_iota(jnp.int32, pair.shape, 1)
    return jnp.where(lane % HD < HD // 2, pltpu.roll(pair, 96, 1), pltpu.roll(pair, 32, 1))


def split_pair(pair):
    lane = lax.broadcasted_iota(jnp.int32, pair.shape, 1)
    zero = jnp.zeros_like(pair)
    return jnp.where(lane < HD, pair, zero), jnp.where(lane < HD, zero, pair)


def both_places(pair, odd):
    low, high = split_pair(pair)
    moved = pltpu.roll(pair.astype(f32), HD, 1).astype(pair.dtype)
    moved_low, moved_high = split_pair(moved)
    return (moved_low, high) if odd else (low, moved_high)


def dot_t(a, b):
    return lax.dot_general(a, b, (((1,), (1,)), ((), ())), preferred_element_type=f32)


def dot_n(a, b):
    return lax.dot_general(a, b, (((1,), (0,)), ((), ())), preferred_element_type=f32)


def dot_tn(a, b):
    return lax.dot_general(a, b, (((0,), (0,)), ((), ())), preferred_element_type=f32)


def mask_keys_rows(seg_col, seg_row, length):
    key_index = lax.broadcasted_iota(jnp.int32, (length, length), 0)
    query_index = lax.broadcasted_iota(jnp.int32, (length, length), 1)
    return (seg_col == seg_row) & (query_index >= key_index)


def attend_kernel(proj, cosine, sine, seg_col, seg_row, qkv, context, log_totals):
    length = proj.shape[0]
    cos, sin = cosine[...], sine[...]
    for c in range(0, D + KW, 128):
        pair = proj[:, c : c + 128]
        qkv[:, c : c + 128] = (pair * cos + halves_swapped(pair) * sin).astype(bf16)
    for c in range(D + KW, D + 2 * KW, 128):
        qkv[:, c : c + 128] = proj[:, c : c + 128].astype(bf16)
    allowed = mask_keys_rows(seg_col[...], seg_row[...], length)
    scale = HD ** (-0.5)
    for group in range(KVH):
        kc = D + (group // 2) * 128
        keys = both_places(qkv[:, kc : kc + 128], group % 2)
        values = both_places(qkv[:, kc + KW : kc + KW + 128], group % 2)

        def pair_step(pair_index, carry):
            pair = group * (GROUP // 2) + pair_index
            lanes = pl.ds(pl.multiple_of(pair * 128, 128), 128)
            queries = qkv[:, lanes]
            total = jnp.zeros((length, 128), f32)
            for side in range(2):
                scores = dot_t(keys[side], queries) * scale
                scores = jnp.where(allowed, scores, -1e30)
                top = jnp.max(scores, axis=0, keepdims=True)
                raised = jnp.exp(scores - top)
                totals = jnp.sum(raised, axis=0, keepdims=True)
                probs = (raised / totals).astype(bf16)
                total = total + dot_tn(probs, values[side])
                log_totals[pl.ds(2 * pair + side, 1), :] = top + jnp.log(totals)
            context[:, lanes] = total.astype(bf16)
            return carry

        lax.fori_loop(0, GROUP // 2, pair_step, 0)


def attend_grad_kernel(qkv, grad_context, log_totals, cosine, sine, seg_col, seg_row, grad_proj):
    length = qkv.shape[0]
    cos, sin = cosine[...], sine[...]
    allowed = mask_keys_rows(seg_col[...], seg_row[...], length)
    scale = HD ** (-0.5)

    def unrotate(pair):
        return pair * cos + halves_swapped(pair * sin)

    key_parts, value_parts = [], []
    for group in range(KVH):
        kc = D + (group // 2) * 128
        keys = both_places(qkv[:, kc : kc + 128], group % 2)
        values = both_places(qkv[:, kc + KW : kc + KW + 128], group % 2)

        def pair_step(pair_index, carry):
            grad_keys, grad_values = list(carry[:2]), list(carry[2:])
            pair = group * (GROUP // 2) + pair_index
            lanes = pl.ds(pl.multiple_of(pair * 128, 128), 128)
            queries = qkv[:, lanes]
            grads = grad_context[:, lanes]
            total = jnp.zeros((length, 128), f32)
            for side in range(2):
                scores = dot_t(keys[side], queries) * scale
                scores = jnp.where(allowed, scores, -1e30)
                probs = jnp.exp(scores - log_totals[pl.ds(2 * pair + side, 1), :])
                grad_probs = dot_t(values[side], grads)
                grad_values[side] = grad_values[side] + dot_n(probs.astype(bf16), grads)
                inner = jnp.sum(probs * grad_probs, axis=0, keepdims=True)
                raw = (probs * (grad_probs - inner) * scale).astype(bf16)
                total = total + dot_tn(raw, keys[side])
                grad_keys[side] = grad_keys[side] + dot_n(raw, queries)
            grad_proj[:, lanes] = unrotate(total).astype(bf16)
            return (*grad_keys, *grad_values)

        empty = jnp.zeros((length, 128), f32)
        out = lax.fori_loop(0, GROUP // 2, pair_step, (empty,) * 4)

        def joined(low_side, high_side):
            low, _ = split_pair(low_side)
            _, high = split_pair(high_side)
            both = low + high
            return both + pltpu.roll(both, HD, 1)

        key_parts.append(joined(out[0], out[1]))
        value_parts.append(joined(out[2], out[3]))
    lane = lax.broadcasted_iota(jnp.int32, (length, 128), 1)
    for c in range(KVH // 2):
        keys = jnp.where(lane < HD, key_parts[2 * c], key_parts[2 * c + 1])
        values = jnp.where(lane < HD, value_parts[2 * c], value_parts[2 * c + 1])
        grad_proj[:, D + c * 128 : D + (c + 1) * 128] = unrotate(keys).astype(bf16)
        grad_proj[:, D + KW + c * 128 : D + KW + (c + 1) * 128] = values.astype(bf16)


vmem_limit = 50 * 1024 * 1024


def attend(projected, cosine, sine, seg_col, seg_row):
    length = projected.shape[0]
    return pl.pallas_call(
        attend_kernel,
        out_shape=(
            jax.ShapeDtypeStruct((length, D + 2 * KW), bf16),
            jax.ShapeDtypeStruct((length, D), bf16),
            jax.ShapeDtypeStruct((HEADS, length), f32),
        ),
        compiler_params=pltpu.CompilerParams(vmem_limit_bytes=vmem_limit),
        name="attend",
    )(projected, cosine, sine, seg_col, seg_row)


def attend_grad(qkv, grad_context, log_totals, cosine, sine, seg_col, seg_row):
    length = qkv.shape[0]
    return pl.pallas_call(
        attend_grad_kernel,
        out_shape=jax.ShapeDtypeStruct((length, D + 2 * KW), bf16),
        compiler_params=pltpu.CompilerParams(vmem_limit_bytes=vmem_limit),
        name="attend_grad",
    )(qkv, grad_context, log_totals, cosine, sine, seg_col, seg_row)


def adam_update(weight, gradient, first, second, rate, decay):
    first = beta_one * first + (1.0 - beta_one) * gradient
    second = beta_two * second + (1.0 - beta_two) * gradient * gradient
    first_hat = first / (1.0 - beta_one**STEP)
    second_hat = second / (1.0 - beta_two**STEP)
    weight = weight - rate * (first_hat / (jnp.sqrt(second_hat) + adam_eps) + decay * weight)
    return (weight, first, second)


def matmul(a, b):
    return jnp.dot(a, b, preferred_element_type=f32)


def matmul_t(a, b):
    return lax.dot_general(a, b, (((1,), (1,)), ((), ())), preferred_element_type=f32)


def matmul_tn(a, b):
    return lax.dot_general(a, b, (((0,), (0,)), ((), ())), preferred_element_type=f32)


def swap_core(block, n_dp):
    return lax.ppermute(block, "dp", [(i, i ^ 1) for i in range(n_dp)])


def plane_swap(block, k, n_tp):
    return lax.ppermute(block, "fsdp", [(i, i ^ k) for i in range(n_tp)])


def core_sum(parts, n_dp):
    core = lax.axis_index("dp") % 2
    mine = lax.dynamic_index_in_dim(parts, core, 1, keepdims=False)
    other = lax.dynamic_index_in_dim(parts, 1 - core, 1, keepdims=False)
    return mine.astype(f32) + swap_core(other, n_dp).astype(f32)


def line_sum(parts, n_dp):
    lines = n_dp // 2
    place = lax.axis_index("dp") // 2
    result = lax.dynamic_index_in_dim(parts, place, 0, keepdims=False)
    for way in (1, -1):
        arrived = None
        for step in range(1, lines):
            target = jnp.clip(place + way * (lines - step), 0, lines - 1)
            load = lax.dynamic_index_in_dim(parts, target, 0, keepdims=False).astype(f32)
            if arrived is not None:
                load = load + arrived.astype(f32)
            senders = range(step) if way == 1 else range(lines - step, lines)
            pairs = [(2 * s + c, 2 * (s + way) + c) for s in senders for c in range(2)]
            arrived = lax.ppermute(load.astype(bf16), "dp", pairs)
        result = result.astype(f32) + arrived.astype(f32)
    return result


def plane_sum(parts, n_tp):
    here = lax.axis_index("fsdp")
    total = lax.dynamic_index_in_dim(parts, here, 0, keepdims=False).astype(f32)
    for k in range(1, n_tp):
        load = lax.dynamic_index_in_dim(parts, here ^ k, 0, keepdims=False).astype(bf16)
        total = total + plane_swap(load, k, n_tp).astype(f32)
    return total


def local(
    n_dp,
    n_tp,
    inputs,
    cotangent,
    segments,
    qkv_weight,
    out_weight,
    mlp_weight,
    down_weight,
    norm_gains,
    qkv_first,
    out_first,
    mlp_first,
    down_first,
    gains_first,
    qkv_second,
    out_second,
    mlp_second,
    down_second,
    gains_second,
):
    length = inputs.shape[0]
    lines = n_dp // 2
    rows = mlp_weight.shape[0]
    down_rows = down_weight.shape[0]
    ff = n_dp * down_rows
    both = ("dp", "fsdp")
    cosine, sine = tables(segments[0])
    seg_row = segments
    seg_col = segments.reshape(length, 1)

    gains_full = lax.all_gather(norm_gains.astype(bf16), both, axis=1, tiled=True).astype(f32)
    qkv_full = lax.all_gather(qkv_weight.astype(bf16), both, axis=0, tiled=True)
    out_full = lax.all_gather(out_weight.astype(bf16), both, axis=0, tiled=True)
    mlp_parts = mlp_weight.astype(bf16).reshape(rows, 2, n_dp, n_tp, down_rows)
    mlp_parts = mlp_parts.transpose(3, 0, 1, 2, 4).reshape(n_tp, rows, 2 * ff)
    mlp_mine = lax.all_to_all(mlp_parts, "fsdp", 0, 0, tiled=True).reshape(n_tp * rows, 2 * ff)
    mlp_cols = lax.all_gather(mlp_mine, "dp", axis=0, tiled=True)
    down_cols = lax.all_gather(down_weight.astype(bf16), "dp", axis=0, tiled=True)
    grads_in = [cotangent] + [plane_swap(cotangent, k, n_tp) for k in range(1, n_tp)]

    tokens_f = inputs.astype(f32)
    gain_one, gain_two = gains_full[0], gains_full[1]
    inverse_one = lax.rsqrt(jnp.mean(tokens_f * tokens_f, axis=-1, keepdims=True) + norm_eps)
    normed_one = (tokens_f * inverse_one * gain_one).astype(bf16)
    projected = matmul(normed_one, qkv_full)
    qkv, attended, log_totals = attend(projected, cosine, sine, seg_col, seg_row)
    middle = tokens_f + matmul(attended, out_full)
    inverse_two = lax.rsqrt(jnp.mean(middle * middle, axis=-1, keepdims=True) + norm_eps)
    normed_two = (middle * inverse_two * gain_two).astype(bf16)

    normed_all = jnp.concatenate(
        [normed_two] + [plane_swap(normed_two, k, n_tp) for k in range(1, n_tp)], axis=0
    )
    grads_all = jnp.concatenate(grads_in, axis=0)
    hidden = matmul(normed_all, mlp_cols)
    gate, up_part = hidden[:, :ff], hidden[:, ff:]
    sigmoid_gate = jax.nn.sigmoid(gate)
    silu_gate = gate * sigmoid_gate
    activated = (silu_gate * up_part).astype(bf16)
    grad_act = matmul_t(grads_all, down_cols)
    grad_gate = grad_act * up_part * sigmoid_gate * (1.0 + gate * (1.0 - sigmoid_gate))
    grad_up = grad_act * silu_gate
    grad_hidden = jnp.concatenate([grad_gate, grad_up], axis=1).astype(bf16)
    grad_normed = matmul_t(grad_hidden, mlp_cols).reshape(n_tp, length, D)
    grad_normed_two = grad_normed[0]
    for k in range(1, n_tp):
        grad_normed_two = grad_normed_two + plane_swap(grad_normed[k].astype(bf16), k, n_tp).astype(f32)
    grad_down = matmul_tn(activated, grads_all).astype(bf16).reshape(lines, 2, down_rows, D)
    grad_mlp = matmul_tn(normed_all, grad_hidden).astype(bf16)
    grad_mlp = grad_mlp.reshape(lines, 2, n_tp * rows, 2 * ff)
    layer_parts = matmul(activated, down_cols).reshape(n_tp, length, D)
    layer_out = middle + layer_parts[0]
    for k in range(1, n_tp):
        layer_out = layer_out + plane_swap(layer_parts[k].astype(bf16), k, n_tp).astype(f32)
    layer_out = layer_out.astype(bf16)

    down_sum = line_sum(core_sum(grad_down, n_dp), n_dp)
    mlp_sum = line_sum(core_sum(grad_mlp, n_dp), n_dp).astype(bf16).reshape(n_tp, rows, 2 * ff)
    mlp_sum = lax.all_to_all(mlp_sum, "fsdp", 0, 0, tiled=True)
    mlp_sum = mlp_sum.reshape(n_tp, rows, 2, n_dp, down_rows).transpose(1, 2, 3, 0, 4)
    mlp_sum = mlp_sum.reshape(rows, 2 * FF).astype(f32)

    gain_grad_two = jnp.sum(grad_normed_two * middle * inverse_two, axis=0)
    weighted_two = grad_normed_two * gain_two
    grad_middle = (
        cotangent.astype(f32)
        + inverse_two * weighted_two
        - middle * inverse_two**3 * jnp.mean(weighted_two * middle, axis=-1, keepdims=True)
    )
    grad_branch = grad_middle.astype(bf16)
    grad_context = matmul_t(grad_branch, out_full).astype(bf16)
    grad_projected = attend_grad(qkv, grad_context, log_totals, cosine, sine, seg_col, seg_row)

    def scatter(grads):
        parts = grads.astype(bf16).reshape(lines, 2, n_tp, rows, -1)
        parts = core_sum(parts, n_dp).transpose(1, 0, 2, 3)
        return line_sum(plane_sum(parts, n_tp), n_dp)

    out_sum = scatter(matmul_tn(attended, grad_branch))
    qkv_sum = scatter(matmul_tn(normed_one, grad_projected))
    grad_normed_one = matmul_t(grad_projected, qkv_full)
    gain_grad_one = jnp.sum(grad_normed_one * tokens_f * inverse_one, axis=0)
    weighted_one = grad_normed_one * gain_one
    grad_inputs = (
        grad_middle
        + inverse_one * weighted_one
        - tokens_f * inverse_one**3 * jnp.mean(weighted_one * tokens_f, axis=-1, keepdims=True)
    )
    input_grad = grad_inputs.astype(bf16)
    gain_grads = jnp.stack([gain_grad_one, gain_grad_two])
    gains_sum = lax.psum_scatter(gain_grads, both, scatter_dimension=1, tiled=True)

    local_squares = (
        jnp.sum(qkv_sum * qkv_sum) + jnp.sum(out_sum * out_sum) + jnp.sum(mlp_sum * mlp_sum)
    )
    local_squares = local_squares + jnp.sum(down_sum * down_sum) + jnp.sum(gains_sum * gains_sum)
    total_squares = lax.psum(local_squares, both)
    grad_norm = jnp.sqrt(total_squares)
    clip_scale = clip_norm / jnp.maximum(grad_norm, clip_norm)
    qkv_out = adam_update(
        qkv_weight, qkv_sum * clip_scale, qkv_first, qkv_second, matrix_rate, weight_decay
    )
    out_out = adam_update(
        out_weight, out_sum * clip_scale, out_first, out_second, matrix_rate, weight_decay
    )
    mlp_out = adam_update(
        mlp_weight, mlp_sum * clip_scale, mlp_first, mlp_second, matrix_rate, weight_decay
    )
    down_out = adam_update(
        down_weight, down_sum * clip_scale, down_first, down_second, matrix_rate, weight_decay
    )
    gains_out = adam_update(
        norm_gains, gains_sum * clip_scale, gains_first, gains_second, gain_rate, 0.0
    )
    news = [[new[i] for new in (qkv_out, out_out, mlp_out, down_out, gains_out)] for i in range(3)]
    return (layer_out, input_grad, grad_norm, *news[0], *news[1], *news[2])


def solution(mesh):
    split_rows = P(("dp", "fsdp"), None)
    split_columns = P(None, ("dp", "fsdp"))
    weights = (split_rows,) * 4 + (split_columns,)
    return jax.shard_map(
        functools.partial(local, mesh.shape["dp"], mesh.shape["fsdp"]),
        mesh=mesh,
        in_specs=(split_rows,) * 3 + weights * 3,
        out_specs=(split_rows, split_rows, P()) + weights * 3,
        check_vma=False,
    )
```

```python
import functools

import jax
import jax.numpy as jnp
from jax import lax
from jax.experimental import pallas as pl
from jax.experimental.pallas import tpu as pltpu
from jax.sharding import PartitionSpec as P

D = 2048
HEADS = 32
KVH = 4
HD = 64
FF = 5632
STEP = 10
KW = KVH * HD
GROUP = HEADS // KVH


norm_eps = 1e-05
rope_base = 10000.0
beta_one = 0.9
beta_two = 0.95
adam_eps = 1e-08
weight_decay = 0.1
matrix_rate = 0.04
gain_rate = 0.8
clip_norm = 1.0

f32 = jnp.float32
bf16 = jnp.bfloat16


def tables(segment_row):
    length = segment_row.shape[0]
    token_index = jnp.arange(length, dtype=jnp.int32)
    previous = jnp.concatenate([segment_row[:1] - 1, segment_row[:-1]])
    starts = lax.cummax(jnp.where(segment_row != previous, token_index, 0), axis=0)
    position = (token_index - starts).astype(f32)
    frequency = rope_base ** (-(jnp.arange(HD // 2, dtype=f32) * 2.0 / HD))
    angles = position[:, None] * frequency[None, :]
    cosine, sine = jnp.cos(angles), jnp.sin(angles)
    cosine = jnp.concatenate([cosine] * 4, axis=-1)
    signed = jnp.concatenate([-sine, sine] * 2, axis=-1)
    return cosine, signed


def halves_swapped(pair):
    lane = lax.broadcasted_iota(jnp.int32, pair.shape, 1)
    return jnp.where(lane % HD < HD // 2, pltpu.roll(pair, 96, 1), pltpu.roll(pair, 32, 1))


def split_pair(pair):
    lane = lax.broadcasted_iota(jnp.int32, pair.shape, 1)
    zero = jnp.zeros_like(pair)
    return jnp.where(lane < HD, pair, zero), jnp.where(lane < HD, zero, pair)


def both_places(pair, odd):
    low, high = split_pair(pair)
    moved = pltpu.roll(pair.astype(f32), HD, 1).astype(pair.dtype)
    moved_low, moved_high = split_pair(moved)
    return (moved_low, high) if odd else (low, moved_high)


def dot_t(a, b):
    return lax.dot_general(a, b, (((1,), (1,)), ((), ())), preferred_element_type=f32)


def dot_n(a, b):
    return lax.dot_general(a, b, (((1,), (0,)), ((), ())), preferred_element_type=f32)


def dot_tn(a, b):
    return lax.dot_general(a, b, (((0,), (0,)), ((), ())), preferred_element_type=f32)


def mask_keys_rows(seg_col, seg_row, length):
    key_index = lax.broadcasted_iota(jnp.int32, (length, length), 0)
    query_index = lax.broadcasted_iota(jnp.int32, (length, length), 1)
    return (seg_col == seg_row) & (query_index >= key_index)


def attend_kernel(proj, cosine, sine, seg_col, seg_row, qkv, context, log_totals):
    length = proj.shape[0]
    cos, sin = cosine[...], sine[...]
    for c in range(0, D + KW, 128):
        pair = proj[:, c : c + 128]
        qkv[:, c : c + 128] = (pair * cos + halves_swapped(pair) * sin).astype(bf16)
    for c in range(D + KW, D + 2 * KW, 128):
        qkv[:, c : c + 128] = proj[:, c : c + 128].astype(bf16)
    allowed = mask_keys_rows(seg_col[...], seg_row[...], length)
    scale = HD ** (-0.5)
    for group in range(KVH):
        kc = D + (group // 2) * 128
        keys = both_places(qkv[:, kc : kc + 128], group % 2)
        values = both_places(qkv[:, kc + KW : kc + KW + 128], group % 2)

        def pair_step(pair_index, carry):
            pair = group * (GROUP // 2) + pair_index
            lanes = pl.ds(pl.multiple_of(pair * 128, 128), 128)
            queries = qkv[:, lanes]
            total = jnp.zeros((length, 128), f32)
            for side in range(2):
                scores = dot_t(keys[side], queries) * scale
                scores = jnp.where(allowed, scores, -1e30)
                top = jnp.max(scores, axis=0, keepdims=True)
                raised = jnp.exp(scores - top)
                totals = jnp.sum(raised, axis=0, keepdims=True)
                probs = (raised / totals).astype(bf16)
                total = total + dot_tn(probs, values[side])
                log_totals[pl.ds(2 * pair + side, 1), :] = top + jnp.log(totals)
            context[:, lanes] = total.astype(bf16)
            return carry

        lax.fori_loop(0, GROUP // 2, pair_step, 0)


def attend_grad_kernel(qkv, grad_context, log_totals, cosine, sine, seg_col, seg_row, grad_proj):
    length = qkv.shape[0]
    cos, sin = cosine[...], sine[...]
    allowed = mask_keys_rows(seg_col[...], seg_row[...], length)
    scale = HD ** (-0.5)

    def unrotate(pair):
        return pair * cos + halves_swapped(pair * sin)

    key_parts, value_parts = [], []
    for group in range(KVH):
        kc = D + (group // 2) * 128
        keys = both_places(qkv[:, kc : kc + 128], group % 2)
        values = both_places(qkv[:, kc + KW : kc + KW + 128], group % 2)

        def pair_step(pair_index, carry):
            grad_keys, grad_values = list(carry[:2]), list(carry[2:])
            pair = group * (GROUP // 2) + pair_index
            lanes = pl.ds(pl.multiple_of(pair * 128, 128), 128)
            queries = qkv[:, lanes]
            grads = grad_context[:, lanes]
            total = jnp.zeros((length, 128), f32)
            for side in range(2):
                scores = dot_t(keys[side], queries) * scale
                scores = jnp.where(allowed, scores, -1e30)
                probs = jnp.exp(scores - log_totals[pl.ds(2 * pair + side, 1), :])
                grad_probs = dot_t(values[side], grads)
                grad_values[side] = grad_values[side] + dot_n(probs.astype(bf16), grads)
                inner = jnp.sum(probs * grad_probs, axis=0, keepdims=True)
                raw = (probs * (grad_probs - inner) * scale).astype(bf16)
                total = total + dot_tn(raw, keys[side])
                grad_keys[side] = grad_keys[side] + dot_n(raw, queries)
            grad_proj[:, lanes] = unrotate(total).astype(bf16)
            return (*grad_keys, *grad_values)

        empty = jnp.zeros((length, 128), f32)
        out = lax.fori_loop(0, GROUP // 2, pair_step, (empty,) * 4)

        def joined(low_side, high_side):
            low, _ = split_pair(low_side)
            _, high = split_pair(high_side)
            both = low + high
            return both + pltpu.roll(both, HD, 1)

        key_parts.append(joined(out[0], out[1]))
        value_parts.append(joined(out[2], out[3]))
    lane = lax.broadcasted_iota(jnp.int32, (length, 128), 1)
    for c in range(KVH // 2):
        keys = jnp.where(lane < HD, key_parts[2 * c], key_parts[2 * c + 1])
        values = jnp.where(lane < HD, value_parts[2 * c], value_parts[2 * c + 1])
        grad_proj[:, D + c * 128 : D + (c + 1) * 128] = unrotate(keys).astype(bf16)
        grad_proj[:, D + KW + c * 128 : D + KW + (c + 1) * 128] = values.astype(bf16)


vmem_limit = 50 * 1024 * 1024


def attend(projected, cosine, sine, seg_col, seg_row):
    length = projected.shape[0]
    return pl.pallas_call(
        attend_kernel,
        out_shape=(
            jax.ShapeDtypeStruct((length, D + 2 * KW), bf16),
            jax.ShapeDtypeStruct((length, D), bf16),
            jax.ShapeDtypeStruct((HEADS, length), f32),
        ),
        compiler_params=pltpu.CompilerParams(vmem_limit_bytes=vmem_limit),
        cost_estimate=cost(18),
        name="attend",
    )(projected, cosine, sine, seg_col, seg_row)


def attend_grad(qkv, grad_context, log_totals, cosine, sine, seg_col, seg_row):
    length = qkv.shape[0]
    return pl.pallas_call(
        attend_grad_kernel,
        out_shape=jax.ShapeDtypeStruct((length, D + 2 * KW), bf16),
        compiler_params=pltpu.CompilerParams(vmem_limit_bytes=vmem_limit),
        cost_estimate=cost(26),
        name="attend_grad",
    )(qkv, grad_context, log_totals, cosine, sine, seg_col, seg_row)


MESH = pl.DeviceIdType.MESH


def cost(microseconds):
    return pl.CostEstimate(flops=0, bytes_accessed=int(microseconds * 3.69e6), transcendentals=0)


def place():
    dp = lax.axis_index("dp")
    return dp // 2, dp % 2, lax.axis_index("fsdp")


def device(line, core, plane):
    return {"dp": line * 2 + core, "fsdp": plane}


def flipped(index, bit):
    return index + bit - 2 * bit * ((index // bit) % 2)


def greet(partners, ends):
    barrier = pltpu.get_barrier_semaphore()
    count = len(partners)
    for partner in partners:
        pl.semaphore_signal(barrier, inc=1, device_id=partner, device_id_type=MESH)
    for there, partner in ends:
        count = count + there

        @pl.when(there == 1)
        def _():
            pl.semaphore_signal(barrier, inc=1, device_id=partner, device_id_type=MESH)

    pl.semaphore_wait(barrier, count)


def gather_kernel(lines, own, weight, down, full, parts, down_full, cut, line_send, line_recv, x_send, x_recv, y_send, y_recv,
                  dx_send, dx_recv, dy_send, dy_recv, core_send, core_recv, cut_send, cut_recv, down_send, down_recv, down_core_send,
                  down_core_recv, here_sem):
    z, c, f = place()
    half = own.shape[0] // 2
    fx, fy = flipped(f, 1), flipped(f, 2)
    fd = flipped(fx, 2)
    x_dev, y_dev, core_dev = device(z, c, fx), device(z, c, fy), device(z, 1 - c, f)
    has_left = jnp.minimum(z, 1)
    has_right = jnp.minimum(lines - 1 - z, 1)
    left_dev = device(jnp.maximum(z - 1, 0), c, f)
    right_dev = device(jnp.minimum(z + 1, lines - 1), c, f)
    far_dev = device(z, c, fd)
    greet([x_dev, y_dev, far_dev, core_dev], [(has_left, left_dev), (has_right, right_dev)])

    def cut_copy(k):
        to = flipped(f, k) if k < 3 else fd
        return pltpu.make_async_remote_copy(
            cut.at[to], parts.at[f], cut_send.at[k], cut_recv.at[k], device_id=device(z, c, to), device_id_type=MESH
        )

    def copy(line, plane, send, recv, dev, src=None, rows=None):
        dst = full.at[line, c, plane]
        src = dst if src is None else src
        if rows is not None:
            dst, src = dst.at[rows], src.at[rows]
        return pltpu.make_async_remote_copy(
            src, dst, send, recv, device_id=dev, device_id_type=MESH
        )

    def to_right(line, src=None):
        return copy(line, f, line_send.at[0, line], line_recv.at[line], right_dev, src)

    def to_left(line, src=None):
        return copy(line, f, line_send.at[1, line], line_recv.at[line], left_dev, src)

    def to_x(line, src=None):
        return copy(line, f, x_send.at[line], x_recv.at[line], x_dev, src)

    def to_y(line, src=None):
        return copy(line, f, y_send.at[line], y_recv.at[line], y_dev, src)

    def diag_y(line):
        return copy(line, fx, dy_send.at[line], dy_recv.at[line], y_dev, None, pl.ds(0, half))

    def diag_x(line):
        return copy(line, fy, dx_send.at[line], dx_recv.at[line], x_dev, None, pl.ds(half, half))

    def to_core(line, plane, src=None):
        return copy(line, plane, core_send.at[line, plane], core_recv.at[line, plane], core_dev, src)

    def down_copy(line, way, src=None):
        dst = down_full.at[line, c]
        return pltpu.make_async_remote_copy(
            dst if src is None else src, dst, down_send.at[way, line], down_recv.at[line],
            device_id=(right_dev, left_dev)[way], device_id_type=MESH,
        )

    def down_core(line, src=None):
        dst = down_full.at[line, c]
        return pltpu.make_async_remote_copy(
            dst if src is None else src, dst, down_core_send.at[line], down_core_recv.at[line],
            device_id=core_dev, device_id_type=MESH,
        )

    here = pltpu.make_async_copy(own, full.at[z, c, f], here_sem.at[0])
    here.start()
    here_down = pltpu.make_async_copy(down, down_full.at[z, c], here_sem.at[2])
    here_down.start()

    @pl.when(has_right == 1)
    def _():
        to_right(z, own).start()

    @pl.when(has_left == 1)
    def _():
        to_left(z, own).start()

    to_x(z, own).start()
    to_y(z, own).start()
    to_core(z, f, own).start()

    cut_columns(weight, cut, 2 * lines, 4)
    here_cut = pltpu.make_async_copy(cut.at[f], parts.at[f], here_sem.at[1])
    here_cut.start()
    for k in range(1, 4):
        cut_copy(k).start()

    down_core(z, down).start()
    for t in range(1, lines):

        @pl.when(z >= t)
        def _():
            line = z - t
            to_right(line).wait_recv()

            @pl.when(has_right == 1)
            def _():
                to_right(line).start()

            to_x(line).start()
            to_y(line).start()
            to_core(line, f).start()

        @pl.when(z + t <= lines - 1)
        def _():
            line = z + t
            to_left(line).wait_recv()

            @pl.when(has_left == 1)
            def _():
                to_left(line).start()

            to_x(line).start()
            to_y(line).start()
            to_core(line, f).start()

    @pl.when(has_right == 1)
    def _():
        down_copy(z, 0, down).start()

    @pl.when(has_left == 1)
    def _():
        down_copy(z, 1, down).start()

    here.wait()
    order = []
    for t in range(lines):
        line = z
        for b in range(lines.bit_length() - 1):
            if t >> b & 1:
                line = flipped(line, 1 << b)
        order.append(line)
    for t, line in enumerate(order):
        to_x(line).wait_recv()
        diag_y(line).start()
        to_core(line, fx).start()
        to_y(line).wait_recv()
        diag_x(line).start()
        to_core(line, fy).start()
        if t == 0:
            continue

        @pl.when(z >= t)
        def _():
            down_copy(z - t, 0).wait_recv()

            @pl.when(has_right == 1)
            def _():
                down_copy(z - t, 0).start()

            down_core(z - t).start()

        @pl.when(z + t <= lines - 1)
        def _():
            down_copy(z + t, 1).wait_recv()

            @pl.when(has_left == 1)
            def _():
                down_copy(z + t, 1).start()

            down_core(z + t).start()

    for line in order:
        diag_y(line).wait_recv()
        diag_x(line).wait_recv()
        to_core(line, fd).start()
    here_cut.wait()
    here_down.wait()
    for k in range(1, 4):
        cut_copy(k).wait()
    for line in range(lines):
        for plane in range(4):
            to_core(line, plane).wait()
        to_x(line).wait_send()
        to_y(line).wait_send()
        diag_x(line).wait_send()
        diag_y(line).wait_send()

        down_core(line).wait()

        @pl.when((line <= z) & (has_right == 1))
        def _():
            to_right(line).wait_send()
            down_copy(line, 0).wait_send()

        @pl.when((line >= z) & (has_left == 1))
        def _():
            to_left(line).wait_send()
            down_copy(line, 1).wait_send()


def gather_all(shard, weight, down, n_dp, n_tp):
    rows, columns = shard.shape
    width = weight.shape[1] // n_tp
    lines = n_dp // 2
    if n_tp != 4 or rows % 32:
        full = lax.all_gather(shard, ("dp", "fsdp"), axis=0, tiled=True)
        down_full = lax.all_gather(down, "dp", axis=0, tiled=True)
        return full, columns_out(weight, n_dp, n_tp), down_full
    dma = pltpu.SemaphoreType.DMA
    hbm = pl.BlockSpec(memory_space=pl.ANY)
    full, parts, down_full = pl.pallas_call(
        functools.partial(gather_kernel, lines),
        out_shape=(
            jax.ShapeDtypeStruct((lines, 2, n_tp, rows, columns), bf16),
            jax.ShapeDtypeStruct((n_tp, rows, width), bf16),
            jax.ShapeDtypeStruct((lines, 2, *down.shape), bf16),
        ),
        in_specs=[hbm, pl.BlockSpec(memory_space=pltpu.VMEM), hbm],
        out_specs=(hbm, hbm, hbm),
        scratch_shapes=[pltpu.VMEM((n_tp, rows, width), bf16), dma((2, lines))]
        + [dma((lines,))] * 9
        + [dma((lines, n_tp))] * 2
        + [dma((n_tp,)), dma((n_tp,)), dma((2, lines)), dma((lines,)), dma((lines,)), dma((lines,)), dma((3,))],
        compiler_params=pltpu.CompilerParams(
            collective_id=0, has_side_effects=True, vmem_limit_bytes=vmem_limit
        ),
        cost_estimate=cost(100),
        name="gather_all",
    )(shard, weight, down)
    full = full.reshape(n_dp * n_tp * rows, columns)
    return full, parts, down_full.reshape(n_dp * down.shape[0], down.shape[1])


def cut_columns(weight, cut, n_dp, n_tp):
    unit = weight.shape[1] // (2 * n_dp * n_tp)
    half = n_dp * unit
    for to in range(n_tp):
        for side in range(2):
            starts = [side * n_tp * half + (j * n_tp + to) * unit for j in range(n_dp)]
            pieces = [weight[:, start : start + unit] for start in starts]
            cut[to, :, side * half : (side + 1) * half] = jnp.concatenate(pieces, axis=1).astype(bf16)


def columns_out_kernel(n_dp, n_tp, weight, parts, cut, send, recv, here_sem):
    z, c, f = place()
    greet([device(z, c, (f + k) % n_tp) for k in range(1, n_tp)], [])

    def away(k):
        to = (f + k) % n_tp
        return pltpu.make_async_remote_copy(
            cut.at[to], parts.at[f], send.at[k], recv.at[k], device_id=device(z, c, to), device_id_type=MESH
        )

    cut_columns(weight, cut, n_dp, n_tp)
    for k in range(1, n_tp):
        away(k).start()
    here = pltpu.make_async_copy(cut.at[f], parts.at[f], here_sem)
    here.start()
    here.wait()
    for k in range(1, n_tp):
        away(k).wait()


def columns_out(weight, n_dp, n_tp):
    rows, width = weight.shape
    dma = pltpu.SemaphoreType.DMA
    return pl.pallas_call(
        functools.partial(columns_out_kernel, n_dp, n_tp),
        out_shape=jax.ShapeDtypeStruct((n_tp, rows, width // n_tp), bf16),
        out_specs=pl.BlockSpec(memory_space=pl.ANY),
        scratch_shapes=[
            pltpu.VMEM((n_tp, rows, width // n_tp), bf16), dma((n_tp,)), dma((n_tp,)), dma(()),
        ],
        compiler_params=pltpu.CompilerParams(
            collective_id=1, has_side_effects=True, vmem_limit_bytes=vmem_limit
        ),
        cost_estimate=cost(20),
        name="columns_out",
    )(weight)


def columns_back_kernel(n_dp, n_tp, parts, whole, got, send, recv, here_sem):
    z, c, f = place()
    greet([device(z, c, (f + k) % n_tp) for k in range(1, n_tp)], [])
    unit = whole.shape[1] // (2 * n_dp * n_tp)
    half = n_dp * unit

    def away(k):
        to = (f + k) % n_tp
        return pltpu.make_async_remote_copy(
            parts.at[to], got.at[f], send.at[k], recv.at[k], device_id=device(z, c, to), device_id_type=MESH
        )

    for k in range(1, n_tp):
        away(k).start()
    here = pltpu.make_async_copy(parts.at[f], got.at[f], here_sem)
    here.start()
    here.wait()
    for k in range(1, n_tp):
        away(k).wait()
    for side in range(2):
        pieces = [
            got[frm, :, side * half + j * unit : side * half + (j + 1) * unit].astype(f32)
            for j in range(n_dp)
            for frm in range(n_tp)
        ]
        whole[:, side * n_tp * half : (side + 1) * n_tp * half] = jnp.concatenate(pieces, axis=1)


def columns_back(parts, n_dp, n_tp):
    _, rows, width = parts.shape
    dma = pltpu.SemaphoreType.DMA
    return pl.pallas_call(
        functools.partial(columns_back_kernel, n_dp, n_tp),
        out_shape=jax.ShapeDtypeStruct((rows, width * n_tp), f32),
        in_specs=[pl.BlockSpec(memory_space=pl.ANY)],
        scratch_shapes=[pltpu.VMEM(parts.shape, bf16), dma((n_tp,)), dma((n_tp,)), dma(())],
        compiler_params=pltpu.CompilerParams(
            collective_id=2, has_side_effects=True, vmem_limit_bytes=vmem_limit
        ),
        cost_estimate=cost(20),
        name="columns_back",
    )(parts)


def total_kernel(n_dp, n_tp, value, total, held, got, send, recv):
    dp, f = lax.axis_index("dp"), lax.axis_index("fsdp")
    partners = []
    for axis, size in (("dp", n_dp), ("fsdp", n_tp)):
        for bit in range(size.bit_length() - 1):
            index = {"dp": dp, "fsdp": f}
            index[axis] = flipped(index[axis], 1 << bit)
            partners.append(index)
    greet(partners, [])
    held[0] = value[...]
    for step, partner in enumerate(partners):
        swap = pltpu.make_async_remote_copy(
            held.at[step], got.at[step], send.at[step], recv.at[step], device_id=partner, device_id_type=MESH
        )
        swap.start()
        swap.wait()
        held[step + 1] = held[step] + got[step]
    total[...] = held[len(partners)]


def total_over_devices(value, n_dp, n_tp):
    steps = (n_dp * n_tp).bit_length() - 1
    dma = pltpu.SemaphoreType.DMA
    tile = (8, 128)
    spread = pl.pallas_call(
        functools.partial(total_kernel, n_dp, n_tp),
        out_shape=jax.ShapeDtypeStruct(tile, f32),
        scratch_shapes=[
            pltpu.VMEM((steps + 1, *tile), f32), pltpu.VMEM((steps, *tile), f32), dma((steps,)), dma((steps,)),
        ],
        compiler_params=pltpu.CompilerParams(collective_id=3, has_side_effects=True),
        cost_estimate=cost(13),
        name="total",
    )(jnp.broadcast_to(value, tile))
    return spread[0, 0]


def adam_update(weight, gradient, first, second, rate, decay):
    first = beta_one * first + (1.0 - beta_one) * gradient
    second = beta_two * second + (1.0 - beta_two) * gradient * gradient
    first_hat = first / (1.0 - beta_one**STEP)
    second_hat = second / (1.0 - beta_two**STEP)
    weight = weight - rate * (first_hat / (jnp.sqrt(second_hat) + adam_eps) + decay * weight)
    return (weight, first, second)


def matmul(a, b):
    return jnp.dot(a, b, preferred_element_type=f32)


def matmul_t(a, b):
    return lax.dot_general(a, b, (((1,), (1,)), ((), ())), preferred_element_type=f32)


def matmul_tn(a, b):
    return lax.dot_general(a, b, (((0,), (0,)), ((), ())), preferred_element_type=f32)


def swap_core(block, n_dp):
    return lax.ppermute(block, "dp", [(i, i ^ 1) for i in range(n_dp)])


def plane_swap(block, k, n_tp):
    return lax.ppermute(block, "fsdp", [(i, i ^ k) for i in range(n_tp)])


def plane_gather(block, n_tp):
    if n_tp != 4:
        return jnp.concatenate([block] + [plane_swap(block, k, n_tp) for k in range(1, n_tp)], axis=0)
    half = block.shape[0] // 2
    over_x, over_y = plane_swap(block, 1, n_tp), plane_swap(block, 2, n_tp)
    far = [plane_swap(over_y[:half], 1, n_tp), plane_swap(over_x[half:], 2, n_tp)]
    return jnp.concatenate([block, over_x, over_y] + far, axis=0)


def core_sum(parts, n_dp):
    core = lax.axis_index("dp") % 2
    mine = lax.dynamic_index_in_dim(parts, core, 1, keepdims=False)
    other = lax.dynamic_index_in_dim(parts, 1 - core, 1, keepdims=False)
    return mine.astype(f32) + swap_core(other, n_dp).astype(f32)


def line_sum(parts, n_dp):
    lines = n_dp // 2
    place = lax.axis_index("dp") // 2
    result = lax.dynamic_index_in_dim(parts, place, 0, keepdims=False)
    for way in (1, -1):
        arrived = None
        for step in range(1, lines):
            target = jnp.clip(place + way * (lines - step), 0, lines - 1)
            load = lax.dynamic_index_in_dim(parts, target, 0, keepdims=False).astype(f32)
            if arrived is not None:
                load = load + arrived.astype(f32)
            senders = range(step) if way == 1 else range(lines - step, lines)
            pairs = [(2 * s + c, 2 * (s + way) + c) for s in senders for c in range(2)]
            arrived = lax.ppermute(load.astype(bf16), "dp", pairs)
        result = result.astype(f32) + arrived.astype(f32)
    return result


def plane_sum(parts, n_tp):
    here = lax.axis_index("fsdp")
    total = lax.dynamic_index_in_dim(parts, here, 0, keepdims=False).astype(f32)
    for k in range(1, n_tp):
        load = lax.dynamic_index_in_dim(parts, here ^ k, 0, keepdims=False).astype(bf16)
        total = total + plane_swap(load, k, n_tp).astype(f32)
    return total


def by_rows(rows, body):
    def step(i, carry):
        body(pl.ds(pl.multiple_of(i * 16, 16), 16))
        return carry

    lax.fori_loop(0, rows // 16, step, 0)


def scatter_kernel(lines, n_arrays, *refs):
    groups = [refs[i * n_arrays : (i + 1) * n_arrays] for i in range(8)]
    arrays, outs, sums, others, firsts, seconds, alongs, leaving = groups
    load_sem, core_send, core_recv, one_send, one_recv, two_send, two_recv, line_send, line_recv = refs[8 * n_arrays :]
    z, c, f = place()
    planes, rows = sums[0].shape[1:3]
    half = rows // 2
    fx, fy = flipped(f, 1), flipped(f, 2)
    fd = flipped(fx, 2)
    x_dev, y_dev, core_dev = device(z, c, fx), device(z, c, fy), device(z, 1 - c, f)
    has_left = jnp.minimum(z, 1)
    has_right = jnp.minimum(lines - 1 - z, 1)
    left_dev = device(jnp.maximum(z - 1, 0), c, f)
    right_dev = device(jnp.minimum(z + 1, lines - 1), c, f)
    greet([x_dev, y_dev, core_dev], [(has_left, left_dev), (has_right, right_dev)])
    halves = (pl.ds(0, half), pl.ds(half, half))
    near, next_near, step_dev = (fx, fy), (fy, fx), (x_dev, y_dev)

    def remote(src, dst, send, recv, dev):
        return pltpu.make_async_remote_copy(src, dst, send, recv, device_id=dev, device_id_type=MESH)

    def to_core(a, d):
        return remote(arrays[a].at[d, 1 - c], others[a].at[d], core_send.at[a, d], core_recv.at[a, d], core_dev)

    def load(a, d):
        return pltpu.make_async_copy(arrays[a].at[d, c], sums[a].at[d], load_sem.at[a, d])

    def one(a, d, way, i):
        block = (near[way], fd)[i]
        return remote(
            sums[a].at[d, block, halves[way]], firsts[a].at[way, d, i],
            one_send.at[a, d, way, i], one_recv.at[a, d, way, i], step_dev[way],
        )

    def two(a, d, way):
        return remote(
            sums[a].at[d, next_near[way], halves[way]], seconds[a].at[way, d],
            two_send.at[a, d, way], two_recv.at[a, d, way], step_dev[1 - way],
        )

    def to_right(a, d):
        return remote(leaving[a].at[d], alongs[a].at[d], line_send.at[a, d], line_recv.at[a, d], right_dev)

    def to_left(a, d, slot):
        return remote(leaving[a].at[d], alongs[a].at[slot], line_send.at[a, d], line_recv.at[a, slot], left_dev)

    def add_along(a, slot):
        def step(r):
            outs[a][r] += alongs[a][slot, r].astype(f32)

        by_rows(rows, step)

    order = []
    for t in reversed(range(lines)):
        line = z
        for b in range(lines.bit_length() - 1):
            if t >> b & 1:
                line = flipped(line, 1 << b)
        order.append(line)
    chunks = [(a, d) for d in order for a in range(n_arrays)]
    for a, d in chunks:
        to_core(a, d).start()
        load(a, d).start()
    for a, d in chunks:
        load(a, d).wait()
        to_core(a, d).wait_recv()

        def core_add(r):
            for plane in range(planes):
                sums[a][d, plane, r] = (sums[a][d, plane, r].astype(f32) + others[a][d, plane, r].astype(f32)).astype(bf16)

        by_rows(rows, core_add)
        for i in (1, 0):
            for way in range(2):
                one(a, d, way, i).start()
    for a, d in chunks:
        for way in range(2):
            one(a, d, way, 1).wait_recv()

            def first_add(r):
                there = pl.ds(pl.multiple_of(r.start + way * half, 16), r.size)
                mine = sums[a][d, next_near[way], there].astype(f32)
                sums[a][d, next_near[way], there] = (mine + firsts[a][way, d, 1, r].astype(f32)).astype(bf16)

            by_rows(half, first_add)
            two(a, d, way).start()
    for a, d in chunks:
        for way in range(2):
            one(a, d, way, 0).wait_recv()
            two(a, d, way).wait_recv()

            def second_add(r):
                there = pl.ds(pl.multiple_of(r.start + way * half, 16), r.size)
                outs[a][there] = (
                    sums[a][d, f, there].astype(f32)
                    + firsts[a][way, d, 0, r].astype(f32)
                    + seconds[a][way, d, r].astype(f32)
                )

            by_rows(half, second_add)

        @pl.when((d > z) & (has_left == 1))
        def _():
            to_right(a, d).wait_recv()
            add_along(a, d)

        @pl.when((d < z) & (has_right == 1))
        def _():
            to_left(a, d, d).wait_recv()
            add_along(a, d)

        @pl.when(d != z)
        def _():
            def leave(r):
                leaving[a][d, r] = outs[a][r].astype(bf16)

            by_rows(rows, leave)

        @pl.when(d > z)
        def _():
            to_right(a, d).start()

        @pl.when((d < z) & (d + 1 < z))
        def _():
            to_left(a, d, d).start()

        @pl.when(d + 1 == z)
        def _():
            to_left(a, d, lines).start()

    for a in range(n_arrays):

        @pl.when(has_left == 1)
        def _():
            to_right(a, z).wait_recv()
            add_along(a, z)

        @pl.when(has_right == 1)
        def _():
            to_left(a, z, lines).wait_recv()
            add_along(a, lines)

    for a, d in chunks:
        to_core(a, d).wait_send()
        for way in range(2):
            one(a, d, way, 0).wait_send()
            one(a, d, way, 1).wait_send()
            two(a, d, way).wait_send()

        @pl.when(d != z)
        def _():
            to_right(a, d).wait_send()


def scatter_all(arrays, n_dp, n_tp):
    lines = n_dp // 2
    rows = arrays[0].shape[0] // (n_dp * n_tp)
    if n_tp != 4 or rows % 32:
        results = []
        for array in arrays:
            parts = core_sum(array.reshape(lines, 2, n_tp, rows, -1), n_dp)
            results.append(line_sum(plane_sum(parts.transpose(1, 0, 2, 3), n_tp), n_dp))
        return results
    dma = pltpu.SemaphoreType.DMA
    widths = [array.shape[1] for array in arrays]
    n = len(widths)
    shapes = [
        (lines, n_tp, rows), (lines, n_tp, rows), (2, lines, 2, rows // 2), (2, lines, rows // 2),
        (lines + 1, rows), (lines, rows),
    ]
    return pl.pallas_call(
        functools.partial(scatter_kernel, lines, n),
        out_shape=[jax.ShapeDtypeStruct((rows, width), f32) for width in widths],
        in_specs=[pl.BlockSpec(memory_space=pl.ANY)] * n,
        scratch_shapes=[pltpu.VMEM((*shape, width), bf16) for shape in shapes for width in widths]
        + [dma((n, lines))] * 3
        + [dma((n, lines, 2, 2))] * 2
        + [dma((n, lines, 2))] * 2
        + [dma((n, lines)), dma((n, lines + 1))],
        compiler_params=pltpu.CompilerParams(
            collective_id=4, has_side_effects=True, vmem_limit_bytes=vmem_limit
        ),
        cost_estimate=cost(110),
        name="scatter_all",
    )(*[array.reshape(lines, 2, n_tp, rows, -1) for array in arrays])


def local(
    n_dp,
    n_tp,
    inputs,
    cotangent,
    segments,
    qkv_weight,
    out_weight,
    mlp_weight,
    down_weight,
    norm_gains,
    qkv_first,
    out_first,
    mlp_first,
    down_first,
    gains_first,
    qkv_second,
    out_second,
    mlp_second,
    down_second,
    gains_second,
):
    length = inputs.shape[0]
    lines = n_dp // 2
    rows = mlp_weight.shape[0]
    down_rows = down_weight.shape[0]
    ff = n_dp * down_rows
    cosine, sine = tables(segments[0])
    seg_row = segments
    seg_col = segments.reshape(length, 1)

    shard = jnp.concatenate(
        [qkv_weight, out_weight, jnp.pad(norm_gains.T, ((0, 0), (0, 126)))], axis=1
    ).astype(bf16)
    attn_full, mlp_parts, down_cols = gather_all(shard, mlp_weight, down_weight.astype(bf16), n_dp, n_tp)
    qkv_full = attn_full[:, : D + 2 * KW]
    out_full = attn_full[:, D + 2 * KW : 2 * D + 2 * KW]
    gains_full = attn_full[:, 2 * D + 2 * KW :].astype(f32).T
    mlp_cols = lax.all_gather(mlp_parts.reshape(n_tp * rows, 2 * ff), "dp", axis=0, tiled=True)
    grads_late, _ = lax.optimization_barrier((cotangent, attn_full))
    grads_all = plane_gather(grads_late, n_tp)

    tokens_f = inputs.astype(f32)
    gain_one, gain_two = gains_full[0], gains_full[1]
    inverse_one = lax.rsqrt(jnp.mean(tokens_f * tokens_f, axis=-1, keepdims=True) + norm_eps)
    normed_one = (tokens_f * inverse_one * gain_one).astype(bf16)
    projected = matmul(normed_one, qkv_full)
    qkv, attended, log_totals = attend(projected, cosine, sine, seg_col, seg_row)
    middle = tokens_f + matmul(attended, out_full)
    inverse_two = lax.rsqrt(jnp.mean(middle * middle, axis=-1, keepdims=True) + norm_eps)
    normed_two = (middle * inverse_two * gain_two).astype(bf16)

    normed_all = plane_gather(normed_two, n_tp)
    hidden = matmul(normed_all, mlp_cols)
    gate, up_part = hidden[:, :ff], hidden[:, ff:]
    sigmoid_gate = jax.nn.sigmoid(gate)
    silu_gate = gate * sigmoid_gate
    activated = (silu_gate * up_part).astype(bf16)
    grad_act = matmul_t(grads_all, down_cols)
    grad_gate = grad_act * up_part * sigmoid_gate * (1.0 + gate * (1.0 - sigmoid_gate))
    grad_up = grad_act * silu_gate
    grad_hidden = jnp.concatenate([grad_gate, grad_up], axis=1).astype(bf16)
    grad_normed = matmul_t(grad_hidden, mlp_cols).reshape(n_tp, length, D)
    grad_normed_two = grad_normed[0]
    for k in range(1, n_tp):
        grad_normed_two = grad_normed_two + plane_swap(grad_normed[k].astype(bf16), k, n_tp).astype(f32)
    grad_down = matmul_tn(activated, grads_all).astype(bf16)
    grad_mlp = matmul_tn(normed_all, grad_hidden).astype(bf16)
    layer_parts = matmul(activated, down_cols).astype(bf16).reshape(n_tp, length, D)
    layer_parts, _ = lax.optimization_barrier((layer_parts, grad_normed_two))
    layer_out = middle + layer_parts[0]
    for k in range(1, n_tp):
        layer_out = layer_out + plane_swap(layer_parts[k], k, n_tp).astype(f32)
    layer_out = layer_out.astype(bf16)

    down_sum = lax.psum_scatter(grad_down, "dp", scatter_dimension=0, tiled=True).astype(f32)
    mlp_sum = lax.psum_scatter(grad_mlp, "dp", scatter_dimension=0, tiled=True)
    mlp_sum = columns_back(mlp_sum.reshape(n_tp, rows, 2 * ff), n_dp, n_tp)

    gain_grad_two = jnp.sum(grad_normed_two * middle * inverse_two, axis=0)
    weighted_two = grad_normed_two * gain_two
    grad_middle = (
        cotangent.astype(f32)
        + inverse_two * weighted_two
        - middle * inverse_two**3 * jnp.mean(weighted_two * middle, axis=-1, keepdims=True)
    )
    grad_branch = grad_middle.astype(bf16)
    grad_context = matmul_t(grad_branch, out_full).astype(bf16)
    grad_projected = attend_grad(qkv, grad_context, log_totals, cosine, sine, seg_col, seg_row)

    grad_out = matmul_tn(attended, grad_branch).astype(bf16)
    grad_qkv = matmul_tn(normed_one, grad_projected)
    grad_normed_one = matmul_t(grad_projected, qkv_full)
    gain_grad_one = jnp.sum(grad_normed_one * tokens_f * inverse_one, axis=0)
    weighted_one = grad_normed_one * gain_one
    grad_inputs = (
        grad_middle
        + inverse_one * weighted_one
        - tokens_f * inverse_one**3 * jnp.mean(weighted_one * tokens_f, axis=-1, keepdims=True)
    )
    input_grad = grad_inputs.astype(bf16)
    gain_grads = jnp.pad(jnp.stack([gain_grad_one, gain_grad_two], axis=1), ((0, 0), (0, 126)))
    grad_qkv = jnp.concatenate([grad_qkv.astype(bf16), gain_grads.astype(bf16)], axis=1)
    out_sum, qkv_sum = scatter_all([grad_out, grad_qkv], n_dp, n_tp)
    gains_sum = qkv_sum[:, D + 2 * KW : D + 2 * KW + 2].T
    qkv_sum = qkv_sum[:, : D + 2 * KW]

    local_squares = (
        jnp.sum(qkv_sum * qkv_sum) + jnp.sum(out_sum * out_sum) + jnp.sum(mlp_sum * mlp_sum)
    )
    local_squares = local_squares + jnp.sum(down_sum * down_sum) + jnp.sum(gains_sum * gains_sum)
    total_squares = total_over_devices(local_squares, n_dp, n_tp)
    grad_norm = jnp.sqrt(total_squares)
    clip_scale = clip_norm / jnp.maximum(grad_norm, clip_norm)
    qkv_out = adam_update(
        qkv_weight, qkv_sum * clip_scale, qkv_first, qkv_second, matrix_rate, weight_decay
    )
    out_out = adam_update(
        out_weight, out_sum * clip_scale, out_first, out_second, matrix_rate, weight_decay
    )
    mlp_out = adam_update(
        mlp_weight, mlp_sum * clip_scale, mlp_first, mlp_second, matrix_rate, weight_decay
    )
    down_out = adam_update(
        down_weight, down_sum * clip_scale, down_first, down_second, matrix_rate, weight_decay
    )
    gains_out = adam_update(
        norm_gains, gains_sum * clip_scale, gains_first, gains_second, gain_rate, 0.0
    )
    news = [[new[i] for new in (qkv_out, out_out, mlp_out, down_out, gains_out)] for i in range(3)]
    return (layer_out, input_grad, grad_norm, *news[0], *news[1], *news[2])


def solution(mesh):
    split_rows = P(("dp", "fsdp"), None)
    split_columns = P(None, ("dp", "fsdp"))
    weights = (split_rows,) * 4 + (split_columns,)
    return jax.shard_map(
        functools.partial(local, mesh.shape["dp"], mesh.shape["fsdp"]),
        mesh=mesh,
        in_specs=(split_rows,) * 3 + weights * 3,
        out_specs=(split_rows, split_rows, P()) + weights * 3,
        check_vma=False,
    )
```

```python
import functools

import jax
import jax.numpy as jnp
from jax import lax
from jax.experimental import pallas as pl
from jax.experimental.pallas import tpu as pltpu
from jax.sharding import PartitionSpec as P

D = 2048
HEADS = 32
KVH = 4
HD = 64
FF = 5632
STEP = 10
KW = KVH * HD
GROUP = HEADS // KVH


norm_eps = 1e-05
rope_base = 10000.0
beta_one = 0.9
beta_two = 0.95
adam_eps = 1e-08
weight_decay = 0.1
matrix_rate = 0.04
gain_rate = 0.8
clip_norm = 1.0

f32 = jnp.float32
bf16 = jnp.bfloat16


def tables(segment_row):
    length = segment_row.shape[0]
    token_index = jnp.arange(length, dtype=jnp.int32)
    previous = jnp.concatenate([segment_row[:1] - 1, segment_row[:-1]])
    starts = lax.cummax(jnp.where(segment_row != previous, token_index, 0), axis=0)
    position = (token_index - starts).astype(f32)
    frequency = rope_base ** (-(jnp.arange(HD // 2, dtype=f32) * 2.0 / HD))
    angles = position[:, None] * frequency[None, :]
    cosine, sine = jnp.cos(angles), jnp.sin(angles)
    cosine = jnp.concatenate([cosine] * 4, axis=-1)
    signed = jnp.concatenate([-sine, sine] * 2, axis=-1)
    return cosine, signed


def halves_swapped(pair):
    lane = lax.broadcasted_iota(jnp.int32, pair.shape, 1)
    return jnp.where(lane % HD < HD // 2, pltpu.roll(pair, 96, 1), pltpu.roll(pair, 32, 1))


def split_pair(pair):
    lane = lax.broadcasted_iota(jnp.int32, pair.shape, 1)
    zero = jnp.zeros_like(pair)
    return jnp.where(lane < HD, pair, zero), jnp.where(lane < HD, zero, pair)


def both_places(pair, odd):
    low, high = split_pair(pair)
    moved = pltpu.roll(pair.astype(f32), HD, 1).astype(pair.dtype)
    moved_low, moved_high = split_pair(moved)
    return (moved_low, high) if odd else (low, moved_high)


def dot_t(a, b):
    return lax.dot_general(a, b, (((1,), (1,)), ((), ())), preferred_element_type=f32)


def dot_n(a, b):
    return lax.dot_general(a, b, (((1,), (0,)), ((), ())), preferred_element_type=f32)


def dot_tn(a, b):
    return lax.dot_general(a, b, (((0,), (0,)), ((), ())), preferred_element_type=f32)


def mask_keys_rows(seg_col, seg_row, length):
    key_index = lax.broadcasted_iota(jnp.int32, (length, length), 0)
    query_index = lax.broadcasted_iota(jnp.int32, (length, length), 1)
    return (seg_col == seg_row) & (query_index >= key_index)


def attend_kernel(proj, cosine, sine, seg_col, seg_row, qkv, context, log_totals):
    length = proj.shape[0]
    cos, sin = cosine[...], sine[...]
    for c in range(0, D + KW, 128):
        pair = proj[:, c : c + 128]
        qkv[:, c : c + 128] = (pair * cos + halves_swapped(pair) * sin).astype(bf16)
    for c in range(D + KW, D + 2 * KW, 128):
        qkv[:, c : c + 128] = proj[:, c : c + 128].astype(bf16)
    allowed = mask_keys_rows(seg_col[...], seg_row[...], length)
    scale = HD ** (-0.5)
    for group in range(KVH):
        kc = D + (group // 2) * 128
        keys = both_places(qkv[:, kc : kc + 128], group % 2)
        values = both_places(qkv[:, kc + KW : kc + KW + 128], group % 2)

        def pair_step(pair_index, carry):
            pair = group * (GROUP // 2) + pair_index
            lanes = pl.ds(pl.multiple_of(pair * 128, 128), 128)
            queries = qkv[:, lanes]
            total = jnp.zeros((length, 128), f32)
            for side in range(2):
                scores = dot_t(keys[side], queries) * scale
                scores = jnp.where(allowed, scores, -1e30)
                top = jnp.max(scores, axis=0, keepdims=True)
                raised = jnp.exp(scores - top)
                totals = jnp.sum(raised, axis=0, keepdims=True)
                probs = (raised / totals).astype(bf16)
                total = total + dot_tn(probs, values[side])
                log_totals[pl.ds(2 * pair + side, 1), :] = top + jnp.log(totals)
            context[:, lanes] = total.astype(bf16)
            return carry

        lax.fori_loop(0, GROUP // 2, pair_step, 0)


def attend_grad_kernel(qkv, grad_context, log_totals, cosine, sine, seg_col, seg_row, grad_proj):
    length = qkv.shape[0]
    cos, sin = cosine[...], sine[...]
    allowed = mask_keys_rows(seg_col[...], seg_row[...], length)
    scale = HD ** (-0.5)

    def unrotate(pair):
        return pair * cos + halves_swapped(pair * sin)

    key_parts, value_parts = [], []
    for group in range(KVH):
        kc = D + (group // 2) * 128
        keys = both_places(qkv[:, kc : kc + 128], group % 2)
        values = both_places(qkv[:, kc + KW : kc + KW + 128], group % 2)

        def pair_step(pair_index, carry):
            grad_keys, grad_values = list(carry[:2]), list(carry[2:])
            pair = group * (GROUP // 2) + pair_index
            lanes = pl.ds(pl.multiple_of(pair * 128, 128), 128)
            queries = qkv[:, lanes]
            grads = grad_context[:, lanes]
            total = jnp.zeros((length, 128), f32)
            for side in range(2):
                scores = dot_t(keys[side], queries) * scale
                scores = jnp.where(allowed, scores, -1e30)
                probs = jnp.exp(scores - log_totals[pl.ds(2 * pair + side, 1), :])
                grad_probs = dot_t(values[side], grads)
                grad_values[side] = grad_values[side] + dot_n(probs.astype(bf16), grads)
                inner = jnp.sum(probs * grad_probs, axis=0, keepdims=True)
                raw = (probs * (grad_probs - inner) * scale).astype(bf16)
                total = total + dot_tn(raw, keys[side])
                grad_keys[side] = grad_keys[side] + dot_n(raw, queries)
            grad_proj[:, lanes] = unrotate(total).astype(bf16)
            return (*grad_keys, *grad_values)

        empty = jnp.zeros((length, 128), f32)
        out = lax.fori_loop(0, GROUP // 2, pair_step, (empty,) * 4)

        def joined(low_side, high_side):
            low, _ = split_pair(low_side)
            _, high = split_pair(high_side)
            both = low + high
            return both + pltpu.roll(both, HD, 1)

        key_parts.append(joined(out[0], out[1]))
        value_parts.append(joined(out[2], out[3]))
    lane = lax.broadcasted_iota(jnp.int32, (length, 128), 1)
    for c in range(KVH // 2):
        keys = jnp.where(lane < HD, key_parts[2 * c], key_parts[2 * c + 1])
        values = jnp.where(lane < HD, value_parts[2 * c], value_parts[2 * c + 1])
        grad_proj[:, D + c * 128 : D + (c + 1) * 128] = unrotate(keys).astype(bf16)
        grad_proj[:, D + KW + c * 128 : D + KW + (c + 1) * 128] = values.astype(bf16)


vmem_limit = 50 * 1024 * 1024
feed_vmem_limit = 62 * 1024 * 1024


def attend(projected, cosine, sine, seg_col, seg_row):
    length = projected.shape[0]
    return pl.pallas_call(
        attend_kernel,
        out_shape=(
            jax.ShapeDtypeStruct((length, D + 2 * KW), bf16),
            jax.ShapeDtypeStruct((length, D), bf16),
            jax.ShapeDtypeStruct((HEADS, length), f32),
        ),
        compiler_params=pltpu.CompilerParams(vmem_limit_bytes=vmem_limit),
        cost_estimate=cost(18),
        name="attend",
    )(projected, cosine, sine, seg_col, seg_row)


def attend_grad(qkv, grad_context, log_totals, cosine, sine, seg_col, seg_row):
    length = qkv.shape[0]
    return pl.pallas_call(
        attend_grad_kernel,
        out_shape=jax.ShapeDtypeStruct((length, D + 2 * KW), bf16),
        compiler_params=pltpu.CompilerParams(vmem_limit_bytes=vmem_limit),
        cost_estimate=cost(26),
        name="attend_grad",
    )(qkv, grad_context, log_totals, cosine, sine, seg_col, seg_row)


MESH = pl.DeviceIdType.MESH


def cost(microseconds):
    return pl.CostEstimate(flops=0, bytes_accessed=int(microseconds * 3.69e6), transcendentals=0)


def place():
    dp = lax.axis_index("dp")
    return dp // 2, dp % 2, lax.axis_index("fsdp")


def device(line, core, plane):
    return {"dp": line * 2 + core, "fsdp": plane}


def flipped(index, bit):
    return index + bit - 2 * bit * ((index // bit) % 2)


def greet(partners, ends):
    barrier = pltpu.get_barrier_semaphore()
    count = len(partners)
    for partner in partners:
        pl.semaphore_signal(barrier, inc=1, device_id=partner, device_id_type=MESH)
    for there, partner in ends:
        count = count + there

        @pl.when(there == 1)
        def _():
            pl.semaphore_signal(barrier, inc=1, device_id=partner, device_id_type=MESH)

    pl.semaphore_wait(barrier, count)


def gather_kernel(lines, own, weight, down, full, parts, down_full, cut, line_send, line_recv, x_send, x_recv, y_send, y_recv,
                  dx_send, dx_recv, dy_send, dy_recv, core_send, core_recv, cut_send, cut_recv, down_send, down_recv, down_core_send,
                  down_core_recv, here_sem):
    z, c, f = place()
    half = own.shape[0] // 2
    fx, fy = flipped(f, 1), flipped(f, 2)
    fd = flipped(fx, 2)
    x_dev, y_dev, core_dev = device(z, c, fx), device(z, c, fy), device(z, 1 - c, f)
    has_left = jnp.minimum(z, 1)
    has_right = jnp.minimum(lines - 1 - z, 1)
    left_dev = device(jnp.maximum(z - 1, 0), c, f)
    right_dev = device(jnp.minimum(z + 1, lines - 1), c, f)
    far_dev = device(z, c, fd)
    greet([x_dev, y_dev, far_dev, core_dev], [(has_left, left_dev), (has_right, right_dev)])

    def cut_copy(k):
        to = flipped(f, k) if k < 3 else fd
        return pltpu.make_async_remote_copy(
            cut.at[to], parts.at[f], cut_send.at[k], cut_recv.at[k], device_id=device(z, c, to), device_id_type=MESH
        )

    def copy(line, plane, send, recv, dev, src=None, rows=None):
        dst = full.at[line, c, plane]
        src = dst if src is None else src
        if rows is not None:
            dst, src = dst.at[rows], src.at[rows]
        return pltpu.make_async_remote_copy(
            src, dst, send, recv, device_id=dev, device_id_type=MESH
        )

    def to_right(line, src=None):
        return copy(line, f, line_send.at[0, line], line_recv.at[line], right_dev, src)

    def to_left(line, src=None):
        return copy(line, f, line_send.at[1, line], line_recv.at[line], left_dev, src)

    def to_x(line, src=None):
        return copy(line, f, x_send.at[line], x_recv.at[line], x_dev, src)

    def to_y(line, src=None):
        return copy(line, f, y_send.at[line], y_recv.at[line], y_dev, src)

    def diag_y(line):
        return copy(line, fx, dy_send.at[line], dy_recv.at[line], y_dev, None, pl.ds(0, half))

    def diag_x(line):
        return copy(line, fy, dx_send.at[line], dx_recv.at[line], x_dev, None, pl.ds(half, half))

    def to_core(line, plane, src=None):
        return copy(line, plane, core_send.at[line, plane], core_recv.at[line, plane], core_dev, src)

    def down_copy(line, way, src=None):
        dst = down_full.at[line, c]
        return pltpu.make_async_remote_copy(
            dst if src is None else src, dst, down_send.at[way, line], down_recv.at[line],
            device_id=(right_dev, left_dev)[way], device_id_type=MESH,
        )

    def down_core(line, src=None):
        dst = down_full.at[line, c]
        return pltpu.make_async_remote_copy(
            dst if src is None else src, dst, down_core_send.at[line], down_core_recv.at[line],
            device_id=core_dev, device_id_type=MESH,
        )

    here = pltpu.make_async_copy(own, full.at[z, c, f], here_sem.at[0])
    here.start()
    here_down = pltpu.make_async_copy(down, down_full.at[z, c], here_sem.at[2])
    here_down.start()

    @pl.when(has_right == 1)
    def _():
        to_right(z, own).start()

    @pl.when(has_left == 1)
    def _():
        to_left(z, own).start()

    to_x(z, own).start()
    to_y(z, own).start()
    to_core(z, f, own).start()

    cut_columns(weight, cut, 2 * lines, 4)
    here_cut = pltpu.make_async_copy(cut.at[f], parts.at[f], here_sem.at[1])
    here_cut.start()
    for k in range(1, 4):
        cut_copy(k).start()

    down_core(z, down).start()
    for t in range(1, lines):

        @pl.when(z >= t)
        def _():
            line = z - t
            to_right(line).wait_recv()

            @pl.when(has_right == 1)
            def _():
                to_right(line).start()

            to_x(line).start()
            to_y(line).start()
            to_core(line, f).start()

        @pl.when(z + t <= lines - 1)
        def _():
            line = z + t
            to_left(line).wait_recv()

            @pl.when(has_left == 1)
            def _():
                to_left(line).start()

            to_x(line).start()
            to_y(line).start()
            to_core(line, f).start()

    @pl.when(has_right == 1)
    def _():
        down_copy(z, 0, down).start()

    @pl.when(has_left == 1)
    def _():
        down_copy(z, 1, down).start()

    here.wait()
    order = []
    for t in range(lines):
        line = z
        for b in range(lines.bit_length() - 1):
            if t >> b & 1:
                line = flipped(line, 1 << b)
        order.append(line)
    for t, line in enumerate(order):
        to_x(line).wait_recv()
        diag_y(line).start()
        to_core(line, fx).start()
        to_y(line).wait_recv()
        diag_x(line).start()
        to_core(line, fy).start()
        if t == 0:
            continue

        @pl.when(z >= t)
        def _():
            down_copy(z - t, 0).wait_recv()

            @pl.when(has_right == 1)
            def _():
                down_copy(z - t, 0).start()

            down_core(z - t).start()

        @pl.when(z + t <= lines - 1)
        def _():
            down_copy(z + t, 1).wait_recv()

            @pl.when(has_left == 1)
            def _():
                down_copy(z + t, 1).start()

            down_core(z + t).start()

    for line in order:
        diag_y(line).wait_recv()
        diag_x(line).wait_recv()
        to_core(line, fd).start()
    here_cut.wait()
    here_down.wait()
    for k in range(1, 4):
        cut_copy(k).wait()
    for line in range(lines):
        for plane in range(4):
            to_core(line, plane).wait()
        to_x(line).wait_send()
        to_y(line).wait_send()
        diag_x(line).wait_send()
        diag_y(line).wait_send()

        down_core(line).wait()

        @pl.when((line <= z) & (has_right == 1))
        def _():
            to_right(line).wait_send()
            down_copy(line, 0).wait_send()

        @pl.when((line >= z) & (has_left == 1))
        def _():
            to_left(line).wait_send()
            down_copy(line, 1).wait_send()


def gather_all(shard, weight, down, n_dp, n_tp):
    rows, columns = shard.shape
    width = weight.shape[1] // n_tp
    lines = n_dp // 2
    if n_tp != 4 or rows % 32:
        full = lax.all_gather(shard, ("dp", "fsdp"), axis=0, tiled=True)
        down_full = lax.all_gather(down, "dp", axis=0, tiled=True)
        return full, columns_out(weight, n_dp, n_tp), down_full
    dma = pltpu.SemaphoreType.DMA
    hbm = pl.BlockSpec(memory_space=pl.ANY)
    full, parts, down_full = pl.pallas_call(
        functools.partial(gather_kernel, lines),
        out_shape=(
            jax.ShapeDtypeStruct((lines, 2, n_tp, rows, columns), bf16),
            jax.ShapeDtypeStruct((n_tp, rows, width), bf16),
            jax.ShapeDtypeStruct((lines, 2, *down.shape), bf16),
        ),
        in_specs=[hbm, pl.BlockSpec(memory_space=pltpu.VMEM), hbm],
        out_specs=(hbm, hbm, hbm),
        scratch_shapes=[pltpu.VMEM((n_tp, rows, width), bf16), dma((2, lines))]
        + [dma((lines,))] * 9
        + [dma((lines, n_tp))] * 2
        + [dma((n_tp,)), dma((n_tp,)), dma((2, lines)), dma((lines,)), dma((lines,)), dma((lines,)), dma((3,))],
        compiler_params=pltpu.CompilerParams(
            collective_id=0, has_side_effects=True, vmem_limit_bytes=vmem_limit
        ),
        cost_estimate=cost(100),
        name="gather_all",
    )(shard, weight, down)
    full = full.reshape(n_dp * n_tp * rows, columns)
    return full, parts, down_full.reshape(n_dp * down.shape[0], down.shape[1])


def cut_columns(weight, cut, n_dp, n_tp):
    unit = weight.shape[1] // (2 * n_dp * n_tp)
    half = n_dp * unit
    for to in range(n_tp):
        for side in range(2):
            starts = [side * n_tp * half + (j * n_tp + to) * unit for j in range(n_dp)]
            pieces = [weight[:, start : start + unit] for start in starts]
            cut[to, :, side * half : (side + 1) * half] = jnp.concatenate(pieces, axis=1).astype(bf16)


def columns_out_kernel(n_dp, n_tp, weight, parts, cut, send, recv, here_sem):
    z, c, f = place()
    greet([device(z, c, (f + k) % n_tp) for k in range(1, n_tp)], [])

    def away(k):
        to = (f + k) % n_tp
        return pltpu.make_async_remote_copy(
            cut.at[to], parts.at[f], send.at[k], recv.at[k], device_id=device(z, c, to), device_id_type=MESH
        )

    cut_columns(weight, cut, n_dp, n_tp)
    for k in range(1, n_tp):
        away(k).start()
    here = pltpu.make_async_copy(cut.at[f], parts.at[f], here_sem)
    here.start()
    here.wait()
    for k in range(1, n_tp):
        away(k).wait()


def columns_out(weight, n_dp, n_tp):
    rows, width = weight.shape
    dma = pltpu.SemaphoreType.DMA
    return pl.pallas_call(
        functools.partial(columns_out_kernel, n_dp, n_tp),
        out_shape=jax.ShapeDtypeStruct((n_tp, rows, width // n_tp), bf16),
        out_specs=pl.BlockSpec(memory_space=pl.ANY),
        scratch_shapes=[
            pltpu.VMEM((n_tp, rows, width // n_tp), bf16), dma((n_tp,)), dma((n_tp,)), dma(()),
        ],
        compiler_params=pltpu.CompilerParams(
            collective_id=1, has_side_effects=True, vmem_limit_bytes=vmem_limit
        ),
        cost_estimate=cost(20),
        name="columns_out",
    )(weight)


def columns_back_kernel(n_dp, n_tp, parts, whole, got, send, recv, here_sem):
    z, c, f = place()
    greet([device(z, c, (f + k) % n_tp) for k in range(1, n_tp)], [])
    unit = whole.shape[1] // (2 * n_dp * n_tp)
    half = n_dp * unit

    def away(k):
        to = (f + k) % n_tp
        return pltpu.make_async_remote_copy(
            parts.at[to], got.at[f], send.at[k], recv.at[k], device_id=device(z, c, to), device_id_type=MESH
        )

    for k in range(1, n_tp):
        away(k).start()
    here = pltpu.make_async_copy(parts.at[f], got.at[f], here_sem)
    here.start()
    here.wait()
    for k in range(1, n_tp):
        away(k).wait()
    for side in range(2):
        pieces = [
            got[frm, :, side * half + j * unit : side * half + (j + 1) * unit].astype(f32)
            for j in range(n_dp)
            for frm in range(n_tp)
        ]
        whole[:, side * n_tp * half : (side + 1) * n_tp * half] = jnp.concatenate(pieces, axis=1)


def columns_back(parts, n_dp, n_tp):
    _, rows, width = parts.shape
    dma = pltpu.SemaphoreType.DMA
    return pl.pallas_call(
        functools.partial(columns_back_kernel, n_dp, n_tp),
        out_shape=jax.ShapeDtypeStruct((rows, width * n_tp), f32),
        in_specs=[pl.BlockSpec(memory_space=pl.ANY)],
        scratch_shapes=[pltpu.VMEM(parts.shape, bf16), dma((n_tp,)), dma((n_tp,)), dma(())],
        compiler_params=pltpu.CompilerParams(
            collective_id=2, has_side_effects=True, vmem_limit_bytes=vmem_limit
        ),
        cost_estimate=cost(20),
        name="columns_back",
    )(parts)


def total_kernel(n_dp, n_tp, value, total, held, got, send, recv):
    dp, f = lax.axis_index("dp"), lax.axis_index("fsdp")
    partners = []
    for axis, size in (("dp", n_dp), ("fsdp", n_tp)):
        for bit in range(size.bit_length() - 1):
            index = {"dp": dp, "fsdp": f}
            index[axis] = flipped(index[axis], 1 << bit)
            partners.append(index)
    greet(partners, [])
    held[0] = value[...]
    for step, partner in enumerate(partners):
        swap = pltpu.make_async_remote_copy(
            held.at[step], got.at[step], send.at[step], recv.at[step], device_id=partner, device_id_type=MESH
        )
        swap.start()
        swap.wait()
        held[step + 1] = held[step] + got[step]
    total[...] = held[len(partners)]


def total_over_devices(value, n_dp, n_tp):
    steps = (n_dp * n_tp).bit_length() - 1
    dma = pltpu.SemaphoreType.DMA
    tile = (8, 128)
    spread = pl.pallas_call(
        functools.partial(total_kernel, n_dp, n_tp),
        out_shape=jax.ShapeDtypeStruct(tile, f32),
        scratch_shapes=[
            pltpu.VMEM((steps + 1, *tile), f32), pltpu.VMEM((steps, *tile), f32), dma((steps,)), dma((steps,)),
        ],
        compiler_params=pltpu.CompilerParams(collective_id=3, has_side_effects=True),
        cost_estimate=cost(13),
        name="total",
    )(jnp.broadcast_to(value, tile))
    return spread[0, 0]


def adam_update(weight, gradient, first, second, rate, decay):
    first = beta_one * first + (1.0 - beta_one) * gradient
    second = beta_two * second + (1.0 - beta_two) * gradient * gradient
    first_hat = first / (1.0 - beta_one**STEP)
    second_hat = second / (1.0 - beta_two**STEP)
    weight = weight - rate * (first_hat / (jnp.sqrt(second_hat) + adam_eps) + decay * weight)
    return (weight, first, second)


def matmul(a, b):
    return jnp.dot(a, b, preferred_element_type=f32)


def matmul_t(a, b):
    return lax.dot_general(a, b, (((1,), (1,)), ((), ())), preferred_element_type=f32)


def matmul_tn(a, b):
    return lax.dot_general(a, b, (((0,), (0,)), ((), ())), preferred_element_type=f32)


def swap_core(block, n_dp):
    return lax.ppermute(block, "dp", [(i, i ^ 1) for i in range(n_dp)])


def plane_swap(block, k, n_tp):
    return lax.ppermute(block, "fsdp", [(i, i ^ k) for i in range(n_tp)])


def plane_gather(block, n_tp):
    if n_tp != 4:
        return jnp.concatenate([block] + [plane_swap(block, k, n_tp) for k in range(1, n_tp)], axis=0)
    half = block.shape[0] // 2
    over_x, over_y = plane_swap(block, 1, n_tp), plane_swap(block, 2, n_tp)
    far = [plane_swap(over_y[:half], 1, n_tp), plane_swap(over_x[half:], 2, n_tp)]
    return jnp.concatenate([block, over_x, over_y] + far, axis=0)


def core_sum(parts, n_dp):
    core = lax.axis_index("dp") % 2
    mine = lax.dynamic_index_in_dim(parts, core, 1, keepdims=False)
    other = lax.dynamic_index_in_dim(parts, 1 - core, 1, keepdims=False)
    return mine.astype(f32) + swap_core(other, n_dp).astype(f32)


def line_sum(parts, n_dp):
    lines = n_dp // 2
    place = lax.axis_index("dp") // 2
    result = lax.dynamic_index_in_dim(parts, place, 0, keepdims=False)
    for way in (1, -1):
        arrived = None
        for step in range(1, lines):
            target = jnp.clip(place + way * (lines - step), 0, lines - 1)
            load = lax.dynamic_index_in_dim(parts, target, 0, keepdims=False).astype(f32)
            if arrived is not None:
                load = load + arrived.astype(f32)
            senders = range(step) if way == 1 else range(lines - step, lines)
            pairs = [(2 * s + c, 2 * (s + way) + c) for s in senders for c in range(2)]
            arrived = lax.ppermute(load.astype(bf16), "dp", pairs)
        result = result.astype(f32) + arrived.astype(f32)
    return result


def plane_sum(parts, n_tp):
    here = lax.axis_index("fsdp")
    total = lax.dynamic_index_in_dim(parts, here, 0, keepdims=False).astype(f32)
    for k in range(1, n_tp):
        load = lax.dynamic_index_in_dim(parts, here ^ k, 0, keepdims=False).astype(bf16)
        total = total + plane_swap(load, k, n_tp).astype(f32)
    return total


def by_rows(rows, body):
    def step(i, carry):
        body(pl.ds(pl.multiple_of(i * 16, 16), 16))
        return carry

    lax.fori_loop(0, rows // 16, step, 0)


def scatter_kernel(lines, n_arrays, *refs):
    groups = [refs[i * n_arrays : (i + 1) * n_arrays] for i in range(8)]
    arrays, outs, sums, others, firsts, seconds, alongs, leaving = groups
    load_sem, core_send, core_recv, one_send, one_recv, two_send, two_recv, line_send, line_recv = refs[8 * n_arrays :]
    z, c, f = place()
    planes, rows = sums[0].shape[1:3]
    half = rows // 2
    fx, fy = flipped(f, 1), flipped(f, 2)
    fd = flipped(fx, 2)
    x_dev, y_dev, core_dev = device(z, c, fx), device(z, c, fy), device(z, 1 - c, f)
    has_left = jnp.minimum(z, 1)
    has_right = jnp.minimum(lines - 1 - z, 1)
    left_dev = device(jnp.maximum(z - 1, 0), c, f)
    right_dev = device(jnp.minimum(z + 1, lines - 1), c, f)
    greet([x_dev, y_dev, core_dev], [(has_left, left_dev), (has_right, right_dev)])
    halves = (pl.ds(0, half), pl.ds(half, half))
    near, next_near, step_dev = (fx, fy), (fy, fx), (x_dev, y_dev)

    def remote(src, dst, send, recv, dev):
        return pltpu.make_async_remote_copy(src, dst, send, recv, device_id=dev, device_id_type=MESH)

    def to_core(a, d):
        return remote(arrays[a].at[d, 1 - c], others[a].at[d], core_send.at[a, d], core_recv.at[a, d], core_dev)

    def load(a, d):
        return pltpu.make_async_copy(arrays[a].at[d, c], sums[a].at[d], load_sem.at[a, d])

    def one(a, d, way, i):
        block = (near[way], fd)[i]
        return remote(
            sums[a].at[d, block, halves[way]], firsts[a].at[way, d, i],
            one_send.at[a, d, way, i], one_recv.at[a, d, way, i], step_dev[way],
        )

    def two(a, d, way):
        return remote(
            sums[a].at[d, next_near[way], halves[way]], seconds[a].at[way, d],
            two_send.at[a, d, way], two_recv.at[a, d, way], step_dev[1 - way],
        )

    def to_right(a, d):
        return remote(leaving[a].at[d], alongs[a].at[d], line_send.at[a, d], line_recv.at[a, d], right_dev)

    def to_left(a, d, slot):
        return remote(leaving[a].at[d], alongs[a].at[slot], line_send.at[a, d], line_recv.at[a, slot], left_dev)

    def add_along(a, slot):
        def step(r):
            outs[a][r] += alongs[a][slot, r].astype(f32)

        by_rows(rows, step)

    order = []
    for t in reversed(range(lines)):
        line = z
        for b in range(lines.bit_length() - 1):
            if t >> b & 1:
                line = flipped(line, 1 << b)
        order.append(line)
    chunks = [(a, d) for d in order for a in range(n_arrays)]
    for a, d in chunks:
        to_core(a, d).start()
        load(a, d).start()
    for a, d in chunks:
        load(a, d).wait()
        to_core(a, d).wait_recv()

        def core_add(r):
            for plane in range(planes):
                sums[a][d, plane, r] = (sums[a][d, plane, r].astype(f32) + others[a][d, plane, r].astype(f32)).astype(bf16)

        by_rows(rows, core_add)
        for i in (1, 0):
            for way in range(2):
                one(a, d, way, i).start()
    for a, d in chunks:
        for way in range(2):
            one(a, d, way, 1).wait_recv()

            def first_add(r):
                there = pl.ds(pl.multiple_of(r.start + way * half, 16), r.size)
                mine = sums[a][d, next_near[way], there].astype(f32)
                sums[a][d, next_near[way], there] = (mine + firsts[a][way, d, 1, r].astype(f32)).astype(bf16)

            by_rows(half, first_add)
            two(a, d, way).start()
    for a, d in chunks:
        for way in range(2):
            one(a, d, way, 0).wait_recv()
            two(a, d, way).wait_recv()

            def second_add(r):
                there = pl.ds(pl.multiple_of(r.start + way * half, 16), r.size)
                outs[a][there] = (
                    sums[a][d, f, there].astype(f32)
                    + firsts[a][way, d, 0, r].astype(f32)
                    + seconds[a][way, d, r].astype(f32)
                )

            by_rows(half, second_add)

        @pl.when((d > z) & (has_left == 1))
        def _():
            to_right(a, d).wait_recv()
            add_along(a, d)

        @pl.when((d < z) & (has_right == 1))
        def _():
            to_left(a, d, d).wait_recv()
            add_along(a, d)

        @pl.when(d != z)
        def _():
            def leave(r):
                leaving[a][d, r] = outs[a][r].astype(bf16)

            by_rows(rows, leave)

        @pl.when(d > z)
        def _():
            to_right(a, d).start()

        @pl.when((d < z) & (d + 1 < z))
        def _():
            to_left(a, d, d).start()

        @pl.when(d + 1 == z)
        def _():
            to_left(a, d, lines).start()

    for a in range(n_arrays):

        @pl.when(has_left == 1)
        def _():
            to_right(a, z).wait_recv()
            add_along(a, z)

        @pl.when(has_right == 1)
        def _():
            to_left(a, z, lines).wait_recv()
            add_along(a, lines)

    for a, d in chunks:
        to_core(a, d).wait_send()
        for way in range(2):
            one(a, d, way, 0).wait_send()
            one(a, d, way, 1).wait_send()
            two(a, d, way).wait_send()

        @pl.when(d != z)
        def _():
            to_right(a, d).wait_send()


def scatter_all(arrays, n_dp, n_tp):
    lines = n_dp // 2
    rows = arrays[0].shape[0] // (n_dp * n_tp)
    if n_tp != 4 or rows % 32:
        results = []
        for array in arrays:
            parts = core_sum(array.reshape(lines, 2, n_tp, rows, -1), n_dp)
            results.append(line_sum(plane_sum(parts.transpose(1, 0, 2, 3), n_tp), n_dp))
        return results
    dma = pltpu.SemaphoreType.DMA
    widths = [array.shape[1] for array in arrays]
    n = len(widths)
    shapes = [
        (lines, n_tp, rows), (lines, n_tp, rows), (2, lines, 2, rows // 2), (2, lines, rows // 2),
        (lines + 1, rows), (lines, rows),
    ]
    return pl.pallas_call(
        functools.partial(scatter_kernel, lines, n),
        out_shape=[jax.ShapeDtypeStruct((rows, width), f32) for width in widths],
        in_specs=[pl.BlockSpec(memory_space=pl.ANY)] * n,
        scratch_shapes=[pltpu.VMEM((*shape, width), bf16) for shape in shapes for width in widths]
        + [dma((n, lines))] * 3
        + [dma((n, lines, 2, 2))] * 2
        + [dma((n, lines, 2))] * 2
        + [dma((n, lines)), dma((n, lines + 1))],
        compiler_params=pltpu.CompilerParams(
            collective_id=4, has_side_effects=True, vmem_limit_bytes=vmem_limit
        ),
        cost_estimate=cost(110),
        name="scatter_all",
    )(*[array.reshape(lines, 2, n_tp, rows, -1) for array in arrays])


def rope_tile(tile, cos, sin):
    pairs = [tile[:, i : i + 128] for i in range(0, tile.shape[1], 128)]
    return jnp.concatenate([pair * cos + halves_swapped(pair) * sin for pair in pairs], axis=1)


def attend_heads(qkv, context, log_totals, allowed):
    length = qkv.shape[0]
    scale = HD ** (-0.5)
    for group in range(KVH):
        kc = D + (group // 2) * 128
        keys = both_places(qkv[:, kc : kc + 128], group % 2)
        values = both_places(qkv[:, kc + KW : kc + KW + 128], group % 2)

        def pair_step(pair_index, carry):
            pair = group * (GROUP // 2) + pair_index
            lanes = pl.ds(pl.multiple_of(pair * 128, 128), 128)
            queries = qkv[:, lanes]
            total = jnp.zeros((length, 128), f32)
            for side in range(2):
                scores = dot_t(keys[side], queries) * scale
                scores = jnp.where(allowed, scores, -1e30)
                top = jnp.max(scores, axis=0, keepdims=True)
                raised = jnp.exp(scores - top)
                totals = jnp.sum(raised, axis=0, keepdims=True)
                probs = (raised / totals).astype(bf16)
                total = total + dot_tn(probs, values[side])
                log_totals[pl.ds(2 * pair + side, 1), :] = top + jnp.log(totals)
            context[:, lanes] = total.astype(bf16)
            return carry

        lax.fori_loop(0, GROUP // 2, pair_step, 0)


def tile_at(i, width, start=0):
    return pl.ds(pl.multiple_of(start + i * width, 128), width)


class Exchange:
    def __init__(self, own, whole, sems, i, x_dev, y_dev):
        send, recv, here = sems
        half = own.shape[0] // 2

        def remote(src, dst, k, dev):
            return pltpu.make_async_remote_copy(
                src, dst, send.at[i, k], recv.at[i, k], device_id=dev, device_id_type=MESH
            )

        low, high = pl.ds(0, half), pl.ds(half, half)
        self.near = [remote(own, whole.at[1], 0, x_dev), remote(own, whole.at[2], 1, y_dev)]
        self.far = [
            remote(whole.at[2, low], whole.at[3, low], 2, x_dev),
            remote(whole.at[1, high], whole.at[3, high], 3, y_dev),
        ]
        self.here = pltpu.make_async_copy(own, whole.at[0], here.at[i])

    def start(self):
        for copy in self.near:
            copy.start()
        self.here.start()

    def pass_on(self):
        for copy in self.near:
            copy.wait_recv()
        for copy in self.far:
            copy.start()

    def finish(self):
        for copy in self.far:
            copy.wait()
        for copy in self.near:
            copy.wait_send()
        self.here.wait()


def forward_kernel(x, grads, gains, cosine, sine, seg_col, seg_row, weights, qkv, context, log_totals, middle,
                   normed_one, normed_all, grads_all, q_weight, o_weight, normed_two, load_sem, *sems):
    z, c, f = place()
    x_dev, y_dev = device(z, c, flipped(f, 1)), device(z, c, flipped(f, 2))
    greet([x_dev, y_dev], [])
    length = x.shape[0]
    width = D + 2 * KW
    of_grads = Exchange(grads, grads_all, sems, 0, x_dev, y_dev)
    of_normed = Exchange(normed_two, normed_all, sems, 1, x_dev, y_dev)
    of_grads.start()
    load_q = pltpu.make_async_copy(weights.at[:, pl.ds(0, width)], q_weight, load_sem.at[0])
    load_o = pltpu.make_async_copy(weights.at[:, pl.ds(width, D)], o_weight, load_sem.at[1])
    load_q.start()
    load_o.start()

    def norm_one(r):
        rows = x[r].astype(f32)
        inverse = lax.rsqrt(jnp.mean(rows * rows, axis=-1, keepdims=True) + norm_eps)
        normed_one[r] = (rows * inverse * gains[0:1, :]).astype(bf16)

    by_rows(length, norm_one)
    load_q.wait()
    cos, sin = cosine[...], sine[...]

    def project(i, carry):
        lanes = tile_at(i, 256)
        qkv[:, lanes] = rope_tile(dot_n(normed_one[...], q_weight[:, lanes]), cos, sin).astype(bf16)
        return carry

    lax.fori_loop(0, (D + KW) // 256, project, 0)
    qkv[:, D + KW :] = dot_n(normed_one[...], q_weight[:, D + KW :]).astype(bf16)
    allowed = mask_keys_rows(seg_col[...], seg_row[...], length)
    attend_heads(qkv, context, log_totals, allowed)
    load_o.wait()

    def project_out(i, carry):
        lanes = tile_at(i, 256)
        middle[:, lanes] = x[:, lanes].astype(f32) + dot_n(context[...], o_weight[:, lanes])
        return carry

    lax.fori_loop(0, D // 256, project_out, 0)

    def norm_two(r):
        rows = middle[r]
        inverse = lax.rsqrt(jnp.mean(rows * rows, axis=-1, keepdims=True) + norm_eps)
        normed_two[r] = (rows * inverse * gains[1:2, :]).astype(bf16)

    by_rows(length, norm_two)
    of_normed.start()
    of_grads.pass_on()
    of_normed.pass_on()
    of_normed.finish()
    of_grads.finish()


def forward(x, grads, gains, cosine, sine, seg_col, seg_row, weights):
    length = x.shape[0]
    dma = pltpu.SemaphoreType.DMA
    vmem, hbm = pl.BlockSpec(memory_space=pltpu.VMEM), pl.BlockSpec(memory_space=pl.ANY)
    width = D + 2 * KW
    return pl.pallas_call(
        forward_kernel,
        out_shape=(
            jax.ShapeDtypeStruct((length, width), bf16),
            jax.ShapeDtypeStruct((length, D), bf16),
            jax.ShapeDtypeStruct((HEADS, length), f32),
            jax.ShapeDtypeStruct((length, D), f32),
            jax.ShapeDtypeStruct((length, D), bf16),
            jax.ShapeDtypeStruct((4, length, D), bf16),
            jax.ShapeDtypeStruct((4, length, D), bf16),
        ),
        in_specs=[vmem, hbm] + [vmem] * 5 + [hbm],
        out_specs=(vmem,) * 5 + (hbm,) * 2,
        scratch_shapes=[
            pltpu.VMEM((D, width), bf16), pltpu.VMEM((D, D), bf16), pltpu.VMEM((length, D), bf16),
            dma((2,)), dma((2, 4)), dma((2, 4)), dma((2,)),
        ],
        compiler_params=pltpu.CompilerParams(
            collective_id=5, has_side_effects=True, vmem_limit_bytes=vmem_limit
        ),
        cost_estimate=cost(95),
        name="forward",
    )(x, grads, gains, cosine, sine, seg_col, seg_row, weights)


def feed_kernel(n_hbm, g_hbm, wm_hbm, wd_hbm, grad_normed, grad_down, grad_mlp, layer, n, g, wm, wd, gh, act,
                parts, ones, twos, stage, load_sem, out_sem, one_send, one_recv, two_send, two_recv):
    z, c, f = place()
    x_dev, y_dev = device(z, c, flipped(f, 1)), device(z, c, flipped(f, 2))
    tokens = n.shape[0]
    length = tokens // 4
    half = length // 2
    ff = wd.shape[0]
    loads = [
        pltpu.make_async_copy(src, dst, load_sem.at[i])
        for i, (src, dst) in enumerate(((n_hbm, n), (wm_hbm, wm), (wd_hbm, wd), (g_hbm, g)))
    ]
    for copy in loads:
        copy.start()
    greet([x_dev, y_dev], [])
    for copy in loads:
        copy.wait()

    def hidden(rows, lanes, up_lanes):
        gate = dot_n(n[rows, :], wm[:, lanes])
        up = dot_n(n[rows, :], wm[:, up_lanes])
        grad = dot_t(g[rows, :], wd[lanes, :])
        sigmoid = jax.nn.sigmoid(gate)
        silu = gate * sigmoid
        act[rows, lanes] = (silu * up).astype(bf16)
        gh[rows, lanes] = (grad * up * sigmoid * (1.0 + gate * (1.0 - sigmoid))).astype(bf16)
        gh[rows, up_lanes] = (grad * silu).astype(bf16)

    wide = ff // 256

    def hidden_step(i, carry):
        rows = pl.ds(pl.multiple_of((i % 4) * length, 16), length)
        hidden(rows, tile_at(i // 4, 256), tile_at(i // 4, 256, ff))
        return carry

    lax.fori_loop(0, 4 * wide, hidden_step, 0)
    for k in range(4):
        if ff % 256:
            hidden(pl.ds(k * length, length), pl.ds(wide * 256, ff % 256), pl.ds(ff + wide * 256, ff % 256))

    def back(k, store):
        def step(i, carry):
            tile = tile_at(i, 1024)
            store(tile, dot_t(gh[k * length : (k + 1) * length, :], wm[tile, :]))
            return carry

        lax.fori_loop(0, D // 1024, step, 0)

    def back_parts(k):
        def store(tile, value):
            parts[k - 1, :, tile] = value.astype(bf16)

        back(k, store)

    halves = (pl.ds(0, half), pl.ds(half, half))
    step_dev = (x_dev, y_dev)

    def one(way, i):
        return pltpu.make_async_remote_copy(
            parts.at[2 if i else way, halves[way]], ones.at[way, i], one_send.at[way, i], one_recv.at[way, i],
            device_id=step_dev[way], device_id_type=MESH,
        )

    def two(way):
        return pltpu.make_async_remote_copy(
            parts.at[1 - way, halves[way]], twos.at[way], two_send.at[way], two_recv.at[way],
            device_id=step_dev[1 - way], device_id_type=MESH,
        )

    back_parts(3)
    one(0, 1).start()
    one(1, 1).start()
    back_parts(1)
    one(0, 0).start()
    back_parts(2)
    one(1, 0).start()

    def store_own(tile, value):
        grad_normed[:, tile] = value

    back(0, store_own)

    def down_out(i, slot, width=256):
        rows = pl.ds(pl.multiple_of((i // 2) * 256, 128), width)
        lanes = tile_at(i % 2, D // 2)
        return pltpu.make_async_copy(
            stage.at[slot, pl.ds(0, width), pl.ds(0, D // 2)], grad_down.at[rows, lanes], out_sem.at[0, slot]
        )

    def down_tile(i, slot, width=256):
        lanes = tile_at(i % 2, D // 2)
        value = dot_tn(act[:, pl.ds(pl.multiple_of((i // 2) * 256, 128), width)], g[:, lanes])
        stage[slot, 0:width, 0 : D // 2] = value.astype(bf16)
        down_out(i, slot, width).start()

    def down_step(i, carry):
        slot = i % 2

        @pl.when(i >= 2)
        def _():
            down_out(i - 2, slot).wait()

        down_tile(i, slot)
        return carry

    lax.fori_loop(0, 2 * wide, down_step, 0)
    for slot in range(2):
        down_out(2 * wide - 2 + slot, slot).wait()
        if ff % 256:
            down_tile(2 * wide + slot, slot, ff % 256)
            down_out(2 * wide + slot, slot, ff % 256).wait()

    for way in range(2):
        one(way, 1).wait_recv()

        def add_far(r):
            there = pl.ds(pl.multiple_of(r.start + way * half, 16), r.size)
            mine = parts[1 - way, there].astype(f32)
            parts[1 - way, there] = (mine + ones[way, 1, r].astype(f32)).astype(bf16)

        by_rows(half, add_far)
        two(way).start()

    def mlp_out(i, slot):
        rows = pl.ds(pl.multiple_of((i // 2) * 256, 256), 256)
        return pltpu.make_async_copy(
            stage.at[slot, :, pl.ds(0, ff)], grad_mlp.at[rows, tile_at(i % 2, ff)], out_sem.at[1, slot]
        )

    def mlp_step(i, carry):
        slot = i % 2

        @pl.when(i >= 2)
        def _():
            mlp_out(i - 2, slot).wait()

        value = dot_tn(n[:, tile_at(i // 2, 256)], gh[:, tile_at(i % 2, ff)])
        stage[slot, :, 0:ff] = value.astype(bf16)
        mlp_out(i, slot).start()
        return carry

    lax.fori_loop(0, 2 * D // 256, mlp_step, 0)
    mlp_out(2 * D // 256 - 2, 0).wait()
    mlp_out(2 * D // 256 - 1, 1).wait()

    def layer_step(i, carry):
        g[:, tile_at(i, 256)] = dot_n(act[...], wd[:, tile_at(i, 256)]).astype(bf16)
        return carry

    lax.fori_loop(0, D // 256, layer_step, 0)
    layer_out = pltpu.make_async_copy(g, layer, load_sem.at[0])
    layer_out.start()
    for way in range(2):
        one(way, 0).wait()
        one(way, 1).wait_send()
        two(way).wait()
    for way in range(2):

        def add_all(r):
            there = pl.ds(pl.multiple_of(r.start + way * half, 16), r.size)
            grad_normed[there] += ones[way, 0, r].astype(f32) + twos[way, r].astype(f32)

        by_rows(half, add_all)
    layer_out.wait()


def feed(normed_all, grads_all, mlp_cols, down_cols):
    tokens, ff = 4 * normed_all.shape[1], down_cols.shape[0]
    length = tokens // 4
    half = length // 2
    dma = pltpu.SemaphoreType.DMA
    vmem, hbm = pl.BlockSpec(memory_space=pltpu.VMEM), pl.BlockSpec(memory_space=pl.ANY)
    return pl.pallas_call(
        feed_kernel,
        out_shape=(
            jax.ShapeDtypeStruct((length, D), f32),
            jax.ShapeDtypeStruct((ff, D), bf16),
            jax.ShapeDtypeStruct((D, 2 * ff), bf16),
            jax.ShapeDtypeStruct((tokens, D), bf16),
        ),
        in_specs=[hbm] * 4,
        out_specs=(vmem, hbm, hbm, hbm),
        scratch_shapes=[
            pltpu.VMEM(shape, bf16)
            for shape in (
                (tokens, D), (tokens, D), (D, 2 * ff), (ff, D), (tokens, 2 * ff), (tokens, ff), (3, length, D),
                (2, 2, half, D), (2, half, D), (2, 256, max(ff, D // 2)),
            )
        ]
        + [dma((4,)), dma((2, 2)), dma((2, 2)), dma((2, 2)), dma((2,)), dma((2,))],
        compiler_params=pltpu.CompilerParams(
            collective_id=6, has_side_effects=True, vmem_limit_bytes=feed_vmem_limit
        ),
        cost_estimate=cost(115),
        name="feed",
    )(normed_all.reshape(tokens, D), grads_all.reshape(tokens, D), mlp_cols, down_cols)


def local(
    n_dp,
    n_tp,
    inputs,
    cotangent,
    segments,
    qkv_weight,
    out_weight,
    mlp_weight,
    down_weight,
    norm_gains,
    qkv_first,
    out_first,
    mlp_first,
    down_first,
    gains_first,
    qkv_second,
    out_second,
    mlp_second,
    down_second,
    gains_second,
):
    length = inputs.shape[0]
    lines = n_dp // 2
    rows = mlp_weight.shape[0]
    down_rows = down_weight.shape[0]
    ff = n_dp * down_rows
    cosine, sine = tables(segments[0])
    seg_row = segments
    seg_col = segments.reshape(length, 1)

    shard = jnp.concatenate(
        [qkv_weight, out_weight, jnp.pad(norm_gains.T, ((0, 0), (0, 126)))], axis=1
    ).astype(bf16)
    attn_full, mlp_parts, down_cols = gather_all(shard, mlp_weight, down_weight.astype(bf16), n_dp, n_tp)
    qkv_full = attn_full[:, : D + 2 * KW]
    out_full = attn_full[:, D + 2 * KW : 2 * D + 2 * KW]
    gains_full = attn_full[:, 2 * D + 2 * KW :].astype(f32).T
    mlp_cols = lax.all_gather(mlp_parts.reshape(n_tp * rows, 2 * ff), "dp", axis=0, tiled=True)
    tokens_f = inputs.astype(f32)
    gain_one, gain_two = gains_full[0], gains_full[1]
    inverse_one = lax.rsqrt(jnp.mean(tokens_f * tokens_f, axis=-1, keepdims=True) + norm_eps)
    if n_tp == 4:
        qkv, attended, log_totals, middle, normed_one, normed_all, grads_all = forward(
            inputs, cotangent, gains_full, cosine, sine, seg_col, seg_row, attn_full
        )
    else:
        normed_one = (tokens_f * inverse_one * gain_one).astype(bf16)
        projected = matmul(normed_one, qkv_full)
        qkv, attended, log_totals = attend(projected, cosine, sine, seg_col, seg_row)
        middle = tokens_f + matmul(attended, out_full)
    inverse_two = lax.rsqrt(jnp.mean(middle * middle, axis=-1, keepdims=True) + norm_eps)
    if n_tp == 4:
        grad_normed_two, grad_down, grad_mlp, layer_parts = feed(normed_all, grads_all, mlp_cols, down_cols)
        layer_parts = layer_parts.reshape(n_tp, length, D)
    else:
        normed_two = (middle * inverse_two * gain_two).astype(bf16)
        normed_all = plane_gather(normed_two, n_tp)
        grads_all = plane_gather(cotangent, n_tp)
        hidden = matmul(normed_all, mlp_cols)
        gate, up_part = hidden[:, :ff], hidden[:, ff:]
        sigmoid_gate = jax.nn.sigmoid(gate)
        silu_gate = gate * sigmoid_gate
        activated = (silu_gate * up_part).astype(bf16)
        grad_act = matmul_t(grads_all, down_cols)
        grad_gate = grad_act * up_part * sigmoid_gate * (1.0 + gate * (1.0 - sigmoid_gate))
        grad_up = grad_act * silu_gate
        grad_hidden = jnp.concatenate([grad_gate, grad_up], axis=1).astype(bf16)
        grad_normed = matmul_t(grad_hidden, mlp_cols).reshape(n_tp, length, D)
        grad_normed_two = grad_normed[0]
        for k in range(1, n_tp):
            swapped = plane_swap(grad_normed[k].astype(bf16), k, n_tp)
            grad_normed_two = grad_normed_two + swapped.astype(f32)
        grad_down = matmul_tn(activated, grads_all).astype(bf16)
        grad_mlp = matmul_tn(normed_all, grad_hidden).astype(bf16)
        layer_parts = matmul(activated, down_cols).astype(bf16).reshape(n_tp, length, D)
    layer_out = middle + layer_parts[0].astype(f32)
    for k in range(1, n_tp):
        layer_out = layer_out + plane_swap(layer_parts[k], k, n_tp).astype(f32)
    layer_out = layer_out.astype(bf16)

    down_sum = lax.psum_scatter(grad_down, "dp", scatter_dimension=0, tiled=True).astype(f32)
    mlp_sum = lax.psum_scatter(grad_mlp, "dp", scatter_dimension=0, tiled=True)
    mlp_sum = columns_back(mlp_sum.reshape(n_tp, rows, 2 * ff), n_dp, n_tp)

    gain_grad_two = jnp.sum(grad_normed_two * middle * inverse_two, axis=0)
    weighted_two = grad_normed_two * gain_two
    grad_middle = (
        cotangent.astype(f32)
        + inverse_two * weighted_two
        - middle * inverse_two**3 * jnp.mean(weighted_two * middle, axis=-1, keepdims=True)
    )
    grad_branch = grad_middle.astype(bf16)
    grad_context = matmul_t(grad_branch, out_full).astype(bf16)
    grad_projected = attend_grad(qkv, grad_context, log_totals, cosine, sine, seg_col, seg_row)

    grad_out = matmul_tn(attended, grad_branch).astype(bf16)
    grad_qkv = matmul_tn(normed_one, grad_projected)
    grad_normed_one = matmul_t(grad_projected, qkv_full)
    gain_grad_one = jnp.sum(grad_normed_one * tokens_f * inverse_one, axis=0)
    weighted_one = grad_normed_one * gain_one
    grad_inputs = (
        grad_middle
        + inverse_one * weighted_one
        - tokens_f * inverse_one**3 * jnp.mean(weighted_one * tokens_f, axis=-1, keepdims=True)
    )
    input_grad = grad_inputs.astype(bf16)
    gain_grads = jnp.pad(jnp.stack([gain_grad_one, gain_grad_two], axis=1), ((0, 0), (0, 126)))
    grad_qkv = jnp.concatenate([grad_qkv.astype(bf16), gain_grads.astype(bf16)], axis=1)
    out_sum, qkv_sum = scatter_all([grad_out, grad_qkv], n_dp, n_tp)
    gains_sum = qkv_sum[:, D + 2 * KW : D + 2 * KW + 2].T
    qkv_sum = qkv_sum[:, : D + 2 * KW]

    local_squares = (
        jnp.sum(qkv_sum * qkv_sum) + jnp.sum(out_sum * out_sum) + jnp.sum(mlp_sum * mlp_sum)
    )
    local_squares = local_squares + jnp.sum(down_sum * down_sum) + jnp.sum(gains_sum * gains_sum)
    total_squares = total_over_devices(local_squares, n_dp, n_tp)
    grad_norm = jnp.sqrt(total_squares)
    clip_scale = clip_norm / jnp.maximum(grad_norm, clip_norm)
    qkv_out = adam_update(
        qkv_weight, qkv_sum * clip_scale, qkv_first, qkv_second, matrix_rate, weight_decay
    )
    out_out = adam_update(
        out_weight, out_sum * clip_scale, out_first, out_second, matrix_rate, weight_decay
    )
    mlp_out = adam_update(
        mlp_weight, mlp_sum * clip_scale, mlp_first, mlp_second, matrix_rate, weight_decay
    )
    down_out = adam_update(
        down_weight, down_sum * clip_scale, down_first, down_second, matrix_rate, weight_decay
    )
    gains_out = adam_update(
        norm_gains, gains_sum * clip_scale, gains_first, gains_second, gain_rate, 0.0
    )
    news = [[new[i] for new in (qkv_out, out_out, mlp_out, down_out, gains_out)] for i in range(3)]
    return (layer_out, input_grad, grad_norm, *news[0], *news[1], *news[2])


def solution(mesh):
    split_rows = P(("dp", "fsdp"), None)
    split_columns = P(None, ("dp", "fsdp"))
    weights = (split_rows,) * 4 + (split_columns,)
    return jax.shard_map(
        functools.partial(local, mesh.shape["dp"], mesh.shape["fsdp"]),
        mesh=mesh,
        in_specs=(split_rows,) * 3 + weights * 3,
        out_specs=(split_rows, split_rows, P()) + weights * 3,
        check_vma=False,
    )
```

```python
import functools

import jax
import jax.numpy as jnp
from jax import lax
from jax.experimental import pallas as pl
from jax.experimental.pallas import tpu as pltpu
from jax.sharding import PartitionSpec as P

D = 2048
HEADS = 32
KVH = 4
HD = 64
FF = 5632
STEP = 10
KW = KVH * HD
GROUP = HEADS // KVH


norm_eps = 1e-05
rope_base = 10000.0
beta_one = 0.9
beta_two = 0.95
adam_eps = 1e-08
weight_decay = 0.1
matrix_rate = 0.04
gain_rate = 0.8
clip_norm = 1.0

f32 = jnp.float32
bf16 = jnp.bfloat16


def tables(segment_row):
    length = segment_row.shape[0]
    token_index = jnp.arange(length, dtype=jnp.int32)
    previous = jnp.concatenate([segment_row[:1] - 1, segment_row[:-1]])
    starts = lax.cummax(jnp.where(segment_row != previous, token_index, 0), axis=0)
    position = (token_index - starts).astype(f32)
    frequency = rope_base ** (-(jnp.arange(HD // 2, dtype=f32) * 2.0 / HD))
    angles = position[:, None] * frequency[None, :]
    cosine, sine = jnp.cos(angles), jnp.sin(angles)
    cosine = jnp.concatenate([cosine] * 4, axis=-1)
    signed = jnp.concatenate([-sine, sine] * 2, axis=-1)
    return cosine, signed


def halves_swapped(pair):
    lane = lax.broadcasted_iota(jnp.int32, pair.shape, 1)
    return jnp.where(lane % HD < HD // 2, pltpu.roll(pair, 96, 1), pltpu.roll(pair, 32, 1))


def split_pair(pair):
    lane = lax.broadcasted_iota(jnp.int32, pair.shape, 1)
    zero = jnp.zeros_like(pair)
    return jnp.where(lane < HD, pair, zero), jnp.where(lane < HD, zero, pair)


def both_places(pair, odd):
    low, high = split_pair(pair)
    moved = pltpu.roll(pair.astype(f32), HD, 1).astype(pair.dtype)
    moved_low, moved_high = split_pair(moved)
    return (moved_low, high) if odd else (low, moved_high)


def dot_t(a, b):
    return lax.dot_general(a, b, (((1,), (1,)), ((), ())), preferred_element_type=f32)


def dot_n(a, b):
    return lax.dot_general(a, b, (((1,), (0,)), ((), ())), preferred_element_type=f32)


def dot_tn(a, b):
    return lax.dot_general(a, b, (((0,), (0,)), ((), ())), preferred_element_type=f32)


def mask_keys_rows(seg_col, seg_row, length):
    key_index = lax.broadcasted_iota(jnp.int32, (length, length), 0)
    query_index = lax.broadcasted_iota(jnp.int32, (length, length), 1)
    return (seg_col == seg_row) & (query_index >= key_index)


def attend_kernel(proj, cosine, sine, seg_col, seg_row, qkv, context, log_totals):
    cos, sin = cosine[...], sine[...]
    for c in range(0, D + KW, 128):
        qkv[:, c : c + 128] = rope_tile(proj[:, c : c + 128], cos, sin).astype(bf16)
    for c in range(D + KW, D + 2 * KW, 128):
        qkv[:, c : c + 128] = proj[:, c : c + 128].astype(bf16)
    allowed = mask_keys_rows(seg_col[...], seg_row[...], proj.shape[0])
    attend_heads(qkv, context, log_totals, allowed)


def attend_grad_kernel(qkv, grad_context, log_totals, cosine, sine, seg_col, seg_row, grad_proj):
    allowed = mask_keys_rows(seg_col[...], seg_row[...], qkv.shape[0])
    attend_heads_grad(qkv, grad_context, log_totals, grad_proj, allowed, cosine[...], sine[...])


vmem_limit = 50 * 1024 * 1024
feed_vmem_limit = 62 * 1024 * 1024


def attend(projected, cosine, sine, seg_col, seg_row):
    length = projected.shape[0]
    return pl.pallas_call(
        attend_kernel,
        out_shape=(
            jax.ShapeDtypeStruct((length, D + 2 * KW), bf16),
            jax.ShapeDtypeStruct((length, D), bf16),
            jax.ShapeDtypeStruct((HEADS, length), f32),
        ),
        compiler_params=pltpu.CompilerParams(vmem_limit_bytes=vmem_limit),
        cost_estimate=cost(18),
        name="attend",
    )(projected, cosine, sine, seg_col, seg_row)


def attend_grad(qkv, grad_context, log_totals, cosine, sine, seg_col, seg_row):
    length = qkv.shape[0]
    return pl.pallas_call(
        attend_grad_kernel,
        out_shape=jax.ShapeDtypeStruct((length, D + 2 * KW), bf16),
        compiler_params=pltpu.CompilerParams(vmem_limit_bytes=vmem_limit),
        cost_estimate=cost(26),
        name="attend_grad",
    )(qkv, grad_context, log_totals, cosine, sine, seg_col, seg_row)


MESH = pl.DeviceIdType.MESH


def cost(microseconds):
    return pl.CostEstimate(flops=0, bytes_accessed=int(microseconds * 3.69e6), transcendentals=0)


def place():
    dp = lax.axis_index("dp")
    return dp // 2, dp % 2, lax.axis_index("fsdp")


def device(line, core, plane):
    return {"dp": line * 2 + core, "fsdp": plane}


def flipped(index, bit):
    return index + bit - 2 * bit * ((index // bit) % 2)


def greet(partners, ends):
    barrier = pltpu.get_barrier_semaphore()
    count = len(partners)
    for partner in partners:
        pl.semaphore_signal(barrier, inc=1, device_id=partner, device_id_type=MESH)
    for there, partner in ends:
        count = count + there

        @pl.when(there == 1)
        def _():
            pl.semaphore_signal(barrier, inc=1, device_id=partner, device_id_type=MESH)

    pl.semaphore_wait(barrier, count)


def gather_kernel(lines, own, weight, down, full, parts, down_full, cut, line_send, line_recv, x_send, x_recv, y_send, y_recv,
                  dx_send, dx_recv, dy_send, dy_recv, core_send, core_recv, cut_send, cut_recv, down_send, down_recv, down_core_send,
                  down_core_recv, here_sem):
    z, c, f = place()
    half = own.shape[0] // 2
    fx, fy = flipped(f, 1), flipped(f, 2)
    fd = flipped(fx, 2)
    x_dev, y_dev, core_dev = device(z, c, fx), device(z, c, fy), device(z, 1 - c, f)
    has_left = jnp.minimum(z, 1)
    has_right = jnp.minimum(lines - 1 - z, 1)
    left_dev = device(jnp.maximum(z - 1, 0), c, f)
    right_dev = device(jnp.minimum(z + 1, lines - 1), c, f)
    far_dev = device(z, c, fd)
    greet([x_dev, y_dev, far_dev, core_dev], [(has_left, left_dev), (has_right, right_dev)])

    def cut_copy(k):
        to = flipped(f, k) if k < 3 else fd
        return pltpu.make_async_remote_copy(
            cut.at[to], parts.at[f], cut_send.at[k], cut_recv.at[k], device_id=device(z, c, to), device_id_type=MESH
        )

    def copy(line, plane, send, recv, dev, src=None, rows=None):
        dst = full.at[line, c, plane]
        src = dst if src is None else src
        if rows is not None:
            dst, src = dst.at[rows], src.at[rows]
        return pltpu.make_async_remote_copy(
            src, dst, send, recv, device_id=dev, device_id_type=MESH
        )

    def to_right(line, src=None):
        return copy(line, f, line_send.at[0, line], line_recv.at[line], right_dev, src)

    def to_left(line, src=None):
        return copy(line, f, line_send.at[1, line], line_recv.at[line], left_dev, src)

    def to_x(line, src=None):
        return copy(line, f, x_send.at[line], x_recv.at[line], x_dev, src)

    def to_y(line, src=None):
        return copy(line, f, y_send.at[line], y_recv.at[line], y_dev, src)

    def diag_y(line):
        return copy(line, fx, dy_send.at[line], dy_recv.at[line], y_dev, None, pl.ds(0, half))

    def diag_x(line):
        return copy(line, fy, dx_send.at[line], dx_recv.at[line], x_dev, None, pl.ds(half, half))

    def to_core(line, plane, src=None):
        return copy(line, plane, core_send.at[line, plane], core_recv.at[line, plane], core_dev, src)

    def down_copy(line, way, src=None):
        dst = down_full.at[line, c]
        return pltpu.make_async_remote_copy(
            dst if src is None else src, dst, down_send.at[way, line], down_recv.at[line],
            device_id=(right_dev, left_dev)[way], device_id_type=MESH,
        )

    def down_core(line, src=None):
        dst = down_full.at[line, c]
        return pltpu.make_async_remote_copy(
            dst if src is None else src, dst, down_core_send.at[line], down_core_recv.at[line],
            device_id=core_dev, device_id_type=MESH,
        )

    here = pltpu.make_async_copy(own, full.at[z, c, f], here_sem.at[0])
    here.start()
    here_down = pltpu.make_async_copy(down, down_full.at[z, c], here_sem.at[2])
    here_down.start()

    @pl.when(has_right == 1)
    def _():
        to_right(z, own).start()

    @pl.when(has_left == 1)
    def _():
        to_left(z, own).start()

    to_x(z, own).start()
    to_y(z, own).start()
    to_core(z, f, own).start()

    cut_columns(weight, cut, 2 * lines, 4)
    here_cut = pltpu.make_async_copy(cut.at[f], parts.at[f], here_sem.at[1])
    here_cut.start()
    for k in range(1, 4):
        cut_copy(k).start()

    down_core(z, down).start()
    for t in range(1, lines):

        @pl.when(z >= t)
        def _():
            line = z - t
            to_right(line).wait_recv()

            @pl.when(has_right == 1)
            def _():
                to_right(line).start()

            to_x(line).start()
            to_y(line).start()
            to_core(line, f).start()

        @pl.when(z + t <= lines - 1)
        def _():
            line = z + t
            to_left(line).wait_recv()

            @pl.when(has_left == 1)
            def _():
                to_left(line).start()

            to_x(line).start()
            to_y(line).start()
            to_core(line, f).start()

    @pl.when(has_right == 1)
    def _():
        down_copy(z, 0, down).start()

    @pl.when(has_left == 1)
    def _():
        down_copy(z, 1, down).start()

    here.wait()
    order = []
    for t in range(lines):
        line = z
        for b in range(lines.bit_length() - 1):
            if t >> b & 1:
                line = flipped(line, 1 << b)
        order.append(line)
    for t, line in enumerate(order):
        to_x(line).wait_recv()
        diag_y(line).start()
        to_core(line, fx).start()
        to_y(line).wait_recv()
        diag_x(line).start()
        to_core(line, fy).start()
        if t == 0:
            continue

        @pl.when(z >= t)
        def _():
            down_copy(z - t, 0).wait_recv()

            @pl.when(has_right == 1)
            def _():
                down_copy(z - t, 0).start()

            down_core(z - t).start()

        @pl.when(z + t <= lines - 1)
        def _():
            down_copy(z + t, 1).wait_recv()

            @pl.when(has_left == 1)
            def _():
                down_copy(z + t, 1).start()

            down_core(z + t).start()

    for line in order:
        diag_y(line).wait_recv()
        diag_x(line).wait_recv()
        to_core(line, fd).start()
    here_cut.wait()
    here_down.wait()
    for k in range(1, 4):
        cut_copy(k).wait()
    for line in range(lines):
        for plane in range(4):
            to_core(line, plane).wait()
        to_x(line).wait_send()
        to_y(line).wait_send()
        diag_x(line).wait_send()
        diag_y(line).wait_send()

        down_core(line).wait()

        @pl.when((line <= z) & (has_right == 1))
        def _():
            to_right(line).wait_send()
            down_copy(line, 0).wait_send()

        @pl.when((line >= z) & (has_left == 1))
        def _():
            to_left(line).wait_send()
            down_copy(line, 1).wait_send()


def gather_all(shard, weight, down, n_dp, n_tp):
    rows, columns = shard.shape
    width = weight.shape[1] // n_tp
    lines = n_dp // 2
    if n_tp != 4 or rows % 32:
        full = lax.all_gather(shard, ("dp", "fsdp"), axis=0, tiled=True)
        down_full = lax.all_gather(down, "dp", axis=0, tiled=True)
        return full, columns_out(weight, n_dp, n_tp), down_full
    dma = pltpu.SemaphoreType.DMA
    hbm = pl.BlockSpec(memory_space=pl.ANY)
    full, parts, down_full = pl.pallas_call(
        functools.partial(gather_kernel, lines),
        out_shape=(
            jax.ShapeDtypeStruct((lines, 2, n_tp, rows, columns), bf16),
            jax.ShapeDtypeStruct((n_tp, rows, width), bf16),
            jax.ShapeDtypeStruct((lines, 2, *down.shape), bf16),
        ),
        in_specs=[hbm, pl.BlockSpec(memory_space=pltpu.VMEM), hbm],
        out_specs=(hbm, hbm, hbm),
        scratch_shapes=[pltpu.VMEM((n_tp, rows, width), bf16), dma((2, lines))]
        + [dma((lines,))] * 9
        + [dma((lines, n_tp))] * 2
        + [dma((n_tp,)), dma((n_tp,)), dma((2, lines)), dma((lines,)), dma((lines,)), dma((lines,)), dma((3,))],
        compiler_params=pltpu.CompilerParams(
            collective_id=0, has_side_effects=True, vmem_limit_bytes=vmem_limit
        ),
        cost_estimate=cost(100),
        name="gather_all",
    )(shard, weight, down)
    full = full.reshape(n_dp * n_tp * rows, columns)
    return full, parts, down_full.reshape(n_dp * down.shape[0], down.shape[1])


def cut_columns(weight, cut, n_dp, n_tp):
    unit = weight.shape[1] // (2 * n_dp * n_tp)
    half = n_dp * unit
    for to in range(n_tp):
        for side in range(2):
            starts = [side * n_tp * half + (j * n_tp + to) * unit for j in range(n_dp)]
            pieces = [weight[:, start : start + unit] for start in starts]
            cut[to, :, side * half : (side + 1) * half] = jnp.concatenate(pieces, axis=1).astype(bf16)


def columns_out_kernel(n_dp, n_tp, weight, parts, cut, send, recv, here_sem):
    z, c, f = place()
    greet([device(z, c, (f + k) % n_tp) for k in range(1, n_tp)], [])

    def away(k):
        to = (f + k) % n_tp
        return pltpu.make_async_remote_copy(
            cut.at[to], parts.at[f], send.at[k], recv.at[k], device_id=device(z, c, to), device_id_type=MESH
        )

    cut_columns(weight, cut, n_dp, n_tp)
    for k in range(1, n_tp):
        away(k).start()
    here = pltpu.make_async_copy(cut.at[f], parts.at[f], here_sem)
    here.start()
    here.wait()
    for k in range(1, n_tp):
        away(k).wait()


def columns_out(weight, n_dp, n_tp):
    rows, width = weight.shape
    dma = pltpu.SemaphoreType.DMA
    return pl.pallas_call(
        functools.partial(columns_out_kernel, n_dp, n_tp),
        out_shape=jax.ShapeDtypeStruct((n_tp, rows, width // n_tp), bf16),
        out_specs=pl.BlockSpec(memory_space=pl.ANY),
        scratch_shapes=[
            pltpu.VMEM((n_tp, rows, width // n_tp), bf16), dma((n_tp,)), dma((n_tp,)), dma(()),
        ],
        compiler_params=pltpu.CompilerParams(
            collective_id=1, has_side_effects=True, vmem_limit_bytes=vmem_limit
        ),
        cost_estimate=cost(20),
        name="columns_out",
    )(weight)


def columns_back_kernel(n_dp, n_tp, parts, whole, got, send, recv, here_sem):
    z, c, f = place()
    greet([device(z, c, (f + k) % n_tp) for k in range(1, n_tp)], [])
    unit = whole.shape[1] // (2 * n_dp * n_tp)
    half = n_dp * unit

    def away(k):
        to = (f + k) % n_tp
        return pltpu.make_async_remote_copy(
            parts.at[to], got.at[f], send.at[k], recv.at[k], device_id=device(z, c, to), device_id_type=MESH
        )

    for k in range(1, n_tp):
        away(k).start()
    here = pltpu.make_async_copy(parts.at[f], got.at[f], here_sem)
    here.start()
    here.wait()
    for k in range(1, n_tp):
        away(k).wait()
    for side in range(2):
        pieces = [
            got[frm, :, side * half + j * unit : side * half + (j + 1) * unit].astype(f32)
            for j in range(n_dp)
            for frm in range(n_tp)
        ]
        whole[:, side * n_tp * half : (side + 1) * n_tp * half] = jnp.concatenate(pieces, axis=1)


def columns_back(parts, n_dp, n_tp):
    _, rows, width = parts.shape
    dma = pltpu.SemaphoreType.DMA
    return pl.pallas_call(
        functools.partial(columns_back_kernel, n_dp, n_tp),
        out_shape=jax.ShapeDtypeStruct((rows, width * n_tp), f32),
        in_specs=[pl.BlockSpec(memory_space=pl.ANY)],
        scratch_shapes=[pltpu.VMEM(parts.shape, bf16), dma((n_tp,)), dma((n_tp,)), dma(())],
        compiler_params=pltpu.CompilerParams(
            collective_id=2, has_side_effects=True, vmem_limit_bytes=vmem_limit
        ),
        cost_estimate=cost(20),
        name="columns_back",
    )(parts)


def total_kernel(n_dp, n_tp, value, total, held, got, send, recv):
    dp, f = lax.axis_index("dp"), lax.axis_index("fsdp")
    partners = []
    for axis, size in (("dp", n_dp), ("fsdp", n_tp)):
        for bit in range(size.bit_length() - 1):
            index = {"dp": dp, "fsdp": f}
            index[axis] = flipped(index[axis], 1 << bit)
            partners.append(index)
    greet(partners, [])
    held[0] = value[...]
    for step, partner in enumerate(partners):
        swap = pltpu.make_async_remote_copy(
            held.at[step], got.at[step], send.at[step], recv.at[step], device_id=partner, device_id_type=MESH
        )
        swap.start()
        swap.wait()
        held[step + 1] = held[step] + got[step]
    total[...] = held[len(partners)]


def total_over_devices(value, n_dp, n_tp):
    steps = (n_dp * n_tp).bit_length() - 1
    dma = pltpu.SemaphoreType.DMA
    tile = (8, 128)
    spread = pl.pallas_call(
        functools.partial(total_kernel, n_dp, n_tp),
        out_shape=jax.ShapeDtypeStruct(tile, f32),
        scratch_shapes=[
            pltpu.VMEM((steps + 1, *tile), f32), pltpu.VMEM((steps, *tile), f32), dma((steps,)), dma((steps,)),
        ],
        compiler_params=pltpu.CompilerParams(collective_id=3, has_side_effects=True),
        cost_estimate=cost(13),
        name="total",
    )(jnp.broadcast_to(value, tile))
    return spread


def adam_update(weight, gradient, first, second, rate, decay):
    first = beta_one * first + (1.0 - beta_one) * gradient
    second = beta_two * second + (1.0 - beta_two) * gradient * gradient
    first_hat = first / (1.0 - beta_one**STEP)
    second_hat = second / (1.0 - beta_two**STEP)
    weight = weight - rate * (first_hat / (jnp.sqrt(second_hat) + adam_eps) + decay * weight)
    return (weight, first, second)


def matmul(a, b):
    return jnp.dot(a, b, preferred_element_type=f32)


def matmul_t(a, b):
    return lax.dot_general(a, b, (((1,), (1,)), ((), ())), preferred_element_type=f32)


def matmul_tn(a, b):
    return lax.dot_general(a, b, (((0,), (0,)), ((), ())), preferred_element_type=f32)


def swap_core(block, n_dp):
    return lax.ppermute(block, "dp", [(i, i ^ 1) for i in range(n_dp)])


def plane_swap(block, k, n_tp):
    return lax.ppermute(block, "fsdp", [(i, i ^ k) for i in range(n_tp)])


def plane_gather(block, n_tp):
    if n_tp != 4:
        return jnp.concatenate([block] + [plane_swap(block, k, n_tp) for k in range(1, n_tp)], axis=0)
    half = block.shape[0] // 2
    over_x, over_y = plane_swap(block, 1, n_tp), plane_swap(block, 2, n_tp)
    far = [plane_swap(over_y[:half], 1, n_tp), plane_swap(over_x[half:], 2, n_tp)]
    return jnp.concatenate([block, over_x, over_y] + far, axis=0)


def core_sum(parts, n_dp):
    core = lax.axis_index("dp") % 2
    mine = lax.dynamic_index_in_dim(parts, core, 1, keepdims=False)
    other = lax.dynamic_index_in_dim(parts, 1 - core, 1, keepdims=False)
    return mine.astype(f32) + swap_core(other, n_dp).astype(f32)


def line_sum(parts, n_dp):
    lines = n_dp // 2
    place = lax.axis_index("dp") // 2
    result = lax.dynamic_index_in_dim(parts, place, 0, keepdims=False)
    for way in (1, -1):
        arrived = None
        for step in range(1, lines):
            target = jnp.clip(place + way * (lines - step), 0, lines - 1)
            load = lax.dynamic_index_in_dim(parts, target, 0, keepdims=False).astype(f32)
            if arrived is not None:
                load = load + arrived.astype(f32)
            senders = range(step) if way == 1 else range(lines - step, lines)
            pairs = [(2 * s + c, 2 * (s + way) + c) for s in senders for c in range(2)]
            arrived = lax.ppermute(load.astype(bf16), "dp", pairs)
        result = result.astype(f32) + arrived.astype(f32)
    return result


def plane_sum(parts, n_tp):
    here = lax.axis_index("fsdp")
    total = lax.dynamic_index_in_dim(parts, here, 0, keepdims=False).astype(f32)
    for k in range(1, n_tp):
        load = lax.dynamic_index_in_dim(parts, here ^ k, 0, keepdims=False).astype(bf16)
        total = total + plane_swap(load, k, n_tp).astype(f32)
    return total


def by_rows(rows, body):
    def step(i, carry):
        body(pl.ds(pl.multiple_of(i * 16, 16), 16))
        return carry

    lax.fori_loop(0, rows // 16, step, 0)


def scatter_kernel(lines, n_arrays, *refs):
    groups = [refs[i * n_arrays : (i + 1) * n_arrays] for i in range(8)]
    arrays, outs, sums, others, firsts, seconds, alongs, leaving = groups
    load_sem, core_send, core_recv, one_send, one_recv, two_send, two_recv, line_send, line_recv = refs[8 * n_arrays :]
    z, c, f = place()
    planes, rows = sums[0].shape[1:3]
    half = rows // 2
    fx, fy = flipped(f, 1), flipped(f, 2)
    fd = flipped(fx, 2)
    x_dev, y_dev, core_dev = device(z, c, fx), device(z, c, fy), device(z, 1 - c, f)
    has_left = jnp.minimum(z, 1)
    has_right = jnp.minimum(lines - 1 - z, 1)
    left_dev = device(jnp.maximum(z - 1, 0), c, f)
    right_dev = device(jnp.minimum(z + 1, lines - 1), c, f)
    greet([x_dev, y_dev, core_dev], [(has_left, left_dev), (has_right, right_dev)])
    halves = (pl.ds(0, half), pl.ds(half, half))
    near, next_near, step_dev = (fx, fy), (fy, fx), (x_dev, y_dev)

    def remote(src, dst, send, recv, dev):
        return pltpu.make_async_remote_copy(src, dst, send, recv, device_id=dev, device_id_type=MESH)

    def to_core(a, d):
        return remote(arrays[a].at[d, 1 - c], others[a].at[d], core_send.at[a, d], core_recv.at[a, d], core_dev)

    def load(a, d):
        return pltpu.make_async_copy(arrays[a].at[d, c], sums[a].at[d], load_sem.at[a, d])

    def one(a, d, way, i):
        block = (near[way], fd)[i]
        return remote(
            sums[a].at[d, block, halves[way]], firsts[a].at[way, d, i],
            one_send.at[a, d, way, i], one_recv.at[a, d, way, i], step_dev[way],
        )

    def two(a, d, way):
        return remote(
            sums[a].at[d, next_near[way], halves[way]], seconds[a].at[way, d],
            two_send.at[a, d, way], two_recv.at[a, d, way], step_dev[1 - way],
        )

    def to_right(a, d):
        return remote(leaving[a].at[d], alongs[a].at[d], line_send.at[a, d], line_recv.at[a, d], right_dev)

    def to_left(a, d, slot):
        return remote(leaving[a].at[d], alongs[a].at[slot], line_send.at[a, d], line_recv.at[a, slot], left_dev)

    def add_along(a, slot):
        def step(r):
            outs[a][r] += alongs[a][slot, r].astype(f32)

        by_rows(rows, step)

    order = []
    for t in reversed(range(lines)):
        line = z
        for b in range(lines.bit_length() - 1):
            if t >> b & 1:
                line = flipped(line, 1 << b)
        order.append(line)
    chunks = [(a, d) for d in order for a in range(n_arrays)]
    for a, d in chunks:
        to_core(a, d).start()
        load(a, d).start()
    for a, d in chunks:
        load(a, d).wait()
        to_core(a, d).wait_recv()

        def core_add(r):
            for plane in range(planes):
                sums[a][d, plane, r] = (sums[a][d, plane, r].astype(f32) + others[a][d, plane, r].astype(f32)).astype(bf16)

        by_rows(rows, core_add)
        for i in (1, 0):
            for way in range(2):
                one(a, d, way, i).start()
    for a, d in chunks:
        for way in range(2):
            one(a, d, way, 1).wait_recv()

            def first_add(r):
                there = pl.ds(pl.multiple_of(r.start + way * half, 16), r.size)
                mine = sums[a][d, next_near[way], there].astype(f32)
                sums[a][d, next_near[way], there] = (mine + firsts[a][way, d, 1, r].astype(f32)).astype(bf16)

            by_rows(half, first_add)
            two(a, d, way).start()
    for a, d in chunks:
        for way in range(2):
            one(a, d, way, 0).wait_recv()
            two(a, d, way).wait_recv()

            def second_add(r):
                there = pl.ds(pl.multiple_of(r.start + way * half, 16), r.size)
                outs[a][there] = (
                    sums[a][d, f, there].astype(f32)
                    + firsts[a][way, d, 0, r].astype(f32)
                    + seconds[a][way, d, r].astype(f32)
                )

            by_rows(half, second_add)

        @pl.when((d > z) & (has_left == 1))
        def _():
            to_right(a, d).wait_recv()
            add_along(a, d)

        @pl.when((d < z) & (has_right == 1))
        def _():
            to_left(a, d, d).wait_recv()
            add_along(a, d)

        @pl.when(d != z)
        def _():
            def leave(r):
                leaving[a][d, r] = outs[a][r].astype(bf16)

            by_rows(rows, leave)

        @pl.when(d > z)
        def _():
            to_right(a, d).start()

        @pl.when((d < z) & (d + 1 < z))
        def _():
            to_left(a, d, d).start()

        @pl.when(d + 1 == z)
        def _():
            to_left(a, d, lines).start()

    for a in range(n_arrays):

        @pl.when(has_left == 1)
        def _():
            to_right(a, z).wait_recv()
            add_along(a, z)

        @pl.when(has_right == 1)
        def _():
            to_left(a, z, lines).wait_recv()
            add_along(a, lines)

    for a, d in chunks:
        to_core(a, d).wait_send()
        for way in range(2):
            one(a, d, way, 0).wait_send()
            one(a, d, way, 1).wait_send()
            two(a, d, way).wait_send()

        @pl.when(d != z)
        def _():
            to_right(a, d).wait_send()


def scatter_all(arrays, n_dp, n_tp):
    lines = n_dp // 2
    rows = arrays[0].shape[0] // (n_dp * n_tp)
    if n_tp != 4 or rows % 32:
        results = []
        for array in arrays:
            parts = core_sum(array.reshape(lines, 2, n_tp, rows, -1), n_dp)
            results.append(line_sum(plane_sum(parts.transpose(1, 0, 2, 3), n_tp), n_dp))
        return results
    dma = pltpu.SemaphoreType.DMA
    widths = [array.shape[1] for array in arrays]
    n = len(widths)
    shapes = [
        (lines, n_tp, rows), (lines, n_tp, rows), (2, lines, 2, rows // 2), (2, lines, rows // 2),
        (lines + 1, rows), (lines, rows),
    ]
    return pl.pallas_call(
        functools.partial(scatter_kernel, lines, n),
        out_shape=[jax.ShapeDtypeStruct((rows, width), f32) for width in widths],
        in_specs=[pl.BlockSpec(memory_space=pl.ANY)] * n,
        scratch_shapes=[pltpu.VMEM((*shape, width), bf16) for shape in shapes for width in widths]
        + [dma((n, lines))] * 3
        + [dma((n, lines, 2, 2))] * 2
        + [dma((n, lines, 2))] * 2
        + [dma((n, lines)), dma((n, lines + 1))],
        compiler_params=pltpu.CompilerParams(
            collective_id=4, has_side_effects=True, vmem_limit_bytes=vmem_limit
        ),
        cost_estimate=cost(110),
        name="scatter_all",
    )(*[array.reshape(lines, 2, n_tp, rows, -1) for array in arrays])


def rope_tile(tile, cos, sin):
    pairs = [tile[:, i : i + 128] for i in range(0, tile.shape[1], 128)]
    return jnp.concatenate([pair * cos + halves_swapped(pair) * sin for pair in pairs], axis=1)


def attend_heads(qkv, context, log_totals, allowed):
    length = qkv.shape[0]
    scale = HD ** (-0.5)
    for group in range(KVH):
        kc = D + (group // 2) * 128
        keys = both_places(qkv[:, kc : kc + 128], group % 2)
        values = both_places(qkv[:, kc + KW : kc + KW + 128], group % 2)

        def pair_step(pair_index, carry):
            pair = group * (GROUP // 2) + pair_index
            lanes = pl.ds(pl.multiple_of(pair * 128, 128), 128)
            queries = qkv[:, lanes]
            total = jnp.zeros((length, 128), f32)
            for side in range(2):
                scores = dot_t(keys[side], queries) * scale
                scores = jnp.where(allowed, scores, -1e30)
                top = jnp.max(scores, axis=0, keepdims=True)
                raised = jnp.exp(scores - top)
                totals = jnp.sum(raised, axis=0, keepdims=True)
                probs = (raised / totals).astype(bf16)
                total = total + dot_tn(probs, values[side])
                log_totals[pl.ds(2 * pair + side, 1), :] = top + jnp.log(totals)
            context[:, lanes] = total.astype(bf16)
            return carry

        lax.fori_loop(0, GROUP // 2, pair_step, 0)


def tile_at(i, width, start=0):
    return pl.ds(pl.multiple_of(start + i * width, 128), width)


class Exchange:
    def __init__(self, own, whole, sems, i, x_dev, y_dev):
        send, recv, here = sems
        half = own.shape[0] // 2

        def remote(src, dst, k, dev):
            return pltpu.make_async_remote_copy(
                src, dst, send.at[i, k], recv.at[i, k], device_id=dev, device_id_type=MESH
            )

        low, high = pl.ds(0, half), pl.ds(half, half)
        self.near = [remote(own, whole.at[1], 0, x_dev), remote(own, whole.at[2], 1, y_dev)]
        self.far = [
            remote(whole.at[2, low], whole.at[3, low], 2, x_dev),
            remote(whole.at[1, high], whole.at[3, high], 3, y_dev),
        ]
        self.here = pltpu.make_async_copy(own, whole.at[0], here.at[i])

    def start(self):
        for copy in self.near:
            copy.start()
        self.here.start()

    def pass_on(self):
        for copy in self.near:
            copy.wait_recv()
        for copy in self.far:
            copy.start()

    def finish(self):
        for copy in self.far:
            copy.wait()
        for copy in self.near:
            copy.wait_send()
        self.here.wait()


def forward_kernel(x, grads, gains, cosine, sine, seg_col, seg_row, weights, qkv, context, log_totals, middle,
                   normed_one, normed_all, grads_all, q_weight, o_weight, normed_two, load_sem, *sems):
    z, c, f = place()
    x_dev, y_dev = device(z, c, flipped(f, 1)), device(z, c, flipped(f, 2))
    greet([x_dev, y_dev], [])
    length = x.shape[0]
    width = D + 2 * KW
    of_grads = Exchange(grads, grads_all, sems, 0, x_dev, y_dev)
    of_normed = Exchange(normed_two, normed_all, sems, 1, x_dev, y_dev)
    of_grads.start()
    load_q = pltpu.make_async_copy(weights.at[:, pl.ds(0, width)], q_weight, load_sem.at[0])
    load_o = pltpu.make_async_copy(weights.at[:, pl.ds(width, D)], o_weight, load_sem.at[1])
    load_q.start()
    load_o.start()

    def norm_one(r):
        rows = x[r].astype(f32)
        inverse = lax.rsqrt(jnp.mean(rows * rows, axis=-1, keepdims=True) + norm_eps)
        normed_one[r] = (rows * inverse * gains[0:1, :]).astype(bf16)

    by_rows(length, norm_one)
    load_q.wait()
    cos, sin = cosine[...], sine[...]

    def project(i, carry):
        lanes = tile_at(i, 256)
        qkv[:, lanes] = rope_tile(dot_n(normed_one[...], q_weight[:, lanes]), cos, sin).astype(bf16)
        return carry

    lax.fori_loop(0, (D + KW) // 256, project, 0)
    qkv[:, D + KW :] = dot_n(normed_one[...], q_weight[:, D + KW :]).astype(bf16)
    allowed = mask_keys_rows(seg_col[...], seg_row[...], length)
    attend_heads(qkv, context, log_totals, allowed)
    load_o.wait()

    def project_out(i, carry):
        lanes = tile_at(i, 256)
        middle[:, lanes] = x[:, lanes].astype(f32) + dot_n(context[...], o_weight[:, lanes])
        return carry

    lax.fori_loop(0, D // 256, project_out, 0)

    def norm_two(r):
        rows = middle[r]
        inverse = lax.rsqrt(jnp.mean(rows * rows, axis=-1, keepdims=True) + norm_eps)
        normed_two[r] = (rows * inverse * gains[1:2, :]).astype(bf16)

    by_rows(length, norm_two)
    of_normed.start()
    of_grads.pass_on()
    of_normed.pass_on()
    of_normed.finish()
    of_grads.finish()


def forward(x, grads, gains, cosine, sine, seg_col, seg_row, weights):
    length = x.shape[0]
    dma = pltpu.SemaphoreType.DMA
    vmem, hbm = pl.BlockSpec(memory_space=pltpu.VMEM), pl.BlockSpec(memory_space=pl.ANY)
    width = D + 2 * KW
    return pl.pallas_call(
        forward_kernel,
        out_shape=(
            jax.ShapeDtypeStruct((length, width), bf16),
            jax.ShapeDtypeStruct((length, D), bf16),
            jax.ShapeDtypeStruct((HEADS, length), f32),
            jax.ShapeDtypeStruct((length, D), f32),
            jax.ShapeDtypeStruct((length, D), bf16),
            jax.ShapeDtypeStruct((4, length, D), bf16),
            jax.ShapeDtypeStruct((4, length, D), bf16),
        ),
        in_specs=[vmem, hbm] + [vmem] * 5 + [hbm],
        out_specs=(vmem,) * 5 + (hbm,) * 2,
        scratch_shapes=[
            pltpu.VMEM((D, width), bf16), pltpu.VMEM((D, D), bf16), pltpu.VMEM((length, D), bf16),
            dma((2,)), dma((2, 4)), dma((2, 4)), dma((2,)),
        ],
        compiler_params=pltpu.CompilerParams(
            collective_id=5, has_side_effects=True, vmem_limit_bytes=vmem_limit
        ),
        cost_estimate=cost(95),
        name="forward",
    )(x, grads, gains, cosine, sine, seg_col, seg_row, weights)


class PlaneSum:
    def __init__(self, parts, ones, twos, sems, x_dev, y_dev):
        one_send, one_recv, two_send, two_recv = sems
        self.half = parts.shape[1] // 2
        self.parts, self.ones, self.twos = parts, ones, twos
        halves = (pl.ds(0, self.half), pl.ds(self.half, self.half))
        step_dev = (x_dev, y_dev)

        def remote(src, dst, send, recv, dev):
            return pltpu.make_async_remote_copy(src, dst, send, recv, device_id=dev, device_id_type=MESH)

        self.near, self.far, self.two = [], [], []
        for way in range(2):
            for i, copies in enumerate((self.near, self.far)):
                block = parts.at[2 if i else way, halves[way]]
                copies.append(
                    remote(block, ones.at[way, i], one_send.at[way, i], one_recv.at[way, i], step_dev[way])
                )
            self.two.append(
                remote(parts.at[1 - way, halves[way]], twos.at[way], two_send.at[way], two_recv.at[way], step_dev[1 - way])
            )

    def there(self, r, way):
        return pl.ds(pl.multiple_of(r.start + way * self.half, 16), r.size)

    def pass_on(self):
        for way in range(2):
            self.far[way].wait_recv()

            def add_far(r):
                there = self.there(r, way)
                mine = self.parts[1 - way, there].astype(f32)
                self.parts[1 - way, there] = (mine + self.ones[way, 1, r].astype(f32)).astype(bf16)

            by_rows(self.half, add_far)
            self.two[way].start()

    def finish(self, add):
        for way in range(2):
            self.near[way].wait()
            self.far[way].wait_send()
            self.two[way].wait()
        for way in range(2):

            def add_all(r):
                add(self.there(r, way), self.ones[way, 0, r].astype(f32) + self.twos[way, r].astype(f32))

            by_rows(self.half, add_all)


def plane_sum_scratch(length, columns):
    dma = pltpu.SemaphoreType.DMA
    shapes = ((3, length, columns), (2, 2, length // 2, columns), (2, length // 2, columns))
    return [pltpu.VMEM(shape, bf16) for shape in shapes], [dma((2, 2)), dma((2, 2)), dma((2,)), dma((2,))]


def attend_heads_grad(qkv, grad_context, log_totals, grad_proj, allowed, cos, sin):
    length = qkv.shape[0]
    scale = HD ** (-0.5)

    def unrotate(pair):
        return pair * cos + halves_swapped(pair * sin)

    key_parts, value_parts = [], []
    for group in range(KVH):
        kc = D + (group // 2) * 128
        keys = both_places(qkv[:, kc : kc + 128], group % 2)
        values = both_places(qkv[:, kc + KW : kc + KW + 128], group % 2)

        def pair_step(pair_index, carry):
            grad_keys, grad_values = list(carry[:2]), list(carry[2:])
            pair = group * (GROUP // 2) + pair_index
            lanes = pl.ds(pl.multiple_of(pair * 128, 128), 128)
            queries = qkv[:, lanes]
            grads = grad_context[:, lanes]
            total = jnp.zeros((length, 128), f32)
            for side in range(2):
                scores = dot_t(keys[side], queries) * scale
                scores = jnp.where(allowed, scores, -1e30)
                probs = jnp.exp(scores - log_totals[pl.ds(2 * pair + side, 1), :])
                grad_probs = dot_t(values[side], grads)
                grad_values[side] = grad_values[side] + dot_n(probs.astype(bf16), grads)
                inner = jnp.sum(probs * grad_probs, axis=0, keepdims=True)
                raw = (probs * (grad_probs - inner) * scale).astype(bf16)
                total = total + dot_tn(raw, keys[side])
                grad_keys[side] = grad_keys[side] + dot_n(raw, queries)
            grad_proj[:, lanes] = unrotate(total).astype(bf16)
            return (*grad_keys, *grad_values)

        empty = jnp.zeros((length, 128), f32)
        out = lax.fori_loop(0, GROUP // 2, pair_step, (empty,) * 4)

        def joined(low_side, high_side):
            low, _ = split_pair(low_side)
            _, high = split_pair(high_side)
            both = low + high
            return both + pltpu.roll(both, HD, 1)

        key_parts.append(joined(out[0], out[1]))
        value_parts.append(joined(out[2], out[3]))
    lane = lax.broadcasted_iota(jnp.int32, (length, 128), 1)
    for c in range(KVH // 2):
        keys = jnp.where(lane < HD, key_parts[2 * c], key_parts[2 * c + 1])
        values = jnp.where(lane < HD, value_parts[2 * c], value_parts[2 * c + 1])
        grad_proj[:, D + c * 128 : D + (c + 1) * 128] = unrotate(keys).astype(bf16)
        grad_proj[:, D + KW + c * 128 : D + KW + (c + 1) * 128] = values.astype(bf16)


def backward_kernel(x, grads, grad_normed, middle, gains, cosine, sine, seg_col, seg_row, normed_one, qkv, context,
                    log_totals, weights, layer, layer_out, input_grad, grad_o, grad_q, weight, grad_middle,
                    grad_branch, grad_context, grad_proj, grad_one, gain_rows, gain_columns, stage, own_layer, parts,
                    ones, twos, *sems):
    sum_sems, (load_sem, out_sem) = sems[:4], sems[4:]
    z, c, f = place()
    x_dev, y_dev = device(z, c, flipped(f, 1)), device(z, c, flipped(f, 2))
    length = x.shape[0]
    width = D + 2 * KW
    load_parts = pltpu.make_async_copy(layer.at[pl.ds(1, 3)], parts, load_sem.at[0])
    load_own = pltpu.make_async_copy(layer.at[0], own_layer, load_sem.at[1])
    load_o = pltpu.make_async_copy(weights.at[:, pl.ds(width, D)], weight.at[:, pl.ds(0, D)], load_sem.at[2])
    load_q = pltpu.make_async_copy(weights.at[:, pl.ds(0, width)], weight, load_sem.at[2])
    load_grads = pltpu.make_async_copy(grad_normed, grad_middle, load_sem.at[3])
    for copy in (load_parts, load_grads, load_o, load_own):
        copy.start()
    greet([x_dev, y_dev], [])
    summed = PlaneSum(parts, ones, twos, sum_sems, x_dev, y_dev)
    load_parts.wait()
    for copy in summed.far + summed.near:
        copy.start()
    gain_rows[...] = jnp.zeros_like(gain_rows)

    def fold(value):
        return jnp.sum(value, axis=0, keepdims=True)

    def middle_grads(r):
        rows, arrived = middle[r], grad_middle[r]
        inverse = lax.rsqrt(jnp.mean(rows * rows, axis=-1, keepdims=True) + norm_eps)
        gain_rows[1:2, :] += fold(arrived * rows * inverse)
        weighted = arrived * gains[1:2, :]
        inner = jnp.mean(weighted * rows, axis=-1, keepdims=True)
        value = grads[r].astype(f32) + inverse * weighted - rows * (inverse * inverse * inverse * inner)
        grad_middle[r] = value
        grad_branch[r] = value.astype(bf16)

    load_grads.wait()
    by_rows(length, middle_grads)
    load_o.wait()

    def context_step(i, carry):
        tile = tile_at(i, 512)
        grad_context[:, tile] = dot_t(grad_branch[...], weight[tile, 0:D]).astype(bf16)
        return carry

    lax.fori_loop(0, D // 512, context_step, 0)
    load_q.start()
    steps = D // 256

    def weight_grads(left, right, target, columns, which):
        def out(i, slot):
            return pltpu.make_async_copy(
                stage.at[slot, :, pl.ds(0, columns)], target.at[tile_at(i, 256), pl.ds(0, columns)], out_sem.at[which, slot]
            )

        def step(i, carry):
            slot = i % 2

            @pl.when(i >= 2)
            def _():
                out(i - 2, slot).wait()

            stage[slot, :, 0:columns] = dot_tn(left[:, tile_at(i, 256)], right[...]).astype(bf16)
            out(i, slot).start()
            return carry

        lax.fori_loop(0, steps, step, 0)
        for i in (steps - 2, steps - 1):
            out(i, i % 2).wait()

    weight_grads(context, grad_branch, grad_o, D, 0)
    allowed = mask_keys_rows(seg_col[...], seg_row[...], length)
    attend_heads_grad(qkv, grad_context, log_totals, grad_proj, allowed, cosine[...], sine[...])
    summed.pass_on()
    weight_grads(normed_one, grad_proj, grad_q, width, 1)
    load_q.wait()

    def normed_step(i, carry):
        tile = tile_at(i, 512)
        grad_one[:, tile] = dot_t(grad_proj[...], weight[tile, :])
        return carry

    lax.fori_loop(0, D // 512, normed_step, 0)

    def input_grads(r):
        rows, arrived = x[r].astype(f32), grad_one[r]
        inverse = lax.rsqrt(jnp.mean(rows * rows, axis=-1, keepdims=True) + norm_eps)
        gain_rows[0:1, :] += fold(arrived * rows * inverse)
        weighted = arrived * gains[0:1, :]
        inner = jnp.mean(weighted * rows, axis=-1, keepdims=True)
        value = grad_middle[r] + inverse * weighted - rows * (inverse * inverse * inverse * inner)
        input_grad[r] = value.astype(bf16)

    by_rows(length, input_grads)
    for i in range(D // 128):
        rows = pl.ds(i * 128, 128)
        square = jnp.concatenate([gain_rows[:, rows], jnp.zeros((120, 128), f32)], axis=0)
        gain_columns[rows, :] = square.T.astype(bf16)
    gains_out = pltpu.make_async_copy(gain_columns, grad_q.at[:, pl.ds(width, 128)], load_sem.at[0])
    gains_out.start()

    def add_layer(r, value):
        layer_out[r] = (middle[r] + own_layer[r].astype(f32) + value).astype(bf16)

    load_own.wait()
    summed.finish(add_layer)
    gains_out.wait()


def backward(x, grads, grad_normed, middle, gains, cosine, sine, seg_col, seg_row, normed_one, qkv, context,
             log_totals, weights, layer):
    length = x.shape[0]
    width = D + 2 * KW
    dma = pltpu.SemaphoreType.DMA
    vmem, hbm = pl.BlockSpec(memory_space=pltpu.VMEM), pl.BlockSpec(memory_space=pl.ANY)
    sum_buffers, sum_sems = plane_sum_scratch(length, D)
    return pl.pallas_call(
        backward_kernel,
        out_shape=(
            jax.ShapeDtypeStruct((length, D), bf16),
            jax.ShapeDtypeStruct((length, D), bf16),
            jax.ShapeDtypeStruct((D, D), bf16),
            jax.ShapeDtypeStruct((D, width + 128), bf16),
        ),
        in_specs=[vmem, vmem, hbm] + [vmem] * 10 + [hbm] * 2,
        out_specs=(vmem, vmem, hbm, hbm),
        scratch_shapes=[
            pltpu.VMEM((D, width), bf16), pltpu.VMEM((length, D), f32), pltpu.VMEM((length, D), bf16),
            pltpu.VMEM((length, D), bf16), pltpu.VMEM((length, width), bf16), pltpu.VMEM((length, D), f32),
            pltpu.VMEM((8, D), f32), pltpu.VMEM((D, 128), bf16), pltpu.VMEM((2, 256, width), bf16),
            pltpu.VMEM((length, D), bf16),
        ]
        + sum_buffers + sum_sems + [dma((4,)), dma((2, 2))],
        compiler_params=pltpu.CompilerParams(
            collective_id=7, has_side_effects=True, vmem_limit_bytes=feed_vmem_limit
        ),
        cost_estimate=cost(65),
        name="backward",
    )(x, grads, grad_normed, middle, gains, cosine, sine, seg_col, seg_row, normed_one, qkv, context, log_totals,
      weights, layer)


def norm_kernel(n_dp, n_tp, parts, qkv, out, down, mlp, total, got, held, got_dp, got_tp, send, recv, total_send,
                total_recv, here_sem):
    z, c, f = place()
    dp = z * 2 + c
    columns = [(f + k) % n_tp for k in range(1, n_tp)]
    lines = [(dp + k) % n_dp for k in range(1, n_dp)]
    greet([device(z, c, to) for to in columns] + [{"dp": to, "fsdp": f} for to in lines], [])
    unit = mlp.shape[1] // (2 * n_dp * n_tp)
    half = n_dp * unit

    def away(k):
        to = columns[k - 1]
        return pltpu.make_async_remote_copy(
            parts.at[to], got.at[f], send.at[k], recv.at[k], device_id=device(z, c, to), device_id_type=MESH
        )

    for k in range(1, n_tp):
        away(k).start()
    here = pltpu.make_async_copy(parts.at[f], got.at[f], here_sem)
    here.start()
    held[...] = jnp.zeros_like(held)

    def add_squares(ref):
        def step(r):
            part = ref[r, :].astype(f32)
            part = part * part
            lanes = [part[:, i : i + 128] for i in range(0, part.shape[1], 128)]
            held[...] += functools.reduce(jnp.add, lanes)

        by_rows(ref.shape[0], step)

    add_squares(qkv)
    add_squares(out)
    add_squares(down)
    here.wait()
    for k in range(1, n_tp):
        away(k).wait()
    for frm in range(n_tp):
        add_squares(got.at[frm])

    def spread(buffer, own, value, partners, base):
        buffer[own] = value
        copies = [
            pltpu.make_async_remote_copy(
                buffer.at[own], buffer.at[own], total_send.at[base + k], total_recv.at[base + k],
                device_id=partner, device_id_type=MESH,
            )
            for k, partner in enumerate(partners)
        ]
        for copy in copies:
            copy.start()
        return copies

    def summed(buffer, copies):
        for copy in copies:
            copy.wait()
        return functools.reduce(jnp.add, [buffer[i] for i in range(buffer.shape[0])])

    own_total = jnp.sum(jnp.sum(held[...], axis=0, keepdims=True), axis=1, keepdims=True)
    copies = spread(
        got_dp, dp, jnp.broadcast_to(own_total, (8, 128)), [{"dp": to, "fsdp": f} for to in lines], 0
    )
    for side in range(2):
        pieces = [
            got[frm, :, side * half + j * unit : side * half + (j + 1) * unit].astype(f32)
            for j in range(n_dp)
            for frm in range(n_tp)
        ]
        mlp[:, side * n_tp * half : (side + 1) * n_tp * half] = jnp.concatenate(pieces, axis=1)
    line_total = summed(got_dp, copies)
    copies = spread(got_tp, f, line_total, [device(z, c, to) for to in columns], n_dp)
    total[...] = summed(got_tp, copies)


def norm_parts(parts, qkv, out, down, n_dp, n_tp):
    _, rows, width = parts.shape
    dma = pltpu.SemaphoreType.DMA
    vmem, hbm = pl.BlockSpec(memory_space=pltpu.VMEM), pl.BlockSpec(memory_space=pl.ANY)
    return pl.pallas_call(
        functools.partial(norm_kernel, n_dp, n_tp),
        out_shape=(jax.ShapeDtypeStruct((rows, width * n_tp), f32), jax.ShapeDtypeStruct((8, 128), f32)),
        in_specs=[hbm, vmem, vmem, vmem],
        scratch_shapes=[
            pltpu.VMEM(parts.shape, bf16), pltpu.VMEM((16, 128), f32), pltpu.VMEM((n_dp, 8, 128), f32),
            pltpu.VMEM((n_tp, 8, 128), f32), dma((n_tp,)), dma((n_tp,)), dma((n_dp + n_tp,)), dma((n_dp + n_tp,)),
            dma(()),
        ],
        compiler_params=pltpu.CompilerParams(
            collective_id=8, has_side_effects=True, vmem_limit_bytes=vmem_limit
        ),
        cost_estimate=cost(35),
        name="norm_parts",
    )(parts, qkv, out, down)


def adam_kernel(total, *refs):
    scale = clip_norm / jnp.maximum(jnp.sqrt(total[0:1, 0:1]), clip_norm)
    grads, refs = refs[:4], refs[4:]
    states, news = refs[:12], refs[12:]
    for i in range(4):
        gradient = grads[i][...].astype(f32) * scale
        new = adam_update(
            states[3 * i][...], gradient, states[3 * i + 1][...], states[3 * i + 2][...], matrix_rate, weight_decay
        )
        for k in range(3):
            news[3 * i + k][...] = new[k]


def adam_all(total, grads, states):
    shapes = [state[0].shape for state in states]

    def block(shape, steps):
        rows, columns = shape
        if rows % (8 * steps) == 0:
            return pl.BlockSpec((rows // steps, columns), lambda i: (i, 0))
        if columns % (128 * steps) == 0:
            return pl.BlockSpec((rows, columns // steps), lambda i: (0, i))
        return None

    steps = 8 if all(block(shape, 8) for shape in shapes) else 4
    specs = [block(shape, steps) for shape in shapes]
    flat = [array for state in states for array in state]
    state_specs = [spec for spec in specs for _ in range(3)]
    return pl.pallas_call(
        adam_kernel,
        grid=(steps,),
        out_shape=[jax.ShapeDtypeStruct(array.shape, f32) for array in flat],
        in_specs=[pl.BlockSpec((8, 128), lambda i: (0, 0))] + specs + state_specs,
        out_specs=state_specs,
        compiler_params=pltpu.CompilerParams(vmem_limit_bytes=vmem_limit),
        cost_estimate=cost(14),
        name="adam",
    )(total, *grads, *flat)


def feed_kernel(n_hbm, g_hbm, wm_hbm, wd_hbm, grad_normed, grad_down, grad_mlp, layer, n, g, wm, wd, gh, act,
                stage, parts, ones, twos, *sems):
    sum_sems, (load_sem, out_sem) = sems[:4], sems[4:]
    z, c, f = place()
    x_dev, y_dev = device(z, c, flipped(f, 1)), device(z, c, flipped(f, 2))
    tokens = n.shape[0]
    length = tokens // 4
    ff = wd.shape[0]
    loads = [
        pltpu.make_async_copy(src, dst, load_sem.at[i])
        for i, (src, dst) in enumerate(((n_hbm, n), (wm_hbm, wm), (wd_hbm, wd), (g_hbm, g)))
    ]
    for copy in loads:
        copy.start()
    greet([x_dev, y_dev], [])
    for copy in loads:
        copy.wait()

    def hidden(rows, lanes, up_lanes):
        gate = dot_n(n[rows, :], wm[:, lanes])
        up = dot_n(n[rows, :], wm[:, up_lanes])
        grad = dot_t(g[rows, :], wd[lanes, :])
        sigmoid = jax.nn.sigmoid(gate)
        silu = gate * sigmoid
        act[rows, lanes] = (silu * up).astype(bf16)
        gh[rows, lanes] = (grad * up * sigmoid * (1.0 + gate * (1.0 - sigmoid))).astype(bf16)
        gh[rows, up_lanes] = (grad * silu).astype(bf16)

    wide = ff // 256

    def hidden_step(i, carry):
        rows = pl.ds(pl.multiple_of((i % 4) * length, 16), length)
        hidden(rows, tile_at(i // 4, 256), tile_at(i // 4, 256, ff))
        return carry

    lax.fori_loop(0, 4 * wide, hidden_step, 0)
    for k in range(4):
        if ff % 256:
            hidden(pl.ds(k * length, length), pl.ds(wide * 256, ff % 256), pl.ds(ff + wide * 256, ff % 256))

    def back(k, store):
        def step(i, carry):
            tile = tile_at(i, 1024)
            store(tile, dot_t(gh[k * length : (k + 1) * length, :], wm[tile, :]))
            return carry

        lax.fori_loop(0, D // 1024, step, 0)

    def back_parts(k):
        def store(tile, value):
            parts[k - 1, :, tile] = value.astype(bf16)

        back(k, store)

    summed = PlaneSum(parts, ones, twos, sum_sems, x_dev, y_dev)
    back_parts(3)
    for copy in summed.far:
        copy.start()
    back_parts(1)
    summed.near[0].start()
    back_parts(2)
    summed.near[1].start()

    def store_own(tile, value):
        grad_normed[:, tile] = value

    back(0, store_own)

    def down_out(i, slot, width=256):
        rows = pl.ds(pl.multiple_of((i // 2) * 256, 128), width)
        lanes = tile_at(i % 2, D // 2)
        return pltpu.make_async_copy(
            stage.at[slot, pl.ds(0, width), pl.ds(0, D // 2)], grad_down.at[rows, lanes], out_sem.at[0, slot]
        )

    def down_tile(i, slot, width=256):
        lanes = tile_at(i % 2, D // 2)
        value = dot_tn(act[:, pl.ds(pl.multiple_of((i // 2) * 256, 128), width)], g[:, lanes])
        stage[slot, 0:width, 0 : D // 2] = value.astype(bf16)
        down_out(i, slot, width).start()

    def down_step(i, carry):
        slot = i % 2

        @pl.when(i >= 2)
        def _():
            down_out(i - 2, slot).wait()

        down_tile(i, slot)
        return carry

    lax.fori_loop(0, 2 * wide, down_step, 0)
    for slot in range(2):
        down_out(2 * wide - 2 + slot, slot).wait()
        if ff % 256:
            down_tile(2 * wide + slot, slot, ff % 256)
            down_out(2 * wide + slot, slot, ff % 256).wait()

    summed.pass_on()

    def mlp_out(i, slot):
        rows = pl.ds(pl.multiple_of((i // 2) * 256, 256), 256)
        return pltpu.make_async_copy(
            stage.at[slot, :, pl.ds(0, ff)], grad_mlp.at[rows, tile_at(i % 2, ff)], out_sem.at[1, slot]
        )

    def mlp_step(i, carry):
        slot = i % 2

        @pl.when(i >= 2)
        def _():
            mlp_out(i - 2, slot).wait()

        value = dot_tn(n[:, tile_at(i // 2, 256)], gh[:, tile_at(i % 2, ff)])
        stage[slot, :, 0:ff] = value.astype(bf16)
        mlp_out(i, slot).start()
        return carry

    lax.fori_loop(0, 2 * D // 256, mlp_step, 0)
    mlp_out(2 * D // 256 - 2, 0).wait()
    mlp_out(2 * D // 256 - 1, 1).wait()

    def layer_step(i, carry):
        g[:, tile_at(i, 256)] = dot_n(act[...], wd[:, tile_at(i, 256)]).astype(bf16)
        return carry

    lax.fori_loop(0, D // 256, layer_step, 0)
    layer_out = pltpu.make_async_copy(g, layer, load_sem.at[0])
    layer_out.start()

    def add_normed(r, value):
        grad_normed[r] += value

    summed.finish(add_normed)
    layer_out.wait()


def feed(normed_all, grads_all, mlp_cols, down_cols):
    tokens, ff = 4 * normed_all.shape[1], down_cols.shape[0]
    length = tokens // 4
    dma = pltpu.SemaphoreType.DMA
    sum_buffers, sum_sems = plane_sum_scratch(length, D)
    vmem, hbm = pl.BlockSpec(memory_space=pltpu.VMEM), pl.BlockSpec(memory_space=pl.ANY)
    return pl.pallas_call(
        feed_kernel,
        out_shape=(
            jax.ShapeDtypeStruct((length, D), f32),
            jax.ShapeDtypeStruct((ff, D), bf16),
            jax.ShapeDtypeStruct((D, 2 * ff), bf16),
            jax.ShapeDtypeStruct((tokens, D), bf16),
        ),
        in_specs=[hbm] * 4,
        out_specs=(vmem, hbm, hbm, hbm),
        scratch_shapes=[
            pltpu.VMEM(shape, bf16)
            for shape in (
                (tokens, D), (tokens, D), (D, 2 * ff), (ff, D), (tokens, 2 * ff), (tokens, ff),
                (2, 256, max(ff, D // 2)),
            )
        ]
        + sum_buffers + sum_sems + [dma((4,)), dma((2, 2))],
        compiler_params=pltpu.CompilerParams(
            collective_id=6, has_side_effects=True, vmem_limit_bytes=feed_vmem_limit
        ),
        cost_estimate=cost(115),
        name="feed",
    )(normed_all.reshape(tokens, D), grads_all.reshape(tokens, D), mlp_cols, down_cols)


def local(
    n_dp,
    n_tp,
    inputs,
    cotangent,
    segments,
    qkv_weight,
    out_weight,
    mlp_weight,
    down_weight,
    norm_gains,
    qkv_first,
    out_first,
    mlp_first,
    down_first,
    gains_first,
    qkv_second,
    out_second,
    mlp_second,
    down_second,
    gains_second,
):
    length = inputs.shape[0]
    lines = n_dp // 2
    rows = mlp_weight.shape[0]
    down_rows = down_weight.shape[0]
    ff = n_dp * down_rows
    cosine, sine = tables(segments[0])
    seg_row = segments
    seg_col = segments.reshape(length, 1)

    shard = jnp.concatenate(
        [qkv_weight, out_weight, jnp.pad(norm_gains.T, ((0, 0), (0, 126)))], axis=1
    ).astype(bf16)
    attn_full, mlp_parts, down_cols = gather_all(shard, mlp_weight, down_weight.astype(bf16), n_dp, n_tp)
    qkv_full = attn_full[:, : D + 2 * KW]
    out_full = attn_full[:, D + 2 * KW : 2 * D + 2 * KW]
    gains_full = attn_full[:, 2 * D + 2 * KW :].astype(f32).T
    mlp_cols = lax.all_gather(mlp_parts.reshape(n_tp * rows, 2 * ff), "dp", axis=0, tiled=True)
    tokens_f = inputs.astype(f32)
    gain_one, gain_two = gains_full[0], gains_full[1]
    inverse_one = lax.rsqrt(jnp.mean(tokens_f * tokens_f, axis=-1, keepdims=True) + norm_eps)
    if n_tp == 4:
        qkv, attended, log_totals, middle, normed_one, normed_all, grads_all = forward(
            inputs, cotangent, gains_full, cosine, sine, seg_col, seg_row, attn_full
        )
    else:
        normed_one = (tokens_f * inverse_one * gain_one).astype(bf16)
        projected = matmul(normed_one, qkv_full)
        qkv, attended, log_totals = attend(projected, cosine, sine, seg_col, seg_row)
        middle = tokens_f + matmul(attended, out_full)
    inverse_two = lax.rsqrt(jnp.mean(middle * middle, axis=-1, keepdims=True) + norm_eps)
    if n_tp == 4:
        grad_normed_two, grad_down, grad_mlp, layer_parts = feed(normed_all, grads_all, mlp_cols, down_cols)
        layer_parts = layer_parts.reshape(n_tp, length, D)
    else:
        normed_two = (middle * inverse_two * gain_two).astype(bf16)
        normed_all = plane_gather(normed_two, n_tp)
        grads_all = plane_gather(cotangent, n_tp)
        hidden = matmul(normed_all, mlp_cols)
        gate, up_part = hidden[:, :ff], hidden[:, ff:]
        sigmoid_gate = jax.nn.sigmoid(gate)
        silu_gate = gate * sigmoid_gate
        activated = (silu_gate * up_part).astype(bf16)
        grad_act = matmul_t(grads_all, down_cols)
        grad_gate = grad_act * up_part * sigmoid_gate * (1.0 + gate * (1.0 - sigmoid_gate))
        grad_up = grad_act * silu_gate
        grad_hidden = jnp.concatenate([grad_gate, grad_up], axis=1).astype(bf16)
        grad_normed = matmul_t(grad_hidden, mlp_cols).reshape(n_tp, length, D)
        grad_normed_two = grad_normed[0]
        for k in range(1, n_tp):
            swapped = plane_swap(grad_normed[k].astype(bf16), k, n_tp)
            grad_normed_two = grad_normed_two + swapped.astype(f32)
        grad_down = matmul_tn(activated, grads_all).astype(bf16)
        grad_mlp = matmul_tn(normed_all, grad_hidden).astype(bf16)
        layer_parts = matmul(activated, down_cols).astype(bf16).reshape(n_tp, length, D)
    down_sum = lax.psum_scatter(grad_down, "dp", scatter_dimension=0, tiled=True)
    mlp_sum = lax.psum_scatter(grad_mlp, "dp", scatter_dimension=0, tiled=True).reshape(n_tp, rows, 2 * ff)

    if n_tp == 4:
        layer_out, input_grad, grad_out, grad_qkv = backward(
            inputs, cotangent, grad_normed_two, middle, gains_full, cosine, sine, seg_col, seg_row, normed_one, qkv,
            attended, log_totals, attn_full, layer_parts,
        )
        out_sum, qkv_sum = scatter_all([grad_out, grad_qkv], n_dp, n_tp)
        mlp_sum, total = norm_parts(mlp_sum, qkv_sum, out_sum, down_sum, n_dp, n_tp)
    else:
        layer_out = middle + layer_parts[0].astype(f32)
        for k in range(1, n_tp):
            layer_out = layer_out + plane_swap(layer_parts[k], k, n_tp).astype(f32)
        layer_out = layer_out.astype(bf16)
        gain_grad_two = jnp.sum(grad_normed_two * middle * inverse_two, axis=0)
        weighted_two = grad_normed_two * gain_two
        grad_middle = (
            cotangent.astype(f32)
            + inverse_two * weighted_two
            - middle * inverse_two**3 * jnp.mean(weighted_two * middle, axis=-1, keepdims=True)
        )
        grad_branch = grad_middle.astype(bf16)
        grad_context = matmul_t(grad_branch, out_full).astype(bf16)
        grad_projected = attend_grad(qkv, grad_context, log_totals, cosine, sine, seg_col, seg_row)
        grad_out = matmul_tn(attended, grad_branch).astype(bf16)
        grad_qkv = matmul_tn(normed_one, grad_projected)
        grad_normed_one = matmul_t(grad_projected, qkv_full)
        gain_grad_one = jnp.sum(grad_normed_one * tokens_f * inverse_one, axis=0)
        weighted_one = grad_normed_one * gain_one
        grad_inputs = (
            grad_middle
            + inverse_one * weighted_one
            - tokens_f * inverse_one**3 * jnp.mean(weighted_one * tokens_f, axis=-1, keepdims=True)
        )
        input_grad = grad_inputs.astype(bf16)
        gain_grads = jnp.pad(jnp.stack([gain_grad_one, gain_grad_two], axis=1), ((0, 0), (0, 126)))
        grad_qkv = jnp.concatenate([grad_qkv.astype(bf16), gain_grads.astype(bf16)], axis=1)
        out_sum, qkv_sum = scatter_all([grad_out, grad_qkv], n_dp, n_tp)
        mlp_sum = columns_back(mlp_sum, n_dp, n_tp)
        squares = jnp.sum(qkv_sum * qkv_sum) + jnp.sum(out_sum * out_sum) + jnp.sum(mlp_sum * mlp_sum)
        squares = squares + jnp.sum(jnp.square(down_sum.astype(f32)))
        total = total_over_devices(squares, n_dp, n_tp)
    gains_sum = qkv_sum[:, D + 2 * KW : D + 2 * KW + 2].T
    grad_norm = jnp.sqrt(total[0, 0])
    clip_scale = clip_norm / jnp.maximum(grad_norm, clip_norm)
    states = (
        (qkv_weight, qkv_first, qkv_second),
        (out_weight, out_first, out_second),
        (mlp_weight, mlp_first, mlp_second),
        (down_weight, down_first, down_second),
    )
    stepped = adam_all(total, (qkv_sum, out_sum, mlp_sum, down_sum), states)
    gains_out = adam_update(
        norm_gains, gains_sum * clip_scale, gains_first, gains_second, gain_rate, 0.0
    )
    news = [[*stepped[i::3], gains_out[i]] for i in range(3)]
    return (layer_out, input_grad, grad_norm, *news[0], *news[1], *news[2])


def solution(mesh):
    split_rows = P(("dp", "fsdp"), None)
    split_columns = P(None, ("dp", "fsdp"))
    weights = (split_rows,) * 4 + (split_columns,)
    return jax.shard_map(
        functools.partial(local, mesh.shape["dp"], mesh.shape["fsdp"]),
        mesh=mesh,
        in_specs=(split_rows,) * 3 + weights * 3,
        out_specs=(split_rows, split_rows, P()) + weights * 3,
        check_vma=False,
    )
```

```python
import functools

import jax
import jax.numpy as jnp
from jax import lax
from jax.experimental import pallas as pl
from jax.experimental.pallas import tpu as pltpu
from jax.sharding import PartitionSpec as P

D = 2048
HEADS = 32
KVH = 4
HD = 64
FF = 5632
STEP = 10
KW = KVH * HD
GROUP = HEADS // KVH


norm_eps = 1e-05
rope_base = 10000.0
beta_one = 0.9
beta_two = 0.95
adam_eps = 1e-08
weight_decay = 0.1
matrix_rate = 0.04
gain_rate = 0.8
clip_norm = 1.0

f32 = jnp.float32
bf16 = jnp.bfloat16


def tables(segment_row):
    length = segment_row.shape[0]
    token_index = jnp.arange(length, dtype=jnp.int32)
    previous = jnp.concatenate([segment_row[:1] - 1, segment_row[:-1]])
    starts = lax.cummax(jnp.where(segment_row != previous, token_index, 0), axis=0)
    position = (token_index - starts).astype(f32)
    frequency = rope_base ** (-(jnp.arange(HD // 2, dtype=f32) * 2.0 / HD))
    angles = position[:, None] * frequency[None, :]
    cosine, sine = jnp.cos(angles), jnp.sin(angles)
    cosine = jnp.concatenate([cosine] * 4, axis=-1)
    signed = jnp.concatenate([-sine, sine] * 2, axis=-1)
    return cosine, signed


def halves_swapped(pair):
    lane = lax.broadcasted_iota(jnp.int32, pair.shape, 1)
    return jnp.where(lane % HD < HD // 2, pltpu.roll(pair, 96, 1), pltpu.roll(pair, 32, 1))


def split_pair(pair):
    lane = lax.broadcasted_iota(jnp.int32, pair.shape, 1)
    zero = jnp.zeros_like(pair)
    return jnp.where(lane < HD, pair, zero), jnp.where(lane < HD, zero, pair)


def both_places(pair, odd):
    low, high = split_pair(pair)
    moved = pltpu.roll(pair.astype(f32), HD, 1).astype(pair.dtype)
    moved_low, moved_high = split_pair(moved)
    return (moved_low, high) if odd else (low, moved_high)


def dot_t(a, b):
    return lax.dot_general(a, b, (((1,), (1,)), ((), ())), preferred_element_type=f32)


def dot_n(a, b):
    return lax.dot_general(a, b, (((1,), (0,)), ((), ())), preferred_element_type=f32)


def dot_tn(a, b):
    return lax.dot_general(a, b, (((0,), (0,)), ((), ())), preferred_element_type=f32)


def mask_keys_rows(seg_col, seg_row, length):
    key_index = lax.broadcasted_iota(jnp.int32, (length, length), 0)
    query_index = lax.broadcasted_iota(jnp.int32, (length, length), 1)
    return (seg_col == seg_row) & (query_index >= key_index)


def attend_kernel(proj, cosine, sine, seg_col, seg_row, qkv, context, log_totals):
    cos, sin = cosine[...], sine[...]
    for c in range(0, D + KW, 128):
        qkv[:, c : c + 128] = rope_tile(proj[:, c : c + 128], cos, sin).astype(bf16)
    for c in range(D + KW, D + 2 * KW, 128):
        qkv[:, c : c + 128] = proj[:, c : c + 128].astype(bf16)
    allowed = mask_keys_rows(seg_col[...], seg_row[...], proj.shape[0])
    attend_heads(qkv, context, log_totals, allowed)


def attend_grad_kernel(qkv, grad_context, log_totals, cosine, sine, seg_col, seg_row, grad_proj):
    allowed = mask_keys_rows(seg_col[...], seg_row[...], qkv.shape[0])
    attend_heads_grad(qkv, grad_context, log_totals, grad_proj, allowed, cosine[...], sine[...])


vmem_limit = 50 * 1024 * 1024
feed_vmem_limit = 62 * 1024 * 1024


def attend(projected, cosine, sine, seg_col, seg_row):
    length = projected.shape[0]
    return pl.pallas_call(
        attend_kernel,
        out_shape=(
            jax.ShapeDtypeStruct((length, D + 2 * KW), bf16),
            jax.ShapeDtypeStruct((length, D), bf16),
            jax.ShapeDtypeStruct((HEADS, length), f32),
        ),
        compiler_params=pltpu.CompilerParams(vmem_limit_bytes=vmem_limit),
        cost_estimate=cost(18),
        name="attend",
    )(projected, cosine, sine, seg_col, seg_row)


def attend_grad(qkv, grad_context, log_totals, cosine, sine, seg_col, seg_row):
    length = qkv.shape[0]
    return pl.pallas_call(
        attend_grad_kernel,
        out_shape=jax.ShapeDtypeStruct((length, D + 2 * KW), bf16),
        compiler_params=pltpu.CompilerParams(vmem_limit_bytes=vmem_limit),
        cost_estimate=cost(26),
        name="attend_grad",
    )(qkv, grad_context, log_totals, cosine, sine, seg_col, seg_row)


MESH = pl.DeviceIdType.MESH


def cost(microseconds):
    return pl.CostEstimate(flops=0, bytes_accessed=int(microseconds * 3.69e6), transcendentals=0)


def place():
    dp = lax.axis_index("dp")
    return dp // 2, dp % 2, lax.axis_index("fsdp")


def device(line, core, plane):
    return {"dp": line * 2 + core, "fsdp": plane}


def flipped(index, bit):
    return index + bit - 2 * bit * ((index // bit) % 2)


def greet(partners, ends):
    barrier = pltpu.get_barrier_semaphore()
    count = len(partners)
    for partner in partners:
        pl.semaphore_signal(barrier, inc=1, device_id=partner, device_id_type=MESH)
    for there, partner in ends:
        count = count + there

        @pl.when(there == 1)
        def _():
            pl.semaphore_signal(barrier, inc=1, device_id=partner, device_id_type=MESH)

    pl.semaphore_wait(barrier, count)


def gather_kernel(lines, own, weight, down, full, parts, down_full, cut, line_send, line_recv, x_send, x_recv, y_send, y_recv,
                  dx_send, dx_recv, dy_send, dy_recv, core_send, core_recv, cut_send, cut_recv, down_send, down_recv, down_core_send,
                  down_core_recv, here_sem):
    z, c, f = place()
    half = own.shape[0] // 2
    fx, fy = flipped(f, 1), flipped(f, 2)
    fd = flipped(fx, 2)
    x_dev, y_dev, core_dev = device(z, c, fx), device(z, c, fy), device(z, 1 - c, f)
    has_left = jnp.minimum(z, 1)
    has_right = jnp.minimum(lines - 1 - z, 1)
    left_dev = device(jnp.maximum(z - 1, 0), c, f)
    right_dev = device(jnp.minimum(z + 1, lines - 1), c, f)
    far_dev = device(z, c, fd)
    greet([x_dev, y_dev, far_dev, core_dev], [(has_left, left_dev), (has_right, right_dev)])

    def cut_copy(k):
        to = flipped(f, k) if k < 3 else fd
        return pltpu.make_async_remote_copy(
            cut.at[to], parts.at[f], cut_send.at[k], cut_recv.at[k], device_id=device(z, c, to), device_id_type=MESH
        )

    def copy(line, plane, send, recv, dev, src=None, rows=None):
        dst = full.at[line, c, plane]
        src = dst if src is None else src
        if rows is not None:
            dst, src = dst.at[rows], src.at[rows]
        return pltpu.make_async_remote_copy(
            src, dst, send, recv, device_id=dev, device_id_type=MESH
        )

    def to_right(line, src=None):
        return copy(line, f, line_send.at[0, line], line_recv.at[line], right_dev, src)

    def to_left(line, src=None):
        return copy(line, f, line_send.at[1, line], line_recv.at[line], left_dev, src)

    def to_x(line, src=None):
        return copy(line, f, x_send.at[line], x_recv.at[line], x_dev, src)

    def to_y(line, src=None):
        return copy(line, f, y_send.at[line], y_recv.at[line], y_dev, src)

    def diag_y(line):
        return copy(line, fx, dy_send.at[line], dy_recv.at[line], y_dev, None, pl.ds(0, half))

    def diag_x(line):
        return copy(line, fy, dx_send.at[line], dx_recv.at[line], x_dev, None, pl.ds(half, half))

    def to_core(line, plane, src=None):
        return copy(line, plane, core_send.at[line, plane], core_recv.at[line, plane], core_dev, src)

    def down_copy(line, way, src=None):
        dst = down_full.at[line, c]
        return pltpu.make_async_remote_copy(
            dst if src is None else src, dst, down_send.at[way, line], down_recv.at[line],
            device_id=(right_dev, left_dev)[way], device_id_type=MESH,
        )

    def down_core(line, src=None):
        dst = down_full.at[line, c]
        return pltpu.make_async_remote_copy(
            dst if src is None else src, dst, down_core_send.at[line], down_core_recv.at[line],
            device_id=core_dev, device_id_type=MESH,
        )

    here = pltpu.make_async_copy(own, full.at[z, c, f], here_sem.at[0])
    here.start()
    here_down = pltpu.make_async_copy(down, down_full.at[z, c], here_sem.at[2])
    here_down.start()

    @pl.when(has_right == 1)
    def _():
        to_right(z, own).start()

    @pl.when(has_left == 1)
    def _():
        to_left(z, own).start()

    to_x(z, own).start()
    to_y(z, own).start()
    to_core(z, f, own).start()

    cut_columns(weight, cut, 2 * lines, 4)
    here_cut = pltpu.make_async_copy(cut.at[f], parts.at[f], here_sem.at[1])
    here_cut.start()
    for k in range(1, 4):
        cut_copy(k).start()

    down_core(z, down).start()
    for t in range(1, lines):

        @pl.when(z >= t)
        def _():
            line = z - t
            to_right(line).wait_recv()

            @pl.when(has_right == 1)
            def _():
                to_right(line).start()

            to_x(line).start()
            to_y(line).start()
            to_core(line, f).start()

        @pl.when(z + t <= lines - 1)
        def _():
            line = z + t
            to_left(line).wait_recv()

            @pl.when(has_left == 1)
            def _():
                to_left(line).start()

            to_x(line).start()
            to_y(line).start()
            to_core(line, f).start()

    @pl.when(has_right == 1)
    def _():
        down_copy(z, 0, down).start()

    @pl.when(has_left == 1)
    def _():
        down_copy(z, 1, down).start()

    here.wait()
    order = []
    for t in range(lines):
        line = z
        for b in range(lines.bit_length() - 1):
            if t >> b & 1:
                line = flipped(line, 1 << b)
        order.append(line)
    for t, line in enumerate(order):
        to_x(line).wait_recv()
        diag_y(line).start()
        to_core(line, fx).start()
        to_y(line).wait_recv()
        diag_x(line).start()
        to_core(line, fy).start()
        if t == 0:
            continue

        @pl.when(z >= t)
        def _():
            down_copy(z - t, 0).wait_recv()

            @pl.when(has_right == 1)
            def _():
                down_copy(z - t, 0).start()

            down_core(z - t).start()

        @pl.when(z + t <= lines - 1)
        def _():
            down_copy(z + t, 1).wait_recv()

            @pl.when(has_left == 1)
            def _():
                down_copy(z + t, 1).start()

            down_core(z + t).start()

    for line in order:
        diag_y(line).wait_recv()
        diag_x(line).wait_recv()
        to_core(line, fd).start()
    here_cut.wait()
    here_down.wait()
    for k in range(1, 4):
        cut_copy(k).wait()
    for line in range(lines):
        for plane in range(4):
            to_core(line, plane).wait()
        to_x(line).wait_send()
        to_y(line).wait_send()
        diag_x(line).wait_send()
        diag_y(line).wait_send()

        down_core(line).wait()

        @pl.when((line <= z) & (has_right == 1))
        def _():
            to_right(line).wait_send()
            down_copy(line, 0).wait_send()

        @pl.when((line >= z) & (has_left == 1))
        def _():
            to_left(line).wait_send()
            down_copy(line, 1).wait_send()


def gather_all(shard, weight, down, n_dp, n_tp):
    rows, columns = shard.shape
    width = weight.shape[1] // n_tp
    lines = n_dp // 2
    if n_tp != 4 or rows % 32:
        full = lax.all_gather(shard, ("dp", "fsdp"), axis=0, tiled=True)
        down_full = lax.all_gather(down, "dp", axis=0, tiled=True)
        return full, columns_out(weight, n_dp, n_tp), down_full
    dma = pltpu.SemaphoreType.DMA
    hbm = pl.BlockSpec(memory_space=pl.ANY)
    full, parts, down_full = pl.pallas_call(
        functools.partial(gather_kernel, lines),
        out_shape=(
            jax.ShapeDtypeStruct((lines, 2, n_tp, rows, columns), bf16),
            jax.ShapeDtypeStruct((n_tp, rows, width), bf16),
            jax.ShapeDtypeStruct((lines, 2, *down.shape), bf16),
        ),
        in_specs=[hbm, pl.BlockSpec(memory_space=pltpu.VMEM), hbm],
        out_specs=(hbm, hbm, hbm),
        scratch_shapes=[pltpu.VMEM((n_tp, rows, width), bf16), dma((2, lines))]
        + [dma((lines,))] * 9
        + [dma((lines, n_tp))] * 2
        + [dma((n_tp,)), dma((n_tp,)), dma((2, lines)), dma((lines,)), dma((lines,)), dma((lines,)), dma((3,))],
        compiler_params=pltpu.CompilerParams(
            collective_id=0, has_side_effects=True, vmem_limit_bytes=vmem_limit
        ),
        cost_estimate=cost(100),
        name="gather_all",
    )(shard, weight, down)
    full = full.reshape(n_dp * n_tp * rows, columns)
    return full, parts, down_full.reshape(n_dp * down.shape[0], down.shape[1])


def cut_columns(weight, cut, n_dp, n_tp):
    unit = weight.shape[1] // (2 * n_dp * n_tp)
    half = n_dp * unit
    for to in range(n_tp):
        for side in range(2):
            starts = [side * n_tp * half + (j * n_tp + to) * unit for j in range(n_dp)]
            pieces = [weight[:, start : start + unit] for start in starts]
            cut[to, :, side * half : (side + 1) * half] = jnp.concatenate(pieces, axis=1).astype(bf16)


def columns_out_kernel(n_dp, n_tp, weight, parts, cut, send, recv, here_sem):
    z, c, f = place()
    greet([device(z, c, (f + k) % n_tp) for k in range(1, n_tp)], [])

    def away(k):
        to = (f + k) % n_tp
        return pltpu.make_async_remote_copy(
            cut.at[to], parts.at[f], send.at[k], recv.at[k], device_id=device(z, c, to), device_id_type=MESH
        )

    cut_columns(weight, cut, n_dp, n_tp)
    for k in range(1, n_tp):
        away(k).start()
    here = pltpu.make_async_copy(cut.at[f], parts.at[f], here_sem)
    here.start()
    here.wait()
    for k in range(1, n_tp):
        away(k).wait()


def columns_out(weight, n_dp, n_tp):
    rows, width = weight.shape
    dma = pltpu.SemaphoreType.DMA
    return pl.pallas_call(
        functools.partial(columns_out_kernel, n_dp, n_tp),
        out_shape=jax.ShapeDtypeStruct((n_tp, rows, width // n_tp), bf16),
        out_specs=pl.BlockSpec(memory_space=pl.ANY),
        scratch_shapes=[
            pltpu.VMEM((n_tp, rows, width // n_tp), bf16), dma((n_tp,)), dma((n_tp,)), dma(()),
        ],
        compiler_params=pltpu.CompilerParams(
            collective_id=1, has_side_effects=True, vmem_limit_bytes=vmem_limit
        ),
        cost_estimate=cost(20),
        name="columns_out",
    )(weight)


def columns_back_kernel(n_dp, n_tp, parts, whole, got, send, recv, here_sem):
    z, c, f = place()
    greet([device(z, c, (f + k) % n_tp) for k in range(1, n_tp)], [])
    unit = whole.shape[1] // (2 * n_dp * n_tp)
    half = n_dp * unit

    def away(k):
        to = (f + k) % n_tp
        return pltpu.make_async_remote_copy(
            parts.at[to], got.at[f], send.at[k], recv.at[k], device_id=device(z, c, to), device_id_type=MESH
        )

    for k in range(1, n_tp):
        away(k).start()
    here = pltpu.make_async_copy(parts.at[f], got.at[f], here_sem)
    here.start()
    here.wait()
    for k in range(1, n_tp):
        away(k).wait()
    for side in range(2):
        pieces = [
            got[frm, :, side * half + j * unit : side * half + (j + 1) * unit].astype(f32)
            for j in range(n_dp)
            for frm in range(n_tp)
        ]
        whole[:, side * n_tp * half : (side + 1) * n_tp * half] = jnp.concatenate(pieces, axis=1)


def columns_back(parts, n_dp, n_tp):
    _, rows, width = parts.shape
    dma = pltpu.SemaphoreType.DMA
    return pl.pallas_call(
        functools.partial(columns_back_kernel, n_dp, n_tp),
        out_shape=jax.ShapeDtypeStruct((rows, width * n_tp), f32),
        in_specs=[pl.BlockSpec(memory_space=pl.ANY)],
        scratch_shapes=[pltpu.VMEM(parts.shape, bf16), dma((n_tp,)), dma((n_tp,)), dma(())],
        compiler_params=pltpu.CompilerParams(
            collective_id=2, has_side_effects=True, vmem_limit_bytes=vmem_limit
        ),
        cost_estimate=cost(20),
        name="columns_back",
    )(parts)


def total_kernel(n_dp, n_tp, value, total, held, got, send, recv):
    dp, f = lax.axis_index("dp"), lax.axis_index("fsdp")
    partners = []
    for axis, size in (("dp", n_dp), ("fsdp", n_tp)):
        for bit in range(size.bit_length() - 1):
            index = {"dp": dp, "fsdp": f}
            index[axis] = flipped(index[axis], 1 << bit)
            partners.append(index)
    greet(partners, [])
    held[0] = value[...]
    for step, partner in enumerate(partners):
        swap = pltpu.make_async_remote_copy(
            held.at[step], got.at[step], send.at[step], recv.at[step], device_id=partner, device_id_type=MESH
        )
        swap.start()
        swap.wait()
        held[step + 1] = held[step] + got[step]
    total[...] = held[len(partners)]


def total_over_devices(value, n_dp, n_tp):
    steps = (n_dp * n_tp).bit_length() - 1
    dma = pltpu.SemaphoreType.DMA
    tile = (8, 128)
    spread = pl.pallas_call(
        functools.partial(total_kernel, n_dp, n_tp),
        out_shape=jax.ShapeDtypeStruct(tile, f32),
        scratch_shapes=[
            pltpu.VMEM((steps + 1, *tile), f32), pltpu.VMEM((steps, *tile), f32), dma((steps,)), dma((steps,)),
        ],
        compiler_params=pltpu.CompilerParams(collective_id=3, has_side_effects=True),
        cost_estimate=cost(13),
        name="total",
    )(jnp.broadcast_to(value, tile))
    return spread


def adam_update(weight, gradient, first, second, rate, decay):
    first = beta_one * first + (1.0 - beta_one) * gradient
    second = beta_two * second + (1.0 - beta_two) * gradient * gradient
    first_hat = first / (1.0 - beta_one**STEP)
    second_hat = second / (1.0 - beta_two**STEP)
    weight = weight - rate * (first_hat / (jnp.sqrt(second_hat) + adam_eps) + decay * weight)
    return (weight, first, second)


def matmul(a, b):
    return jnp.dot(a, b, preferred_element_type=f32)


def matmul_t(a, b):
    return lax.dot_general(a, b, (((1,), (1,)), ((), ())), preferred_element_type=f32)


def matmul_tn(a, b):
    return lax.dot_general(a, b, (((0,), (0,)), ((), ())), preferred_element_type=f32)


def swap_core(block, n_dp):
    return lax.ppermute(block, "dp", [(i, i ^ 1) for i in range(n_dp)])


def plane_swap(block, k, n_tp):
    return lax.ppermute(block, "fsdp", [(i, i ^ k) for i in range(n_tp)])


def plane_gather(block, n_tp):
    if n_tp != 4:
        return jnp.concatenate([block] + [plane_swap(block, k, n_tp) for k in range(1, n_tp)], axis=0)
    half = block.shape[0] // 2
    over_x, over_y = plane_swap(block, 1, n_tp), plane_swap(block, 2, n_tp)
    far = [plane_swap(over_y[:half], 1, n_tp), plane_swap(over_x[half:], 2, n_tp)]
    return jnp.concatenate([block, over_x, over_y] + far, axis=0)


def core_sum(parts, n_dp):
    core = lax.axis_index("dp") % 2
    mine = lax.dynamic_index_in_dim(parts, core, 1, keepdims=False)
    other = lax.dynamic_index_in_dim(parts, 1 - core, 1, keepdims=False)
    return mine.astype(f32) + swap_core(other, n_dp).astype(f32)


def line_sum(parts, n_dp):
    lines = n_dp // 2
    place = lax.axis_index("dp") // 2
    result = lax.dynamic_index_in_dim(parts, place, 0, keepdims=False)
    for way in (1, -1):
        arrived = None
        for step in range(1, lines):
            target = jnp.clip(place + way * (lines - step), 0, lines - 1)
            load = lax.dynamic_index_in_dim(parts, target, 0, keepdims=False).astype(f32)
            if arrived is not None:
                load = load + arrived.astype(f32)
            senders = range(step) if way == 1 else range(lines - step, lines)
            pairs = [(2 * s + c, 2 * (s + way) + c) for s in senders for c in range(2)]
            arrived = lax.ppermute(load.astype(bf16), "dp", pairs)
        result = result.astype(f32) + arrived.astype(f32)
    return result


def plane_sum(parts, n_tp):
    here = lax.axis_index("fsdp")
    total = lax.dynamic_index_in_dim(parts, here, 0, keepdims=False).astype(f32)
    for k in range(1, n_tp):
        load = lax.dynamic_index_in_dim(parts, here ^ k, 0, keepdims=False).astype(bf16)
        total = total + plane_swap(load, k, n_tp).astype(f32)
    return total


def by_rows(rows, body):
    def step(i, carry):
        body(pl.ds(pl.multiple_of(i * 16, 16), 16))
        return carry

    lax.fori_loop(0, rows // 16, step, 0)


class Scatter:
    def __init__(self, lines, groups, sems):
        self.sums, self.others, self.firsts, self.seconds, self.alongs, self.leaving, self.outs = groups
        core_send, core_recv, one_send, one_recv, two_send, two_recv, line_send, line_recv = sems
        z, c, f = place()
        self.z, self.f, self.lines = z, f, lines
        self.planes, self.rows = self.sums[0].shape[1:3]
        self.half = self.rows // 2
        fx, fy = flipped(f, 1), flipped(f, 2)
        fd = flipped(fx, 2)
        x_dev, y_dev, core_dev = device(z, c, fx), device(z, c, fy), device(z, 1 - c, f)
        self.has_left = jnp.minimum(z, 1)
        self.has_right = jnp.minimum(lines - 1 - z, 1)
        left_dev = device(jnp.maximum(z - 1, 0), c, f)
        right_dev = device(jnp.minimum(z + 1, lines - 1), c, f)
        greet([x_dev, y_dev, core_dev], [(self.has_left, left_dev), (self.has_right, right_dev)])
        halves = (pl.ds(0, self.half), pl.ds(self.half, self.half))
        near, self.next_near, step_dev = (fx, fy), (fy, fx), (x_dev, y_dev)
        self.order = []
        for t in reversed(range(lines)):
            line = z
            for b in range(lines.bit_length() - 1):
                if t >> b & 1:
                    line = flipped(line, 1 << b)
            self.order.append(line)

        def remote(src, dst, send, recv, dev):
            return pltpu.make_async_remote_copy(src, dst, send, recv, device_id=dev, device_id_type=MESH)

        def to_core(a, d, src):
            return remote(src, self.others[a].at[d], core_send.at[a, d], core_recv.at[a, d], core_dev)

        def one(a, d, way, i):
            block = (near[way], fd)[i]
            return remote(
                self.sums[a].at[d, block, halves[way]], self.firsts[a].at[way, d, i],
                one_send.at[a, d, way, i], one_recv.at[a, d, way, i], step_dev[way],
            )

        def two(a, d, way):
            return remote(
                self.sums[a].at[d, self.next_near[way], halves[way]], self.seconds[a].at[way, d],
                two_send.at[a, d, way], two_recv.at[a, d, way], step_dev[1 - way],
            )

        def to_right(a, d):
            return remote(
                self.leaving[a].at[d], self.alongs[a].at[d], line_send.at[a, d], line_recv.at[a, d], right_dev
            )

        def to_left(a, d, slot):
            return remote(
                self.leaving[a].at[d], self.alongs[a].at[slot], line_send.at[a, d], line_recv.at[a, slot], left_dev
            )

        self.to_core, self.one, self.two, self.to_right, self.to_left = to_core, one, two, to_right, to_left

    def add_along(self, a, slot):
        def step(r):
            self.outs[a][r] += self.alongs[a][slot, r].astype(f32)

        by_rows(self.rows, step)

    def over_core(self, a, d):
        sums, others = self.sums[a], self.others[a]
        self.to_core(a, d, others.at[d]).wait_recv()

        def core_add(r):
            for plane in range(self.planes):
                sums[d, plane, r] = (sums[d, plane, r].astype(f32) + others[d, plane, r].astype(f32)).astype(bf16)

        by_rows(self.rows, core_add)
        for i in (1, 0):
            for way in range(2):
                self.one(a, d, way, i).start()

    def there(self, r, way):
        return pl.ds(pl.multiple_of(r.start + way * self.half, 16), r.size)

    def over_first(self, a, d):
        sums, firsts = self.sums[a], self.firsts[a]
        for way in range(2):
            self.one(a, d, way, 1).wait_recv()
            block = self.next_near[way]

            def first_add(r):
                there = self.there(r, way)
                mine = sums[d, block, there].astype(f32)
                sums[d, block, there] = (mine + firsts[way, d, 1, r].astype(f32)).astype(bf16)

            by_rows(self.half, first_add)
            self.two(a, d, way).start()

    def over_second(self, a, d):
        sums, firsts, seconds, outs, z = self.sums[a], self.firsts[a], self.seconds[a], self.outs[a], self.z
        for way in range(2):
            self.one(a, d, way, 0).wait_recv()
            self.two(a, d, way).wait_recv()

            def second_add(r):
                there = self.there(r, way)
                outs[there] = (
                    sums[d, self.f, there].astype(f32)
                    + firsts[way, d, 0, r].astype(f32)
                    + seconds[way, d, r].astype(f32)
                )

            by_rows(self.half, second_add)

        @pl.when((d > z) & (self.has_left == 1))
        def _():
            self.to_right(a, d).wait_recv()
            self.add_along(a, d)

        @pl.when((d < z) & (self.has_right == 1))
        def _():
            self.to_left(a, d, d).wait_recv()
            self.add_along(a, d)

        @pl.when(d != z)
        def _():
            def leave(r):
                self.leaving[a][d, r] = outs[r].astype(bf16)

            by_rows(self.rows, leave)

        @pl.when(d > z)
        def _():
            self.to_right(a, d).start()

        @pl.when((d < z) & (d + 1 < z))
        def _():
            self.to_left(a, d, d).start()

        @pl.when(d + 1 == z)
        def _():
            self.to_left(a, d, self.lines).start()

    def finish(self):
        for a in range(len(self.sums)):

            @pl.when(self.has_left == 1)
            def _():
                self.to_right(a, self.z).wait_recv()
                self.add_along(a, self.z)

            @pl.when(self.has_right == 1)
            def _():
                self.to_left(a, self.z, self.lines).wait_recv()
                self.add_along(a, self.lines)

            for d in self.order:
                for way in range(2):
                    self.one(a, d, way, 0).wait_send()
                    self.one(a, d, way, 1).wait_send()
                    self.two(a, d, way).wait_send()

                @pl.when(d != self.z)
                def _():
                    self.to_right(a, d).wait_send()


def scatter_scratch(lines, n_tp, rows, widths):
    dma = pltpu.SemaphoreType.DMA
    n = len(widths)
    shapes = [
        (lines, n_tp, rows), (lines, n_tp, rows), (2, lines, 2, rows // 2), (2, lines, rows // 2),
        (lines + 1, rows), (lines, rows),
    ]
    buffers = [pltpu.VMEM((*shape, width), bf16) for shape in shapes for width in widths]
    sems = [dma((n, lines))] * 2 + [dma((n, lines, 2, 2))] * 2 + [dma((n, lines, 2))] * 2
    return buffers, sems + [dma((n, lines)), dma((n, lines + 1))]


def scatter_all(arrays, n_dp, n_tp):
    lines = n_dp // 2
    rows = arrays[0].shape[0] // (n_dp * n_tp)
    results = []
    for array in arrays:
        parts = core_sum(array.reshape(lines, 2, n_tp, rows, -1), n_dp)
        results.append(line_sum(plane_sum(parts.transpose(1, 0, 2, 3), n_tp), n_dp))
    return results


def rope_tile(tile, cos, sin):
    pairs = [tile[:, i : i + 128] for i in range(0, tile.shape[1], 128)]
    return jnp.concatenate([pair * cos + halves_swapped(pair) * sin for pair in pairs], axis=1)


def attend_heads(qkv, context, log_totals, allowed):
    length = qkv.shape[0]
    scale = HD ** (-0.5)
    for group in range(KVH):
        kc = D + (group // 2) * 128
        keys = both_places(qkv[:, kc : kc + 128], group % 2)
        values = both_places(qkv[:, kc + KW : kc + KW + 128], group % 2)

        def pair_step(pair_index, carry):
            pair = group * (GROUP // 2) + pair_index
            lanes = pl.ds(pl.multiple_of(pair * 128, 128), 128)
            queries = qkv[:, lanes]
            total = jnp.zeros((length, 128), f32)
            for side in range(2):
                scores = dot_t(keys[side], queries) * scale
                scores = jnp.where(allowed, scores, -1e30)
                top = jnp.max(scores, axis=0, keepdims=True)
                raised = jnp.exp(scores - top)
                totals = jnp.sum(raised, axis=0, keepdims=True)
                probs = (raised / totals).astype(bf16)
                total = total + dot_tn(probs, values[side])
                log_totals[pl.ds(2 * pair + side, 1), :] = top + jnp.log(totals)
            context[:, lanes] = total.astype(bf16)
            return carry

        lax.fori_loop(0, GROUP // 2, pair_step, 0)


def tile_at(i, width, start=0):
    return pl.ds(pl.multiple_of(start + i * width, 128), width)


class Exchange:
    def __init__(self, own, whole, sems, i, x_dev, y_dev):
        send, recv, here = sems
        half = own.shape[0] // 2

        def remote(src, dst, k, dev):
            return pltpu.make_async_remote_copy(
                src, dst, send.at[i, k], recv.at[i, k], device_id=dev, device_id_type=MESH
            )

        low, high = pl.ds(0, half), pl.ds(half, half)
        self.near = [remote(own, whole.at[1], 0, x_dev), remote(own, whole.at[2], 1, y_dev)]
        self.far = [
            remote(whole.at[2, low], whole.at[3, low], 2, x_dev),
            remote(whole.at[1, high], whole.at[3, high], 3, y_dev),
        ]
        self.here = pltpu.make_async_copy(own, whole.at[0], here.at[i])

    def start(self):
        for copy in self.near:
            copy.start()
        self.here.start()

    def pass_on(self):
        for copy in self.near:
            copy.wait_recv()
        for copy in self.far:
            copy.start()

    def finish(self):
        for copy in self.far:
            copy.wait()
        for copy in self.near:
            copy.wait_send()
        self.here.wait()


def forward_kernel(x, grads, gains, cosine, sine, seg_col, seg_row, weights, qkv, context, log_totals, middle,
                   normed_one, normed_all, grads_all, q_weight, o_weight, normed_two, load_sem, *sems):
    z, c, f = place()
    x_dev, y_dev = device(z, c, flipped(f, 1)), device(z, c, flipped(f, 2))
    greet([x_dev, y_dev], [])
    length = x.shape[0]
    width = D + 2 * KW
    of_grads = Exchange(grads, grads_all, sems, 0, x_dev, y_dev)
    of_normed = Exchange(normed_two, normed_all, sems, 1, x_dev, y_dev)
    of_grads.start()
    load_q = pltpu.make_async_copy(weights.at[:, pl.ds(0, width)], q_weight, load_sem.at[0])
    load_o = pltpu.make_async_copy(weights.at[:, pl.ds(width, D)], o_weight, load_sem.at[1])
    load_q.start()
    load_o.start()

    def norm_one(r):
        rows = x[r].astype(f32)
        inverse = lax.rsqrt(jnp.mean(rows * rows, axis=-1, keepdims=True) + norm_eps)
        normed_one[r] = (rows * inverse * gains[0:1, :]).astype(bf16)

    by_rows(length, norm_one)
    load_q.wait()
    cos, sin = cosine[...], sine[...]

    def project(i, carry):
        lanes = tile_at(i, 256)
        qkv[:, lanes] = rope_tile(dot_n(normed_one[...], q_weight[:, lanes]), cos, sin).astype(bf16)
        return carry

    lax.fori_loop(0, (D + KW) // 256, project, 0)
    qkv[:, D + KW :] = dot_n(normed_one[...], q_weight[:, D + KW :]).astype(bf16)
    allowed = mask_keys_rows(seg_col[...], seg_row[...], length)
    attend_heads(qkv, context, log_totals, allowed)
    load_o.wait()

    def project_out(i, carry):
        lanes = tile_at(i, 256)
        middle[:, lanes] = x[:, lanes].astype(f32) + dot_n(context[...], o_weight[:, lanes])
        return carry

    lax.fori_loop(0, D // 256, project_out, 0)

    def norm_two(r):
        rows = middle[r]
        inverse = lax.rsqrt(jnp.mean(rows * rows, axis=-1, keepdims=True) + norm_eps)
        normed_two[r] = (rows * inverse * gains[1:2, :]).astype(bf16)

    by_rows(length, norm_two)
    of_normed.start()
    of_grads.pass_on()
    of_normed.pass_on()
    of_normed.finish()
    of_grads.finish()


def forward(x, grads, gains, cosine, sine, seg_col, seg_row, weights):
    length = x.shape[0]
    dma = pltpu.SemaphoreType.DMA
    vmem, hbm = pl.BlockSpec(memory_space=pltpu.VMEM), pl.BlockSpec(memory_space=pl.ANY)
    width = D + 2 * KW
    return pl.pallas_call(
        forward_kernel,
        out_shape=(
            jax.ShapeDtypeStruct((length, width), bf16),
            jax.ShapeDtypeStruct((length, D), bf16),
            jax.ShapeDtypeStruct((HEADS, length), f32),
            jax.ShapeDtypeStruct((length, D), f32),
            jax.ShapeDtypeStruct((length, D), bf16),
            jax.ShapeDtypeStruct((4, length, D), bf16),
            jax.ShapeDtypeStruct((4, length, D), bf16),
        ),
        in_specs=[vmem, hbm] + [vmem] * 5 + [hbm],
        out_specs=(vmem,) * 5 + (hbm,) * 2,
        scratch_shapes=[
            pltpu.VMEM((D, width), bf16), pltpu.VMEM((D, D), bf16), pltpu.VMEM((length, D), bf16),
            dma((2,)), dma((2, 4)), dma((2, 4)), dma((2,)),
        ],
        compiler_params=pltpu.CompilerParams(
            collective_id=5, has_side_effects=True, vmem_limit_bytes=feed_vmem_limit
        ),
        cost_estimate=cost(95),
        name="forward",
    )(x, grads, gains, cosine, sine, seg_col, seg_row, weights)


class PlaneSum:
    def __init__(self, parts, ones, twos, sems, x_dev, y_dev):
        one_send, one_recv, two_send, two_recv = sems
        self.half = parts.shape[1] // 2
        self.parts, self.ones, self.twos = parts, ones, twos
        halves = (pl.ds(0, self.half), pl.ds(self.half, self.half))
        step_dev = (x_dev, y_dev)

        def remote(src, dst, send, recv, dev):
            return pltpu.make_async_remote_copy(src, dst, send, recv, device_id=dev, device_id_type=MESH)

        self.near, self.far, self.two = [], [], []
        for way in range(2):
            for i, copies in enumerate((self.near, self.far)):
                block = parts.at[2 if i else way, halves[way]]
                copies.append(
                    remote(block, ones.at[way, i], one_send.at[way, i], one_recv.at[way, i], step_dev[way])
                )
            self.two.append(
                remote(parts.at[1 - way, halves[way]], twos.at[way], two_send.at[way], two_recv.at[way], step_dev[1 - way])
            )

    def there(self, r, way):
        return pl.ds(pl.multiple_of(r.start + way * self.half, 16), r.size)

    def pass_on(self):
        for way in range(2):
            self.far[way].wait_recv()

            def add_far(r):
                there = self.there(r, way)
                mine = self.parts[1 - way, there].astype(f32)
                self.parts[1 - way, there] = (mine + self.ones[way, 1, r].astype(f32)).astype(bf16)

            by_rows(self.half, add_far)
            self.two[way].start()

    def finish(self, add):
        for way in range(2):
            self.near[way].wait()
            self.far[way].wait_send()
            self.two[way].wait()
        for way in range(2):

            def add_all(r):
                add(self.there(r, way), self.ones[way, 0, r].astype(f32) + self.twos[way, r].astype(f32))

            by_rows(self.half, add_all)


def plane_sum_scratch(length, columns):
    dma = pltpu.SemaphoreType.DMA
    shapes = ((3, length, columns), (2, 2, length // 2, columns), (2, length // 2, columns))
    return [pltpu.VMEM(shape, bf16) for shape in shapes], [dma((2, 2)), dma((2, 2)), dma((2,)), dma((2,))]


def attend_heads_grad(qkv, grad_context, log_totals, grad_proj, allowed, cos, sin, between=None):
    length = qkv.shape[0]
    scale = HD ** (-0.5)

    def unrotate(pair):
        return pair * cos + halves_swapped(pair * sin)

    key_parts, value_parts = [], []
    for group in range(KVH):
        kc = D + (group // 2) * 128
        keys = both_places(qkv[:, kc : kc + 128], group % 2)
        values = both_places(qkv[:, kc + KW : kc + KW + 128], group % 2)

        def pair_step(pair_index, carry):
            grad_keys, grad_values = list(carry[:2]), list(carry[2:])
            pair = group * (GROUP // 2) + pair_index
            lanes = pl.ds(pl.multiple_of(pair * 128, 128), 128)
            queries = qkv[:, lanes]
            grads = grad_context[:, lanes]
            total = jnp.zeros((length, 128), f32)
            for side in range(2):
                scores = dot_t(keys[side], queries) * scale
                scores = jnp.where(allowed, scores, -1e30)
                probs = jnp.exp(scores - log_totals[pl.ds(2 * pair + side, 1), :])
                grad_probs = dot_t(values[side], grads)
                grad_values[side] = grad_values[side] + dot_n(probs.astype(bf16), grads)
                inner = jnp.sum(probs * grad_probs, axis=0, keepdims=True)
                raw = (probs * (grad_probs - inner) * scale).astype(bf16)
                total = total + dot_tn(raw, keys[side])
                grad_keys[side] = grad_keys[side] + dot_n(raw, queries)
            grad_proj[:, lanes] = unrotate(total).astype(bf16)
            return (*grad_keys, *grad_values)

        empty = jnp.zeros((length, 128), f32)
        out = lax.fori_loop(0, GROUP // 2, pair_step, (empty,) * 4)

        def joined(low_side, high_side):
            low, _ = split_pair(low_side)
            _, high = split_pair(high_side)
            both = low + high
            return both + pltpu.roll(both, HD, 1)

        key_parts.append(joined(out[0], out[1]))
        value_parts.append(joined(out[2], out[3]))
        if between is not None:
            between(group)
    lane = lax.broadcasted_iota(jnp.int32, (length, 128), 1)
    for c in range(KVH // 2):
        keys = jnp.where(lane < HD, key_parts[2 * c], key_parts[2 * c + 1])
        values = jnp.where(lane < HD, value_parts[2 * c], value_parts[2 * c + 1])
        grad_proj[:, D + c * 128 : D + (c + 1) * 128] = unrotate(keys).astype(bf16)
        grad_proj[:, D + KW + c * 128 : D + KW + (c + 1) * 128] = values.astype(bf16)


def fold(value):
    return jnp.sum(value, axis=0, keepdims=True)


def branch_kernel(grads, grad_normed, middle, gains, context, weights, layer, layer_out, grad_branch, grad_context,
                  grad_o, gain_rows, weight, stage, load_sem, out_sem):
    length, width = middle.shape[0], D + 2 * KW
    load_o = pltpu.make_async_copy(weights.at[:, pl.ds(width, D)], weight, load_sem.at[0])
    load_o.start()
    gain_rows[...] = jnp.zeros_like(gain_rows)

    def middle_grads(r):
        rows, arrived = middle[r], grad_normed[r]
        inverse = lax.rsqrt(jnp.mean(rows * rows, axis=-1, keepdims=True) + norm_eps)
        gain_rows[1:2, :] += fold(arrived * rows * inverse)
        weighted = arrived * gains[1:2, :]
        inner = jnp.mean(weighted * rows, axis=-1, keepdims=True)
        value = grads[r].astype(f32) + inverse * weighted - rows * (inverse * inverse * inverse * inner)
        grad_branch[r] = value.astype(bf16)
        layer_out[r] = (rows + layer[r].astype(f32)).astype(bf16)

    by_rows(length, middle_grads)
    load_o.wait()

    def context_step(i, carry):
        tile = tile_at(i, 512)
        grad_context[:, tile] = dot_t(grad_branch[...], weight[tile, :]).astype(bf16)
        return carry

    lax.fori_loop(0, D // 512, context_step, 0)
    steps = D // 512

    def out(i, slot):
        return pltpu.make_async_copy(stage.at[slot], grad_o.at[tile_at(i, 512)], out_sem.at[slot])

    def step(i, carry):
        slot = i % 2

        @pl.when(i >= 2)
        def _():
            out(i - 2, slot).wait()

        stage[slot] = dot_tn(context[:, tile_at(i, 512)], grad_branch[...]).astype(bf16)
        out(i, slot).start()
        return carry

    lax.fori_loop(0, steps, step, 0)
    out(steps - 2, 0).wait()
    out(steps - 1, 1).wait()


def branch(grads, grad_normed, middle, gains, context, weights, layer):
    length = middle.shape[0]
    dma = pltpu.SemaphoreType.DMA
    vmem, hbm = pl.BlockSpec(memory_space=pltpu.VMEM), pl.BlockSpec(memory_space=pl.ANY)
    rows = jax.ShapeDtypeStruct((length, D), bf16)
    return pl.pallas_call(
        branch_kernel,
        out_shape=(rows, rows, rows, jax.ShapeDtypeStruct((D, D), bf16), jax.ShapeDtypeStruct((8, D), f32)),
        in_specs=[vmem] * 5 + [hbm, vmem],
        out_specs=(vmem, vmem, vmem, hbm, vmem),
        scratch_shapes=[pltpu.VMEM((D, D), bf16), pltpu.VMEM((2, 512, D), bf16), dma((1,)), dma((2,))],
        compiler_params=pltpu.CompilerParams(vmem_limit_bytes=feed_vmem_limit),
        cost_estimate=cost(22),
        name="branch",
    )(grads, grad_normed, middle, gains, context, weights, layer)


def backward_kernel(lines, x, normed_one, qkv, grad_context, log_totals, gains, cosine, sine, seg_col, seg_row, gain_two,
                    grad_o, branch_hbm, weights, input_grad, out_o, out_q, weight, grad_proj, grad_one, gain_rows,
                    gain_columns, staged, *refs):
    groups = [refs[i * 2 : i * 2 + 2] for i in range(6)] + [(out_o, out_q)]
    scatter_sems, (load_sem, weight_sem) = refs[12:20], refs[20:]
    scatter = Scatter(lines, groups, scatter_sems)
    z, c, f = place()
    length, width = x.shape[0], D + 2 * KW
    order = scatter.order
    rows = scatter.rows

    def load(d):
        return pltpu.make_async_copy(grad_o.at[d, c], scatter.sums[0].at[d], load_sem.at[d])

    def load_weight(i):
        tile = pl.ds(i * 512, 512)
        return pltpu.make_async_copy(weights.at[tile, pl.ds(0, width)], weight.at[i % 2], weight_sem.at[i % 2])

    for d in order:
        scatter.to_core(0, d, grad_o.at[d, 1 - c]).start()
        load(d).start()
    load_branch = pltpu.make_async_copy(branch_hbm, input_grad, load_sem.at[lines])
    load_branch.start()
    load_weight(0).start()
    load_weight(1).start()
    gain_rows[...] = gain_two[...]

    def between(group):
        if group == 0:
            for d in order:
                load(d).wait()
                scatter.over_core(0, d)
        elif group == 1:
            scatter.over_first(0, order[0])
            scatter.over_first(0, order[1])
        elif group == 2:
            for d in order[2:]:
                scatter.over_first(0, d)
        else:
            scatter.over_second(0, order[0])

    allowed = mask_keys_rows(seg_col[...], seg_row[...], length)
    attend_heads_grad(
        qkv, grad_context, log_totals, grad_proj, allowed, cosine[...], sine[...], between if lines > 1 else None
    )
    for i in range(D // 512):
        load_weight(i).wait()
        grad_one[:, i * 512 : (i + 1) * 512] = dot_t(grad_proj[...], weight[i % 2])
        if i + 2 < D // 512:
            load_weight(i + 2).start()
    load_branch.wait()

    def input_grads(r):
        values, arrived = x[r].astype(f32), grad_one[r]
        inverse = lax.rsqrt(jnp.mean(values * values, axis=-1, keepdims=True) + norm_eps)
        gain_rows[0:1, :] += fold(arrived * values * inverse)
        weighted = arrived * gains[0:1, :]
        inner = jnp.mean(weighted * values, axis=-1, keepdims=True)
        value = inverse * weighted - values * (inverse * inverse * inverse * inner)
        input_grad[r] = (input_grad[r].astype(f32) + value).astype(bf16)

    by_rows(length, input_grads)
    for i in range(D // 128):
        lanes = pl.ds(i * 128, 128)
        square = jnp.concatenate([gain_rows[:, lanes], jnp.zeros((120, 128), f32)], axis=0)
        gain_columns[lanes, :] = square.T.astype(bf16)

    def blocks(d, core):
        start = pl.multiple_of((2 * d + core) * (4 * rows), 128)
        tile = pl.ds(start, 4 * rows)
        value = dot_tn(normed_one[:, tile], grad_proj[...]).astype(bf16)
        return value.reshape(4, rows, width), gain_columns[tile, :].reshape(4, rows, 128)

    def put(target, value):
        target[:, :, 0:width] = value[0]
        target[:, :, width:] = value[1]

    def staged_copy(j):
        return scatter.to_core(1, order[j], staged.at[j % 2])

    for j, d in enumerate(order):
        if j >= 2:
            staged_copy(j - 2).wait_send()
        put(staged.at[j % 2], blocks(d, 1 - c))
        staged_copy(j).start()
        put(scatter.sums[1].at[d], blocks(d, c))
        if j:
            scatter.over_core(1, order[j - 1])
        if j == 1:
            scatter.over_second(0, order[1])
    scatter.over_core(1, order[-1])
    for d in order[2:]:
        scatter.over_second(0, d)
    for j in range(len(order) + 1):
        if j < len(order):
            scatter.over_first(1, order[j])
        if j:
            scatter.over_second(1, order[j - 1])
    for d in order:
        scatter.to_core(0, d, grad_o.at[d, 1 - c]).wait_send()
    for j in range(max(0, len(order) - 2), len(order)):
        staged_copy(j).wait_send()
    scatter.finish()


def backward(x, normed_one, qkv, grad_context, log_totals, gains, cosine, sine, seg_col, seg_row, gain_two, grad_o,
             grad_branch, weights, n_dp, n_tp):
    length = x.shape[0]
    lines, rows = n_dp // 2, D // (n_dp * n_tp)
    width = D + 2 * KW
    dma = pltpu.SemaphoreType.DMA
    vmem, hbm = pl.BlockSpec(memory_space=pltpu.VMEM), pl.BlockSpec(memory_space=pl.ANY)
    buffers, sems = scatter_scratch(lines, n_tp, rows, (D, width + 128))
    return pl.pallas_call(
        functools.partial(backward_kernel, lines),
        out_shape=(
            jax.ShapeDtypeStruct((length, D), bf16),
            jax.ShapeDtypeStruct((rows, D), f32),
            jax.ShapeDtypeStruct((rows, width + 128), f32),
        ),
        in_specs=[vmem] * 11 + [hbm] * 3,
        out_specs=(vmem,) * 3,
        scratch_shapes=[
            pltpu.VMEM((2, 512, width), bf16), pltpu.VMEM((length, width), bf16), pltpu.VMEM((length, D), f32),
            pltpu.VMEM((8, D), f32), pltpu.VMEM((D, 128), bf16), pltpu.VMEM((2, n_tp, rows, width + 128), bf16),
        ]
        + buffers + sems + [dma((lines + 1,)), dma((2,))],
        compiler_params=pltpu.CompilerParams(
            collective_id=7, has_side_effects=True, vmem_limit_bytes=feed_vmem_limit
        ),
        cost_estimate=cost(105),
        name="backward",
    )(x, normed_one, qkv, grad_context, log_totals, gains, cosine, sine, seg_col, seg_row, gain_two,
      grad_o.reshape(lines, 2, n_tp, rows, D), grad_branch, weights)


def norm_kernel(n_dp, n_tp, parts, qkv, out, down, mlp, total, got, held, got_dp, got_tp, send, recv, total_send,
                total_recv, here_sem):
    z, c, f = place()
    dp = z * 2 + c
    columns = [(f + k) % n_tp for k in range(1, n_tp)]
    lines = [(dp + k) % n_dp for k in range(1, n_dp)]
    greet([device(z, c, to) for to in columns] + [{"dp": to, "fsdp": f} for to in lines], [])
    unit = mlp.shape[1] // (2 * n_dp * n_tp)
    half = n_dp * unit

    def away(k):
        to = columns[k - 1]
        return pltpu.make_async_remote_copy(
            parts.at[to], got.at[f], send.at[k], recv.at[k], device_id=device(z, c, to), device_id_type=MESH
        )

    for k in range(1, n_tp):
        away(k).start()
    here = pltpu.make_async_copy(parts.at[f], got.at[f], here_sem)
    here.start()
    held[...] = jnp.zeros_like(held)

    def add_squares(ref):
        def step(r):
            part = ref[r, :].astype(f32)
            part = part * part
            lanes = [part[:, i : i + 128] for i in range(0, part.shape[1], 128)]
            held[...] += functools.reduce(jnp.add, lanes)

        by_rows(ref.shape[0], step)

    add_squares(qkv)
    add_squares(out)
    add_squares(down)
    here.wait()
    for k in range(1, n_tp):
        away(k).wait()
    for frm in range(n_tp):
        add_squares(got.at[frm])

    def spread(buffer, own, value, partners, base):
        buffer[own] = value
        copies = [
            pltpu.make_async_remote_copy(
                buffer.at[own], buffer.at[own], total_send.at[base + k], total_recv.at[base + k],
                device_id=partner, device_id_type=MESH,
            )
            for k, partner in enumerate(partners)
        ]
        for copy in copies:
            copy.start()
        return copies

    def summed(buffer, copies):
        for copy in copies:
            copy.wait()
        return functools.reduce(jnp.add, [buffer[i] for i in range(buffer.shape[0])])

    own_total = jnp.sum(jnp.sum(held[...], axis=0, keepdims=True), axis=1, keepdims=True)
    copies = spread(
        got_dp, dp, jnp.broadcast_to(own_total, (8, 128)), [{"dp": to, "fsdp": f} for to in lines], 0
    )
    for side in range(2):
        pieces = [
            got[frm, :, side * half + j * unit : side * half + (j + 1) * unit].astype(f32)
            for j in range(n_dp)
            for frm in range(n_tp)
        ]
        mlp[:, side * n_tp * half : (side + 1) * n_tp * half] = jnp.concatenate(pieces, axis=1)
    line_total = summed(got_dp, copies)
    copies = spread(got_tp, f, line_total, [device(z, c, to) for to in columns], n_dp)
    total[...] = summed(got_tp, copies)


def norm_parts(parts, qkv, out, down, n_dp, n_tp):
    _, rows, width = parts.shape
    dma = pltpu.SemaphoreType.DMA
    vmem, hbm = pl.BlockSpec(memory_space=pltpu.VMEM), pl.BlockSpec(memory_space=pl.ANY)
    return pl.pallas_call(
        functools.partial(norm_kernel, n_dp, n_tp),
        out_shape=(jax.ShapeDtypeStruct((rows, width * n_tp), f32), jax.ShapeDtypeStruct((8, 128), f32)),
        in_specs=[hbm, vmem, vmem, vmem],
        scratch_shapes=[
            pltpu.VMEM(parts.shape, bf16), pltpu.VMEM((16, 128), f32), pltpu.VMEM((n_dp, 8, 128), f32),
            pltpu.VMEM((n_tp, 8, 128), f32), dma((n_tp,)), dma((n_tp,)), dma((n_dp + n_tp,)), dma((n_dp + n_tp,)),
            dma(()),
        ],
        compiler_params=pltpu.CompilerParams(
            collective_id=8, has_side_effects=True, vmem_limit_bytes=feed_vmem_limit
        ),
        cost_estimate=cost(35),
        name="norm_parts",
    )(parts, qkv, out, down)


def adam_kernel(total, gain_block, *refs):
    scale = clip_norm / jnp.maximum(jnp.sqrt(total[0:1, 0:1]), clip_norm)
    grads, refs = refs[:4], refs[4:]
    states, news = refs[:15], refs[15:]

    def update(i, gradient, rate, decay):
        new = adam_update(
            states[3 * i][...], gradient * scale, states[3 * i + 1][...], states[3 * i + 2][...], rate, decay
        )
        for k in range(3):
            news[3 * i + k][...] = new[k]

    for i in range(4):
        update(i, grads[i][...].astype(f32), matrix_rate, weight_decay)

    @pl.when(pl.program_id(0) == 0)
    def _():
        rows = gain_block.shape[0]
        square = jnp.concatenate([gain_block[...], jnp.zeros((128 - rows, 128), f32)], axis=0)
        update(4, square.T[0:2, 0:rows], gain_rate, 0.0)


def adam_all(total, grads, states):
    shapes = [state[0].shape for state in states[:4]]

    def block(shape, steps):
        rows, columns = shape
        if rows % (8 * steps) == 0:
            return pl.BlockSpec((rows // steps, columns), lambda i: (i, 0))
        if columns % (128 * steps) == 0:
            return pl.BlockSpec((rows, columns // steps), lambda i: (0, i))
        return None

    steps = 8 if all(block(shape, 8) for shape in shapes) else 4
    specs = [block(shape, steps) for shape in shapes]
    flat = [array for state in states for array in state]
    gains = pl.BlockSpec(states[4][0].shape, lambda i: (0, 0))
    state_specs = [spec for spec in specs + [gains] for _ in range(3)]
    last = grads[0].shape[1] // 128 - 1
    gain_block = pl.BlockSpec((grads[0].shape[0], 128), lambda i: (0, last))
    return pl.pallas_call(
        adam_kernel,
        grid=(steps,),
        out_shape=[jax.ShapeDtypeStruct(array.shape, f32) for array in flat],
        in_specs=[pl.BlockSpec((8, 128), lambda i: (0, 0)), gain_block] + specs + state_specs,
        out_specs=state_specs,
        compiler_params=pltpu.CompilerParams(vmem_limit_bytes=feed_vmem_limit),
        cost_estimate=cost(14),
        name="adam",
    )(total, grads[0], *grads, *flat)


def feed_front_kernel(n_hbm, g_hbm, wm_hbm, wd_hbm, gh_hbm, grad_down, layer_sum, n, g, wm, wd, act, gh, stage, parts,
                      ones, twos, *sems):
    sum_sems, (load_sem, weight_sem, out_sem) = sems[:4], sems[4:]
    z, c, f = place()
    x_dev, y_dev = device(z, c, flipped(f, 1)), device(z, c, flipped(f, 2))
    tokens = n.shape[0]
    length = tokens // 4
    ff = wd.shape[0]
    order = (3, 1, 2, 0)

    def rows_of(k):
        return pl.ds(k * length, length)

    load_n = [pltpu.make_async_copy(n_hbm.at[rows_of(k)], n.at[rows_of(k)], load_sem.at[0, k]) for k in range(4)]
    load_g = [pltpu.make_async_copy(g_hbm.at[rows_of(k)], g.at[rows_of(k)], load_sem.at[1, k]) for k in range(4)]
    tiles = [(start, min(256, ff - start)) for start in range(0, ff, 256)]
    load_w = []
    for t, (start, size) in enumerate(tiles):
        gate, up = pl.ds(start, size), pl.ds(ff + start, size)
        load_w.append(
            [
                pltpu.make_async_copy(wm_hbm.at[:, gate], wm.at[:, gate], weight_sem.at[0, t]),
                pltpu.make_async_copy(wm_hbm.at[:, up], wm.at[:, up], weight_sem.at[1, t]),
                pltpu.make_async_copy(wd_hbm.at[gate], wd.at[gate], weight_sem.at[2, t]),
            ]
        )
    load_n[order[0]].start()
    load_g[order[0]].start()
    for copies in load_w:
        for copy in copies:
            copy.start()
    for k in order[1:]:
        load_n[k].start()
        load_g[k].start()
    greet([x_dev, y_dev], [])
    summed = PlaneSum(parts, ones, twos, sum_sems, x_dev, y_dev)

    def hidden(k, slot, lanes, up_lanes):
        rows = rows_of(k)
        gate = dot_n(n[rows, :], wm[:, lanes])
        up = dot_n(n[rows, :], wm[:, up_lanes])
        grad = dot_t(g[rows, :], wd[lanes, :])
        sigmoid = jax.nn.sigmoid(gate)
        silu = gate * sigmoid
        act[rows, lanes] = (silu * up).astype(bf16)
        gh[slot, :, lanes] = (grad * up * sigmoid * (1.0 + gate * (1.0 - sigmoid))).astype(bf16)
        gh[slot, :, up_lanes] = (grad * silu).astype(bf16)

    def hidden_out(i):
        return pltpu.make_async_copy(gh.at[i % 2], gh_hbm.at[rows_of(order[i])], out_sem.at[1, i % 2])

    for i, k in enumerate(order):
        load_n[k].wait()
        load_g[k].wait()
        if i >= 2:
            hidden_out(i - 2).wait()
        if i == 0:
            for copies, (start, size) in zip(load_w, tiles):
                for copy in copies:
                    copy.wait()
                hidden(k, 0, pl.ds(start, size), pl.ds(ff + start, size))
        else:

            def hidden_step(t, carry):
                hidden(k, i % 2, tile_at(t, 256), tile_at(t, 256, ff))
                return carry

            lax.fori_loop(0, ff // 256, hidden_step, 0)
            if ff % 256:
                start, size = tiles[-1]
                hidden(k, i % 2, pl.ds(start, size), pl.ds(ff + start, size))
        hidden_out(i).start()

        def layer_step(t, carry):
            value = dot_n(act[rows_of(k), :], wd[:, tile_at(t, 512)]).astype(bf16)
            if k:
                parts[k - 1, :, tile_at(t, 512)] = value
            else:
                layer_sum[:, tile_at(t, 512)] = value
            return carry

        lax.fori_loop(0, D // 512, layer_step, 0)
        if k == 3:
            for copy in summed.far:
                copy.start()
        elif k:
            summed.near[k - 1].start()
        if k == 2:
            summed.pass_on()
    wide = ff // 256

    def down_out(i, slot, width=256):
        rows = pl.ds(pl.multiple_of((i // 2) * 256, 128), width)
        lanes = tile_at(i % 2, D // 2)
        return pltpu.make_async_copy(stage.at[slot, pl.ds(0, width)], grad_down.at[rows, lanes], out_sem.at[0, slot])

    def down_tile(i, slot, width=256):
        lanes = tile_at(i % 2, D // 2)
        value = dot_tn(act[:, pl.ds(pl.multiple_of((i // 2) * 256, 128), width)], g[:, lanes])
        stage[slot, 0:width] = value.astype(bf16)
        down_out(i, slot, width).start()

    def down_step(i, carry):
        slot = i % 2

        @pl.when(i >= 2)
        def _():
            down_out(i - 2, slot).wait()

        down_tile(i, slot)
        return carry

    lax.fori_loop(0, 2 * wide, down_step, 0)
    for slot in range(2):
        down_out(2 * wide - 2 + slot, slot).wait()
        if ff % 256:
            down_tile(2 * wide + slot, slot, ff % 256)
    for slot in range(2):
        if ff % 256:
            down_out(2 * wide + slot, slot, ff % 256).wait()
        hidden_out(2 + slot).wait()

    def add_layer(r, value):
        layer_sum[r] = (layer_sum[r].astype(f32) + value).astype(bf16)

    summed.finish(add_layer)


def feed_back_kernel(gh_hbm, wm_hbm, n_hbm, grad_normed, grad_mlp, gh, wm, n, stage, parts, ones, twos, *sems):
    sum_sems, (load_sem, out_sem) = sems[:4], sems[4:]
    z, c, f = place()
    x_dev, y_dev = device(z, c, flipped(f, 1)), device(z, c, flipped(f, 2))
    tokens = n.shape[0]
    length = tokens // 4
    ff = gh.shape[1] // 2
    order = (3, 1, 2, 0)
    rows_of = [pl.ds(k * length, length) for k in range(4)]
    load_gh = [pltpu.make_async_copy(gh_hbm.at[rows_of[k]], gh.at[rows_of[k]], load_sem.at[0, k]) for k in range(4)]
    wide_tiles = [pl.ds(start, 1024) for start in range(0, D, 1024)]
    load_w = [
        pltpu.make_async_copy(wm_hbm.at[tile], wm.at[tile], load_sem.at[1, t]) for t, tile in enumerate(wide_tiles)
    ]
    load_n = pltpu.make_async_copy(n_hbm, n, load_sem.at[1, 3])
    for copy in [load_gh[order[0]]] + load_w + [load_gh[k] for k in order[1:]] + [load_n]:
        copy.start()
    greet([x_dev, y_dev], [])
    summed = PlaneSum(parts, ones, twos, sum_sems, x_dev, y_dev)
    for k in order:
        load_gh[k].wait()
        for t, tile in enumerate(wide_tiles):
            if k == order[0]:
                load_w[t].wait()
            value = dot_t(gh[rows_of[k], :], wm[tile, :])
            if k:
                parts[k - 1, :, tile] = value.astype(bf16)
            else:
                grad_normed[:, tile] = value
        if k == 3:
            for copy in summed.far:
                copy.start()
        elif k:
            summed.near[k - 1].start()
    summed.pass_on()
    load_n.wait()
    steps = 2 * D // 512

    def mlp_out(i, slot):
        rows = pl.ds(pl.multiple_of((i // 2) * 512, 512), 512)
        return pltpu.make_async_copy(stage.at[slot], grad_mlp.at[rows, tile_at(i % 2, ff)], out_sem.at[slot])

    def mlp_step(i, carry):
        slot = i % 2

        @pl.when(i >= 2)
        def _():
            mlp_out(i - 2, slot).wait()

        stage[slot] = dot_tn(n[:, tile_at(i // 2, 512)], gh[:, tile_at(i % 2, ff)]).astype(bf16)
        mlp_out(i, slot).start()
        return carry

    lax.fori_loop(0, steps, mlp_step, 0)

    def add_normed(r, value):
        grad_normed[r] += value

    summed.finish(add_normed)
    mlp_out(steps - 2, 0).wait()
    mlp_out(steps - 1, 1).wait()


def feed(normed_all, grads_all, mlp_cols, down_cols):
    tokens, ff = 4 * normed_all.shape[1], down_cols.shape[0]
    length = tokens // 4
    dma = pltpu.SemaphoreType.DMA
    vmem, hbm = pl.BlockSpec(memory_space=pltpu.VMEM), pl.BlockSpec(memory_space=pl.ANY)
    sum_buffers, sum_sems = plane_sum_scratch(length, D)
    normed_all = normed_all.reshape(tokens, D)

    def buffers(*shapes):
        return [pltpu.VMEM(shape, bf16) for shape in shapes] + sum_buffers + sum_sems

    grad_hidden, grad_down, layer_sum = pl.pallas_call(
        feed_front_kernel,
        out_shape=(
            jax.ShapeDtypeStruct((tokens, 2 * ff), bf16),
            jax.ShapeDtypeStruct((ff, D), bf16),
            jax.ShapeDtypeStruct((length, D), bf16),
        ),
        in_specs=[hbm] * 4,
        out_specs=(hbm, hbm, vmem),
        scratch_shapes=buffers(
            (tokens, D), (tokens, D), (D, 2 * ff), (ff, D), (tokens, ff), (2, length, 2 * ff), (2, 256, D // 2)
        )
        + [dma((2, 4)), dma((3, -(-ff // 256))), dma((2, 2))],
        compiler_params=pltpu.CompilerParams(
            collective_id=6, has_side_effects=True, vmem_limit_bytes=feed_vmem_limit
        ),
        cost_estimate=cost(65),
        name="feed_front",
    )(normed_all, grads_all.reshape(tokens, D), mlp_cols, down_cols)
    grad_normed, grad_mlp = pl.pallas_call(
        feed_back_kernel,
        out_shape=(jax.ShapeDtypeStruct((length, D), f32), jax.ShapeDtypeStruct((D, 2 * ff), bf16)),
        in_specs=[hbm] * 3,
        out_specs=(vmem, hbm),
        scratch_shapes=buffers((tokens, 2 * ff), (D, 2 * ff), (tokens, D), (2, 512, ff))
        + [dma((2, 4)), dma((2,))],
        compiler_params=pltpu.CompilerParams(
            collective_id=9, has_side_effects=True, vmem_limit_bytes=feed_vmem_limit
        ),
        cost_estimate=cost(60),
        name="feed_back",
    )(grad_hidden, mlp_cols, normed_all)
    return grad_normed, grad_down, grad_mlp, layer_sum


def local(
    n_dp,
    n_tp,
    inputs,
    cotangent,
    segments,
    qkv_weight,
    out_weight,
    mlp_weight,
    down_weight,
    norm_gains,
    qkv_first,
    out_first,
    mlp_first,
    down_first,
    gains_first,
    qkv_second,
    out_second,
    mlp_second,
    down_second,
    gains_second,
):
    length = inputs.shape[0]
    lines = n_dp // 2
    rows = mlp_weight.shape[0]
    down_rows = down_weight.shape[0]
    ff = n_dp * down_rows
    cosine, sine = tables(segments[0])
    seg_row = segments
    seg_col = segments.reshape(length, 1)

    shard = jnp.concatenate(
        [qkv_weight, out_weight, jnp.pad(norm_gains.T, ((0, 0), (0, 126)))], axis=1
    ).astype(bf16)
    attn_full, mlp_parts, down_cols = gather_all(shard, mlp_weight, down_weight.astype(bf16), n_dp, n_tp)
    qkv_full = attn_full[:, : D + 2 * KW]
    out_full = attn_full[:, D + 2 * KW : 2 * D + 2 * KW]
    gains_full = attn_full[:, 2 * D + 2 * KW :].astype(f32).T
    mlp_cols = lax.all_gather(mlp_parts.reshape(n_tp * rows, 2 * ff), "dp", axis=0, tiled=True)
    tokens_f = inputs.astype(f32)
    gain_one, gain_two = gains_full[0], gains_full[1]
    inverse_one = lax.rsqrt(jnp.mean(tokens_f * tokens_f, axis=-1, keepdims=True) + norm_eps)
    if n_tp == 4:
        qkv, attended, log_totals, middle, normed_one, normed_all, grads_all = forward(
            inputs, cotangent, gains_full, cosine, sine, seg_col, seg_row, attn_full
        )
    else:
        normed_one = (tokens_f * inverse_one * gain_one).astype(bf16)
        projected = matmul(normed_one, qkv_full)
        qkv, attended, log_totals = attend(projected, cosine, sine, seg_col, seg_row)
        middle = tokens_f + matmul(attended, out_full)
    inverse_two = lax.rsqrt(jnp.mean(middle * middle, axis=-1, keepdims=True) + norm_eps)
    if n_tp == 4:
        grad_normed_two, grad_down, grad_mlp, layer_parts = feed(normed_all, grads_all, mlp_cols, down_cols)
    else:
        normed_two = (middle * inverse_two * gain_two).astype(bf16)
        normed_all = plane_gather(normed_two, n_tp)
        grads_all = plane_gather(cotangent, n_tp)
        hidden = matmul(normed_all, mlp_cols)
        gate, up_part = hidden[:, :ff], hidden[:, ff:]
        sigmoid_gate = jax.nn.sigmoid(gate)
        silu_gate = gate * sigmoid_gate
        activated = (silu_gate * up_part).astype(bf16)
        grad_act = matmul_t(grads_all, down_cols)
        grad_gate = grad_act * up_part * sigmoid_gate * (1.0 + gate * (1.0 - sigmoid_gate))
        grad_up = grad_act * silu_gate
        grad_hidden = jnp.concatenate([grad_gate, grad_up], axis=1).astype(bf16)
        grad_normed = matmul_t(grad_hidden, mlp_cols).reshape(n_tp, length, D)
        grad_normed_two = grad_normed[0]
        for k in range(1, n_tp):
            swapped = plane_swap(grad_normed[k].astype(bf16), k, n_tp)
            grad_normed_two = grad_normed_two + swapped.astype(f32)
        grad_down = matmul_tn(activated, grads_all).astype(bf16)
        grad_mlp = matmul_tn(normed_all, grad_hidden).astype(bf16)
        layer_parts = matmul(activated, down_cols).astype(bf16).reshape(n_tp, length, D)
    down_sum = lax.psum_scatter(grad_down, "dp", scatter_dimension=0, tiled=True)
    mlp_sum = lax.psum_scatter(grad_mlp, "dp", scatter_dimension=0, tiled=True).reshape(n_tp, rows, 2 * ff)

    if n_tp == 4:
        layer_out, grad_branch, grad_context, grad_out, gain_two_rows = branch(
            cotangent, grad_normed_two, middle, gains_full, attended, attn_full, layer_parts
        )
        input_grad, out_sum, qkv_sum = backward(
            inputs, normed_one, qkv, grad_context, log_totals, gains_full, cosine, sine, seg_col, seg_row,
            gain_two_rows, grad_out, grad_branch, attn_full, n_dp, n_tp,
        )
        mlp_sum, total = norm_parts(mlp_sum, qkv_sum, out_sum, down_sum, n_dp, n_tp)
    else:
        layer_out = middle + layer_parts[0].astype(f32)
        for k in range(1, n_tp):
            layer_out = layer_out + plane_swap(layer_parts[k], k, n_tp).astype(f32)
        layer_out = layer_out.astype(bf16)
        gain_grad_two = jnp.sum(grad_normed_two * middle * inverse_two, axis=0)
        weighted_two = grad_normed_two * gain_two
        grad_middle = (
            cotangent.astype(f32)
            + inverse_two * weighted_two
            - middle * inverse_two**3 * jnp.mean(weighted_two * middle, axis=-1, keepdims=True)
        )
        grad_branch = grad_middle.astype(bf16)
        grad_context = matmul_t(grad_branch, out_full).astype(bf16)
        grad_projected = attend_grad(qkv, grad_context, log_totals, cosine, sine, seg_col, seg_row)
        grad_out = matmul_tn(attended, grad_branch).astype(bf16)
        grad_qkv = matmul_tn(normed_one, grad_projected)
        grad_normed_one = matmul_t(grad_projected, qkv_full)
        gain_grad_one = jnp.sum(grad_normed_one * tokens_f * inverse_one, axis=0)
        weighted_one = grad_normed_one * gain_one
        grad_inputs = (
            grad_middle
            + inverse_one * weighted_one
            - tokens_f * inverse_one**3 * jnp.mean(weighted_one * tokens_f, axis=-1, keepdims=True)
        )
        input_grad = grad_inputs.astype(bf16)
        gain_grads = jnp.pad(jnp.stack([gain_grad_one, gain_grad_two], axis=1), ((0, 0), (0, 126)))
        grad_qkv = jnp.concatenate([grad_qkv.astype(bf16), gain_grads.astype(bf16)], axis=1)
        out_sum, qkv_sum = scatter_all([grad_out, grad_qkv], n_dp, n_tp)
        mlp_sum = columns_back(mlp_sum, n_dp, n_tp)
        squares = jnp.sum(qkv_sum * qkv_sum) + jnp.sum(out_sum * out_sum) + jnp.sum(mlp_sum * mlp_sum)
        squares = squares + jnp.sum(jnp.square(down_sum.astype(f32)))
        total = total_over_devices(squares, n_dp, n_tp)
    grad_norm = jnp.sqrt(total[0, 0])
    states = (
        (qkv_weight, qkv_first, qkv_second),
        (out_weight, out_first, out_second),
        (mlp_weight, mlp_first, mlp_second),
        (down_weight, down_first, down_second),
        (norm_gains, gains_first, gains_second),
    )
    stepped = adam_all(total, (qkv_sum, out_sum, mlp_sum, down_sum), states)
    news = [stepped[i::3] for i in range(3)]
    return (layer_out, input_grad, grad_norm, *news[0], *news[1], *news[2])


def solution(mesh):
    split_rows = P(("dp", "fsdp"), None)
    split_columns = P(None, ("dp", "fsdp"))
    weights = (split_rows,) * 4 + (split_columns,)
    return jax.shard_map(
        functools.partial(local, mesh.shape["dp"], mesh.shape["fsdp"]),
        mesh=mesh,
        in_specs=(split_rows,) * 3 + weights * 3,
        out_specs=(split_rows, split_rows, P()) + weights * 3,
        check_vma=False,
    )
```

```python
import functools

import jax
import jax.numpy as jnp
from jax import lax
from jax.experimental import pallas as pl
from jax.experimental.pallas import tpu as pltpu
from jax.sharding import PartitionSpec as P

D = 2048
HEADS = 32
KVH = 4
HD = 64
FF = 5632
STEP = 10
KW = KVH * HD
GROUP = HEADS // KVH


norm_eps = 1e-05
rope_base = 10000.0
beta_one = 0.9
beta_two = 0.95
adam_eps = 1e-08
weight_decay = 0.1
matrix_rate = 0.04
gain_rate = 0.8
clip_norm = 1.0

f32 = jnp.float32
bf16 = jnp.bfloat16


def tables(segment_row):
    length = segment_row.shape[0]
    token_index = jnp.arange(length, dtype=jnp.int32)
    previous = jnp.concatenate([segment_row[:1] - 1, segment_row[:-1]])
    starts = lax.cummax(jnp.where(segment_row != previous, token_index, 0), axis=0)
    position = (token_index - starts).astype(f32)
    frequency = rope_base ** (-(jnp.arange(HD // 2, dtype=f32) * 2.0 / HD))
    angles = position[:, None] * frequency[None, :]
    cosine, sine = jnp.cos(angles), jnp.sin(angles)
    cosine = jnp.concatenate([cosine] * 4, axis=-1)
    signed = jnp.concatenate([-sine, sine] * 2, axis=-1)
    return cosine, signed


def halves_swapped(pair):
    lane = lax.broadcasted_iota(jnp.int32, pair.shape, 1)
    return jnp.where(lane % HD < HD // 2, pltpu.roll(pair, 96, 1), pltpu.roll(pair, 32, 1))


def split_pair(pair):
    lane = lax.broadcasted_iota(jnp.int32, pair.shape, 1)
    zero = jnp.zeros_like(pair)
    return jnp.where(lane < HD, pair, zero), jnp.where(lane < HD, zero, pair)


def both_places(pair, odd):
    low, high = split_pair(pair)
    moved = pltpu.roll(pair.astype(f32), HD, 1).astype(pair.dtype)
    moved_low, moved_high = split_pair(moved)
    return (moved_low, high) if odd else (low, moved_high)


def dot_t(a, b):
    return lax.dot_general(a, b, (((1,), (1,)), ((), ())), preferred_element_type=f32)


def dot_n(a, b):
    return lax.dot_general(a, b, (((1,), (0,)), ((), ())), preferred_element_type=f32)


def dot_tn(a, b):
    return lax.dot_general(a, b, (((0,), (0,)), ((), ())), preferred_element_type=f32)


def mask_keys_rows(seg_col, seg_row, length):
    key_index = lax.broadcasted_iota(jnp.int32, (length, length), 0)
    query_index = lax.broadcasted_iota(jnp.int32, (length, length), 1)
    return (seg_col == seg_row) & (query_index >= key_index)


def attend_kernel(proj, cosine, sine, seg_col, seg_row, qkv, context, log_totals):
    cos, sin = cosine[...], sine[...]
    for c in range(0, D + KW, 128):
        qkv[:, c : c + 128] = rope_tile(proj[:, c : c + 128], cos, sin).astype(bf16)
    for c in range(D + KW, D + 2 * KW, 128):
        qkv[:, c : c + 128] = proj[:, c : c + 128].astype(bf16)
    allowed = mask_keys_rows(seg_col[...], seg_row[...], proj.shape[0])
    attend_heads(qkv, context, log_totals, allowed)


def attend_grad_kernel(qkv, grad_context, log_totals, cosine, sine, seg_col, seg_row, grad_proj):
    allowed = mask_keys_rows(seg_col[...], seg_row[...], qkv.shape[0])
    attend_heads_grad(qkv, grad_context, log_totals, grad_proj, allowed, cosine[...], sine[...])


vmem_limit = 50 * 1024 * 1024
feed_vmem_limit = 62 * 1024 * 1024


def attend(projected, cosine, sine, seg_col, seg_row):
    length = projected.shape[0]
    return pl.pallas_call(
        attend_kernel,
        out_shape=(
            jax.ShapeDtypeStruct((length, D + 2 * KW), bf16),
            jax.ShapeDtypeStruct((length, D), bf16),
            jax.ShapeDtypeStruct((HEADS, length), f32),
        ),
        compiler_params=pltpu.CompilerParams(vmem_limit_bytes=vmem_limit),
        cost_estimate=cost(18),
        name="attend",
    )(projected, cosine, sine, seg_col, seg_row)


def attend_grad(qkv, grad_context, log_totals, cosine, sine, seg_col, seg_row):
    length = qkv.shape[0]
    return pl.pallas_call(
        attend_grad_kernel,
        out_shape=jax.ShapeDtypeStruct((length, D + 2 * KW), bf16),
        compiler_params=pltpu.CompilerParams(vmem_limit_bytes=vmem_limit),
        cost_estimate=cost(26),
        name="attend_grad",
    )(qkv, grad_context, log_totals, cosine, sine, seg_col, seg_row)


MESH = pl.DeviceIdType.MESH


def cost(microseconds):
    return pl.CostEstimate(flops=0, bytes_accessed=int(microseconds * 3.69e6), transcendentals=0)


def place():
    dp = lax.axis_index("dp")
    return dp // 2, dp % 2, lax.axis_index("fsdp")


def device(line, core, plane):
    return {"dp": line * 2 + core, "fsdp": plane}


def flipped(index, bit):
    return index + bit - 2 * bit * ((index // bit) % 2)


def greet(partners, ends):
    barrier = pltpu.get_barrier_semaphore()
    count = len(partners)
    for partner in partners:
        pl.semaphore_signal(barrier, inc=1, device_id=partner, device_id_type=MESH)
    for there, partner in ends:
        count = count + there

        @pl.when(there == 1)
        def _():
            pl.semaphore_signal(barrier, inc=1, device_id=partner, device_id_type=MESH)

    pl.semaphore_wait(barrier, count)


def gather_kernel(lines, own, weight, down, full, parts, down_full, cut, line_send, line_recv, x_send, x_recv, y_send, y_recv,
                  dx_send, dx_recv, dy_send, dy_recv, core_send, core_recv, cut_send, cut_recv, down_send, down_recv, down_core_send,
                  down_core_recv, here_sem):
    z, c, f = place()
    half = own.shape[0] // 2
    fx, fy = flipped(f, 1), flipped(f, 2)
    fd = flipped(fx, 2)
    x_dev, y_dev, core_dev = device(z, c, fx), device(z, c, fy), device(z, 1 - c, f)
    has_left = jnp.minimum(z, 1)
    has_right = jnp.minimum(lines - 1 - z, 1)
    left_dev = device(jnp.maximum(z - 1, 0), c, f)
    right_dev = device(jnp.minimum(z + 1, lines - 1), c, f)
    far_dev = device(z, c, fd)
    greet([x_dev, y_dev, far_dev, core_dev], [(has_left, left_dev), (has_right, right_dev)])

    def cut_copy(k):
        to = flipped(f, k) if k < 3 else fd
        return pltpu.make_async_remote_copy(
            cut.at[to], parts.at[f], cut_send.at[k], cut_recv.at[k], device_id=device(z, c, to), device_id_type=MESH
        )

    def copy(line, plane, send, recv, dev, src=None, rows=None):
        dst = full.at[line, c, plane]
        src = dst if src is None else src
        if rows is not None:
            dst, src = dst.at[rows], src.at[rows]
        return pltpu.make_async_remote_copy(
            src, dst, send, recv, device_id=dev, device_id_type=MESH
        )

    def to_right(line, src=None):
        return copy(line, f, line_send.at[0, line], line_recv.at[line], right_dev, src)

    def to_left(line, src=None):
        return copy(line, f, line_send.at[1, line], line_recv.at[line], left_dev, src)

    def to_x(line, src=None):
        return copy(line, f, x_send.at[line], x_recv.at[line], x_dev, src)

    def to_y(line, src=None):
        return copy(line, f, y_send.at[line], y_recv.at[line], y_dev, src)

    def diag_y(line):
        return copy(line, fx, dy_send.at[line], dy_recv.at[line], y_dev, None, pl.ds(0, half))

    def diag_x(line):
        return copy(line, fy, dx_send.at[line], dx_recv.at[line], x_dev, None, pl.ds(half, half))

    def to_core(line, plane, src=None):
        return copy(line, plane, core_send.at[line, plane], core_recv.at[line, plane], core_dev, src)

    def down_copy(line, way, src=None):
        dst = down_full.at[line, c]
        return pltpu.make_async_remote_copy(
            dst if src is None else src, dst, down_send.at[way, line], down_recv.at[line],
            device_id=(right_dev, left_dev)[way], device_id_type=MESH,
        )

    def down_core(line, src=None):
        dst = down_full.at[line, c]
        return pltpu.make_async_remote_copy(
            dst if src is None else src, dst, down_core_send.at[line], down_core_recv.at[line],
            device_id=core_dev, device_id_type=MESH,
        )

    here = pltpu.make_async_copy(own, full.at[z, c, f], here_sem.at[0])
    here.start()
    here_down = pltpu.make_async_copy(down, down_full.at[z, c], here_sem.at[2])
    here_down.start()

    @pl.when(has_right == 1)
    def _():
        to_right(z, own).start()

    @pl.when(has_left == 1)
    def _():
        to_left(z, own).start()

    to_x(z, own).start()
    to_y(z, own).start()
    to_core(z, f, own).start()

    cut_columns(weight, cut, 2 * lines, 4)
    here_cut = pltpu.make_async_copy(cut.at[f], parts.at[f], here_sem.at[1])
    here_cut.start()
    for k in range(1, 4):
        cut_copy(k).start()

    down_core(z, down).start()
    for t in range(1, lines):

        @pl.when(z >= t)
        def _():
            line = z - t
            to_right(line).wait_recv()

            @pl.when(has_right == 1)
            def _():
                to_right(line).start()

            to_x(line).start()
            to_y(line).start()
            to_core(line, f).start()

        @pl.when(z + t <= lines - 1)
        def _():
            line = z + t
            to_left(line).wait_recv()

            @pl.when(has_left == 1)
            def _():
                to_left(line).start()

            to_x(line).start()
            to_y(line).start()
            to_core(line, f).start()

    @pl.when(has_right == 1)
    def _():
        down_copy(z, 0, down).start()

    @pl.when(has_left == 1)
    def _():
        down_copy(z, 1, down).start()

    here.wait()
    order = []
    for t in range(lines):
        line = z
        for b in range(lines.bit_length() - 1):
            if t >> b & 1:
                line = flipped(line, 1 << b)
        order.append(line)
    for t, line in enumerate(order):
        to_x(line).wait_recv()
        diag_y(line).start()
        to_core(line, fx).start()
        to_y(line).wait_recv()
        diag_x(line).start()
        to_core(line, fy).start()
        if t == 0:
            continue

        @pl.when(z >= t)
        def _():
            down_copy(z - t, 0).wait_recv()

            @pl.when(has_right == 1)
            def _():
                down_copy(z - t, 0).start()

            down_core(z - t).start()

        @pl.when(z + t <= lines - 1)
        def _():
            down_copy(z + t, 1).wait_recv()

            @pl.when(has_left == 1)
            def _():
                down_copy(z + t, 1).start()

            down_core(z + t).start()

    for line in order:
        diag_y(line).wait_recv()
        diag_x(line).wait_recv()
        to_core(line, fd).start()
    here_cut.wait()
    here_down.wait()
    for k in range(1, 4):
        cut_copy(k).wait()
    for line in range(lines):
        for plane in range(4):
            to_core(line, plane).wait()
        to_x(line).wait_send()
        to_y(line).wait_send()
        diag_x(line).wait_send()
        diag_y(line).wait_send()

        down_core(line).wait()

        @pl.when((line <= z) & (has_right == 1))
        def _():
            to_right(line).wait_send()
            down_copy(line, 0).wait_send()

        @pl.when((line >= z) & (has_left == 1))
        def _():
            to_left(line).wait_send()
            down_copy(line, 1).wait_send()


def gather_all(shard, weight, down, n_dp, n_tp):
    rows, columns = shard.shape
    width = weight.shape[1] // n_tp
    lines = n_dp // 2
    if n_tp != 4 or rows % 32:
        full = lax.all_gather(shard, ("dp", "fsdp"), axis=0, tiled=True)
        down_full = lax.all_gather(down, "dp", axis=0, tiled=True)
        return full, columns_out(weight, n_dp, n_tp), down_full
    dma = pltpu.SemaphoreType.DMA
    hbm = pl.BlockSpec(memory_space=pl.ANY)
    full, parts, down_full = pl.pallas_call(
        functools.partial(gather_kernel, lines),
        out_shape=(
            jax.ShapeDtypeStruct((lines, 2, n_tp, rows, columns), bf16),
            jax.ShapeDtypeStruct((n_tp, rows, width), bf16),
            jax.ShapeDtypeStruct((lines, 2, *down.shape), bf16),
        ),
        in_specs=[hbm, pl.BlockSpec(memory_space=pltpu.VMEM), hbm],
        out_specs=(hbm, hbm, hbm),
        scratch_shapes=[pltpu.VMEM((n_tp, rows, width), bf16), dma((2, lines))]
        + [dma((lines,))] * 9
        + [dma((lines, n_tp))] * 2
        + [dma((n_tp,)), dma((n_tp,)), dma((2, lines)), dma((lines,)), dma((lines,)), dma((lines,)), dma((3,))],
        compiler_params=pltpu.CompilerParams(
            collective_id=0, has_side_effects=True, vmem_limit_bytes=vmem_limit
        ),
        cost_estimate=cost(100),
        name="gather_all",
    )(shard, weight, down)
    full = full.reshape(n_dp * n_tp * rows, columns)
    return full, parts, down_full.reshape(n_dp * down.shape[0], down.shape[1])


def cut_columns(weight, cut, n_dp, n_tp):
    unit = weight.shape[1] // (2 * n_dp * n_tp)
    half = n_dp * unit
    for to in range(n_tp):
        for side in range(2):
            starts = [side * n_tp * half + (j * n_tp + to) * unit for j in range(n_dp)]
            pieces = [weight[:, start : start + unit] for start in starts]
            cut[to, :, side * half : (side + 1) * half] = jnp.concatenate(pieces, axis=1).astype(bf16)


def columns_out_kernel(n_dp, n_tp, weight, parts, cut, send, recv, here_sem):
    z, c, f = place()
    greet([device(z, c, (f + k) % n_tp) for k in range(1, n_tp)], [])

    def away(k):
        to = (f + k) % n_tp
        return pltpu.make_async_remote_copy(
            cut.at[to], parts.at[f], send.at[k], recv.at[k], device_id=device(z, c, to), device_id_type=MESH
        )

    cut_columns(weight, cut, n_dp, n_tp)
    for k in range(1, n_tp):
        away(k).start()
    here = pltpu.make_async_copy(cut.at[f], parts.at[f], here_sem)
    here.start()
    here.wait()
    for k in range(1, n_tp):
        away(k).wait()


def columns_out(weight, n_dp, n_tp):
    rows, width = weight.shape
    dma = pltpu.SemaphoreType.DMA
    return pl.pallas_call(
        functools.partial(columns_out_kernel, n_dp, n_tp),
        out_shape=jax.ShapeDtypeStruct((n_tp, rows, width // n_tp), bf16),
        out_specs=pl.BlockSpec(memory_space=pl.ANY),
        scratch_shapes=[
            pltpu.VMEM((n_tp, rows, width // n_tp), bf16), dma((n_tp,)), dma((n_tp,)), dma(()),
        ],
        compiler_params=pltpu.CompilerParams(
            collective_id=1, has_side_effects=True, vmem_limit_bytes=vmem_limit
        ),
        cost_estimate=cost(20),
        name="columns_out",
    )(weight)


def columns_back_kernel(n_dp, n_tp, parts, whole, got, send, recv, here_sem):
    z, c, f = place()
    greet([device(z, c, (f + k) % n_tp) for k in range(1, n_tp)], [])
    unit = whole.shape[1] // (2 * n_dp * n_tp)
    half = n_dp * unit

    def away(k):
        to = (f + k) % n_tp
        return pltpu.make_async_remote_copy(
            parts.at[to], got.at[f], send.at[k], recv.at[k], device_id=device(z, c, to), device_id_type=MESH
        )

    for k in range(1, n_tp):
        away(k).start()
    here = pltpu.make_async_copy(parts.at[f], got.at[f], here_sem)
    here.start()
    here.wait()
    for k in range(1, n_tp):
        away(k).wait()
    for side in range(2):
        pieces = [
            got[frm, :, side * half + j * unit : side * half + (j + 1) * unit].astype(f32)
            for j in range(n_dp)
            for frm in range(n_tp)
        ]
        whole[:, side * n_tp * half : (side + 1) * n_tp * half] = jnp.concatenate(pieces, axis=1)


def columns_back(parts, n_dp, n_tp):
    _, rows, width = parts.shape
    dma = pltpu.SemaphoreType.DMA
    return pl.pallas_call(
        functools.partial(columns_back_kernel, n_dp, n_tp),
        out_shape=jax.ShapeDtypeStruct((rows, width * n_tp), f32),
        in_specs=[pl.BlockSpec(memory_space=pl.ANY)],
        scratch_shapes=[pltpu.VMEM(parts.shape, bf16), dma((n_tp,)), dma((n_tp,)), dma(())],
        compiler_params=pltpu.CompilerParams(
            collective_id=2, has_side_effects=True, vmem_limit_bytes=vmem_limit
        ),
        cost_estimate=cost(20),
        name="columns_back",
    )(parts)


def total_kernel(n_dp, n_tp, value, total, held, got, send, recv):
    dp, f = lax.axis_index("dp"), lax.axis_index("fsdp")
    partners = []
    for axis, size in (("dp", n_dp), ("fsdp", n_tp)):
        for bit in range(size.bit_length() - 1):
            index = {"dp": dp, "fsdp": f}
            index[axis] = flipped(index[axis], 1 << bit)
            partners.append(index)
    greet(partners, [])
    held[0] = value[...]
    for step, partner in enumerate(partners):
        swap = pltpu.make_async_remote_copy(
            held.at[step], got.at[step], send.at[step], recv.at[step], device_id=partner, device_id_type=MESH
        )
        swap.start()
        swap.wait()
        held[step + 1] = held[step] + got[step]
    total[...] = held[len(partners)]


def total_over_devices(value, n_dp, n_tp):
    steps = (n_dp * n_tp).bit_length() - 1
    dma = pltpu.SemaphoreType.DMA
    tile = (8, 128)
    spread = pl.pallas_call(
        functools.partial(total_kernel, n_dp, n_tp),
        out_shape=jax.ShapeDtypeStruct(tile, f32),
        scratch_shapes=[
            pltpu.VMEM((steps + 1, *tile), f32), pltpu.VMEM((steps, *tile), f32), dma((steps,)), dma((steps,)),
        ],
        compiler_params=pltpu.CompilerParams(collective_id=3, has_side_effects=True),
        cost_estimate=cost(13),
        name="total",
    )(jnp.broadcast_to(value, tile))
    return spread


def adam_update(weight, gradient, first, second, rate, decay):
    first = beta_one * first + (1.0 - beta_one) * gradient
    second = beta_two * second + (1.0 - beta_two) * gradient * gradient
    first_hat = first / (1.0 - beta_one**STEP)
    second_hat = second / (1.0 - beta_two**STEP)
    weight = weight - rate * (first_hat / (jnp.sqrt(second_hat) + adam_eps) + decay * weight)
    return (weight, first, second)


def matmul(a, b):
    return jnp.dot(a, b, preferred_element_type=f32)


def matmul_t(a, b):
    return lax.dot_general(a, b, (((1,), (1,)), ((), ())), preferred_element_type=f32)


def matmul_tn(a, b):
    return lax.dot_general(a, b, (((0,), (0,)), ((), ())), preferred_element_type=f32)


def swap_core(block, n_dp):
    return lax.ppermute(block, "dp", [(i, i ^ 1) for i in range(n_dp)])


def plane_swap(block, k, n_tp):
    return lax.ppermute(block, "fsdp", [(i, i ^ k) for i in range(n_tp)])


def plane_gather(block, n_tp):
    if n_tp != 4:
        return jnp.concatenate([block] + [plane_swap(block, k, n_tp) for k in range(1, n_tp)], axis=0)
    half = block.shape[0] // 2
    over_x, over_y = plane_swap(block, 1, n_tp), plane_swap(block, 2, n_tp)
    far = [plane_swap(over_y[:half], 1, n_tp), plane_swap(over_x[half:], 2, n_tp)]
    return jnp.concatenate([block, over_x, over_y] + far, axis=0)


def core_sum(parts, n_dp):
    core = lax.axis_index("dp") % 2
    mine = lax.dynamic_index_in_dim(parts, core, 1, keepdims=False)
    other = lax.dynamic_index_in_dim(parts, 1 - core, 1, keepdims=False)
    return mine.astype(f32) + swap_core(other, n_dp).astype(f32)


def line_sum(parts, n_dp):
    lines = n_dp // 2
    place = lax.axis_index("dp") // 2
    result = lax.dynamic_index_in_dim(parts, place, 0, keepdims=False)
    for way in (1, -1):
        arrived = None
        for step in range(1, lines):
            target = jnp.clip(place + way * (lines - step), 0, lines - 1)
            load = lax.dynamic_index_in_dim(parts, target, 0, keepdims=False).astype(f32)
            if arrived is not None:
                load = load + arrived.astype(f32)
            senders = range(step) if way == 1 else range(lines - step, lines)
            pairs = [(2 * s + c, 2 * (s + way) + c) for s in senders for c in range(2)]
            arrived = lax.ppermute(load.astype(bf16), "dp", pairs)
        result = result.astype(f32) + arrived.astype(f32)
    return result


def plane_sum(parts, n_tp):
    here = lax.axis_index("fsdp")
    total = lax.dynamic_index_in_dim(parts, here, 0, keepdims=False).astype(f32)
    for k in range(1, n_tp):
        load = lax.dynamic_index_in_dim(parts, here ^ k, 0, keepdims=False).astype(bf16)
        total = total + plane_swap(load, k, n_tp).astype(f32)
    return total


def by_rows(rows, body):
    def step(i, carry):
        body(pl.ds(pl.multiple_of(i * 16, 16), 16))
        return carry

    lax.fori_loop(0, rows // 16, step, 0)


def places_by_distance(z, lines):
    tables = [
        sorted(range(lines), key=lambda d: (-abs(d - here), min(d, lines - 1 - d), d)) for here in range(lines)
    ]
    power = 1
    for bit in range(lines.bit_length() - 1):
        power = power * (1 + (lines ** (1 << bit) - 1) * (z // (1 << bit) % 2))
    return [sum(table[t] * lines**here for here, table in enumerate(tables)) // power % lines for t in range(lines)]


class Scatter:
    def __init__(self, lines, groups, sems):
        self.sums, self.others, self.firsts, self.seconds, self.alongs, self.leaving, self.outs = groups
        core_send, core_recv, one_send, one_recv, two_send, two_recv, line_send, line_recv = sems
        z, c, f = place()
        self.z, self.f, self.lines = z, f, lines
        self.planes, self.rows = self.sums[0].shape[1:3]
        self.half = self.rows // 2
        fx, fy = flipped(f, 1), flipped(f, 2)
        fd = flipped(fx, 2)
        x_dev, y_dev, core_dev = device(z, c, fx), device(z, c, fy), device(z, 1 - c, f)
        self.has_left = jnp.minimum(z, 1)
        self.has_right = jnp.minimum(lines - 1 - z, 1)
        left_dev = device(jnp.maximum(z - 1, 0), c, f)
        right_dev = device(jnp.minimum(z + 1, lines - 1), c, f)
        greet([x_dev, y_dev, core_dev], [(self.has_left, left_dev), (self.has_right, right_dev)])
        halves = (pl.ds(0, self.half), pl.ds(self.half, self.half))
        near, self.next_near, step_dev = (fx, fy), (fy, fx), (x_dev, y_dev)
        self.order = places_by_distance(z, lines)

        def remote(src, dst, send, recv, dev):
            return pltpu.make_async_remote_copy(src, dst, send, recv, device_id=dev, device_id_type=MESH)

        def to_core(a, d, src):
            return remote(src, self.others[a].at[d], core_send.at[a, d], core_recv.at[a, d], core_dev)

        def one(a, d, way, i):
            block = (near[way], fd)[i]
            return remote(
                self.sums[a].at[d, block, halves[way]], self.firsts[a].at[way, d, i],
                one_send.at[a, d, way, i], one_recv.at[a, d, way, i], step_dev[way],
            )

        def two(a, d, way):
            return remote(
                self.sums[a].at[d, self.next_near[way], halves[way]], self.seconds[a].at[way, d],
                two_send.at[a, d, way], two_recv.at[a, d, way], step_dev[1 - way],
            )

        def to_right(a, d):
            return remote(
                self.leaving[a].at[d], self.alongs[a].at[d], line_send.at[a, d], line_recv.at[a, d], right_dev
            )

        def to_left(a, d, slot):
            return remote(
                self.leaving[a].at[d], self.alongs[a].at[slot], line_send.at[a, d], line_recv.at[a, slot], left_dev
            )

        self.to_core, self.one, self.two, self.to_right, self.to_left = to_core, one, two, to_right, to_left

    def add_along(self, a, slot):
        def step(r):
            self.outs[a][r] += self.alongs[a][slot, r].astype(f32)

        by_rows(self.rows, step)

    def over_core(self, a, d):
        sums, others = self.sums[a], self.others[a]
        self.to_core(a, d, others.at[d]).wait_recv()

        def core_add(r):
            for plane in range(self.planes):
                sums[d, plane, r] = (sums[d, plane, r].astype(f32) + others[d, plane, r].astype(f32)).astype(bf16)

        by_rows(self.rows, core_add)
        for i in (1, 0):
            for way in range(2):
                self.one(a, d, way, i).start()

    def there(self, r, way):
        return pl.ds(pl.multiple_of(r.start + way * self.half, 16), r.size)

    def over_first(self, a, d):
        sums, firsts = self.sums[a], self.firsts[a]
        for way in range(2):
            self.one(a, d, way, 1).wait_recv()
            block = self.next_near[way]

            def first_add(r):
                there = self.there(r, way)
                mine = sums[d, block, there].astype(f32)
                sums[d, block, there] = (mine + firsts[way, d, 1, r].astype(f32)).astype(bf16)

            by_rows(self.half, first_add)
            self.two(a, d, way).start()

    def over_second(self, a, d):
        sums, firsts, seconds, z = self.sums[a], self.firsts[a], self.seconds[a], self.z
        for way in range(2):
            self.one(a, d, way, 0).wait_recv()
            self.two(a, d, way).wait_recv()

            def total(r, there):
                return (
                    sums[d, self.f, there].astype(f32)
                    + firsts[way, d, 0, r].astype(f32)
                    + seconds[way, d, r].astype(f32)
                )

            @pl.when(d == z)
            def _():
                def stay(r):
                    there = self.there(r, way)
                    self.outs[a][there] = total(r, there)

                by_rows(self.half, stay)

            @pl.when(d != z)
            def _():
                def leave(r):
                    there = self.there(r, way)
                    self.leaving[a][d, there] = total(r, there).astype(bf16)

                by_rows(self.half, leave)

    def over_line(self, a, d):
        leaving, alongs, z = self.leaving[a], self.alongs[a], self.z

        def add_arrived():
            def step(r):
                leaving[d, r] = (leaving[d, r].astype(f32) + alongs[d, r].astype(f32)).astype(bf16)

            by_rows(self.rows, step)

        @pl.when((d > z) & (self.has_left == 1))
        def _():
            self.to_right(a, d).wait_recv()
            add_arrived()

        @pl.when((d < z) & (self.has_right == 1))
        def _():
            self.to_left(a, d, d).wait_recv()
            add_arrived()

        @pl.when(d > z)
        def _():
            self.to_right(a, d).start()

        @pl.when((d < z) & (d + 1 < z))
        def _():
            self.to_left(a, d, d).start()

        @pl.when(d + 1 == z)
        def _():
            self.to_left(a, d, self.lines).start()

    def finish(self):
        for a in range(len(self.sums)):

            @pl.when(self.has_left == 1)
            def _():
                self.to_right(a, self.z).wait_recv()
                self.add_along(a, self.z)

            @pl.when(self.has_right == 1)
            def _():
                self.to_left(a, self.z, self.lines).wait_recv()
                self.add_along(a, self.lines)

            for d in self.order:
                for way in range(2):
                    self.one(a, d, way, 0).wait_send()
                    self.one(a, d, way, 1).wait_send()
                    self.two(a, d, way).wait_send()

                @pl.when(d != self.z)
                def _():
                    self.to_right(a, d).wait_send()


def scatter_scratch(lines, n_tp, rows, widths):
    dma = pltpu.SemaphoreType.DMA
    n = len(widths)
    shapes = [
        (lines, n_tp, rows), (lines, n_tp, rows), (2, lines, 2, rows // 2), (2, lines, rows // 2),
        (lines + 1, rows), (lines, rows),
    ]
    buffers = [pltpu.VMEM((*shape, width), bf16) for shape in shapes for width in widths]
    sems = [dma((n, lines))] * 2 + [dma((n, lines, 2, 2))] * 2 + [dma((n, lines, 2))] * 2
    return buffers, sems + [dma((n, lines)), dma((n, lines + 1))]


def scatter_all(arrays, n_dp, n_tp):
    lines = n_dp // 2
    rows = arrays[0].shape[0] // (n_dp * n_tp)
    results = []
    for array in arrays:
        parts = core_sum(array.reshape(lines, 2, n_tp, rows, -1), n_dp)
        results.append(line_sum(plane_sum(parts.transpose(1, 0, 2, 3), n_tp), n_dp))
    return results


def rope_tile(tile, cos, sin):
    pairs = [tile[:, i : i + 128] for i in range(0, tile.shape[1], 128)]
    return jnp.concatenate([pair * cos + halves_swapped(pair) * sin for pair in pairs], axis=1)


def attend_heads(qkv, context, log_totals, allowed):
    length = qkv.shape[0]
    scale = HD ** (-0.5)
    for group in range(KVH):
        kc = D + (group // 2) * 128
        keys = both_places(qkv[:, kc : kc + 128], group % 2)
        values = both_places(qkv[:, kc + KW : kc + KW + 128], group % 2)

        def pair_step(pair_index, carry):
            pair = group * (GROUP // 2) + pair_index
            lanes = pl.ds(pl.multiple_of(pair * 128, 128), 128)
            queries = qkv[:, lanes]
            total = jnp.zeros((length, 128), f32)
            for side in range(2):
                scores = dot_t(keys[side], queries) * scale
                scores = jnp.where(allowed, scores, -1e30)
                top = jnp.max(scores, axis=0, keepdims=True)
                raised = jnp.exp(scores - top)
                totals = jnp.sum(raised, axis=0, keepdims=True)
                probs = (raised / totals).astype(bf16)
                total = total + dot_tn(probs, values[side])
                log_totals[pl.ds(2 * pair + side, 1), :] = top + jnp.log(totals)
            context[:, lanes] = total.astype(bf16)
            return carry

        lax.fori_loop(0, GROUP // 2, pair_step, 0)


def tile_at(i, width, start=0):
    return pl.ds(pl.multiple_of(start + i * width, 128), width)


class Exchange:
    def __init__(self, own, whole, sems, i, x_dev, y_dev):
        send, recv, here = sems
        half = own.shape[0] // 2

        def remote(src, dst, k, dev):
            return pltpu.make_async_remote_copy(
                src, dst, send.at[i, k], recv.at[i, k], device_id=dev, device_id_type=MESH
            )

        low, high = pl.ds(0, half), pl.ds(half, half)
        self.near = [remote(own, whole.at[1], 0, x_dev), remote(own, whole.at[2], 1, y_dev)]
        self.far = [
            remote(whole.at[2, low], whole.at[3, low], 2, x_dev),
            remote(whole.at[1, high], whole.at[3, high], 3, y_dev),
        ]
        self.here = pltpu.make_async_copy(own, whole.at[0], here.at[i])

    def start(self):
        for copy in self.near:
            copy.start()
        self.here.start()

    def pass_on(self):
        for copy in self.near:
            copy.wait_recv()
        for copy in self.far:
            copy.start()

    def finish(self):
        for copy in self.far:
            copy.wait()
        for copy in self.near:
            copy.wait_send()
        self.here.wait()


def forward_kernel(x, grads, gains, cosine, sine, seg_col, seg_row, weights, qkv, context, log_totals, middle,
                   normed_one, normed_all, grads_all, q_weight, o_weight, normed_two, load_sem, *sems):
    z, c, f = place()
    x_dev, y_dev = device(z, c, flipped(f, 1)), device(z, c, flipped(f, 2))
    greet([x_dev, y_dev], [])
    length = x.shape[0]
    width = D + 2 * KW
    of_grads = Exchange(grads, grads_all, sems, 0, x_dev, y_dev)
    of_normed = Exchange(normed_two, normed_all, sems, 1, x_dev, y_dev)
    of_grads.start()
    load_q = pltpu.make_async_copy(weights.at[:, pl.ds(0, width)], q_weight, load_sem.at[0])
    load_o = pltpu.make_async_copy(weights.at[:, pl.ds(width, D)], o_weight, load_sem.at[1])
    load_q.start()
    load_o.start()

    def norm_one(r):
        rows = x[r].astype(f32)
        inverse = lax.rsqrt(jnp.mean(rows * rows, axis=-1, keepdims=True) + norm_eps)
        normed_one[r] = (rows * inverse * gains[0:1, :]).astype(bf16)

    by_rows(length, norm_one)
    load_q.wait()
    cos, sin = cosine[...], sine[...]

    def project(i, carry):
        lanes = tile_at(i, 256)
        qkv[:, lanes] = rope_tile(dot_n(normed_one[...], q_weight[:, lanes]), cos, sin).astype(bf16)
        return carry

    lax.fori_loop(0, (D + KW) // 256, project, 0)
    qkv[:, D + KW :] = dot_n(normed_one[...], q_weight[:, D + KW :]).astype(bf16)
    allowed = mask_keys_rows(seg_col[...], seg_row[...], length)
    attend_heads(qkv, context, log_totals, allowed)
    load_o.wait()

    def project_out(i, carry):
        lanes = tile_at(i, 256)
        middle[:, lanes] = x[:, lanes].astype(f32) + dot_n(context[...], o_weight[:, lanes])
        return carry

    lax.fori_loop(0, D // 256, project_out, 0)

    def norm_two(r):
        rows = middle[r]
        inverse = lax.rsqrt(jnp.mean(rows * rows, axis=-1, keepdims=True) + norm_eps)
        normed_two[r] = (rows * inverse * gains[1:2, :]).astype(bf16)

    by_rows(length, norm_two)
    of_normed.start()
    of_grads.pass_on()
    of_normed.pass_on()
    of_normed.finish()
    of_grads.finish()


def forward(x, grads, gains, cosine, sine, seg_col, seg_row, weights):
    length = x.shape[0]
    dma = pltpu.SemaphoreType.DMA
    vmem, hbm = pl.BlockSpec(memory_space=pltpu.VMEM), pl.BlockSpec(memory_space=pl.ANY)
    width = D + 2 * KW
    return pl.pallas_call(
        forward_kernel,
        out_shape=(
            jax.ShapeDtypeStruct((length, width), bf16),
            jax.ShapeDtypeStruct((length, D), bf16),
            jax.ShapeDtypeStruct((HEADS, length), f32),
            jax.ShapeDtypeStruct((length, D), f32),
            jax.ShapeDtypeStruct((length, D), bf16),
            jax.ShapeDtypeStruct((4, length, D), bf16),
            jax.ShapeDtypeStruct((4, length, D), bf16),
        ),
        in_specs=[vmem, hbm] + [vmem] * 5 + [hbm],
        out_specs=(vmem,) * 5 + (hbm,) * 2,
        scratch_shapes=[
            pltpu.VMEM((D, width), bf16), pltpu.VMEM((D, D), bf16), pltpu.VMEM((length, D), bf16),
            dma((2,)), dma((2, 4)), dma((2, 4)), dma((2,)),
        ],
        compiler_params=pltpu.CompilerParams(
            collective_id=5, has_side_effects=True, vmem_limit_bytes=feed_vmem_limit
        ),
        cost_estimate=cost(95),
        name="forward",
    )(x, grads, gains, cosine, sine, seg_col, seg_row, weights)


class PlaneSum:
    def __init__(self, parts, ones, twos, sems, x_dev, y_dev):
        one_send, one_recv, two_send, two_recv = sems
        self.half = parts.shape[1] // 2
        self.parts, self.ones, self.twos = parts, ones, twos
        halves = (pl.ds(0, self.half), pl.ds(self.half, self.half))
        step_dev = (x_dev, y_dev)

        def remote(src, dst, send, recv, dev):
            return pltpu.make_async_remote_copy(src, dst, send, recv, device_id=dev, device_id_type=MESH)

        self.near, self.far, self.two = [], [], []
        for way in range(2):
            for i, copies in enumerate((self.near, self.far)):
                block = parts.at[2 if i else way, halves[way]]
                copies.append(
                    remote(block, ones.at[way, i], one_send.at[way, i], one_recv.at[way, i], step_dev[way])
                )
            if twos is not None:
                block = parts.at[1 - way, halves[way]]
                self.two.append(remote(block, twos.at[way], two_send.at[way], two_recv.at[way], step_dev[1 - way]))

    def there(self, r, way):
        return pl.ds(pl.multiple_of(r.start + way * self.half, 16), r.size)

    def pass_on(self):
        for way in range(2):
            self.far[way].wait_recv()

            def add_far(r):
                there = self.there(r, way)
                mine = self.parts[1 - way, there].astype(f32)
                self.parts[1 - way, there] = (mine + self.ones[way, 1, r].astype(f32)).astype(bf16)

            by_rows(self.half, add_far)
            self.two[way].start()

    def finish(self, add):
        for way in range(2):
            self.near[way].wait()
            self.far[way].wait_send()
            self.two[way].wait()
        for way in range(2):

            def add_all(r):
                add(self.there(r, way), self.ones[way, 0, r].astype(f32) + self.twos[way, r].astype(f32))

            by_rows(self.half, add_all)


def plane_sum_scratch(length, columns):
    dma = pltpu.SemaphoreType.DMA
    shapes = ((3, length, columns), (2, 2, length // 2, columns), (2, length // 2, columns))
    return [pltpu.VMEM(shape, bf16) for shape in shapes], [dma((2, 2)), dma((2, 2)), dma((2,)), dma((2,))]


def attend_heads_grad(qkv, grad_context, log_totals, grad_proj, allowed, cos, sin, between=None):
    length = qkv.shape[0]
    scale = HD ** (-0.5)

    def unrotate(pair):
        return pair * cos + halves_swapped(pair * sin)

    key_parts, value_parts = [], []
    for group in range(KVH):
        kc = D + (group // 2) * 128
        keys = both_places(qkv[:, kc : kc + 128], group % 2)
        values = both_places(qkv[:, kc + KW : kc + KW + 128], group % 2)

        def pair_step(pair_index, carry):
            grad_keys, grad_values = list(carry[:2]), list(carry[2:])
            pair = group * (GROUP // 2) + pair_index
            lanes = pl.ds(pl.multiple_of(pair * 128, 128), 128)
            queries = qkv[:, lanes]
            grads = grad_context[:, lanes]
            total = jnp.zeros((length, 128), f32)
            for side in range(2):
                scores = dot_t(keys[side], queries) * scale
                scores = jnp.where(allowed, scores, -1e30)
                probs = jnp.exp(scores - log_totals[pl.ds(2 * pair + side, 1), :])
                grad_probs = dot_t(values[side], grads)
                grad_values[side] = grad_values[side] + dot_n(probs.astype(bf16), grads)
                inner = jnp.sum(probs * grad_probs, axis=0, keepdims=True)
                raw = (probs * (grad_probs - inner) * scale).astype(bf16)
                total = total + dot_tn(raw, keys[side])
                grad_keys[side] = grad_keys[side] + dot_n(raw, queries)
            grad_proj[:, lanes] = unrotate(total).astype(bf16)
            return (*grad_keys, *grad_values)

        empty = jnp.zeros((length, 128), f32)
        out = lax.fori_loop(0, GROUP // 2, pair_step, (empty,) * 4)

        def joined(low_side, high_side):
            low, _ = split_pair(low_side)
            _, high = split_pair(high_side)
            both = low + high
            return both + pltpu.roll(both, HD, 1)

        key_parts.append(joined(out[0], out[1]))
        value_parts.append(joined(out[2], out[3]))
        if between is not None:
            between(group)
    lane = lax.broadcasted_iota(jnp.int32, (length, 128), 1)
    for c in range(KVH // 2):
        keys = jnp.where(lane < HD, key_parts[2 * c], key_parts[2 * c + 1])
        values = jnp.where(lane < HD, value_parts[2 * c], value_parts[2 * c + 1])
        grad_proj[:, D + c * 128 : D + (c + 1) * 128] = unrotate(keys).astype(bf16)
        grad_proj[:, D + KW + c * 128 : D + KW + (c + 1) * 128] = values.astype(bf16)


def fold(value):
    return jnp.sum(value, axis=0, keepdims=True)


def branch_kernel(grads, grad_normed, middle, gains, context, weights, layer, onward, layer_out, grad_branch,
                  grad_context, grad_o, gain_rows, weight, stage, arrived_layer, load_sem, out_sem, send, recv):
    length, width = middle.shape[0], D + 2 * KW
    half = length // 2
    z, c, f = place()
    near = (device(z, c, flipped(f, 1)), device(z, c, flipped(f, 2)))
    greet(near, [])
    last = [
        pltpu.make_async_remote_copy(
            onward.at[way], arrived_layer.at[way], send.at[way], recv.at[way], device_id=near[1 - way], device_id_type=MESH
        )
        for way in range(2)
    ]
    for copy in last:
        copy.start()
    load_o = pltpu.make_async_copy(weights.at[:, pl.ds(width, D)], weight, load_sem.at[0])
    load_o.start()
    gain_rows[...] = jnp.zeros_like(gain_rows)

    def middle_grads(r):
        rows, arrived = middle[r], grad_normed[r]
        inverse = lax.rsqrt(jnp.mean(rows * rows, axis=-1, keepdims=True) + norm_eps)
        gain_rows[1:2, :] += fold(arrived * rows * inverse)
        weighted = arrived * gains[1:2, :]
        inner = jnp.mean(weighted * rows, axis=-1, keepdims=True)
        value = grads[r].astype(f32) + inverse * weighted - rows * (inverse * inverse * inverse * inner)
        grad_branch[r] = value.astype(bf16)

    by_rows(length, middle_grads)
    load_o.wait()

    def context_step(i, carry):
        tile = tile_at(i, 512)
        grad_context[:, tile] = dot_t(grad_branch[...], weight[tile, :]).astype(bf16)
        return carry

    lax.fori_loop(0, D // 512, context_step, 0)
    steps = D // 512

    def out(i, slot):
        return pltpu.make_async_copy(stage.at[slot], grad_o.at[tile_at(i, 512)], out_sem.at[slot])

    def step(i, carry):
        slot = i % 2

        @pl.when(i >= 2)
        def _():
            out(i - 2, slot).wait()

        stage[slot] = dot_tn(context[:, tile_at(i, 512)], grad_branch[...]).astype(bf16)
        out(i, slot).start()
        return carry

    lax.fori_loop(0, steps, step, 0)
    for way in range(2):
        last[way].wait()

        def add_last(r):
            there = pl.ds(pl.multiple_of(r.start + way * half, 16), r.size)
            layer_out[there] = (middle[there] + layer[there].astype(f32) + arrived_layer[way, r].astype(f32)).astype(bf16)

        by_rows(half, add_last)
    out(steps - 2, 0).wait()
    out(steps - 1, 1).wait()


def branch(grads, grad_normed, middle, gains, context, weights, layer, onward):
    length = middle.shape[0]
    dma = pltpu.SemaphoreType.DMA
    vmem, hbm = pl.BlockSpec(memory_space=pltpu.VMEM), pl.BlockSpec(memory_space=pl.ANY)
    rows = jax.ShapeDtypeStruct((length, D), bf16)
    return pl.pallas_call(
        branch_kernel,
        out_shape=(rows, rows, rows, jax.ShapeDtypeStruct((D, D), bf16), jax.ShapeDtypeStruct((8, D), f32)),
        in_specs=[vmem] * 5 + [hbm, vmem, vmem],
        out_specs=(vmem, vmem, vmem, hbm, vmem),
        scratch_shapes=[
            pltpu.VMEM((D, D), bf16), pltpu.VMEM((2, 512, D), bf16), pltpu.VMEM((2, length // 2, D), bf16),
            dma((1,)), dma((2,)), dma((2,)), dma((2,)),
        ],
        compiler_params=pltpu.CompilerParams(
            collective_id=4, has_side_effects=True, vmem_limit_bytes=feed_vmem_limit
        ),
        cost_estimate=cost(22),
        name="branch",
    )(grads, grad_normed, middle, gains, context, weights, layer, onward)


def backward_kernel(lines, x, normed_one, qkv, grad_context, log_totals, gains, cosine, sine, seg_col, seg_row, gain_two,
                    grad_o, branch_hbm, weights, input_grad, out_o, out_q, weight, grad_proj, grad_one, gain_rows,
                    gain_columns, staged, *refs):
    groups = [refs[i * 2 : i * 2 + 2] for i in range(6)] + [(out_o, out_q)]
    scatter_sems, (load_sem, weight_sem) = refs[12:20], refs[20:]
    scatter = Scatter(lines, groups, scatter_sems)
    z, c, f = place()
    length, width = x.shape[0], D + 2 * KW
    order = scatter.order
    rows = scatter.rows

    def load(d):
        return pltpu.make_async_copy(grad_o.at[d, c], scatter.sums[0].at[d], load_sem.at[d])

    def load_weight(i):
        tile = pl.ds(i * 512, 512)
        return pltpu.make_async_copy(weights.at[tile, pl.ds(0, width)], weight.at[i % 2], weight_sem.at[i % 2])

    for d in order:
        scatter.to_core(0, d, grad_o.at[d, 1 - c]).start()
        load(d).start()
    load_branch = pltpu.make_async_copy(branch_hbm, input_grad, load_sem.at[lines])
    load_branch.start()
    load_weight(0).start()
    load_weight(1).start()
    gain_rows[...] = gain_two[...]

    def between(group):
        if group == 0:
            for d in order:
                load(d).wait()
                scatter.over_core(0, d)
        elif group == 1:
            scatter.over_first(0, order[0])
            scatter.over_first(0, order[1])
        elif group == 2:
            for d in order[2:]:
                scatter.over_first(0, d)
        else:
            scatter.over_second(0, order[0])
            scatter.over_second(0, order[1])

    allowed = mask_keys_rows(seg_col[...], seg_row[...], length)
    attend_heads_grad(
        qkv, grad_context, log_totals, grad_proj, allowed, cosine[...], sine[...], between if lines > 1 else None
    )
    for i in range(D // 512):
        load_weight(i).wait()
        grad_one[:, i * 512 : (i + 1) * 512] = dot_t(grad_proj[...], weight[i % 2])
        if i + 2 < D // 512:
            load_weight(i + 2).start()
    for d in order[2:]:
        scatter.over_second(0, d)
    load_branch.wait()

    def input_grads(r):
        values, arrived = x[r].astype(f32), grad_one[r]
        inverse = lax.rsqrt(jnp.mean(values * values, axis=-1, keepdims=True) + norm_eps)
        gain_rows[0:1, :] += fold(arrived * values * inverse)
        weighted = arrived * gains[0:1, :]
        inner = jnp.mean(weighted * values, axis=-1, keepdims=True)
        value = inverse * weighted - values * (inverse * inverse * inverse * inner)
        input_grad[r] = (input_grad[r].astype(f32) + value).astype(bf16)

    by_rows(length, input_grads)
    for i in range(D // 128):
        lanes = pl.ds(i * 128, 128)
        square = jnp.concatenate([gain_rows[:, lanes], jnp.zeros((120, 128), f32)], axis=0)
        gain_columns[lanes, :] = square.T.astype(bf16)

    def blocks(d, core):
        start = pl.multiple_of((2 * d + core) * (4 * rows), 128)
        tile = pl.ds(start, 4 * rows)
        value = dot_tn(normed_one[:, tile], grad_proj[...]).astype(bf16)
        return value.reshape(4, rows, width), gain_columns[tile, :].reshape(4, rows, 128)

    def put(target, value):
        target[:, :, 0:width] = value[0]
        target[:, :, width:] = value[1]

    def staged_copy(j):
        return scatter.to_core(1, order[j], staged.at[j % 2])

    for j, d in enumerate(order):
        if j >= 2:
            staged_copy(j - 2).wait_send()
        put(staged.at[j % 2], blocks(d, 1 - c))
        staged_copy(j).start()
        put(scatter.sums[1].at[d], blocks(d, c))
        if j:
            scatter.over_core(1, order[j - 1])
        if j < len(order) - 1:
            scatter.over_line(0, d)
    scatter.over_core(1, order[-1])
    for j in range(len(order) + 2):
        if j < len(order):
            scatter.over_first(1, order[j])
        if 0 <= j - 1 < len(order):
            scatter.over_second(1, order[j - 1])
        if 0 <= j - 2 < len(order) - 1:
            scatter.over_line(1, order[j - 2])
    for d in order:
        scatter.to_core(0, d, grad_o.at[d, 1 - c]).wait_send()
    for j in range(max(0, len(order) - 2), len(order)):
        staged_copy(j).wait_send()
    scatter.finish()


def backward(x, normed_one, qkv, grad_context, log_totals, gains, cosine, sine, seg_col, seg_row, gain_two, grad_o,
             grad_branch, weights, n_dp, n_tp):
    length = x.shape[0]
    lines, rows = n_dp // 2, D // (n_dp * n_tp)
    width = D + 2 * KW
    dma = pltpu.SemaphoreType.DMA
    vmem, hbm = pl.BlockSpec(memory_space=pltpu.VMEM), pl.BlockSpec(memory_space=pl.ANY)
    buffers, sems = scatter_scratch(lines, n_tp, rows, (D, width + 128))
    return pl.pallas_call(
        functools.partial(backward_kernel, lines),
        out_shape=(
            jax.ShapeDtypeStruct((length, D), bf16),
            jax.ShapeDtypeStruct((rows, D), f32),
            jax.ShapeDtypeStruct((rows, width + 128), f32),
        ),
        in_specs=[vmem] * 11 + [hbm] * 3,
        out_specs=(vmem,) * 3,
        scratch_shapes=[
            pltpu.VMEM((2, 512, width), bf16), pltpu.VMEM((length, width), bf16), pltpu.VMEM((length, D), f32),
            pltpu.VMEM((8, D), f32), pltpu.VMEM((D, 128), bf16), pltpu.VMEM((2, n_tp, rows, width + 128), bf16),
        ]
        + buffers + sems + [dma((lines + 1,)), dma((2,))],
        compiler_params=pltpu.CompilerParams(
            collective_id=7, has_side_effects=True, vmem_limit_bytes=feed_vmem_limit
        ),
        cost_estimate=cost(105),
        name="backward",
    )(x, normed_one, qkv, grad_context, log_totals, gains, cosine, sine, seg_col, seg_row, gain_two,
      grad_o.reshape(lines, 2, n_tp, rows, D), grad_branch, weights)


def norm_kernel(n_dp, n_tp, parts, qkv, out, down, mlp, total, got, held, got_dp, got_tp, send, recv, total_send,
                total_recv, here_sem):
    z, c, f = place()
    dp = z * 2 + c
    columns = [(f + k) % n_tp for k in range(1, n_tp)]
    lines = [(dp + k) % n_dp for k in range(1, n_dp)]
    greet([device(z, c, to) for to in columns] + [{"dp": to, "fsdp": f} for to in lines], [])
    unit = mlp.shape[1] // (2 * n_dp * n_tp)
    half = n_dp * unit

    def away(k):
        to = columns[k - 1]
        return pltpu.make_async_remote_copy(
            parts.at[to], got.at[f], send.at[k], recv.at[k], device_id=device(z, c, to), device_id_type=MESH
        )

    for k in range(1, n_tp):
        away(k).start()
    here = pltpu.make_async_copy(parts.at[f], got.at[f], here_sem)
    here.start()
    held[...] = jnp.zeros_like(held)

    def add_squares(ref):
        def step(r):
            part = ref[r, :].astype(f32)
            part = part * part
            lanes = [part[:, i : i + 128] for i in range(0, part.shape[1], 128)]
            held[...] += functools.reduce(jnp.add, lanes)

        by_rows(ref.shape[0], step)

    add_squares(qkv)
    add_squares(out)
    add_squares(down)
    here.wait()
    for k in range(1, n_tp):
        away(k).wait()
    for frm in range(n_tp):
        add_squares(got.at[frm])

    def spread(buffer, own, value, partners, base):
        buffer[own] = value
        copies = [
            pltpu.make_async_remote_copy(
                buffer.at[own], buffer.at[own], total_send.at[base + k], total_recv.at[base + k],
                device_id=partner, device_id_type=MESH,
            )
            for k, partner in enumerate(partners)
        ]
        for copy in copies:
            copy.start()
        return copies

    def summed(buffer, copies):
        for copy in copies:
            copy.wait()
        return functools.reduce(jnp.add, [buffer[i] for i in range(buffer.shape[0])])

    own_total = jnp.sum(jnp.sum(held[...], axis=0, keepdims=True), axis=1, keepdims=True)
    copies = spread(
        got_dp, dp, jnp.broadcast_to(own_total, (8, 128)), [{"dp": to, "fsdp": f} for to in lines], 0
    )
    for side in range(2):
        pieces = [
            got[frm, :, side * half + j * unit : side * half + (j + 1) * unit].astype(f32)
            for j in range(n_dp)
            for frm in range(n_tp)
        ]
        mlp[:, side * n_tp * half : (side + 1) * n_tp * half] = jnp.concatenate(pieces, axis=1)
    line_total = summed(got_dp, copies)
    copies = spread(got_tp, f, line_total, [device(z, c, to) for to in columns], n_dp)
    total[...] = summed(got_tp, copies)


def norm_parts(parts, qkv, out, down, n_dp, n_tp):
    _, rows, width = parts.shape
    dma = pltpu.SemaphoreType.DMA
    vmem, hbm = pl.BlockSpec(memory_space=pltpu.VMEM), pl.BlockSpec(memory_space=pl.ANY)
    return pl.pallas_call(
        functools.partial(norm_kernel, n_dp, n_tp),
        out_shape=(jax.ShapeDtypeStruct((rows, width * n_tp), f32), jax.ShapeDtypeStruct((8, 128), f32)),
        in_specs=[hbm, vmem, vmem, vmem],
        scratch_shapes=[
            pltpu.VMEM(parts.shape, bf16), pltpu.VMEM((16, 128), f32), pltpu.VMEM((n_dp, 8, 128), f32),
            pltpu.VMEM((n_tp, 8, 128), f32), dma((n_tp,)), dma((n_tp,)), dma((n_dp + n_tp,)), dma((n_dp + n_tp,)),
            dma(()),
        ],
        compiler_params=pltpu.CompilerParams(
            collective_id=8, has_side_effects=True, vmem_limit_bytes=feed_vmem_limit
        ),
        cost_estimate=cost(35),
        name="norm_parts",
    )(parts, qkv, out, down)


def adam_kernel(total, gain_block, *refs):
    scale = clip_norm / jnp.maximum(jnp.sqrt(total[0:1, 0:1]), clip_norm)
    grads, refs = refs[:4], refs[4:]
    states, news = refs[:15], refs[15:]

    def update(i, gradient, rate, decay):
        new = adam_update(
            states[3 * i][...], gradient * scale, states[3 * i + 1][...], states[3 * i + 2][...], rate, decay
        )
        for k in range(3):
            news[3 * i + k][...] = new[k]

    for i in range(4):
        update(i, grads[i][...].astype(f32), matrix_rate, weight_decay)

    @pl.when(pl.program_id(0) == 0)
    def _():
        rows = gain_block.shape[0]
        square = jnp.concatenate([gain_block[...], jnp.zeros((128 - rows, 128), f32)], axis=0)
        update(4, square.T[0:2, 0:rows], gain_rate, 0.0)


def adam_all(total, grads, states):
    shapes = [state[0].shape for state in states[:4]]

    def block(shape, steps):
        rows, columns = shape
        if rows % (8 * steps) == 0:
            return pl.BlockSpec((rows // steps, columns), lambda i: (i, 0))
        if columns % (128 * steps) == 0:
            return pl.BlockSpec((rows, columns // steps), lambda i: (0, i))
        return None

    steps = 8 if all(block(shape, 8) for shape in shapes) else 4
    specs = [block(shape, steps) for shape in shapes]
    flat = [array for state in states for array in state]
    gains = pl.BlockSpec(states[4][0].shape, lambda i: (0, 0))
    state_specs = [spec for spec in specs + [gains] for _ in range(3)]
    last = grads[0].shape[1] // 128 - 1
    gain_block = pl.BlockSpec((grads[0].shape[0], 128), lambda i: (0, last))
    return pl.pallas_call(
        adam_kernel,
        grid=(steps,),
        out_shape=[jax.ShapeDtypeStruct(array.shape, f32) for array in flat],
        in_specs=[pl.BlockSpec((8, 128), lambda i: (0, 0)), gain_block] + specs + state_specs,
        out_specs=state_specs,
        compiler_params=pltpu.CompilerParams(vmem_limit_bytes=feed_vmem_limit),
        cost_estimate=cost(14),
        name="adam",
    )(total, grads[0], *grads, *flat)


def feed_front_kernel(n_hbm, g_hbm, wm_hbm, wd_hbm, gh_hbm, grad_down, layer_sum, onward, n, g, wm, wd, act, gh, stage,
                      parts, ones, *sems):
    sum_sems, (load_sem, weight_sem, out_sem) = sems[:2], sems[2:]
    z, c, f = place()
    x_dev, y_dev = device(z, c, flipped(f, 1)), device(z, c, flipped(f, 2))
    tokens = n.shape[0]
    length = tokens // 4
    ff = wd.shape[0]
    order = (3, 1, 2, 0)

    def rows_of(k):
        return pl.ds(k * length, length)

    load_n = [pltpu.make_async_copy(n_hbm.at[rows_of(k)], n.at[rows_of(k)], load_sem.at[0, k]) for k in range(4)]
    load_g = [pltpu.make_async_copy(g_hbm.at[rows_of(k)], g.at[rows_of(k)], load_sem.at[1, k]) for k in range(4)]
    tiles = [(start, min(256, ff - start)) for start in range(0, ff, 256)]
    load_w = []
    for t, (start, size) in enumerate(tiles):
        gate, up = pl.ds(start, size), pl.ds(ff + start, size)
        load_w.append(
            [
                pltpu.make_async_copy(wm_hbm.at[:, gate], wm.at[:, gate], weight_sem.at[0, t]),
                pltpu.make_async_copy(wm_hbm.at[:, up], wm.at[:, up], weight_sem.at[1, t]),
                pltpu.make_async_copy(wd_hbm.at[gate], wd.at[gate], weight_sem.at[2, t]),
            ]
        )
    load_n[order[0]].start()
    load_g[order[0]].start()
    for copies in load_w:
        for copy in copies:
            copy.start()
    for k in order[1:]:
        load_n[k].start()
        load_g[k].start()
    greet([x_dev, y_dev], [])
    summed = PlaneSum(parts, ones, None, (*sum_sems, None, None), x_dev, y_dev)

    def hidden(k, slot, lanes, up_lanes):
        rows = rows_of(k)
        gate = dot_n(n[rows, :], wm[:, lanes])
        up = dot_n(n[rows, :], wm[:, up_lanes])
        grad = dot_t(g[rows, :], wd[lanes, :])
        sigmoid = jax.nn.sigmoid(gate)
        silu = gate * sigmoid
        act[rows, lanes] = (silu * up).astype(bf16)
        gh[slot, :, lanes] = (grad * up * sigmoid * (1.0 + gate * (1.0 - sigmoid))).astype(bf16)
        gh[slot, :, up_lanes] = (grad * silu).astype(bf16)

    def hidden_out(i):
        return pltpu.make_async_copy(gh.at[i % 2], gh_hbm.at[rows_of(order[i])], out_sem.at[1, i % 2])

    for i, k in enumerate(order):
        load_n[k].wait()
        load_g[k].wait()
        if i >= 2:
            hidden_out(i - 2).wait()
        if i == 0:
            for copies, (start, size) in zip(load_w, tiles):
                for copy in copies:
                    copy.wait()
                hidden(k, 0, pl.ds(start, size), pl.ds(ff + start, size))
        else:

            def hidden_step(t, carry):
                hidden(k, i % 2, tile_at(t, 256), tile_at(t, 256, ff))
                return carry

            lax.fori_loop(0, ff // 256, hidden_step, 0)
            if ff % 256:
                start, size = tiles[-1]
                hidden(k, i % 2, pl.ds(start, size), pl.ds(ff + start, size))
        hidden_out(i).start()

        def layer_step(t, carry):
            value = dot_n(act[rows_of(k), :], wd[:, tile_at(t, 512)]).astype(bf16)
            if k:
                parts[k - 1, :, tile_at(t, 512)] = value
            else:
                layer_sum[:, tile_at(t, 512)] = value
            return carry

        lax.fori_loop(0, D // 512, layer_step, 0)
        if k == 3:
            for copy in summed.far:
                copy.start()
        elif k:
            summed.near[k - 1].start()
    wide = ff // 256

    def down_out(i, slot, width=256):
        rows = pl.ds(pl.multiple_of((i // 2) * 256, 128), width)
        lanes = tile_at(i % 2, D // 2)
        return pltpu.make_async_copy(stage.at[slot, pl.ds(0, width)], grad_down.at[rows, lanes], out_sem.at[0, slot])

    def down_tile(i, slot, width=256):
        lanes = tile_at(i % 2, D // 2)
        value = dot_tn(act[:, pl.ds(pl.multiple_of((i // 2) * 256, 128), width)], g[:, lanes])
        stage[slot, 0:width] = value.astype(bf16)
        down_out(i, slot, width).start()

    def down_step(i, carry):
        slot = i % 2

        @pl.when(i >= 2)
        def _():
            down_out(i - 2, slot).wait()

        down_tile(i, slot)
        return carry

    lax.fori_loop(0, 2 * wide, down_step, 0)
    for slot in range(2):
        down_out(2 * wide - 2 + slot, slot).wait()
        if ff % 256:
            down_tile(2 * wide + slot, slot, ff % 256)
    for slot in range(2):
        if ff % 256:
            down_out(2 * wide + slot, slot, ff % 256).wait()
        hidden_out(2 + slot).wait()

    for way in range(2):
        summed.far[way].wait()

        def add_far(r):
            mine = parts[1 - way, summed.there(r, way)].astype(f32)
            onward[way, r] = (mine + ones[way, 1, r].astype(f32)).astype(bf16)

        by_rows(summed.half, add_far)
    for way in range(2):
        summed.near[way].wait()

        def add_near(r):
            there = summed.there(r, way)
            layer_sum[there] = (layer_sum[there].astype(f32) + ones[way, 0, r].astype(f32)).astype(bf16)

        by_rows(summed.half, add_near)


def feed_back_kernel(gh_hbm, wm_hbm, n_hbm, grad_normed, grad_mlp, gh, wm, n, stage, parts, ones, twos, *sems):
    sum_sems, (load_sem, out_sem) = sems[:4], sems[4:]
    z, c, f = place()
    x_dev, y_dev = device(z, c, flipped(f, 1)), device(z, c, flipped(f, 2))
    tokens = n.shape[0]
    length = tokens // 4
    ff = gh.shape[1] // 2
    order = (3, 1, 2, 0)
    rows_of = [pl.ds(k * length, length) for k in range(4)]
    load_gh = [pltpu.make_async_copy(gh_hbm.at[rows_of[k]], gh.at[rows_of[k]], load_sem.at[0, k]) for k in range(4)]
    wide_tiles = [pl.ds(start, 1024) for start in range(0, D, 1024)]
    load_w = [
        pltpu.make_async_copy(wm_hbm.at[tile], wm.at[tile], load_sem.at[1, t]) for t, tile in enumerate(wide_tiles)
    ]
    load_n = pltpu.make_async_copy(n_hbm, n, load_sem.at[1, 3])
    for copy in [load_gh[order[0]]] + load_w + [load_gh[k] for k in order[1:]] + [load_n]:
        copy.start()
    greet([x_dev, y_dev], [])
    summed = PlaneSum(parts, ones, twos, sum_sems, x_dev, y_dev)
    for k in order:
        load_gh[k].wait()
        for t, tile in enumerate(wide_tiles):
            if k == order[0]:
                load_w[t].wait()
            value = dot_t(gh[rows_of[k], :], wm[tile, :])
            if k:
                parts[k - 1, :, tile] = value.astype(bf16)
            else:
                grad_normed[:, tile] = value
        if k == 3:
            for copy in summed.far:
                copy.start()
        elif k:
            summed.near[k - 1].start()
    summed.pass_on()
    load_n.wait()
    steps = 2 * D // 512

    def mlp_out(i, slot):
        rows = pl.ds(pl.multiple_of((i // 2) * 512, 512), 512)
        return pltpu.make_async_copy(stage.at[slot], grad_mlp.at[rows, tile_at(i % 2, ff)], out_sem.at[slot])

    def mlp_step(i, carry):
        slot = i % 2

        @pl.when(i >= 2)
        def _():
            mlp_out(i - 2, slot).wait()

        stage[slot] = dot_tn(n[:, tile_at(i // 2, 512)], gh[:, tile_at(i % 2, ff)]).astype(bf16)
        mlp_out(i, slot).start()
        return carry

    lax.fori_loop(0, steps, mlp_step, 0)

    def add_normed(r, value):
        grad_normed[r] += value

    summed.finish(add_normed)
    mlp_out(steps - 2, 0).wait()
    mlp_out(steps - 1, 1).wait()


def feed(normed_all, grads_all, mlp_cols, down_cols):
    tokens, ff = 4 * normed_all.shape[1], down_cols.shape[0]
    length = tokens // 4
    dma = pltpu.SemaphoreType.DMA
    vmem, hbm = pl.BlockSpec(memory_space=pltpu.VMEM), pl.BlockSpec(memory_space=pl.ANY)
    sum_buffers, sum_sems = plane_sum_scratch(length, D)
    normed_all = normed_all.reshape(tokens, D)

    def buffers(*shapes):
        return [pltpu.VMEM(shape, bf16) for shape in shapes]

    grad_hidden, grad_down, layer_sum, onward = pl.pallas_call(
        feed_front_kernel,
        out_shape=(
            jax.ShapeDtypeStruct((tokens, 2 * ff), bf16),
            jax.ShapeDtypeStruct((ff, D), bf16),
            jax.ShapeDtypeStruct((length, D), bf16),
            jax.ShapeDtypeStruct((2, length // 2, D), bf16),
        ),
        in_specs=[hbm] * 4,
        out_specs=(hbm, hbm, vmem, vmem),
        scratch_shapes=buffers(
            (tokens, D), (tokens, D), (D, 2 * ff), (ff, D), (tokens, ff), (2, length, 2 * ff), (2, 256, D // 2)
        )
        + sum_buffers[:2] + sum_sems[:2] + [dma((2, 4)), dma((3, -(-ff // 256))), dma((2, 2))],
        compiler_params=pltpu.CompilerParams(
            collective_id=6, has_side_effects=True, vmem_limit_bytes=feed_vmem_limit
        ),
        cost_estimate=cost(65),
        name="feed_front",
    )(normed_all, grads_all.reshape(tokens, D), mlp_cols, down_cols)
    grad_normed, grad_mlp = pl.pallas_call(
        feed_back_kernel,
        out_shape=(jax.ShapeDtypeStruct((length, D), f32), jax.ShapeDtypeStruct((D, 2 * ff), bf16)),
        in_specs=[hbm] * 3,
        out_specs=(vmem, hbm),
        scratch_shapes=buffers((tokens, 2 * ff), (D, 2 * ff), (tokens, D), (2, 512, ff))
        + sum_buffers + sum_sems + [dma((2, 4)), dma((2,))],
        compiler_params=pltpu.CompilerParams(
            collective_id=9, has_side_effects=True, vmem_limit_bytes=feed_vmem_limit
        ),
        cost_estimate=cost(60),
        name="feed_back",
    )(grad_hidden, mlp_cols, normed_all)
    return grad_normed, grad_down, grad_mlp, layer_sum, onward


def local(
    n_dp,
    n_tp,
    inputs,
    cotangent,
    segments,
    qkv_weight,
    out_weight,
    mlp_weight,
    down_weight,
    norm_gains,
    qkv_first,
    out_first,
    mlp_first,
    down_first,
    gains_first,
    qkv_second,
    out_second,
    mlp_second,
    down_second,
    gains_second,
):
    length = inputs.shape[0]
    lines = n_dp // 2
    rows = mlp_weight.shape[0]
    down_rows = down_weight.shape[0]
    ff = n_dp * down_rows
    cosine, sine = tables(segments[0])
    seg_row = segments
    seg_col = segments.reshape(length, 1)

    shard = jnp.concatenate(
        [qkv_weight, out_weight, jnp.pad(norm_gains.T, ((0, 0), (0, 126)))], axis=1
    ).astype(bf16)
    attn_full, mlp_parts, down_cols = gather_all(shard, mlp_weight, down_weight.astype(bf16), n_dp, n_tp)
    qkv_full = attn_full[:, : D + 2 * KW]
    out_full = attn_full[:, D + 2 * KW : 2 * D + 2 * KW]
    gains_full = attn_full[:, 2 * D + 2 * KW :].astype(f32).T
    mlp_cols = lax.all_gather(mlp_parts.reshape(n_tp * rows, 2 * ff), "dp", axis=0, tiled=True)
    tokens_f = inputs.astype(f32)
    gain_one, gain_two = gains_full[0], gains_full[1]
    inverse_one = lax.rsqrt(jnp.mean(tokens_f * tokens_f, axis=-1, keepdims=True) + norm_eps)
    if n_tp == 4:
        qkv, attended, log_totals, middle, normed_one, normed_all, grads_all = forward(
            inputs, cotangent, gains_full, cosine, sine, seg_col, seg_row, attn_full
        )
    else:
        normed_one = (tokens_f * inverse_one * gain_one).astype(bf16)
        projected = matmul(normed_one, qkv_full)
        qkv, attended, log_totals = attend(projected, cosine, sine, seg_col, seg_row)
        middle = tokens_f + matmul(attended, out_full)
    inverse_two = lax.rsqrt(jnp.mean(middle * middle, axis=-1, keepdims=True) + norm_eps)
    if n_tp == 4:
        grad_normed_two, grad_down, grad_mlp, layer_sum, onward = feed(normed_all, grads_all, mlp_cols, down_cols)
    else:
        normed_two = (middle * inverse_two * gain_two).astype(bf16)
        normed_all = plane_gather(normed_two, n_tp)
        grads_all = plane_gather(cotangent, n_tp)
        hidden = matmul(normed_all, mlp_cols)
        gate, up_part = hidden[:, :ff], hidden[:, ff:]
        sigmoid_gate = jax.nn.sigmoid(gate)
        silu_gate = gate * sigmoid_gate
        activated = (silu_gate * up_part).astype(bf16)
        grad_act = matmul_t(grads_all, down_cols)
        grad_gate = grad_act * up_part * sigmoid_gate * (1.0 + gate * (1.0 - sigmoid_gate))
        grad_up = grad_act * silu_gate
        grad_hidden = jnp.concatenate([grad_gate, grad_up], axis=1).astype(bf16)
        grad_normed = matmul_t(grad_hidden, mlp_cols).reshape(n_tp, length, D)
        grad_normed_two = grad_normed[0]
        for k in range(1, n_tp):
            swapped = plane_swap(grad_normed[k].astype(bf16), k, n_tp)
            grad_normed_two = grad_normed_two + swapped.astype(f32)
        grad_down = matmul_tn(activated, grads_all).astype(bf16)
        grad_mlp = matmul_tn(normed_all, grad_hidden).astype(bf16)
        layer_parts = matmul(activated, down_cols).astype(bf16).reshape(n_tp, length, D)
    down_sum = lax.psum_scatter(grad_down, "dp", scatter_dimension=0, tiled=True)
    mlp_sum = lax.psum_scatter(grad_mlp, "dp", scatter_dimension=0, tiled=True).reshape(n_tp, rows, 2 * ff)

    if n_tp == 4:
        layer_out, grad_branch, grad_context, grad_out, gain_two_rows = branch(
            cotangent, grad_normed_two, middle, gains_full, attended, attn_full, layer_sum, onward
        )
        input_grad, out_sum, qkv_sum = backward(
            inputs, normed_one, qkv, grad_context, log_totals, gains_full, cosine, sine, seg_col, seg_row,
            gain_two_rows, grad_out, grad_branch, attn_full, n_dp, n_tp,
        )
        mlp_sum, total = norm_parts(mlp_sum, qkv_sum, out_sum, down_sum, n_dp, n_tp)
    else:
        layer_out = middle + layer_parts[0].astype(f32)
        for k in range(1, n_tp):
            layer_out = layer_out + plane_swap(layer_parts[k], k, n_tp).astype(f32)
        layer_out = layer_out.astype(bf16)
        gain_grad_two = jnp.sum(grad_normed_two * middle * inverse_two, axis=0)
        weighted_two = grad_normed_two * gain_two
        grad_middle = (
            cotangent.astype(f32)
            + inverse_two * weighted_two
            - middle * inverse_two**3 * jnp.mean(weighted_two * middle, axis=-1, keepdims=True)
        )
        grad_branch = grad_middle.astype(bf16)
        grad_context = matmul_t(grad_branch, out_full).astype(bf16)
        grad_projected = attend_grad(qkv, grad_context, log_totals, cosine, sine, seg_col, seg_row)
        grad_out = matmul_tn(attended, grad_branch).astype(bf16)
        grad_qkv = matmul_tn(normed_one, grad_projected)
        grad_normed_one = matmul_t(grad_projected, qkv_full)
        gain_grad_one = jnp.sum(grad_normed_one * tokens_f * inverse_one, axis=0)
        weighted_one = grad_normed_one * gain_one
        grad_inputs = (
            grad_middle
            + inverse_one * weighted_one
            - tokens_f * inverse_one**3 * jnp.mean(weighted_one * tokens_f, axis=-1, keepdims=True)
        )
        input_grad = grad_inputs.astype(bf16)
        gain_grads = jnp.pad(jnp.stack([gain_grad_one, gain_grad_two], axis=1), ((0, 0), (0, 126)))
        grad_qkv = jnp.concatenate([grad_qkv.astype(bf16), gain_grads.astype(bf16)], axis=1)
        out_sum, qkv_sum = scatter_all([grad_out, grad_qkv], n_dp, n_tp)
        mlp_sum = columns_back(mlp_sum, n_dp, n_tp)
        squares = jnp.sum(qkv_sum * qkv_sum) + jnp.sum(out_sum * out_sum) + jnp.sum(mlp_sum * mlp_sum)
        squares = squares + jnp.sum(jnp.square(down_sum.astype(f32)))
        total = total_over_devices(squares, n_dp, n_tp)
    grad_norm = jnp.sqrt(total[0, 0])
    states = (
        (qkv_weight, qkv_first, qkv_second),
        (out_weight, out_first, out_second),
        (mlp_weight, mlp_first, mlp_second),
        (down_weight, down_first, down_second),
        (norm_gains, gains_first, gains_second),
    )
    stepped = adam_all(total, (qkv_sum, out_sum, mlp_sum, down_sum), states)
    news = [stepped[i::3] for i in range(3)]
    return (layer_out, input_grad, grad_norm, *news[0], *news[1], *news[2])


def solution(mesh):
    split_rows = P(("dp", "fsdp"), None)
    split_columns = P(None, ("dp", "fsdp"))
    weights = (split_rows,) * 4 + (split_columns,)
    return jax.shard_map(
        functools.partial(local, mesh.shape["dp"], mesh.shape["fsdp"]),
        mesh=mesh,
        in_specs=(split_rows,) * 3 + weights * 3,
        out_specs=(split_rows, split_rows, P()) + weights * 3,
        check_vma=False,
    )
```

```python
import functools

import jax
import jax.numpy as jnp
from jax import lax
from jax.experimental import pallas as pl
from jax.experimental.pallas import tpu as pltpu
from jax.sharding import PartitionSpec as P

D = 2048
HEADS = 32
KVH = 4
HD = 64
FF = 5632
STEP = 10
KW = KVH * HD
GROUP = HEADS // KVH


norm_eps = 1e-05
rope_base = 10000.0
beta_one = 0.9
beta_two = 0.95
adam_eps = 1e-08
weight_decay = 0.1
matrix_rate = 0.04
gain_rate = 0.8
clip_norm = 1.0

f32 = jnp.float32
bf16 = jnp.bfloat16


def tables(segment_row):
    length = segment_row.shape[0]
    token_index = jnp.arange(length, dtype=jnp.int32)
    previous = jnp.concatenate([segment_row[:1] - 1, segment_row[:-1]])
    starts = lax.cummax(jnp.where(segment_row != previous, token_index, 0), axis=0)
    position = (token_index - starts).astype(f32)
    frequency = rope_base ** (-(jnp.arange(HD // 2, dtype=f32) * 2.0 / HD))
    angles = position[:, None] * frequency[None, :]
    cosine, sine = jnp.cos(angles), jnp.sin(angles)
    cosine = jnp.concatenate([cosine] * 4, axis=-1)
    signed = jnp.concatenate([-sine, sine] * 2, axis=-1)
    return cosine, signed


def halves_swapped(pair):
    lane = lax.broadcasted_iota(jnp.int32, pair.shape, 1)
    return jnp.where(lane % HD < HD // 2, pltpu.roll(pair, 96, 1), pltpu.roll(pair, 32, 1))


def split_pair(pair):
    lane = lax.broadcasted_iota(jnp.int32, pair.shape, 1)
    zero = jnp.zeros_like(pair)
    return jnp.where(lane < HD, pair, zero), jnp.where(lane < HD, zero, pair)


def both_places(pair, odd):
    low, high = split_pair(pair)
    moved = pltpu.roll(pair.astype(f32), HD, 1).astype(pair.dtype)
    moved_low, moved_high = split_pair(moved)
    return (moved_low, high) if odd else (low, moved_high)


def dot_t(a, b):
    return lax.dot_general(a, b, (((1,), (1,)), ((), ())), preferred_element_type=f32)


def dot_n(a, b):
    return lax.dot_general(a, b, (((1,), (0,)), ((), ())), preferred_element_type=f32)


def dot_tn(a, b):
    return lax.dot_general(a, b, (((0,), (0,)), ((), ())), preferred_element_type=f32)


def mask_keys_rows(seg_col, seg_row, length):
    key_index = lax.broadcasted_iota(jnp.int32, (length, length), 0)
    query_index = lax.broadcasted_iota(jnp.int32, (length, length), 1)
    return (seg_col == seg_row) & (query_index >= key_index)


def attend_kernel(proj, cosine, sine, seg_col, seg_row, qkv, context, log_totals):
    cos, sin = cosine[...], sine[...]
    for c in range(0, D + KW, 128):
        qkv[:, c : c + 128] = rope_tile(proj[:, c : c + 128], cos, sin).astype(bf16)
    for c in range(D + KW, D + 2 * KW, 128):
        qkv[:, c : c + 128] = proj[:, c : c + 128].astype(bf16)
    allowed = mask_keys_rows(seg_col[...], seg_row[...], proj.shape[0])
    attend_heads(qkv, context, log_totals, allowed)


def attend_grad_kernel(qkv, grad_context, log_totals, cosine, sine, seg_col, seg_row, grad_proj):
    allowed = mask_keys_rows(seg_col[...], seg_row[...], qkv.shape[0])
    attend_heads_grad(qkv, grad_context, log_totals, grad_proj, allowed, cosine[...], sine[...])


vmem_limit = 50 * 1024 * 1024
feed_vmem_limit = 62 * 1024 * 1024


def attend(projected, cosine, sine, seg_col, seg_row):
    length = projected.shape[0]
    return pl.pallas_call(
        attend_kernel,
        out_shape=(
            jax.ShapeDtypeStruct((length, D + 2 * KW), bf16),
            jax.ShapeDtypeStruct((length, D), bf16),
            jax.ShapeDtypeStruct((HEADS, length), f32),
        ),
        compiler_params=pltpu.CompilerParams(vmem_limit_bytes=vmem_limit),
        cost_estimate=cost(18),
        name="attend",
    )(projected, cosine, sine, seg_col, seg_row)


def attend_grad(qkv, grad_context, log_totals, cosine, sine, seg_col, seg_row):
    length = qkv.shape[0]
    return pl.pallas_call(
        attend_grad_kernel,
        out_shape=jax.ShapeDtypeStruct((length, D + 2 * KW), bf16),
        compiler_params=pltpu.CompilerParams(vmem_limit_bytes=vmem_limit),
        cost_estimate=cost(26),
        name="attend_grad",
    )(qkv, grad_context, log_totals, cosine, sine, seg_col, seg_row)


MESH = pl.DeviceIdType.MESH


def cost(microseconds):
    return pl.CostEstimate(flops=0, bytes_accessed=int(microseconds * 3.69e6), transcendentals=0)


def place():
    dp = lax.axis_index("dp")
    return dp // 2, dp % 2, lax.axis_index("fsdp")


def device(line, core, plane):
    return {"dp": line * 2 + core, "fsdp": plane}


def flipped(index, bit):
    return index + bit - 2 * bit * ((index // bit) % 2)


def greet(partners, ends):
    barrier = pltpu.get_barrier_semaphore()
    count = len(partners)
    for partner in partners:
        pl.semaphore_signal(barrier, inc=1, device_id=partner, device_id_type=MESH)
    for there, partner in ends:
        count = count + there

        @pl.when(there == 1)
        def _():
            pl.semaphore_signal(barrier, inc=1, device_id=partner, device_id_type=MESH)

    pl.semaphore_wait(barrier, count)


def gather_kernel(lines, own, weight, down, full, parts, down_full, cut, line_send, line_recv, x_send, x_recv, y_send, y_recv,
                  dx_send, dx_recv, dy_send, dy_recv, core_send, core_recv, cut_send, cut_recv, down_send, down_recv, down_core_send,
                  down_core_recv, here_sem):
    z, c, f = place()
    half = own.shape[0] // 2
    fx, fy = flipped(f, 1), flipped(f, 2)
    fd = flipped(fx, 2)
    x_dev, y_dev, core_dev = device(z, c, fx), device(z, c, fy), device(z, 1 - c, f)
    has_left = jnp.minimum(z, 1)
    has_right = jnp.minimum(lines - 1 - z, 1)
    left_dev = device(jnp.maximum(z - 1, 0), c, f)
    right_dev = device(jnp.minimum(z + 1, lines - 1), c, f)
    far_dev = device(z, c, fd)
    greet([x_dev, y_dev, far_dev, core_dev], [(has_left, left_dev), (has_right, right_dev)])

    def cut_copy(k):
        to = flipped(f, k) if k < 3 else fd
        return pltpu.make_async_remote_copy(
            cut.at[to], parts.at[f], cut_send.at[k], cut_recv.at[k], device_id=device(z, c, to), device_id_type=MESH
        )

    def copy(line, plane, send, recv, dev, src=None, rows=None):
        dst = full.at[line, c, plane]
        src = dst if src is None else src
        if rows is not None:
            dst, src = dst.at[rows], src.at[rows]
        return pltpu.make_async_remote_copy(
            src, dst, send, recv, device_id=dev, device_id_type=MESH
        )

    def to_right(line, src=None):
        return copy(line, f, line_send.at[0, line], line_recv.at[line], right_dev, src)

    def to_left(line, src=None):
        return copy(line, f, line_send.at[1, line], line_recv.at[line], left_dev, src)

    def to_x(line, src=None):
        return copy(line, f, x_send.at[line], x_recv.at[line], x_dev, src)

    def to_y(line, src=None):
        return copy(line, f, y_send.at[line], y_recv.at[line], y_dev, src)

    def diag_y(line):
        return copy(line, fx, dy_send.at[line], dy_recv.at[line], y_dev, None, pl.ds(0, half))

    def diag_x(line):
        return copy(line, fy, dx_send.at[line], dx_recv.at[line], x_dev, None, pl.ds(half, half))

    def to_core(line, plane, src=None):
        return copy(line, plane, core_send.at[line, plane], core_recv.at[line, plane], core_dev, src)

    def down_copy(line, way, src=None):
        dst = down_full.at[line, c]
        return pltpu.make_async_remote_copy(
            dst if src is None else src, dst, down_send.at[way, line], down_recv.at[line],
            device_id=(right_dev, left_dev)[way], device_id_type=MESH,
        )

    def down_core(line, src=None):
        dst = down_full.at[line, c]
        return pltpu.make_async_remote_copy(
            dst if src is None else src, dst, down_core_send.at[line], down_core_recv.at[line],
            device_id=core_dev, device_id_type=MESH,
        )

    here = pltpu.make_async_copy(own, full.at[z, c, f], here_sem.at[0])
    here.start()
    here_down = pltpu.make_async_copy(down, down_full.at[z, c], here_sem.at[2])
    here_down.start()

    @pl.when(has_right == 1)
    def _():
        to_right(z, own).start()

    @pl.when(has_left == 1)
    def _():
        to_left(z, own).start()

    to_x(z, own).start()
    to_y(z, own).start()
    to_core(z, f, own).start()

    cut_columns(weight, cut, 2 * lines, 4)
    here_cut = pltpu.make_async_copy(cut.at[f], parts.at[f], here_sem.at[1])
    here_cut.start()
    for k in range(1, 4):
        cut_copy(k).start()

    down_core(z, down).start()
    for t in range(1, lines):

        @pl.when(z >= t)
        def _():
            line = z - t
            to_right(line).wait_recv()

            @pl.when(has_right == 1)
            def _():
                to_right(line).start()

            to_x(line).start()
            to_y(line).start()
            to_core(line, f).start()

        @pl.when(z + t <= lines - 1)
        def _():
            line = z + t
            to_left(line).wait_recv()

            @pl.when(has_left == 1)
            def _():
                to_left(line).start()

            to_x(line).start()
            to_y(line).start()
            to_core(line, f).start()

    @pl.when(has_right == 1)
    def _():
        down_copy(z, 0, down).start()

    @pl.when(has_left == 1)
    def _():
        down_copy(z, 1, down).start()

    here.wait()
    order = []
    for t in range(lines):
        line = z
        for b in range(lines.bit_length() - 1):
            if t >> b & 1:
                line = flipped(line, 1 << b)
        order.append(line)
    for t, line in enumerate(order):
        to_x(line).wait_recv()
        diag_y(line).start()
        to_core(line, fx).start()
        to_y(line).wait_recv()
        diag_x(line).start()
        to_core(line, fy).start()
        if t == 0:
            continue

        @pl.when(z >= t)
        def _():
            down_copy(z - t, 0).wait_recv()

            @pl.when(has_right == 1)
            def _():
                down_copy(z - t, 0).start()

            down_core(z - t).start()

        @pl.when(z + t <= lines - 1)
        def _():
            down_copy(z + t, 1).wait_recv()

            @pl.when(has_left == 1)
            def _():
                down_copy(z + t, 1).start()

            down_core(z + t).start()

    for line in order:
        diag_y(line).wait_recv()
        diag_x(line).wait_recv()
        to_core(line, fd).start()
    here_cut.wait()
    here_down.wait()
    for k in range(1, 4):
        cut_copy(k).wait()
    for line in range(lines):
        for plane in range(4):
            to_core(line, plane).wait()
        to_x(line).wait_send()
        to_y(line).wait_send()
        diag_x(line).wait_send()
        diag_y(line).wait_send()

        down_core(line).wait()

        @pl.when((line <= z) & (has_right == 1))
        def _():
            to_right(line).wait_send()
            down_copy(line, 0).wait_send()

        @pl.when((line >= z) & (has_left == 1))
        def _():
            to_left(line).wait_send()
            down_copy(line, 1).wait_send()


def gather_all(shard, weight, down, n_dp, n_tp):
    rows, columns = shard.shape
    width = weight.shape[1] // n_tp
    lines = n_dp // 2
    if n_tp != 4 or rows % 32:
        full = lax.all_gather(shard, ("dp", "fsdp"), axis=0, tiled=True)
        down_full = lax.all_gather(down, "dp", axis=0, tiled=True)
        return full, columns_out(weight, n_dp, n_tp), down_full
    dma = pltpu.SemaphoreType.DMA
    hbm = pl.BlockSpec(memory_space=pl.ANY)
    full, parts, down_full = pl.pallas_call(
        functools.partial(gather_kernel, lines),
        out_shape=(
            jax.ShapeDtypeStruct((lines, 2, n_tp, rows, columns), bf16),
            jax.ShapeDtypeStruct((n_tp, rows, width), bf16),
            jax.ShapeDtypeStruct((lines, 2, *down.shape), bf16),
        ),
        in_specs=[hbm, pl.BlockSpec(memory_space=pltpu.VMEM), hbm],
        out_specs=(hbm, hbm, hbm),
        scratch_shapes=[pltpu.VMEM((n_tp, rows, width), bf16), dma((2, lines))]
        + [dma((lines,))] * 9
        + [dma((lines, n_tp))] * 2
        + [dma((n_tp,)), dma((n_tp,)), dma((2, lines)), dma((lines,)), dma((lines,)), dma((lines,)), dma((3,))],
        compiler_params=pltpu.CompilerParams(
            collective_id=0, has_side_effects=True, vmem_limit_bytes=vmem_limit
        ),
        cost_estimate=cost(100),
        name="gather_all",
    )(shard, weight, down)
    full = full.reshape(n_dp * n_tp * rows, columns)
    return full, parts, down_full.reshape(n_dp * down.shape[0], down.shape[1])


def cut_columns(weight, cut, n_dp, n_tp):
    unit = weight.shape[1] // (2 * n_dp * n_tp)
    half = n_dp * unit
    for to in range(n_tp):
        for side in range(2):
            starts = [side * n_tp * half + (j * n_tp + to) * unit for j in range(n_dp)]
            pieces = [weight[:, start : start + unit] for start in starts]
            cut[to, :, side * half : (side + 1) * half] = jnp.concatenate(pieces, axis=1).astype(bf16)


def columns_out_kernel(n_dp, n_tp, weight, parts, cut, send, recv, here_sem):
    z, c, f = place()
    greet([device(z, c, (f + k) % n_tp) for k in range(1, n_tp)], [])

    def away(k):
        to = (f + k) % n_tp
        return pltpu.make_async_remote_copy(
            cut.at[to], parts.at[f], send.at[k], recv.at[k], device_id=device(z, c, to), device_id_type=MESH
        )

    cut_columns(weight, cut, n_dp, n_tp)
    for k in range(1, n_tp):
        away(k).start()
    here = pltpu.make_async_copy(cut.at[f], parts.at[f], here_sem)
    here.start()
    here.wait()
    for k in range(1, n_tp):
        away(k).wait()


def columns_out(weight, n_dp, n_tp):
    rows, width = weight.shape
    dma = pltpu.SemaphoreType.DMA
    return pl.pallas_call(
        functools.partial(columns_out_kernel, n_dp, n_tp),
        out_shape=jax.ShapeDtypeStruct((n_tp, rows, width // n_tp), bf16),
        out_specs=pl.BlockSpec(memory_space=pl.ANY),
        scratch_shapes=[
            pltpu.VMEM((n_tp, rows, width // n_tp), bf16), dma((n_tp,)), dma((n_tp,)), dma(()),
        ],
        compiler_params=pltpu.CompilerParams(
            collective_id=1, has_side_effects=True, vmem_limit_bytes=vmem_limit
        ),
        cost_estimate=cost(20),
        name="columns_out",
    )(weight)


def columns_back_kernel(n_dp, n_tp, parts, whole, got, send, recv, here_sem):
    z, c, f = place()
    greet([device(z, c, (f + k) % n_tp) for k in range(1, n_tp)], [])
    unit = whole.shape[1] // (2 * n_dp * n_tp)
    half = n_dp * unit

    def away(k):
        to = (f + k) % n_tp
        return pltpu.make_async_remote_copy(
            parts.at[to], got.at[f], send.at[k], recv.at[k], device_id=device(z, c, to), device_id_type=MESH
        )

    for k in range(1, n_tp):
        away(k).start()
    here = pltpu.make_async_copy(parts.at[f], got.at[f], here_sem)
    here.start()
    here.wait()
    for k in range(1, n_tp):
        away(k).wait()
    for side in range(2):
        pieces = [
            got[frm, :, side * half + j * unit : side * half + (j + 1) * unit].astype(f32)
            for j in range(n_dp)
            for frm in range(n_tp)
        ]
        whole[:, side * n_tp * half : (side + 1) * n_tp * half] = jnp.concatenate(pieces, axis=1)


def columns_back(parts, n_dp, n_tp):
    _, rows, width = parts.shape
    dma = pltpu.SemaphoreType.DMA
    return pl.pallas_call(
        functools.partial(columns_back_kernel, n_dp, n_tp),
        out_shape=jax.ShapeDtypeStruct((rows, width * n_tp), f32),
        in_specs=[pl.BlockSpec(memory_space=pl.ANY)],
        scratch_shapes=[pltpu.VMEM(parts.shape, bf16), dma((n_tp,)), dma((n_tp,)), dma(())],
        compiler_params=pltpu.CompilerParams(
            collective_id=2, has_side_effects=True, vmem_limit_bytes=vmem_limit
        ),
        cost_estimate=cost(20),
        name="columns_back",
    )(parts)


def total_kernel(n_dp, n_tp, value, total, held, got, send, recv):
    dp, f = lax.axis_index("dp"), lax.axis_index("fsdp")
    partners = []
    for axis, size in (("dp", n_dp), ("fsdp", n_tp)):
        for bit in range(size.bit_length() - 1):
            index = {"dp": dp, "fsdp": f}
            index[axis] = flipped(index[axis], 1 << bit)
            partners.append(index)
    greet(partners, [])
    held[0] = value[...]
    for step, partner in enumerate(partners):
        swap = pltpu.make_async_remote_copy(
            held.at[step], got.at[step], send.at[step], recv.at[step], device_id=partner, device_id_type=MESH
        )
        swap.start()
        swap.wait()
        held[step + 1] = held[step] + got[step]
    total[...] = held[len(partners)]


def total_over_devices(value, n_dp, n_tp):
    steps = (n_dp * n_tp).bit_length() - 1
    dma = pltpu.SemaphoreType.DMA
    tile = (8, 128)
    spread = pl.pallas_call(
        functools.partial(total_kernel, n_dp, n_tp),
        out_shape=jax.ShapeDtypeStruct(tile, f32),
        scratch_shapes=[
            pltpu.VMEM((steps + 1, *tile), f32), pltpu.VMEM((steps, *tile), f32), dma((steps,)), dma((steps,)),
        ],
        compiler_params=pltpu.CompilerParams(collective_id=3, has_side_effects=True),
        cost_estimate=cost(13),
        name="total",
    )(jnp.broadcast_to(value, tile))
    return spread


def adam_update(weight, gradient, first, second, rate, decay):
    first = beta_one * first + (1.0 - beta_one) * gradient
    second = beta_two * second + (1.0 - beta_two) * gradient * gradient
    first_hat = first / (1.0 - beta_one**STEP)
    second_hat = second / (1.0 - beta_two**STEP)
    weight = weight - rate * (first_hat / (jnp.sqrt(second_hat) + adam_eps) + decay * weight)
    return (weight, first, second)


def matmul(a, b):
    return jnp.dot(a, b, preferred_element_type=f32)


def matmul_t(a, b):
    return lax.dot_general(a, b, (((1,), (1,)), ((), ())), preferred_element_type=f32)


def matmul_tn(a, b):
    return lax.dot_general(a, b, (((0,), (0,)), ((), ())), preferred_element_type=f32)


def swap_core(block, n_dp):
    return lax.ppermute(block, "dp", [(i, i ^ 1) for i in range(n_dp)])


def plane_swap(block, k, n_tp):
    return lax.ppermute(block, "fsdp", [(i, i ^ k) for i in range(n_tp)])


def plane_gather(block, n_tp):
    if n_tp != 4:
        return jnp.concatenate([block] + [plane_swap(block, k, n_tp) for k in range(1, n_tp)], axis=0)
    half = block.shape[0] // 2
    over_x, over_y = plane_swap(block, 1, n_tp), plane_swap(block, 2, n_tp)
    far = [plane_swap(over_y[:half], 1, n_tp), plane_swap(over_x[half:], 2, n_tp)]
    return jnp.concatenate([block, over_x, over_y] + far, axis=0)


def core_sum(parts, n_dp):
    core = lax.axis_index("dp") % 2
    mine = lax.dynamic_index_in_dim(parts, core, 1, keepdims=False)
    other = lax.dynamic_index_in_dim(parts, 1 - core, 1, keepdims=False)
    return mine.astype(f32) + swap_core(other, n_dp).astype(f32)


def line_sum(parts, n_dp):
    lines = n_dp // 2
    place = lax.axis_index("dp") // 2
    result = lax.dynamic_index_in_dim(parts, place, 0, keepdims=False)
    for way in (1, -1):
        arrived = None
        for step in range(1, lines):
            target = jnp.clip(place + way * (lines - step), 0, lines - 1)
            load = lax.dynamic_index_in_dim(parts, target, 0, keepdims=False).astype(f32)
            if arrived is not None:
                load = load + arrived.astype(f32)
            senders = range(step) if way == 1 else range(lines - step, lines)
            pairs = [(2 * s + c, 2 * (s + way) + c) for s in senders for c in range(2)]
            arrived = lax.ppermute(load.astype(bf16), "dp", pairs)
        result = result.astype(f32) + arrived.astype(f32)
    return result


def plane_sum(parts, n_tp):
    here = lax.axis_index("fsdp")
    total = lax.dynamic_index_in_dim(parts, here, 0, keepdims=False).astype(f32)
    for k in range(1, n_tp):
        load = lax.dynamic_index_in_dim(parts, here ^ k, 0, keepdims=False).astype(bf16)
        total = total + plane_swap(load, k, n_tp).astype(f32)
    return total


def by_rows(rows, body):
    def step(i, carry):
        body(pl.ds(pl.multiple_of(i * 16, 16), 16))
        return carry

    lax.fori_loop(0, rows // 16, step, 0)


def places_by_distance(z, lines):
    tables = [
        sorted(range(lines), key=lambda d: (-abs(d - here), min(d, lines - 1 - d), d)) for here in range(lines)
    ]
    power = 1
    for bit in range(lines.bit_length() - 1):
        power = power * (1 + (lines ** (1 << bit) - 1) * (z // (1 << bit) % 2))
    return [sum(table[t] * lines**here for here, table in enumerate(tables)) // power % lines for t in range(lines)]


class Scatter:
    def __init__(self, lines, groups, sems):
        self.sums, self.others, self.firsts, self.seconds, self.alongs, self.leaving, self.outs = groups
        core_send, core_recv, one_send, one_recv, two_send, two_recv, line_send, line_recv = sems
        z, c, f = place()
        self.z, self.f, self.lines = z, f, lines
        self.planes, self.rows = self.sums[0].shape[1:3]
        self.half = self.rows // 2
        fx, fy = flipped(f, 1), flipped(f, 2)
        fd = flipped(fx, 2)
        x_dev, y_dev, core_dev = device(z, c, fx), device(z, c, fy), device(z, 1 - c, f)
        self.has_left = jnp.minimum(z, 1)
        self.has_right = jnp.minimum(lines - 1 - z, 1)
        left_dev = device(jnp.maximum(z - 1, 0), c, f)
        right_dev = device(jnp.minimum(z + 1, lines - 1), c, f)
        greet([x_dev, y_dev, core_dev], [(self.has_left, left_dev), (self.has_right, right_dev)])
        halves = (pl.ds(0, self.half), pl.ds(self.half, self.half))
        near, self.next_near, step_dev = (fx, fy), (fy, fx), (x_dev, y_dev)
        self.order = places_by_distance(z, lines)

        def remote(src, dst, send, recv, dev):
            return pltpu.make_async_remote_copy(src, dst, send, recv, device_id=dev, device_id_type=MESH)

        def to_core(a, d, src):
            return remote(src, self.others[a].at[d], core_send.at[a, d], core_recv.at[a, d], core_dev)

        def one(a, d, way, i):
            block = (near[way], fd)[i]
            return remote(
                self.sums[a].at[d, block, halves[way]], self.firsts[a].at[way, d, i],
                one_send.at[a, d, way, i], one_recv.at[a, d, way, i], step_dev[way],
            )

        def two(a, d, way):
            return remote(
                self.sums[a].at[d, self.next_near[way], halves[way]], self.seconds[a].at[way, d],
                two_send.at[a, d, way], two_recv.at[a, d, way], step_dev[1 - way],
            )

        def to_right(a, d):
            return remote(
                self.leaving[a].at[d], self.alongs[a].at[d], line_send.at[a, d], line_recv.at[a, d], right_dev
            )

        def to_left(a, d, slot):
            return remote(
                self.leaving[a].at[d], self.alongs[a].at[slot], line_send.at[a, d], line_recv.at[a, slot], left_dev
            )

        self.to_core, self.one, self.two, self.to_right, self.to_left = to_core, one, two, to_right, to_left

    def add_along(self, a, slot):
        def step(r):
            self.outs[a][r] += self.alongs[a][slot, r].astype(f32)

        by_rows(self.rows, step)

    def over_core(self, a, d):
        sums, others = self.sums[a], self.others[a]
        self.to_core(a, d, others.at[d]).wait_recv()

        def core_add(r):
            for plane in range(self.planes):
                sums[d, plane, r] = (sums[d, plane, r].astype(f32) + others[d, plane, r].astype(f32)).astype(bf16)

        by_rows(self.rows, core_add)
        for i in (1, 0):
            for way in range(2):
                self.one(a, d, way, i).start()

    def there(self, r, way):
        return pl.ds(pl.multiple_of(r.start + way * self.half, 16), r.size)

    def over_first(self, a, d):
        sums, firsts = self.sums[a], self.firsts[a]
        for way in range(2):
            self.one(a, d, way, 1).wait_recv()
            block = self.next_near[way]

            def first_add(r):
                there = self.there(r, way)
                mine = sums[d, block, there].astype(f32)
                sums[d, block, there] = (mine + firsts[way, d, 1, r].astype(f32)).astype(bf16)

            by_rows(self.half, first_add)
            self.two(a, d, way).start()

    def over_second(self, a, d):
        sums, firsts, seconds, z = self.sums[a], self.firsts[a], self.seconds[a], self.z
        for way in range(2):
            self.one(a, d, way, 0).wait_recv()
            self.two(a, d, way).wait_recv()

            def total(r, there):
                return (
                    sums[d, self.f, there].astype(f32)
                    + firsts[way, d, 0, r].astype(f32)
                    + seconds[way, d, r].astype(f32)
                )

            @pl.when(d == z)
            def _():
                def stay(r):
                    there = self.there(r, way)
                    self.outs[a][there] = total(r, there)

                by_rows(self.half, stay)

            @pl.when(d != z)
            def _():
                def leave(r):
                    there = self.there(r, way)
                    self.leaving[a][d, there] = total(r, there).astype(bf16)

                by_rows(self.half, leave)

    def over_line(self, a, d):
        leaving, alongs, z = self.leaving[a], self.alongs[a], self.z

        def add_arrived():
            def step(r):
                leaving[d, r] = (leaving[d, r].astype(f32) + alongs[d, r].astype(f32)).astype(bf16)

            by_rows(self.rows, step)

        @pl.when((d > z) & (self.has_left == 1))
        def _():
            self.to_right(a, d).wait_recv()
            add_arrived()

        @pl.when((d < z) & (self.has_right == 1))
        def _():
            self.to_left(a, d, d).wait_recv()
            add_arrived()

        @pl.when(d > z)
        def _():
            self.to_right(a, d).start()

        @pl.when((d < z) & (d + 1 < z))
        def _():
            self.to_left(a, d, d).start()

        @pl.when(d + 1 == z)
        def _():
            self.to_left(a, d, self.lines).start()

    def finish(self):
        for a in range(len(self.sums)):

            @pl.when(self.has_left == 1)
            def _():
                self.to_right(a, self.z).wait_recv()
                self.add_along(a, self.z)

            @pl.when(self.has_right == 1)
            def _():
                self.to_left(a, self.z, self.lines).wait_recv()
                self.add_along(a, self.lines)

            for d in self.order:
                for way in range(2):
                    self.one(a, d, way, 0).wait_send()
                    self.one(a, d, way, 1).wait_send()
                    self.two(a, d, way).wait_send()

                @pl.when(d != self.z)
                def _():
                    self.to_right(a, d).wait_send()


def scatter_scratch(lines, n_tp, rows, widths):
    dma = pltpu.SemaphoreType.DMA
    n = len(widths)
    shapes = [
        (lines, n_tp, rows), (lines, n_tp, rows), (2, lines, 2, rows // 2), (2, lines, rows // 2),
        (lines + 1, rows), (lines, rows),
    ]
    buffers = [pltpu.VMEM((*shape, width), bf16) for shape in shapes for width in widths]
    sems = [dma((n, lines))] * 2 + [dma((n, lines, 2, 2))] * 2 + [dma((n, lines, 2))] * 2
    return buffers, sems + [dma((n, lines)), dma((n, lines + 1))]


def scatter_all(arrays, n_dp, n_tp):
    lines = n_dp // 2
    rows = arrays[0].shape[0] // (n_dp * n_tp)
    results = []
    for array in arrays:
        parts = core_sum(array.reshape(lines, 2, n_tp, rows, -1), n_dp)
        results.append(line_sum(plane_sum(parts.transpose(1, 0, 2, 3), n_tp), n_dp))
    return results


def rope_tile(tile, cos, sin):
    pairs = [tile[:, i : i + 128] for i in range(0, tile.shape[1], 128)]
    return jnp.concatenate([pair * cos + halves_swapped(pair) * sin for pair in pairs], axis=1)


def attend_heads(qkv, context, log_totals, allowed):
    length = qkv.shape[0]
    scale = HD ** (-0.5)
    for group in range(KVH):
        kc = D + (group // 2) * 128
        keys = both_places(qkv[:, kc : kc + 128], group % 2)
        values = both_places(qkv[:, kc + KW : kc + KW + 128], group % 2)

        def pair_step(pair_index, carry):
            pair = group * (GROUP // 2) + pair_index
            lanes = pl.ds(pl.multiple_of(pair * 128, 128), 128)
            queries = qkv[:, lanes]
            total = jnp.zeros((length, 128), f32)
            for side in range(2):
                scores = dot_t(keys[side], queries) * scale
                scores = jnp.where(allowed, scores, -1e30)
                top = jnp.max(scores, axis=0, keepdims=True)
                raised = jnp.exp(scores - top)
                totals = jnp.sum(raised, axis=0, keepdims=True)
                probs = (raised / totals).astype(bf16)
                total = total + dot_tn(probs, values[side])
                log_totals[pl.ds(2 * pair + side, 1), :] = top + jnp.log(totals)
            context[:, lanes] = total.astype(bf16)
            return carry

        lax.fori_loop(0, GROUP // 2, pair_step, 0)


def tile_at(i, width, start=0):
    return pl.ds(pl.multiple_of(start + i * width, 128), width)


class Exchange:
    def __init__(self, own, whole, sems, i, x_dev, y_dev):
        send, recv, here = sems
        half = own.shape[0] // 2

        def remote(src, dst, k, dev):
            return pltpu.make_async_remote_copy(
                src, dst, send.at[i, k], recv.at[i, k], device_id=dev, device_id_type=MESH
            )

        low, high = pl.ds(0, half), pl.ds(half, half)
        self.near = [remote(own, whole.at[1], 0, x_dev), remote(own, whole.at[2], 1, y_dev)]
        self.far = []
        if whole.shape[0] > 3:
            self.far = [
                remote(whole.at[2, low], whole.at[3, low], 2, x_dev),
                remote(whole.at[1, high], whole.at[3, high], 3, y_dev),
            ]
        self.here = pltpu.make_async_copy(own, whole.at[0], here.at[i])

    def start(self):
        for copy in self.near:
            copy.start()
        self.here.start()

    def pass_on(self):
        for copy in self.near:
            copy.wait_recv()
        for copy in self.far:
            copy.start()

    def finish(self):
        for copy in self.far:
            copy.wait()
        for copy in self.near:
            copy.wait_send()
        self.here.wait()


def forward_kernel(x, grads, gains, cosine, sine, seg_col, seg_row, weights, qkv, context, log_totals, middle,
                   normed_one, normed_all, grads_all, q_weight, o_weight, normed_two, load_sem, *sems):
    z, c, f = place()
    x_dev, y_dev = device(z, c, flipped(f, 1)), device(z, c, flipped(f, 2))
    greet([x_dev, y_dev], [])
    length = x.shape[0]
    width = D + 2 * KW
    of_grads = Exchange(grads, grads_all, sems, 0, x_dev, y_dev)
    of_normed = Exchange(normed_two, normed_all, sems, 1, x_dev, y_dev)
    of_grads.start()
    load_q = pltpu.make_async_copy(weights.at[:, pl.ds(0, width)], q_weight, load_sem.at[0])
    load_o = pltpu.make_async_copy(weights.at[:, pl.ds(width, D)], o_weight, load_sem.at[1])
    load_q.start()
    load_o.start()

    def norm_one(r):
        rows = x[r].astype(f32)
        inverse = lax.rsqrt(jnp.mean(rows * rows, axis=-1, keepdims=True) + norm_eps)
        normed_one[r] = (rows * inverse * gains[0:1, :]).astype(bf16)

    by_rows(length, norm_one)
    load_q.wait()
    cos, sin = cosine[...], sine[...]

    def project(i, carry):
        lanes = tile_at(i, 256)
        qkv[:, lanes] = rope_tile(dot_n(normed_one[...], q_weight[:, lanes]), cos, sin).astype(bf16)
        return carry

    lax.fori_loop(0, (D + KW) // 256, project, 0)
    qkv[:, D + KW :] = dot_n(normed_one[...], q_weight[:, D + KW :]).astype(bf16)
    allowed = mask_keys_rows(seg_col[...], seg_row[...], length)
    attend_heads(qkv, context, log_totals, allowed)
    load_o.wait()

    def project_out(i, carry):
        lanes = tile_at(i, 256)
        middle[:, lanes] = x[:, lanes].astype(f32) + dot_n(context[...], o_weight[:, lanes])
        return carry

    lax.fori_loop(0, D // 256, project_out, 0)

    def norm_two(r):
        rows = middle[r]
        inverse = lax.rsqrt(jnp.mean(rows * rows, axis=-1, keepdims=True) + norm_eps)
        normed_two[r] = (rows * inverse * gains[1:2, :]).astype(bf16)

    by_rows(length, norm_two)
    of_normed.start()
    of_grads.pass_on()
    of_normed.pass_on()
    of_normed.finish()
    of_grads.finish()


def forward(x, grads, gains, cosine, sine, seg_col, seg_row, weights):
    length = x.shape[0]
    dma = pltpu.SemaphoreType.DMA
    vmem, hbm = pl.BlockSpec(memory_space=pltpu.VMEM), pl.BlockSpec(memory_space=pl.ANY)
    width = D + 2 * KW
    return pl.pallas_call(
        forward_kernel,
        out_shape=(
            jax.ShapeDtypeStruct((length, width), bf16),
            jax.ShapeDtypeStruct((length, D), bf16),
            jax.ShapeDtypeStruct((HEADS, length), f32),
            jax.ShapeDtypeStruct((length, D), f32),
            jax.ShapeDtypeStruct((length, D), bf16),
            jax.ShapeDtypeStruct((4, length, D), bf16),
            jax.ShapeDtypeStruct((3, length, D), bf16),
        ),
        in_specs=[vmem, hbm] + [vmem] * 5 + [hbm],
        out_specs=(vmem,) * 5 + (hbm,) * 2,
        scratch_shapes=[
            pltpu.VMEM((D, width), bf16), pltpu.VMEM((D, D), bf16), pltpu.VMEM((length, D), bf16),
            dma((2,)), dma((2, 4)), dma((2, 4)), dma((2,)),
        ],
        compiler_params=pltpu.CompilerParams(
            collective_id=5, has_side_effects=True, vmem_limit_bytes=feed_vmem_limit
        ),
        cost_estimate=cost(95),
        name="forward",
    )(x, grads, gains, cosine, sine, seg_col, seg_row, weights)


class PlaneSum:
    def __init__(self, parts, ones, twos, sems, x_dev, y_dev):
        one_send, one_recv, two_send, two_recv = sems
        self.half = parts.shape[1] // 2
        self.parts, self.ones, self.twos = parts, ones, twos
        halves = (pl.ds(0, self.half), pl.ds(self.half, self.half))
        step_dev = (x_dev, y_dev)

        def remote(src, dst, send, recv, dev):
            return pltpu.make_async_remote_copy(src, dst, send, recv, device_id=dev, device_id_type=MESH)

        self.near, self.far, self.two = [], [], []
        for way in range(2):
            for i, copies in enumerate((self.near, self.far)):
                block = parts.at[2 if i else way, halves[way]]
                copies.append(
                    remote(block, ones.at[way, i], one_send.at[way, i], one_recv.at[way, i], step_dev[way])
                )
            if twos is not None:
                block = parts.at[1 - way, halves[way]]
                self.two.append(remote(block, twos.at[way], two_send.at[way], two_recv.at[way], step_dev[1 - way]))

    def there(self, r, way):
        return pl.ds(pl.multiple_of(r.start + way * self.half, 16), r.size)

    def pass_on(self):
        for way in range(2):
            self.far[way].wait_recv()

            def add_far(r):
                there = self.there(r, way)
                mine = self.parts[1 - way, there].astype(f32)
                self.parts[1 - way, there] = (mine + self.ones[way, 1, r].astype(f32)).astype(bf16)

            by_rows(self.half, add_far)
            self.two[way].start()

    def finish(self, add):
        for way in range(2):
            self.near[way].wait()
            self.far[way].wait_send()
            self.two[way].wait()
        for way in range(2):

            def add_all(r):
                add(self.there(r, way), self.ones[way, 0, r].astype(f32) + self.twos[way, r].astype(f32))

            by_rows(self.half, add_all)


def plane_sum_scratch(length, columns):
    dma = pltpu.SemaphoreType.DMA
    shapes = ((3, length, columns), (2, 2, length // 2, columns), (2, length // 2, columns))
    return [pltpu.VMEM(shape, bf16) for shape in shapes], [dma((2, 2)), dma((2, 2)), dma((2,)), dma((2,))]


def attend_heads_grad(qkv, grad_context, log_totals, grad_proj, allowed, cos, sin, between=None):
    length = qkv.shape[0]
    scale = HD ** (-0.5)

    def unrotate(pair):
        return pair * cos + halves_swapped(pair * sin)

    key_parts, value_parts = [], []
    for group in range(KVH):
        kc = D + (group // 2) * 128
        keys = both_places(qkv[:, kc : kc + 128], group % 2)
        values = both_places(qkv[:, kc + KW : kc + KW + 128], group % 2)

        def pair_step(pair_index, carry):
            grad_keys, grad_values = list(carry[:2]), list(carry[2:])
            pair = group * (GROUP // 2) + pair_index
            lanes = pl.ds(pl.multiple_of(pair * 128, 128), 128)
            queries = qkv[:, lanes]
            grads = grad_context[:, lanes]
            total = jnp.zeros((length, 128), f32)
            for side in range(2):
                scores = dot_t(keys[side], queries) * scale
                scores = jnp.where(allowed, scores, -1e30)
                probs = jnp.exp(scores - log_totals[pl.ds(2 * pair + side, 1), :])
                grad_probs = dot_t(values[side], grads)
                grad_values[side] = grad_values[side] + dot_n(probs.astype(bf16), grads)
                inner = jnp.sum(probs * grad_probs, axis=0, keepdims=True)
                raw = (probs * (grad_probs - inner) * scale).astype(bf16)
                total = total + dot_tn(raw, keys[side])
                grad_keys[side] = grad_keys[side] + dot_n(raw, queries)
            grad_proj[:, lanes] = unrotate(total).astype(bf16)
            return (*grad_keys, *grad_values)

        empty = jnp.zeros((length, 128), f32)
        out = lax.fori_loop(0, GROUP // 2, pair_step, (empty,) * 4)

        def joined(low_side, high_side):
            low, _ = split_pair(low_side)
            _, high = split_pair(high_side)
            both = low + high
            return both + pltpu.roll(both, HD, 1)

        key_parts.append(joined(out[0], out[1]))
        value_parts.append(joined(out[2], out[3]))
        if between is not None:
            between(group)
    lane = lax.broadcasted_iota(jnp.int32, (length, 128), 1)
    for c in range(KVH // 2):
        keys = jnp.where(lane < HD, key_parts[2 * c], key_parts[2 * c + 1])
        values = jnp.where(lane < HD, value_parts[2 * c], value_parts[2 * c + 1])
        grad_proj[:, D + c * 128 : D + (c + 1) * 128] = unrotate(keys).astype(bf16)
        grad_proj[:, D + KW + c * 128 : D + KW + (c + 1) * 128] = values.astype(bf16)


def fold(value):
    return jnp.sum(value, axis=0, keepdims=True)


def branch_kernel(grads, grad_normed, middle, gains, context, weights, layer, onward, layer_out, grad_branch,
                  grad_context, grad_o, gain_rows, weight, stage, arrived_layer, load_sem, out_sem, send, recv):
    length, width = middle.shape[0], D + 2 * KW
    half = length // 2
    z, c, f = place()
    near = (device(z, c, flipped(f, 1)), device(z, c, flipped(f, 2)))
    greet(near, [])
    last = [
        pltpu.make_async_remote_copy(
            onward.at[way], arrived_layer.at[way], send.at[way], recv.at[way], device_id=near[1 - way], device_id_type=MESH
        )
        for way in range(2)
    ]
    for copy in last:
        copy.start()
    load_o = pltpu.make_async_copy(weights.at[:, pl.ds(width, D)], weight, load_sem.at[0])
    load_o.start()
    gain_rows[...] = jnp.zeros_like(gain_rows)

    def middle_grads(r):
        rows, arrived = middle[r], grad_normed[r]
        inverse = lax.rsqrt(jnp.mean(rows * rows, axis=-1, keepdims=True) + norm_eps)
        gain_rows[1:2, :] += fold(arrived * rows * inverse)
        weighted = arrived * gains[1:2, :]
        inner = jnp.mean(weighted * rows, axis=-1, keepdims=True)
        value = grads[r].astype(f32) + inverse * weighted - rows * (inverse * inverse * inverse * inner)
        grad_branch[r] = value.astype(bf16)

    by_rows(length, middle_grads)
    load_o.wait()

    def context_step(i, carry):
        tile = tile_at(i, 512)
        grad_context[:, tile] = dot_t(grad_branch[...], weight[tile, :]).astype(bf16)
        return carry

    lax.fori_loop(0, D // 512, context_step, 0)
    steps = D // 512

    def out(i, slot):
        return pltpu.make_async_copy(stage.at[slot], grad_o.at[tile_at(i, 512)], out_sem.at[slot])

    def step(i, carry):
        slot = i % 2

        @pl.when(i >= 2)
        def _():
            out(i - 2, slot).wait()

        stage[slot] = dot_tn(context[:, tile_at(i, 512)], grad_branch[...]).astype(bf16)
        out(i, slot).start()
        return carry

    lax.fori_loop(0, steps, step, 0)
    for way in range(2):
        last[way].wait()

        def add_last(r):
            there = pl.ds(pl.multiple_of(r.start + way * half, 16), r.size)
            layer_out[there] = (middle[there] + layer[there].astype(f32) + arrived_layer[way, r].astype(f32)).astype(bf16)

        by_rows(half, add_last)
    out(steps - 2, 0).wait()
    out(steps - 1, 1).wait()


def branch(grads, grad_normed, middle, gains, context, weights, layer, onward):
    length = middle.shape[0]
    dma = pltpu.SemaphoreType.DMA
    vmem, hbm = pl.BlockSpec(memory_space=pltpu.VMEM), pl.BlockSpec(memory_space=pl.ANY)
    rows = jax.ShapeDtypeStruct((length, D), bf16)
    return pl.pallas_call(
        branch_kernel,
        out_shape=(rows, rows, rows, jax.ShapeDtypeStruct((D, D), bf16), jax.ShapeDtypeStruct((8, D), f32)),
        in_specs=[vmem] * 5 + [hbm, vmem, vmem],
        out_specs=(vmem, vmem, vmem, hbm, vmem),
        scratch_shapes=[
            pltpu.VMEM((D, D), bf16), pltpu.VMEM((2, 512, D), bf16), pltpu.VMEM((2, length // 2, D), bf16),
            dma((1,)), dma((2,)), dma((2,)), dma((2,)),
        ],
        compiler_params=pltpu.CompilerParams(
            collective_id=4, has_side_effects=True, vmem_limit_bytes=feed_vmem_limit
        ),
        cost_estimate=cost(22),
        name="branch",
    )(grads, grad_normed, middle, gains, context, weights, layer, onward)


def backward_kernel(lines, x, normed_one, qkv, grad_context, log_totals, gains, cosine, sine, seg_col, seg_row, gain_two,
                    grad_o, branch_hbm, weights, input_grad, out_o, out_q, weight, grad_proj, grad_one, gain_rows,
                    gain_columns, staged, *refs):
    groups = [refs[i * 2 : i * 2 + 2] for i in range(6)] + [(out_o, out_q)]
    scatter_sems, (load_sem, weight_sem) = refs[12:20], refs[20:]
    scatter = Scatter(lines, groups, scatter_sems)
    z, c, f = place()
    length, width = x.shape[0], D + 2 * KW
    order = scatter.order
    rows = scatter.rows

    def load(d):
        return pltpu.make_async_copy(grad_o.at[d, c], scatter.sums[0].at[d], load_sem.at[d])

    def load_weight(i):
        tile = pl.ds(i * 512, 512)
        return pltpu.make_async_copy(weights.at[tile, pl.ds(0, width)], weight.at[i % 2], weight_sem.at[i % 2])

    for d in order:
        scatter.to_core(0, d, grad_o.at[d, 1 - c]).start()
        load(d).start()
    load_branch = pltpu.make_async_copy(branch_hbm, input_grad, load_sem.at[lines])
    load_branch.start()
    load_weight(0).start()
    load_weight(1).start()
    gain_rows[...] = gain_two[...]

    def between(group):
        if group == 0:
            for d in order:
                load(d).wait()
                scatter.over_core(0, d)
        elif group == 1:
            scatter.over_first(0, order[0])
            scatter.over_first(0, order[1])
        elif group == 2:
            for d in order[2:]:
                scatter.over_first(0, d)
        else:
            scatter.over_second(0, order[0])
            scatter.over_second(0, order[1])

    allowed = mask_keys_rows(seg_col[...], seg_row[...], length)
    attend_heads_grad(
        qkv, grad_context, log_totals, grad_proj, allowed, cosine[...], sine[...], between if lines > 1 else None
    )
    for i in range(D // 512):
        load_weight(i).wait()
        grad_one[:, i * 512 : (i + 1) * 512] = dot_t(grad_proj[...], weight[i % 2])
        if i + 2 < D // 512:
            load_weight(i + 2).start()
    for d in order[2:]:
        scatter.over_second(0, d)
    load_branch.wait()

    def input_grads(r):
        values, arrived = x[r].astype(f32), grad_one[r]
        inverse = lax.rsqrt(jnp.mean(values * values, axis=-1, keepdims=True) + norm_eps)
        gain_rows[0:1, :] += fold(arrived * values * inverse)
        weighted = arrived * gains[0:1, :]
        inner = jnp.mean(weighted * values, axis=-1, keepdims=True)
        value = inverse * weighted - values * (inverse * inverse * inverse * inner)
        input_grad[r] = (input_grad[r].astype(f32) + value).astype(bf16)

    by_rows(length, input_grads)
    for i in range(D // 128):
        lanes = pl.ds(i * 128, 128)
        square = jnp.concatenate([gain_rows[:, lanes], jnp.zeros((120, 128), f32)], axis=0)
        gain_columns[lanes, :] = square.T.astype(bf16)

    def blocks(d, core):
        start = pl.multiple_of((2 * d + core) * (4 * rows), 128)
        tile = pl.ds(start, 4 * rows)
        value = dot_tn(normed_one[:, tile], grad_proj[...]).astype(bf16)
        return value.reshape(4, rows, width), gain_columns[tile, :].reshape(4, rows, 128)

    def put(target, value):
        target[:, :, 0:width] = value[0]
        target[:, :, width:] = value[1]

    def staged_copy(j):
        return scatter.to_core(1, order[j], staged.at[j % 2])

    for j, d in enumerate(order):
        if j >= 2:
            staged_copy(j - 2).wait_send()
        put(staged.at[j % 2], blocks(d, 1 - c))
        staged_copy(j).start()
        put(scatter.sums[1].at[d], blocks(d, c))
        if j:
            scatter.over_core(1, order[j - 1])
        if j < len(order) - 1:
            scatter.over_line(0, d)
    scatter.over_core(1, order[-1])
    for j in range(len(order) + 2):
        if j < len(order):
            scatter.over_first(1, order[j])
        if 0 <= j - 1 < len(order):
            scatter.over_second(1, order[j - 1])
        if 0 <= j - 2 < len(order) - 1:
            scatter.over_line(1, order[j - 2])
    for d in order:
        scatter.to_core(0, d, grad_o.at[d, 1 - c]).wait_send()
    for j in range(max(0, len(order) - 2), len(order)):
        staged_copy(j).wait_send()
    scatter.finish()


def backward(x, normed_one, qkv, grad_context, log_totals, gains, cosine, sine, seg_col, seg_row, gain_two, grad_o,
             grad_branch, weights, n_dp, n_tp):
    length = x.shape[0]
    lines, rows = n_dp // 2, D // (n_dp * n_tp)
    width = D + 2 * KW
    dma = pltpu.SemaphoreType.DMA
    vmem, hbm = pl.BlockSpec(memory_space=pltpu.VMEM), pl.BlockSpec(memory_space=pl.ANY)
    buffers, sems = scatter_scratch(lines, n_tp, rows, (D, width + 128))
    return pl.pallas_call(
        functools.partial(backward_kernel, lines),
        out_shape=(
            jax.ShapeDtypeStruct((length, D), bf16),
            jax.ShapeDtypeStruct((rows, D), f32),
            jax.ShapeDtypeStruct((rows, width + 128), f32),
        ),
        in_specs=[vmem] * 11 + [hbm] * 3,
        out_specs=(vmem,) * 3,
        scratch_shapes=[
            pltpu.VMEM((2, 512, width), bf16), pltpu.VMEM((length, width), bf16), pltpu.VMEM((length, D), f32),
            pltpu.VMEM((8, D), f32), pltpu.VMEM((D, 128), bf16), pltpu.VMEM((2, n_tp, rows, width + 128), bf16),
        ]
        + buffers + sems + [dma((lines + 1,)), dma((2,))],
        compiler_params=pltpu.CompilerParams(
            collective_id=7, has_side_effects=True, vmem_limit_bytes=feed_vmem_limit
        ),
        cost_estimate=cost(105),
        name="backward",
    )(x, normed_one, qkv, grad_context, log_totals, gains, cosine, sine, seg_col, seg_row, gain_two,
      grad_o.reshape(lines, 2, n_tp, rows, D), grad_branch, weights)


def norm_kernel(n_dp, n_tp, parts, qkv, out, down, mlp, total, got, held, got_dp, got_tp, send, recv, total_send,
                total_recv, here_sem):
    z, c, f = place()
    dp = z * 2 + c
    columns = [(f + k) % n_tp for k in range(1, n_tp)]
    lines = [(dp + k) % n_dp for k in range(1, n_dp)]
    greet([device(z, c, to) for to in columns] + [{"dp": to, "fsdp": f} for to in lines], [])
    unit = mlp.shape[1] // (2 * n_dp * n_tp)
    half = n_dp * unit

    def away(k):
        to = columns[k - 1]
        return pltpu.make_async_remote_copy(
            parts.at[to], got.at[f], send.at[k], recv.at[k], device_id=device(z, c, to), device_id_type=MESH
        )

    for k in range(1, n_tp):
        away(k).start()
    here = pltpu.make_async_copy(parts.at[f], got.at[f], here_sem)
    here.start()
    held[...] = jnp.zeros_like(held)

    def add_squares(ref):
        def step(r):
            part = ref[r, :].astype(f32)
            part = part * part
            lanes = [part[:, i : i + 128] for i in range(0, part.shape[1], 128)]
            held[...] += functools.reduce(jnp.add, lanes)

        by_rows(ref.shape[0], step)

    add_squares(qkv)
    add_squares(out)
    add_squares(down)
    here.wait()
    for k in range(1, n_tp):
        away(k).wait()
    for frm in range(n_tp):
        add_squares(got.at[frm])

    def spread(buffer, own, value, partners, base):
        buffer[own] = value
        copies = [
            pltpu.make_async_remote_copy(
                buffer.at[own], buffer.at[own], total_send.at[base + k], total_recv.at[base + k],
                device_id=partner, device_id_type=MESH,
            )
            for k, partner in enumerate(partners)
        ]
        for copy in copies:
            copy.start()
        return copies

    def summed(buffer, copies):
        for copy in copies:
            copy.wait()
        return functools.reduce(jnp.add, [buffer[i] for i in range(buffer.shape[0])])

    own_total = jnp.sum(jnp.sum(held[...], axis=0, keepdims=True), axis=1, keepdims=True)
    copies = spread(
        got_dp, dp, jnp.broadcast_to(own_total, (8, 128)), [{"dp": to, "fsdp": f} for to in lines], 0
    )
    for side in range(2):
        pieces = [
            got[frm, :, side * half + j * unit : side * half + (j + 1) * unit].astype(f32)
            for j in range(n_dp)
            for frm in range(n_tp)
        ]
        mlp[:, side * n_tp * half : (side + 1) * n_tp * half] = jnp.concatenate(pieces, axis=1)
    line_total = summed(got_dp, copies)
    copies = spread(got_tp, f, line_total, [device(z, c, to) for to in columns], n_dp)
    total[...] = summed(got_tp, copies)


def norm_parts(parts, qkv, out, down, n_dp, n_tp):
    _, rows, width = parts.shape
    dma = pltpu.SemaphoreType.DMA
    vmem, hbm = pl.BlockSpec(memory_space=pltpu.VMEM), pl.BlockSpec(memory_space=pl.ANY)
    return pl.pallas_call(
        functools.partial(norm_kernel, n_dp, n_tp),
        out_shape=(jax.ShapeDtypeStruct((rows, width * n_tp), f32), jax.ShapeDtypeStruct((8, 128), f32)),
        in_specs=[hbm, vmem, vmem, vmem],
        scratch_shapes=[
            pltpu.VMEM(parts.shape, bf16), pltpu.VMEM((16, 128), f32), pltpu.VMEM((n_dp, 8, 128), f32),
            pltpu.VMEM((n_tp, 8, 128), f32), dma((n_tp,)), dma((n_tp,)), dma((n_dp + n_tp,)), dma((n_dp + n_tp,)),
            dma(()),
        ],
        compiler_params=pltpu.CompilerParams(
            collective_id=8, has_side_effects=True, vmem_limit_bytes=feed_vmem_limit
        ),
        cost_estimate=cost(35),
        name="norm_parts",
    )(parts, qkv, out, down)


def adam_kernel(total, gain_block, *refs):
    scale = clip_norm / jnp.maximum(jnp.sqrt(total[0:1, 0:1]), clip_norm)
    grads, refs = refs[:4], refs[4:]
    states, news = refs[:15], refs[15:]

    def update(i, gradient, rate, decay):
        new = adam_update(
            states[3 * i][...], gradient * scale, states[3 * i + 1][...], states[3 * i + 2][...], rate, decay
        )
        for k in range(3):
            news[3 * i + k][...] = new[k]

    for i in range(4):
        update(i, grads[i][...].astype(f32), matrix_rate, weight_decay)

    @pl.when(pl.program_id(0) == 0)
    def _():
        rows = gain_block.shape[0]
        square = jnp.concatenate([gain_block[...], jnp.zeros((128 - rows, 128), f32)], axis=0)
        update(4, square.T[0:2, 0:rows], gain_rate, 0.0)


def adam_all(total, grads, states):
    shapes = [state[0].shape for state in states[:4]]

    def block(shape, steps):
        rows, columns = shape
        if rows % (8 * steps) == 0:
            return pl.BlockSpec((rows // steps, columns), lambda i: (i, 0))
        if columns % (128 * steps) == 0:
            return pl.BlockSpec((rows, columns // steps), lambda i: (0, i))
        return None

    steps = 8 if all(block(shape, 8) for shape in shapes) else 4
    specs = [block(shape, steps) for shape in shapes]
    flat = [array for state in states for array in state]
    gains = pl.BlockSpec(states[4][0].shape, lambda i: (0, 0))
    state_specs = [spec for spec in specs + [gains] for _ in range(3)]
    last = grads[0].shape[1] // 128 - 1
    gain_block = pl.BlockSpec((grads[0].shape[0], 128), lambda i: (0, last))
    return pl.pallas_call(
        adam_kernel,
        grid=(steps,),
        out_shape=[jax.ShapeDtypeStruct(array.shape, f32) for array in flat],
        in_specs=[pl.BlockSpec((8, 128), lambda i: (0, 0)), gain_block] + specs + state_specs,
        out_specs=state_specs,
        compiler_params=pltpu.CompilerParams(vmem_limit_bytes=feed_vmem_limit),
        cost_estimate=cost(14),
        name="adam",
    )(total, grads[0], *grads, *flat)


def feed_front_kernel(n_hbm, g_hbm, wm_hbm, wd_hbm, gh_hbm, grad_down, layer_sum, onward, n, g, wm, wd, act, gh, stage,
                      parts, ones, *sems):
    sum_sems, (load_sem, weight_sem, out_sem, far_send, far_recv) = sems[:2], sems[2:]
    z, c, f = place()
    x_dev, y_dev = device(z, c, flipped(f, 1)), device(z, c, flipped(f, 2))
    tokens = n.shape[0]
    length = tokens // 4
    ff = wd.shape[0]
    half = length // 2
    order = (1, 2, 3, 0)

    def rows_of(k):
        return pl.ds(k * length, length)

    load_n = [pltpu.make_async_copy(n_hbm.at[rows_of(k)], n.at[rows_of(k)], load_sem.at[0, k]) for k in range(4)]
    load_g = [pltpu.make_async_copy(g_hbm.at[rows_of(k)], g.at[rows_of(k)], load_sem.at[1, k]) for k in range(3)]
    tiles = [(start, min(256, ff - start)) for start in range(0, ff, 256)]
    load_w = []
    for t, (start, size) in enumerate(tiles):
        gate, up = pl.ds(start, size), pl.ds(ff + start, size)
        load_w.append(
            [
                pltpu.make_async_copy(wm_hbm.at[:, gate], wm.at[:, gate], weight_sem.at[0, t]),
                pltpu.make_async_copy(wm_hbm.at[:, up], wm.at[:, up], weight_sem.at[1, t]),
                pltpu.make_async_copy(wd_hbm.at[gate], wd.at[gate], weight_sem.at[2, t]),
            ]
        )
    load_n[order[0]].start()
    load_g[order[0]].start()
    for copies in load_w:
        for copy in copies:
            copy.start()
    for k in order[1:]:
        load_n[k].start()
        if k < 3:
            load_g[k].start()
    greet([x_dev, y_dev], [])
    far_grads = [
        pltpu.make_async_remote_copy(
            g_hbm.at[pl.ds(start, half)], g.at[pl.ds(to, half)], far_send.at[i], far_recv.at[i], device_id=dev,
            device_id_type=MESH,
        )
        for i, (start, to, dev) in enumerate(
            ((2 * length, 3 * length, x_dev), (length + half, 3 * length + half, y_dev))
        )
    ]
    for copy in far_grads:
        copy.start()
    summed = PlaneSum(parts, ones, None, (*sum_sems, None, None), x_dev, y_dev)

    def hidden(k, slot, lanes, up_lanes):
        rows = rows_of(k)
        gate = dot_n(n[rows, :], wm[:, lanes])
        up = dot_n(n[rows, :], wm[:, up_lanes])
        grad = dot_t(g[rows, :], wd[lanes, :])
        sigmoid = jax.nn.sigmoid(gate)
        silu = gate * sigmoid
        act[rows, lanes] = (silu * up).astype(bf16)
        gh[slot, :, lanes] = (grad * up * sigmoid * (1.0 + gate * (1.0 - sigmoid))).astype(bf16)
        gh[slot, :, up_lanes] = (grad * silu).astype(bf16)

    def hidden_out(i):
        return pltpu.make_async_copy(gh.at[i % 2], gh_hbm.at[rows_of(order[i])], out_sem.at[1, i % 2])

    for i, k in enumerate(order):
        load_n[k].wait()
        for copy in load_g[k : k + 1] or far_grads:
            copy.wait()
        if i >= 2:
            hidden_out(i - 2).wait()
        if i == 0:
            for copies, (start, size) in zip(load_w, tiles):
                for copy in copies:
                    copy.wait()
                hidden(k, 0, pl.ds(start, size), pl.ds(ff + start, size))
        else:

            def hidden_step(t, carry):
                hidden(k, i % 2, tile_at(t, 256), tile_at(t, 256, ff))
                return carry

            lax.fori_loop(0, ff // 256, hidden_step, 0)
            if ff % 256:
                start, size = tiles[-1]
                hidden(k, i % 2, pl.ds(start, size), pl.ds(ff + start, size))
        hidden_out(i).start()

        def layer_step(t, carry):
            value = dot_n(act[rows_of(k), :], wd[:, tile_at(t, 512)]).astype(bf16)
            if k:
                parts[k - 1, :, tile_at(t, 512)] = value
            else:
                layer_sum[:, tile_at(t, 512)] = value
            return carry

        lax.fori_loop(0, D // 512, layer_step, 0)
        if k == 3:
            for copy in summed.far:
                copy.start()
        elif k:
            summed.near[k - 1].start()
    wide = ff // 256

    def down_out(i, slot, width=256):
        rows = pl.ds(pl.multiple_of((i // 2) * 256, 128), width)
        lanes = tile_at(i % 2, D // 2)
        return pltpu.make_async_copy(stage.at[slot, pl.ds(0, width)], grad_down.at[rows, lanes], out_sem.at[0, slot])

    def down_tile(i, slot, width=256):
        lanes = tile_at(i % 2, D // 2)
        value = dot_tn(act[:, pl.ds(pl.multiple_of((i // 2) * 256, 128), width)], g[:, lanes])
        stage[slot, 0:width] = value.astype(bf16)
        down_out(i, slot, width).start()

    def down_step(i, carry):
        slot = i % 2

        @pl.when(i >= 2)
        def _():
            down_out(i - 2, slot).wait()

        down_tile(i, slot)
        return carry

    lax.fori_loop(0, 2 * wide, down_step, 0)
    for slot in range(2):
        down_out(2 * wide - 2 + slot, slot).wait()
        if ff % 256:
            down_tile(2 * wide + slot, slot, ff % 256)
    for slot in range(2):
        if ff % 256:
            down_out(2 * wide + slot, slot, ff % 256).wait()
        hidden_out(2 + slot).wait()

    for way in range(2):
        summed.far[way].wait()

        def add_far(r):
            mine = parts[1 - way, summed.there(r, way)].astype(f32)
            onward[way, r] = (mine + ones[way, 1, r].astype(f32)).astype(bf16)

        by_rows(summed.half, add_far)
    for way in range(2):
        summed.near[way].wait()

        def add_near(r):
            there = summed.there(r, way)
            layer_sum[there] = (layer_sum[there].astype(f32) + ones[way, 0, r].astype(f32)).astype(bf16)

        by_rows(summed.half, add_near)


def feed_back_kernel(gh_hbm, wm_hbm, n_hbm, grad_normed, grad_mlp, gh, wm, n, stage, parts, ones, twos, *sems):
    sum_sems, (load_sem, out_sem) = sems[:4], sems[4:]
    z, c, f = place()
    x_dev, y_dev = device(z, c, flipped(f, 1)), device(z, c, flipped(f, 2))
    tokens = n.shape[0]
    length = tokens // 4
    ff = gh.shape[1] // 2
    order = (3, 1, 2, 0)
    rows_of = [pl.ds(k * length, length) for k in range(4)]
    load_gh = [pltpu.make_async_copy(gh_hbm.at[rows_of[k]], gh.at[rows_of[k]], load_sem.at[0, k]) for k in range(4)]
    wide_tiles = [pl.ds(start, 1024) for start in range(0, D, 1024)]
    load_w = [
        pltpu.make_async_copy(wm_hbm.at[tile], wm.at[tile], load_sem.at[1, t]) for t, tile in enumerate(wide_tiles)
    ]
    load_n = pltpu.make_async_copy(n_hbm, n, load_sem.at[1, 3])
    for copy in [load_gh[order[0]]] + load_w + [load_gh[k] for k in order[1:]] + [load_n]:
        copy.start()
    greet([x_dev, y_dev], [])
    summed = PlaneSum(parts, ones, twos, sum_sems, x_dev, y_dev)
    for k in order:
        load_gh[k].wait()
        for t, tile in enumerate(wide_tiles):
            if k == order[0]:
                load_w[t].wait()
            value = dot_t(gh[rows_of[k], :], wm[tile, :])
            if k:
                parts[k - 1, :, tile] = value.astype(bf16)
            else:
                grad_normed[:, tile] = value
        if k == 3:
            for copy in summed.far:
                copy.start()
        elif k:
            summed.near[k - 1].start()
    summed.pass_on()
    load_n.wait()
    steps = 2 * D // 512

    def mlp_out(i, slot):
        rows = pl.ds(pl.multiple_of((i // 2) * 512, 512), 512)
        return pltpu.make_async_copy(stage.at[slot], grad_mlp.at[rows, tile_at(i % 2, ff)], out_sem.at[slot])

    def mlp_step(i, carry):
        slot = i % 2

        @pl.when(i >= 2)
        def _():
            mlp_out(i - 2, slot).wait()

        stage[slot] = dot_tn(n[:, tile_at(i // 2, 512)], gh[:, tile_at(i % 2, ff)]).astype(bf16)
        mlp_out(i, slot).start()
        return carry

    lax.fori_loop(0, steps, mlp_step, 0)

    def add_normed(r, value):
        grad_normed[r] += value

    summed.finish(add_normed)
    mlp_out(steps - 2, 0).wait()
    mlp_out(steps - 1, 1).wait()


def feed(normed_all, grads_all, mlp_cols, down_cols):
    tokens, ff = 4 * normed_all.shape[1], down_cols.shape[0]
    length = tokens // 4
    dma = pltpu.SemaphoreType.DMA
    vmem, hbm = pl.BlockSpec(memory_space=pltpu.VMEM), pl.BlockSpec(memory_space=pl.ANY)
    sum_buffers, sum_sems = plane_sum_scratch(length, D)
    normed_all = normed_all.reshape(tokens, D)

    def buffers(*shapes):
        return [pltpu.VMEM(shape, bf16) for shape in shapes]

    grad_hidden, grad_down, layer_sum, onward = pl.pallas_call(
        feed_front_kernel,
        out_shape=(
            jax.ShapeDtypeStruct((tokens, 2 * ff), bf16),
            jax.ShapeDtypeStruct((ff, D), bf16),
            jax.ShapeDtypeStruct((length, D), bf16),
            jax.ShapeDtypeStruct((2, length // 2, D), bf16),
        ),
        in_specs=[hbm] * 4,
        out_specs=(hbm, hbm, vmem, vmem),
        scratch_shapes=buffers(
            (tokens, D), (tokens, D), (D, 2 * ff), (ff, D), (tokens, ff), (2, length, 2 * ff), (2, 256, D // 2)
        )
        + sum_buffers[:2] + sum_sems[:2]
        + [dma((2, 4)), dma((3, -(-ff // 256))), dma((2, 2)), dma((2,)), dma((2,))],
        compiler_params=pltpu.CompilerParams(
            collective_id=6, has_side_effects=True, vmem_limit_bytes=feed_vmem_limit
        ),
        cost_estimate=cost(65),
        name="feed_front",
    )(normed_all, grads_all.reshape(-1, D), mlp_cols, down_cols)
    grad_normed, grad_mlp = pl.pallas_call(
        feed_back_kernel,
        out_shape=(jax.ShapeDtypeStruct((length, D), f32), jax.ShapeDtypeStruct((D, 2 * ff), bf16)),
        in_specs=[hbm] * 3,
        out_specs=(vmem, hbm),
        scratch_shapes=buffers((tokens, 2 * ff), (D, 2 * ff), (tokens, D), (2, 512, ff))
        + sum_buffers + sum_sems + [dma((2, 4)), dma((2,))],
        compiler_params=pltpu.CompilerParams(
            collective_id=9, has_side_effects=True, vmem_limit_bytes=feed_vmem_limit
        ),
        cost_estimate=cost(60),
        name="feed_back",
    )(grad_hidden, mlp_cols, normed_all)
    return grad_normed, grad_down, grad_mlp, layer_sum, onward


def local(
    n_dp,
    n_tp,
    inputs,
    cotangent,
    segments,
    qkv_weight,
    out_weight,
    mlp_weight,
    down_weight,
    norm_gains,
    qkv_first,
    out_first,
    mlp_first,
    down_first,
    gains_first,
    qkv_second,
    out_second,
    mlp_second,
    down_second,
    gains_second,
):
    length = inputs.shape[0]
    lines = n_dp // 2
    rows = mlp_weight.shape[0]
    down_rows = down_weight.shape[0]
    ff = n_dp * down_rows
    cosine, sine = tables(segments[0])
    seg_row = segments
    seg_col = segments.reshape(length, 1)

    shard = jnp.concatenate(
        [qkv_weight, out_weight, jnp.pad(norm_gains.T, ((0, 0), (0, 126)))], axis=1
    ).astype(bf16)
    attn_full, mlp_parts, down_cols = gather_all(shard, mlp_weight, down_weight.astype(bf16), n_dp, n_tp)
    qkv_full = attn_full[:, : D + 2 * KW]
    out_full = attn_full[:, D + 2 * KW : 2 * D + 2 * KW]
    gains_full = attn_full[:, 2 * D + 2 * KW :].astype(f32).T
    mlp_cols = lax.all_gather(mlp_parts.reshape(n_tp * rows, 2 * ff), "dp", axis=0, tiled=True)
    tokens_f = inputs.astype(f32)
    gain_one, gain_two = gains_full[0], gains_full[1]
    inverse_one = lax.rsqrt(jnp.mean(tokens_f * tokens_f, axis=-1, keepdims=True) + norm_eps)
    if n_tp == 4:
        qkv, attended, log_totals, middle, normed_one, normed_all, grads_all = forward(
            inputs, cotangent, gains_full, cosine, sine, seg_col, seg_row, attn_full
        )
    else:
        normed_one = (tokens_f * inverse_one * gain_one).astype(bf16)
        projected = matmul(normed_one, qkv_full)
        qkv, attended, log_totals = attend(projected, cosine, sine, seg_col, seg_row)
        middle = tokens_f + matmul(attended, out_full)
    inverse_two = lax.rsqrt(jnp.mean(middle * middle, axis=-1, keepdims=True) + norm_eps)
    if n_tp == 4:
        grad_normed_two, grad_down, grad_mlp, layer_sum, onward = feed(normed_all, grads_all, mlp_cols, down_cols)
    else:
        normed_two = (middle * inverse_two * gain_two).astype(bf16)
        normed_all = plane_gather(normed_two, n_tp)
        grads_all = plane_gather(cotangent, n_tp)
        hidden = matmul(normed_all, mlp_cols)
        gate, up_part = hidden[:, :ff], hidden[:, ff:]
        sigmoid_gate = jax.nn.sigmoid(gate)
        silu_gate = gate * sigmoid_gate
        activated = (silu_gate * up_part).astype(bf16)
        grad_act = matmul_t(grads_all, down_cols)
        grad_gate = grad_act * up_part * sigmoid_gate * (1.0 + gate * (1.0 - sigmoid_gate))
        grad_up = grad_act * silu_gate
        grad_hidden = jnp.concatenate([grad_gate, grad_up], axis=1).astype(bf16)
        grad_normed = matmul_t(grad_hidden, mlp_cols).reshape(n_tp, length, D)
        grad_normed_two = grad_normed[0]
        for k in range(1, n_tp):
            swapped = plane_swap(grad_normed[k].astype(bf16), k, n_tp)
            grad_normed_two = grad_normed_two + swapped.astype(f32)
        grad_down = matmul_tn(activated, grads_all).astype(bf16)
        grad_mlp = matmul_tn(normed_all, grad_hidden).astype(bf16)
        layer_parts = matmul(activated, down_cols).astype(bf16).reshape(n_tp, length, D)
    down_sum = lax.psum_scatter(grad_down, "dp", scatter_dimension=0, tiled=True)
    mlp_sum = lax.psum_scatter(grad_mlp, "dp", scatter_dimension=0, tiled=True).reshape(n_tp, rows, 2 * ff)

    if n_tp == 4:
        layer_out, grad_branch, grad_context, grad_out, gain_two_rows = branch(
            cotangent, grad_normed_two, middle, gains_full, attended, attn_full, layer_sum, onward
        )
        input_grad, out_sum, qkv_sum = backward(
            inputs, normed_one, qkv, grad_context, log_totals, gains_full, cosine, sine, seg_col, seg_row,
            gain_two_rows, grad_out, grad_branch, attn_full, n_dp, n_tp,
        )
        mlp_sum, total = norm_parts(mlp_sum, qkv_sum, out_sum, down_sum, n_dp, n_tp)
    else:
        layer_out = middle + layer_parts[0].astype(f32)
        for k in range(1, n_tp):
            layer_out = layer_out + plane_swap(layer_parts[k], k, n_tp).astype(f32)
        layer_out = layer_out.astype(bf16)
        gain_grad_two = jnp.sum(grad_normed_two * middle * inverse_two, axis=0)
        weighted_two = grad_normed_two * gain_two
        grad_middle = (
            cotangent.astype(f32)
            + inverse_two * weighted_two
            - middle * inverse_two**3 * jnp.mean(weighted_two * middle, axis=-1, keepdims=True)
        )
        grad_branch = grad_middle.astype(bf16)
        grad_context = matmul_t(grad_branch, out_full).astype(bf16)
        grad_projected = attend_grad(qkv, grad_context, log_totals, cosine, sine, seg_col, seg_row)
        grad_out = matmul_tn(attended, grad_branch).astype(bf16)
        grad_qkv = matmul_tn(normed_one, grad_projected)
        grad_normed_one = matmul_t(grad_projected, qkv_full)
        gain_grad_one = jnp.sum(grad_normed_one * tokens_f * inverse_one, axis=0)
        weighted_one = grad_normed_one * gain_one
        grad_inputs = (
            grad_middle
            + inverse_one * weighted_one
            - tokens_f * inverse_one**3 * jnp.mean(weighted_one * tokens_f, axis=-1, keepdims=True)
        )
        input_grad = grad_inputs.astype(bf16)
        gain_grads = jnp.pad(jnp.stack([gain_grad_one, gain_grad_two], axis=1), ((0, 0), (0, 126)))
        grad_qkv = jnp.concatenate([grad_qkv.astype(bf16), gain_grads.astype(bf16)], axis=1)
        out_sum, qkv_sum = scatter_all([grad_out, grad_qkv], n_dp, n_tp)
        mlp_sum = columns_back(mlp_sum, n_dp, n_tp)
        squares = jnp.sum(qkv_sum * qkv_sum) + jnp.sum(out_sum * out_sum) + jnp.sum(mlp_sum * mlp_sum)
        squares = squares + jnp.sum(jnp.square(down_sum.astype(f32)))
        total = total_over_devices(squares, n_dp, n_tp)
    grad_norm = jnp.sqrt(total[0, 0])
    states = (
        (qkv_weight, qkv_first, qkv_second),
        (out_weight, out_first, out_second),
        (mlp_weight, mlp_first, mlp_second),
        (down_weight, down_first, down_second),
        (norm_gains, gains_first, gains_second),
    )
    stepped = adam_all(total, (qkv_sum, out_sum, mlp_sum, down_sum), states)
    news = [stepped[i::3] for i in range(3)]
    return (layer_out, input_grad, grad_norm, *news[0], *news[1], *news[2])


def solution(mesh):
    split_rows = P(("dp", "fsdp"), None)
    split_columns = P(None, ("dp", "fsdp"))
    weights = (split_rows,) * 4 + (split_columns,)
    return jax.shard_map(
        functools.partial(local, mesh.shape["dp"], mesh.shape["fsdp"]),
        mesh=mesh,
        in_specs=(split_rows,) * 3 + weights * 3,
        out_specs=(split_rows, split_rows, P()) + weights * 3,
        check_vma=False,
    )
```

```python
import functools

import jax
import jax.numpy as jnp
from jax import lax
from jax.experimental import pallas as pl
from jax.experimental.pallas import tpu as pltpu
from jax.sharding import PartitionSpec as P

D = 2048
HEADS = 32
KVH = 4
HD = 64
FF = 5632
STEP = 10
KW = KVH * HD
GROUP = HEADS // KVH


norm_eps = 1e-05
rope_base = 10000.0
beta_one = 0.9
beta_two = 0.95
adam_eps = 1e-08
weight_decay = 0.1
matrix_rate = 0.04
gain_rate = 0.8
clip_norm = 1.0

f32 = jnp.float32
bf16 = jnp.bfloat16


def tables(segment_row):
    length = segment_row.shape[0]
    token_index = jnp.arange(length, dtype=jnp.int32)
    previous = jnp.concatenate([segment_row[:1] - 1, segment_row[:-1]])
    starts = lax.cummax(jnp.where(segment_row != previous, token_index, 0), axis=0)
    position = (token_index - starts).astype(f32)
    frequency = rope_base ** (-(jnp.arange(HD // 2, dtype=f32) * 2.0 / HD))
    angles = position[:, None] * frequency[None, :]
    cosine, sine = jnp.cos(angles), jnp.sin(angles)
    cosine = jnp.concatenate([cosine] * 4, axis=-1)
    signed = jnp.concatenate([-sine, sine] * 2, axis=-1)
    return cosine, signed


def halves_swapped(pair):
    lane = lax.broadcasted_iota(jnp.int32, pair.shape, 1)
    return jnp.where(lane % HD < HD // 2, pltpu.roll(pair, 96, 1), pltpu.roll(pair, 32, 1))


def split_pair(pair):
    lane = lax.broadcasted_iota(jnp.int32, pair.shape, 1)
    zero = jnp.zeros_like(pair)
    return jnp.where(lane < HD, pair, zero), jnp.where(lane < HD, zero, pair)


def both_places(pair, odd):
    low, high = split_pair(pair)
    moved = pltpu.roll(pair.astype(f32), HD, 1).astype(pair.dtype)
    moved_low, moved_high = split_pair(moved)
    return (moved_low, high) if odd else (low, moved_high)


def dot_t(a, b):
    return lax.dot_general(a, b, (((1,), (1,)), ((), ())), preferred_element_type=f32)


def dot_n(a, b):
    return lax.dot_general(a, b, (((1,), (0,)), ((), ())), preferred_element_type=f32)


def dot_tn(a, b):
    return lax.dot_general(a, b, (((0,), (0,)), ((), ())), preferred_element_type=f32)


def mask_keys_rows(seg_col, seg_row, length):
    key_index = lax.broadcasted_iota(jnp.int32, (length, length), 0)
    query_index = lax.broadcasted_iota(jnp.int32, (length, length), 1)
    return (seg_col == seg_row) & (query_index >= key_index)


def attend_kernel(proj, cosine, sine, seg_col, seg_row, qkv, context, log_totals):
    cos, sin = cosine[...], sine[...]
    for c in range(0, D + KW, 128):
        qkv[:, c : c + 128] = rope_tile(proj[:, c : c + 128], cos, sin).astype(bf16)
    for c in range(D + KW, D + 2 * KW, 128):
        qkv[:, c : c + 128] = proj[:, c : c + 128].astype(bf16)
    allowed = mask_keys_rows(seg_col[...], seg_row[...], proj.shape[0])
    attend_heads(qkv, context, log_totals, allowed)


def attend_grad_kernel(qkv, grad_context, log_totals, cosine, sine, seg_col, seg_row, grad_proj):
    allowed = mask_keys_rows(seg_col[...], seg_row[...], qkv.shape[0])
    attend_heads_grad(qkv, grad_context, log_totals, grad_proj, allowed, cosine[...], sine[...])


vmem_limit = 50 * 1024 * 1024
feed_vmem_limit = 62 * 1024 * 1024


def attend(projected, cosine, sine, seg_col, seg_row):
    length = projected.shape[0]
    return pl.pallas_call(
        attend_kernel,
        out_shape=(
            jax.ShapeDtypeStruct((length, D + 2 * KW), bf16),
            jax.ShapeDtypeStruct((length, D), bf16),
            jax.ShapeDtypeStruct((HEADS, length), f32),
        ),
        compiler_params=pltpu.CompilerParams(vmem_limit_bytes=vmem_limit),
        cost_estimate=cost(18),
        name="attend",
    )(projected, cosine, sine, seg_col, seg_row)


def attend_grad(qkv, grad_context, log_totals, cosine, sine, seg_col, seg_row):
    length = qkv.shape[0]
    return pl.pallas_call(
        attend_grad_kernel,
        out_shape=jax.ShapeDtypeStruct((length, D + 2 * KW), bf16),
        compiler_params=pltpu.CompilerParams(vmem_limit_bytes=vmem_limit),
        cost_estimate=cost(26),
        name="attend_grad",
    )(qkv, grad_context, log_totals, cosine, sine, seg_col, seg_row)


MESH = pl.DeviceIdType.MESH


def cost(microseconds):
    return pl.CostEstimate(flops=0, bytes_accessed=int(microseconds * 3.69e6), transcendentals=0)


def place():
    dp = lax.axis_index("dp")
    return dp // 2, dp % 2, lax.axis_index("fsdp")


def device(line, core, plane):
    return {"dp": line * 2 + core, "fsdp": plane}


def flipped(index, bit):
    return index + bit - 2 * bit * ((index // bit) % 2)


def greet(partners, ends):
    barrier = pltpu.get_barrier_semaphore()
    count = len(partners)
    for partner in partners:
        pl.semaphore_signal(barrier, inc=1, device_id=partner, device_id_type=MESH)
    for there, partner in ends:
        count = count + there

        @pl.when(there == 1)
        def _():
            pl.semaphore_signal(barrier, inc=1, device_id=partner, device_id_type=MESH)

    pl.semaphore_wait(barrier, count)


def gather_kernel(lines, own, weight, down, full, parts, down_full, cut, line_send, line_recv, x_send, x_recv, y_send, y_recv,
                  dx_send, dx_recv, dy_send, dy_recv, core_send, core_recv, cut_send, cut_recv, down_send, down_recv, down_core_send,
                  down_core_recv, here_sem):
    z, c, f = place()
    half = own.shape[0] // 2
    fx, fy = flipped(f, 1), flipped(f, 2)
    fd = flipped(fx, 2)
    x_dev, y_dev, core_dev = device(z, c, fx), device(z, c, fy), device(z, 1 - c, f)
    has_left = jnp.minimum(z, 1)
    has_right = jnp.minimum(lines - 1 - z, 1)
    left_dev = device(jnp.maximum(z - 1, 0), c, f)
    right_dev = device(jnp.minimum(z + 1, lines - 1), c, f)
    far_dev = device(z, c, fd)
    greet([x_dev, y_dev, far_dev, core_dev], [(has_left, left_dev), (has_right, right_dev)])

    def cut_copy(k):
        to = flipped(f, k) if k < 3 else fd
        return pltpu.make_async_remote_copy(
            cut.at[to], parts.at[f], cut_send.at[k], cut_recv.at[k], device_id=device(z, c, to), device_id_type=MESH
        )

    def copy(line, plane, send, recv, dev, src=None, rows=None):
        dst = full.at[line, c, plane]
        src = dst if src is None else src
        if rows is not None:
            dst, src = dst.at[rows], src.at[rows]
        return pltpu.make_async_remote_copy(
            src, dst, send, recv, device_id=dev, device_id_type=MESH
        )

    def to_right(line, src=None):
        return copy(line, f, line_send.at[0, line], line_recv.at[line], right_dev, src)

    def to_left(line, src=None):
        return copy(line, f, line_send.at[1, line], line_recv.at[line], left_dev, src)

    def to_x(line, src=None):
        return copy(line, f, x_send.at[line], x_recv.at[line], x_dev, src)

    def to_y(line, src=None):
        return copy(line, f, y_send.at[line], y_recv.at[line], y_dev, src)

    def diag_y(line):
        return copy(line, fx, dy_send.at[line], dy_recv.at[line], y_dev, None, pl.ds(0, half))

    def diag_x(line):
        return copy(line, fy, dx_send.at[line], dx_recv.at[line], x_dev, None, pl.ds(half, half))

    def to_core(line, plane, src=None):
        return copy(line, plane, core_send.at[line, plane], core_recv.at[line, plane], core_dev, src)

    def down_copy(line, way, src=None):
        dst = down_full.at[line, c]
        return pltpu.make_async_remote_copy(
            dst if src is None else src, dst, down_send.at[way, line], down_recv.at[line],
            device_id=(right_dev, left_dev)[way], device_id_type=MESH,
        )

    def down_core(line, src=None):
        dst = down_full.at[line, c]
        return pltpu.make_async_remote_copy(
            dst if src is None else src, dst, down_core_send.at[line], down_core_recv.at[line],
            device_id=core_dev, device_id_type=MESH,
        )

    here = pltpu.make_async_copy(own, full.at[z, c, f], here_sem.at[0])
    here.start()
    here_down = pltpu.make_async_copy(down, down_full.at[z, c], here_sem.at[2])
    here_down.start()

    @pl.when(has_right == 1)
    def _():
        to_right(z, own).start()

    @pl.when(has_left == 1)
    def _():
        to_left(z, own).start()

    to_x(z, own).start()
    to_y(z, own).start()
    to_core(z, f, own).start()

    cut_columns(weight, cut, 2 * lines, 4)
    here_cut = pltpu.make_async_copy(cut.at[f], parts.at[f], here_sem.at[1])
    here_cut.start()
    for k in range(1, 4):
        cut_copy(k).start()

    down_core(z, down).start()
    for t in range(1, lines):

        @pl.when(z >= t)
        def _():
            line = z - t
            to_right(line).wait_recv()

            @pl.when(has_right == 1)
            def _():
                to_right(line).start()

            to_x(line).start()
            to_y(line).start()
            to_core(line, f).start()

        @pl.when(z + t <= lines - 1)
        def _():
            line = z + t
            to_left(line).wait_recv()

            @pl.when(has_left == 1)
            def _():
                to_left(line).start()

            to_x(line).start()
            to_y(line).start()
            to_core(line, f).start()

    @pl.when(has_right == 1)
    def _():
        down_copy(z, 0, down).start()

    @pl.when(has_left == 1)
    def _():
        down_copy(z, 1, down).start()

    here.wait()
    order = []
    for t in range(lines):
        line = z
        for b in range(lines.bit_length() - 1):
            if t >> b & 1:
                line = flipped(line, 1 << b)
        order.append(line)
    for t, line in enumerate(order):
        to_x(line).wait_recv()
        diag_y(line).start()
        to_core(line, fx).start()
        to_y(line).wait_recv()
        diag_x(line).start()
        to_core(line, fy).start()
        if t == 0:
            continue

        @pl.when(z >= t)
        def _():
            down_copy(z - t, 0).wait_recv()

            @pl.when(has_right == 1)
            def _():
                down_copy(z - t, 0).start()

            down_core(z - t).start()

        @pl.when(z + t <= lines - 1)
        def _():
            down_copy(z + t, 1).wait_recv()

            @pl.when(has_left == 1)
            def _():
                down_copy(z + t, 1).start()

            down_core(z + t).start()

    for line in order:
        diag_y(line).wait_recv()
        diag_x(line).wait_recv()
        to_core(line, fd).start()
    here_cut.wait()
    here_down.wait()
    for k in range(1, 4):
        cut_copy(k).wait()
    for line in range(lines):
        for plane in range(4):
            to_core(line, plane).wait()
        to_x(line).wait_send()
        to_y(line).wait_send()
        diag_x(line).wait_send()
        diag_y(line).wait_send()

        down_core(line).wait()

        @pl.when((line <= z) & (has_right == 1))
        def _():
            to_right(line).wait_send()
            down_copy(line, 0).wait_send()

        @pl.when((line >= z) & (has_left == 1))
        def _():
            to_left(line).wait_send()
            down_copy(line, 1).wait_send()


def gather_all(shard, weight, down, n_dp, n_tp):
    rows, columns = shard.shape
    width = weight.shape[1] // n_tp
    lines = n_dp // 2
    if n_tp != 4 or rows % 32:
        full = lax.all_gather(shard, ("dp", "fsdp"), axis=0, tiled=True)
        down_full = lax.all_gather(down, "dp", axis=0, tiled=True)
        return full, columns_out(weight, n_dp, n_tp), down_full
    dma = pltpu.SemaphoreType.DMA
    hbm = pl.BlockSpec(memory_space=pl.ANY)
    full, parts, down_full = pl.pallas_call(
        functools.partial(gather_kernel, lines),
        out_shape=(
            jax.ShapeDtypeStruct((lines, 2, n_tp, rows, columns), bf16),
            jax.ShapeDtypeStruct((n_tp, rows, width), bf16),
            jax.ShapeDtypeStruct((lines, 2, *down.shape), bf16),
        ),
        in_specs=[hbm, pl.BlockSpec(memory_space=pltpu.VMEM), hbm],
        out_specs=(hbm, hbm, hbm),
        scratch_shapes=[pltpu.VMEM((n_tp, rows, width), bf16), dma((2, lines))]
        + [dma((lines,))] * 9
        + [dma((lines, n_tp))] * 2
        + [dma((n_tp,)), dma((n_tp,)), dma((2, lines)), dma((lines,)), dma((lines,)), dma((lines,)), dma((3,))],
        compiler_params=pltpu.CompilerParams(
            collective_id=0, has_side_effects=True, vmem_limit_bytes=vmem_limit
        ),
        cost_estimate=cost(100),
        name="gather_all",
    )(shard, weight, down)
    full = full.reshape(n_dp * n_tp * rows, columns)
    return full, parts, down_full.reshape(n_dp * down.shape[0], down.shape[1])


def cut_columns(weight, cut, n_dp, n_tp):
    unit = weight.shape[1] // (2 * n_dp * n_tp)
    half = n_dp * unit
    for to in range(n_tp):
        for side in range(2):
            starts = [side * n_tp * half + (j * n_tp + to) * unit for j in range(n_dp)]
            pieces = [weight[:, start : start + unit] for start in starts]
            cut[to, :, side * half : (side + 1) * half] = jnp.concatenate(pieces, axis=1).astype(bf16)


def columns_out_kernel(n_dp, n_tp, weight, parts, cut, send, recv, here_sem):
    z, c, f = place()
    greet([device(z, c, (f + k) % n_tp) for k in range(1, n_tp)], [])

    def away(k):
        to = (f + k) % n_tp
        return pltpu.make_async_remote_copy(
            cut.at[to], parts.at[f], send.at[k], recv.at[k], device_id=device(z, c, to), device_id_type=MESH
        )

    cut_columns(weight, cut, n_dp, n_tp)
    for k in range(1, n_tp):
        away(k).start()
    here = pltpu.make_async_copy(cut.at[f], parts.at[f], here_sem)
    here.start()
    here.wait()
    for k in range(1, n_tp):
        away(k).wait()


def columns_out(weight, n_dp, n_tp):
    rows, width = weight.shape
    dma = pltpu.SemaphoreType.DMA
    return pl.pallas_call(
        functools.partial(columns_out_kernel, n_dp, n_tp),
        out_shape=jax.ShapeDtypeStruct((n_tp, rows, width // n_tp), bf16),
        out_specs=pl.BlockSpec(memory_space=pl.ANY),
        scratch_shapes=[
            pltpu.VMEM((n_tp, rows, width // n_tp), bf16), dma((n_tp,)), dma((n_tp,)), dma(()),
        ],
        compiler_params=pltpu.CompilerParams(
            collective_id=1, has_side_effects=True, vmem_limit_bytes=vmem_limit
        ),
        cost_estimate=cost(20),
        name="columns_out",
    )(weight)


def columns_back_kernel(n_dp, n_tp, parts, whole, got, send, recv, here_sem):
    z, c, f = place()
    greet([device(z, c, (f + k) % n_tp) for k in range(1, n_tp)], [])
    unit = whole.shape[1] // (2 * n_dp * n_tp)
    half = n_dp * unit

    def away(k):
        to = (f + k) % n_tp
        return pltpu.make_async_remote_copy(
            parts.at[to], got.at[f], send.at[k], recv.at[k], device_id=device(z, c, to), device_id_type=MESH
        )

    for k in range(1, n_tp):
        away(k).start()
    here = pltpu.make_async_copy(parts.at[f], got.at[f], here_sem)
    here.start()
    here.wait()
    for k in range(1, n_tp):
        away(k).wait()
    for side in range(2):
        pieces = [
            got[frm, :, side * half + j * unit : side * half + (j + 1) * unit].astype(f32)
            for j in range(n_dp)
            for frm in range(n_tp)
        ]
        whole[:, side * n_tp * half : (side + 1) * n_tp * half] = jnp.concatenate(pieces, axis=1)


def columns_back(parts, n_dp, n_tp):
    _, rows, width = parts.shape
    dma = pltpu.SemaphoreType.DMA
    return pl.pallas_call(
        functools.partial(columns_back_kernel, n_dp, n_tp),
        out_shape=jax.ShapeDtypeStruct((rows, width * n_tp), f32),
        in_specs=[pl.BlockSpec(memory_space=pl.ANY)],
        scratch_shapes=[pltpu.VMEM(parts.shape, bf16), dma((n_tp,)), dma((n_tp,)), dma(())],
        compiler_params=pltpu.CompilerParams(
            collective_id=2, has_side_effects=True, vmem_limit_bytes=vmem_limit
        ),
        cost_estimate=cost(20),
        name="columns_back",
    )(parts)


def total_kernel(n_dp, n_tp, value, total, held, got, send, recv):
    dp, f = lax.axis_index("dp"), lax.axis_index("fsdp")
    partners = []
    for axis, size in (("dp", n_dp), ("fsdp", n_tp)):
        for bit in range(size.bit_length() - 1):
            index = {"dp": dp, "fsdp": f}
            index[axis] = flipped(index[axis], 1 << bit)
            partners.append(index)
    greet(partners, [])
    held[0] = value[...]
    for step, partner in enumerate(partners):
        swap = pltpu.make_async_remote_copy(
            held.at[step], got.at[step], send.at[step], recv.at[step], device_id=partner, device_id_type=MESH
        )
        swap.start()
        swap.wait()
        held[step + 1] = held[step] + got[step]
    total[...] = held[len(partners)]


def total_over_devices(value, n_dp, n_tp):
    steps = (n_dp * n_tp).bit_length() - 1
    dma = pltpu.SemaphoreType.DMA
    tile = (8, 128)
    spread = pl.pallas_call(
        functools.partial(total_kernel, n_dp, n_tp),
        out_shape=jax.ShapeDtypeStruct(tile, f32),
        scratch_shapes=[
            pltpu.VMEM((steps + 1, *tile), f32), pltpu.VMEM((steps, *tile), f32), dma((steps,)), dma((steps,)),
        ],
        compiler_params=pltpu.CompilerParams(collective_id=3, has_side_effects=True),
        cost_estimate=cost(13),
        name="total",
    )(jnp.broadcast_to(value, tile))
    return spread


def adam_update(weight, gradient, first, second, rate, decay):
    first = beta_one * first + (1.0 - beta_one) * gradient
    second = beta_two * second + (1.0 - beta_two) * gradient * gradient
    first_hat = first / (1.0 - beta_one**STEP)
    second_hat = second / (1.0 - beta_two**STEP)
    weight = weight - rate * (first_hat / (jnp.sqrt(second_hat) + adam_eps) + decay * weight)
    return (weight, first, second)


def matmul(a, b):
    return jnp.dot(a, b, preferred_element_type=f32)


def matmul_t(a, b):
    return lax.dot_general(a, b, (((1,), (1,)), ((), ())), preferred_element_type=f32)


def matmul_tn(a, b):
    return lax.dot_general(a, b, (((0,), (0,)), ((), ())), preferred_element_type=f32)


def swap_core(block, n_dp):
    return lax.ppermute(block, "dp", [(i, i ^ 1) for i in range(n_dp)])


def plane_swap(block, k, n_tp):
    return lax.ppermute(block, "fsdp", [(i, i ^ k) for i in range(n_tp)])


def plane_gather(block, n_tp):
    if n_tp != 4:
        return jnp.concatenate([block] + [plane_swap(block, k, n_tp) for k in range(1, n_tp)], axis=0)
    half = block.shape[0] // 2
    over_x, over_y = plane_swap(block, 1, n_tp), plane_swap(block, 2, n_tp)
    far = [plane_swap(over_y[:half], 1, n_tp), plane_swap(over_x[half:], 2, n_tp)]
    return jnp.concatenate([block, over_x, over_y] + far, axis=0)


def core_sum(parts, n_dp):
    core = lax.axis_index("dp") % 2
    mine = lax.dynamic_index_in_dim(parts, core, 1, keepdims=False)
    other = lax.dynamic_index_in_dim(parts, 1 - core, 1, keepdims=False)
    return mine.astype(f32) + swap_core(other, n_dp).astype(f32)


def line_sum(parts, n_dp):
    lines = n_dp // 2
    place = lax.axis_index("dp") // 2
    result = lax.dynamic_index_in_dim(parts, place, 0, keepdims=False)
    for way in (1, -1):
        arrived = None
        for step in range(1, lines):
            target = jnp.clip(place + way * (lines - step), 0, lines - 1)
            load = lax.dynamic_index_in_dim(parts, target, 0, keepdims=False).astype(f32)
            if arrived is not None:
                load = load + arrived.astype(f32)
            senders = range(step) if way == 1 else range(lines - step, lines)
            pairs = [(2 * s + c, 2 * (s + way) + c) for s in senders for c in range(2)]
            arrived = lax.ppermute(load.astype(bf16), "dp", pairs)
        result = result.astype(f32) + arrived.astype(f32)
    return result


def plane_sum(parts, n_tp):
    here = lax.axis_index("fsdp")
    total = lax.dynamic_index_in_dim(parts, here, 0, keepdims=False).astype(f32)
    for k in range(1, n_tp):
        load = lax.dynamic_index_in_dim(parts, here ^ k, 0, keepdims=False).astype(bf16)
        total = total + plane_swap(load, k, n_tp).astype(f32)
    return total


def by_rows(rows, body):
    def step(i, carry):
        body(pl.ds(pl.multiple_of(i * 16, 16), 16))
        return carry

    lax.fori_loop(0, rows // 16, step, 0)


def places_by_distance(z, lines):
    tables = [
        sorted(range(lines), key=lambda d: (-abs(d - here), min(d, lines - 1 - d), d)) for here in range(lines)
    ]
    power = 1
    for bit in range(lines.bit_length() - 1):
        power = power * (1 + (lines ** (1 << bit) - 1) * (z // (1 << bit) % 2))
    return [sum(table[t] * lines**here for here, table in enumerate(tables)) // power % lines for t in range(lines)]


class Scatter:
    def __init__(self, lines, groups, sems):
        self.sums, self.others, self.firsts, self.seconds, self.alongs, self.leaving, self.outs = groups
        core_send, core_recv, one_send, one_recv, two_send, two_recv, line_send, line_recv = sems
        z, c, f = place()
        self.z, self.f, self.lines = z, f, lines
        self.planes, self.rows = self.sums[0].shape[1:3]
        self.half = self.rows // 2
        fx, fy = flipped(f, 1), flipped(f, 2)
        fd = flipped(fx, 2)
        x_dev, y_dev, core_dev = device(z, c, fx), device(z, c, fy), device(z, 1 - c, f)
        self.has_left = jnp.minimum(z, 1)
        self.has_right = jnp.minimum(lines - 1 - z, 1)
        left_dev = device(jnp.maximum(z - 1, 0), c, f)
        right_dev = device(jnp.minimum(z + 1, lines - 1), c, f)
        greet([x_dev, y_dev, core_dev], [(self.has_left, left_dev), (self.has_right, right_dev)])
        halves = (pl.ds(0, self.half), pl.ds(self.half, self.half))
        near, self.next_near, step_dev = (fx, fy), (fy, fx), (x_dev, y_dev)
        self.order = places_by_distance(z, lines)

        def remote(src, dst, send, recv, dev):
            return pltpu.make_async_remote_copy(src, dst, send, recv, device_id=dev, device_id_type=MESH)

        def to_core(a, d, src):
            return remote(src, self.others[a].at[d], core_send.at[a, d], core_recv.at[a, d], core_dev)

        def one(a, d, way, i):
            block = (near[way], fd)[i]
            return remote(
                self.sums[a].at[d, block, halves[way]], self.firsts[a].at[way, d, i],
                one_send.at[a, d, way, i], one_recv.at[a, d, way, i], step_dev[way],
            )

        def two(a, d, way):
            return remote(
                self.sums[a].at[d, self.next_near[way], halves[way]], self.seconds[a].at[way, d],
                two_send.at[a, d, way], two_recv.at[a, d, way], step_dev[1 - way],
            )

        def to_right(a, d):
            return remote(
                self.leaving[a].at[d], self.alongs[a].at[d], line_send.at[a, d], line_recv.at[a, d], right_dev
            )

        def to_left(a, d, slot):
            return remote(
                self.leaving[a].at[d], self.alongs[a].at[slot], line_send.at[a, d], line_recv.at[a, slot], left_dev
            )

        self.to_core, self.one, self.two, self.to_right, self.to_left = to_core, one, two, to_right, to_left

    def add_along(self, a, slot):
        def step(r):
            self.outs[a][r] += self.alongs[a][slot, r].astype(f32)

        by_rows(self.rows, step)

    def over_core(self, a, d):
        sums, others = self.sums[a], self.others[a]
        self.to_core(a, d, others.at[d]).wait_recv()

        def core_add(r):
            for plane in range(self.planes):
                sums[d, plane, r] = (sums[d, plane, r].astype(f32) + others[d, plane, r].astype(f32)).astype(bf16)

        by_rows(self.rows, core_add)
        for i in (1, 0):
            for way in range(2):
                self.one(a, d, way, i).start()

    def there(self, r, way):
        return pl.ds(pl.multiple_of(r.start + way * self.half, 16), r.size)

    def over_first(self, a, d):
        sums, firsts = self.sums[a], self.firsts[a]
        for way in range(2):
            self.one(a, d, way, 1).wait_recv()
            block = self.next_near[way]

            def first_add(r):
                there = self.there(r, way)
                mine = sums[d, block, there].astype(f32)
                sums[d, block, there] = (mine + firsts[way, d, 1, r].astype(f32)).astype(bf16)

            by_rows(self.half, first_add)
            self.two(a, d, way).start()

    def over_second(self, a, d):
        sums, firsts, seconds, z = self.sums[a], self.firsts[a], self.seconds[a], self.z
        for way in range(2):
            self.one(a, d, way, 0).wait_recv()
            self.two(a, d, way).wait_recv()

            def total(r, there):
                return (
                    sums[d, self.f, there].astype(f32)
                    + firsts[way, d, 0, r].astype(f32)
                    + seconds[way, d, r].astype(f32)
                )

            @pl.when(d == z)
            def _():
                def stay(r):
                    there = self.there(r, way)
                    self.outs[a][there] = total(r, there)

                by_rows(self.half, stay)

            @pl.when(d != z)
            def _():
                def leave(r):
                    there = self.there(r, way)
                    self.leaving[a][d, there] = total(r, there).astype(bf16)

                by_rows(self.half, leave)

    def over_line(self, a, d):
        leaving, alongs, z = self.leaving[a], self.alongs[a], self.z

        def add_arrived():
            def step(r):
                leaving[d, r] = (leaving[d, r].astype(f32) + alongs[d, r].astype(f32)).astype(bf16)

            by_rows(self.rows, step)

        @pl.when((d > z) & (self.has_left == 1))
        def _():
            self.to_right(a, d).wait_recv()
            add_arrived()

        @pl.when((d < z) & (self.has_right == 1))
        def _():
            self.to_left(a, d, d).wait_recv()
            add_arrived()

        @pl.when(d > z)
        def _():
            self.to_right(a, d).start()

        @pl.when((d < z) & (d + 1 < z))
        def _():
            self.to_left(a, d, d).start()

        @pl.when(d + 1 == z)
        def _():
            self.to_left(a, d, self.lines).start()

    def finish(self):
        for a in range(len(self.sums)):

            @pl.when(self.has_left == 1)
            def _():
                self.to_right(a, self.z).wait_recv()
                self.add_along(a, self.z)

            @pl.when(self.has_right == 1)
            def _():
                self.to_left(a, self.z, self.lines).wait_recv()
                self.add_along(a, self.lines)

            for d in self.order:
                for way in range(2):
                    self.one(a, d, way, 0).wait_send()
                    self.one(a, d, way, 1).wait_send()
                    self.two(a, d, way).wait_send()

                @pl.when(d != self.z)
                def _():
                    self.to_right(a, d).wait_send()


def scatter_scratch(lines, n_tp, rows, widths):
    dma = pltpu.SemaphoreType.DMA
    n = len(widths)
    shapes = [
        (lines, n_tp, rows), (lines, n_tp, rows), (2, lines, 2, rows // 2), (2, lines, rows // 2),
        (lines + 1, rows), (lines, rows),
    ]
    buffers = [pltpu.VMEM((*shape, width), bf16) for shape in shapes for width in widths]
    sems = [dma((n, lines))] * 2 + [dma((n, lines, 2, 2))] * 2 + [dma((n, lines, 2))] * 2
    return buffers, sems + [dma((n, lines)), dma((n, lines + 1))]


def scatter_all(arrays, n_dp, n_tp):
    lines = n_dp // 2
    rows = arrays[0].shape[0] // (n_dp * n_tp)
    results = []
    for array in arrays:
        parts = core_sum(array.reshape(lines, 2, n_tp, rows, -1), n_dp)
        results.append(line_sum(plane_sum(parts.transpose(1, 0, 2, 3), n_tp), n_dp))
    return results


def rope_tile(tile, cos, sin):
    pairs = [tile[:, i : i + 128] for i in range(0, tile.shape[1], 128)]
    return jnp.concatenate([pair * cos + halves_swapped(pair) * sin for pair in pairs], axis=1)


def attend_heads(qkv, context, log_totals, allowed):
    length = qkv.shape[0]
    scale = HD ** (-0.5)
    for group in range(KVH):
        kc = D + (group // 2) * 128
        keys = both_places(qkv[:, kc : kc + 128], group % 2)
        values = both_places(qkv[:, kc + KW : kc + KW + 128], group % 2)

        def pair_step(pair_index, carry):
            pair = group * (GROUP // 2) + pair_index
            lanes = pl.ds(pl.multiple_of(pair * 128, 128), 128)
            queries = qkv[:, lanes]
            total = jnp.zeros((length, 128), f32)
            for side in range(2):
                scores = dot_t(keys[side], queries) * scale
                scores = jnp.where(allowed, scores, -1e30)
                top = jnp.max(scores, axis=0, keepdims=True)
                raised = jnp.exp(scores - top)
                totals = jnp.sum(raised, axis=0, keepdims=True)
                probs = (raised / totals).astype(bf16)
                total = total + dot_tn(probs, values[side])
                log_totals[pl.ds(2 * pair + side, 1), :] = top + jnp.log(totals)
            context[:, lanes] = total.astype(bf16)
            return carry

        lax.fori_loop(0, GROUP // 2, pair_step, 0)


def tile_at(i, width, start=0):
    return pl.ds(pl.multiple_of(start + i * width, 128), width)


class Exchange:
    def __init__(self, own, whole, sems, i, x_dev, y_dev):
        send, recv, here = sems
        half = own.shape[0] // 2

        def remote(src, dst, k, dev):
            return pltpu.make_async_remote_copy(
                src, dst, send.at[i, k], recv.at[i, k], device_id=dev, device_id_type=MESH
            )

        low, high = pl.ds(0, half), pl.ds(half, half)
        self.near = [remote(own, whole.at[1], 0, x_dev), remote(own, whole.at[2], 1, y_dev)]
        self.far = []
        if whole.shape[0] > 3:
            self.far = [
                remote(whole.at[2, low], whole.at[3, low], 2, x_dev),
                remote(whole.at[1, high], whole.at[3, high], 3, y_dev),
            ]
        self.here = pltpu.make_async_copy(own, whole.at[0], here.at[i])

    def start(self):
        for copy in self.near:
            copy.start()
        self.here.start()

    def pass_on(self):
        for copy in self.near:
            copy.wait_recv()
        for copy in self.far:
            copy.start()

    def finish(self):
        for copy in self.far:
            copy.wait()
        for copy in self.near:
            copy.wait_send()
        self.here.wait()


def forward_kernel(x, grads, gains, cosine, sine, seg_col, seg_row, weights, qkv, context, log_totals, middle,
                   normed_one, normed_all, grads_all, q_weight, o_weight, normed_two, load_sem, *sems):
    z, c, f = place()
    x_dev, y_dev = device(z, c, flipped(f, 1)), device(z, c, flipped(f, 2))
    greet([x_dev, y_dev], [])
    length = x.shape[0]
    width = D + 2 * KW
    of_grads = Exchange(grads, grads_all, sems, 0, x_dev, y_dev)
    of_normed = Exchange(normed_two, normed_all, sems, 1, x_dev, y_dev)
    of_grads.start()
    load_q = pltpu.make_async_copy(weights.at[:, pl.ds(0, width)], q_weight, load_sem.at[0])
    load_o = pltpu.make_async_copy(weights.at[:, pl.ds(width, D)], o_weight, load_sem.at[1])
    load_q.start()
    load_o.start()

    def norm_one(r):
        rows = x[r].astype(f32)
        inverse = lax.rsqrt(jnp.mean(rows * rows, axis=-1, keepdims=True) + norm_eps)
        normed_one[r] = (rows * inverse * gains[0:1, :]).astype(bf16)

    by_rows(length, norm_one)
    load_q.wait()
    cos, sin = cosine[...], sine[...]

    def project(i, carry):
        lanes = tile_at(i, 256)
        qkv[:, lanes] = rope_tile(dot_n(normed_one[...], q_weight[:, lanes]), cos, sin).astype(bf16)
        return carry

    lax.fori_loop(0, (D + KW) // 256, project, 0)
    qkv[:, D + KW :] = dot_n(normed_one[...], q_weight[:, D + KW :]).astype(bf16)
    allowed = mask_keys_rows(seg_col[...], seg_row[...], length)
    attend_heads(qkv, context, log_totals, allowed)
    load_o.wait()

    def project_out(i, carry):
        lanes = tile_at(i, 256)
        middle[:, lanes] = x[:, lanes].astype(f32) + dot_n(context[...], o_weight[:, lanes])
        return carry

    lax.fori_loop(0, D // 256, project_out, 0)

    def norm_two(r):
        rows = middle[r]
        inverse = lax.rsqrt(jnp.mean(rows * rows, axis=-1, keepdims=True) + norm_eps)
        normed_two[r] = (rows * inverse * gains[1:2, :]).astype(bf16)

    by_rows(length, norm_two)
    of_normed.start()
    of_grads.pass_on()
    of_normed.pass_on()
    of_normed.finish()
    of_grads.finish()


def forward(x, grads, gains, cosine, sine, seg_col, seg_row, weights):
    length = x.shape[0]
    dma = pltpu.SemaphoreType.DMA
    vmem, hbm = pl.BlockSpec(memory_space=pltpu.VMEM), pl.BlockSpec(memory_space=pl.ANY)
    width = D + 2 * KW
    return pl.pallas_call(
        forward_kernel,
        out_shape=(
            jax.ShapeDtypeStruct((length, width), bf16),
            jax.ShapeDtypeStruct((length, D), bf16),
            jax.ShapeDtypeStruct((HEADS, length), f32),
            jax.ShapeDtypeStruct((length, D), f32),
            jax.ShapeDtypeStruct((length, D), bf16),
            jax.ShapeDtypeStruct((4, length, D), bf16),
            jax.ShapeDtypeStruct((3, length, D), bf16),
        ),
        in_specs=[vmem, hbm] + [vmem] * 5 + [hbm],
        out_specs=(vmem,) * 5 + (hbm,) * 2,
        scratch_shapes=[
            pltpu.VMEM((D, width), bf16), pltpu.VMEM((D, D), bf16), pltpu.VMEM((length, D), bf16),
            dma((2,)), dma((2, 4)), dma((2, 4)), dma((2,)),
        ],
        compiler_params=pltpu.CompilerParams(
            collective_id=5, has_side_effects=True, vmem_limit_bytes=feed_vmem_limit
        ),
        cost_estimate=cost(95),
        name="forward",
    )(x, grads, gains, cosine, sine, seg_col, seg_row, weights)


class PlaneSum:
    def __init__(self, parts, ones, twos, sems, x_dev, y_dev):
        one_send, one_recv, two_send, two_recv = sems
        self.half = parts.shape[1] // 2
        self.parts, self.ones, self.twos = parts, ones, twos
        halves = (pl.ds(0, self.half), pl.ds(self.half, self.half))
        step_dev = (x_dev, y_dev)

        def remote(src, dst, send, recv, dev):
            return pltpu.make_async_remote_copy(src, dst, send, recv, device_id=dev, device_id_type=MESH)

        self.near, self.far, self.two = [], [], []
        for way in range(2):
            for i, copies in enumerate((self.near, self.far)):
                block = parts.at[2 if i else way, halves[way]]
                copies.append(
                    remote(block, ones.at[way, i], one_send.at[way, i], one_recv.at[way, i], step_dev[way])
                )
            if twos is not None:
                block = parts.at[1 - way, halves[way]]
                self.two.append(remote(block, twos.at[way], two_send.at[way], two_recv.at[way], step_dev[1 - way]))

    def there(self, r, way):
        return pl.ds(pl.multiple_of(r.start + way * self.half, 16), r.size)

    def pass_on(self):
        for way in range(2):
            self.far[way].wait_recv()

            def add_far(r):
                there = self.there(r, way)
                mine = self.parts[1 - way, there].astype(f32)
                self.parts[1 - way, there] = (mine + self.ones[way, 1, r].astype(f32)).astype(bf16)

            by_rows(self.half, add_far)
            self.two[way].start()

    def finish(self, add):
        for way in range(2):
            self.near[way].wait()
            self.far[way].wait_send()
            self.two[way].wait()
        for way in range(2):

            def add_all(r):
                add(self.there(r, way), self.ones[way, 0, r].astype(f32) + self.twos[way, r].astype(f32))

            by_rows(self.half, add_all)


def plane_sum_scratch(length, columns):
    dma = pltpu.SemaphoreType.DMA
    shapes = ((3, length, columns), (2, 2, length // 2, columns), (2, length // 2, columns))
    return [pltpu.VMEM(shape, bf16) for shape in shapes], [dma((2, 2)), dma((2, 2)), dma((2,)), dma((2,))]


def attend_heads_grad(qkv, grad_context, log_totals, grad_proj, allowed, cos, sin, between=None):
    length = qkv.shape[0]
    scale = HD ** (-0.5)

    def unrotate(pair):
        return pair * cos + halves_swapped(pair * sin)

    key_parts, value_parts = [], []
    for group in range(KVH):
        kc = D + (group // 2) * 128
        keys = both_places(qkv[:, kc : kc + 128], group % 2)
        values = both_places(qkv[:, kc + KW : kc + KW + 128], group % 2)

        def pair_step(pair_index, carry):
            grad_keys, grad_values = list(carry[:2]), list(carry[2:])
            pair = group * (GROUP // 2) + pair_index
            lanes = pl.ds(pl.multiple_of(pair * 128, 128), 128)
            queries = qkv[:, lanes]
            grads = grad_context[:, lanes]
            total = jnp.zeros((length, 128), f32)
            for side in range(2):
                scores = dot_t(keys[side], queries) * scale
                scores = jnp.where(allowed, scores, -1e30)
                probs = jnp.exp(scores - log_totals[pl.ds(2 * pair + side, 1), :])
                grad_probs = dot_t(values[side], grads)
                grad_values[side] = grad_values[side] + dot_n(probs.astype(bf16), grads)
                inner = jnp.sum(probs * grad_probs, axis=0, keepdims=True)
                raw = (probs * (grad_probs - inner) * scale).astype(bf16)
                total = total + dot_tn(raw, keys[side])
                grad_keys[side] = grad_keys[side] + dot_n(raw, queries)
            grad_proj[:, lanes] = unrotate(total).astype(bf16)
            return (*grad_keys, *grad_values)

        empty = jnp.zeros((length, 128), f32)
        out = lax.fori_loop(0, GROUP // 2, pair_step, (empty,) * 4)

        def joined(low_side, high_side):
            low, _ = split_pair(low_side)
            _, high = split_pair(high_side)
            both = low + high
            return both + pltpu.roll(both, HD, 1)

        key_parts.append(joined(out[0], out[1]))
        value_parts.append(joined(out[2], out[3]))
        if between is not None:
            between(group)
    lane = lax.broadcasted_iota(jnp.int32, (length, 128), 1)
    for c in range(KVH // 2):
        keys = jnp.where(lane < HD, key_parts[2 * c], key_parts[2 * c + 1])
        values = jnp.where(lane < HD, value_parts[2 * c], value_parts[2 * c + 1])
        grad_proj[:, D + c * 128 : D + (c + 1) * 128] = unrotate(keys).astype(bf16)
        grad_proj[:, D + KW + c * 128 : D + KW + (c + 1) * 128] = values.astype(bf16)


def fold(value):
    return jnp.sum(value, axis=0, keepdims=True)


def branch_kernel(grads, grad_normed, middle, gains, context_hbm, weights, layer_hbm, onward, layer_out, grad_branch,
                  grad_context, grad_o, gain_rows, weight, stage, arrived_layer, context, layer, load_sem, out_sem, send, recv):
    length, width = middle.shape[0], D + 2 * KW
    half = length // 2
    z, c, f = place()
    near = (device(z, c, flipped(f, 1)), device(z, c, flipped(f, 2)))
    greet(near, [])
    last = [
        pltpu.make_async_remote_copy(
            onward.at[way], arrived_layer.at[way], send.at[way], recv.at[way], device_id=near[1 - way], device_id_type=MESH
        )
        for way in range(2)
    ]
    for copy in last:
        copy.start()
    load_o = pltpu.make_async_copy(weights.at[:, pl.ds(width, D)], weight, load_sem.at[0])
    load_o.start()
    load_context = pltpu.make_async_copy(context_hbm, context, load_sem.at[1])
    load_layer = pltpu.make_async_copy(layer_hbm, layer, load_sem.at[2])
    load_context.start()
    load_layer.start()
    gain_rows[...] = jnp.zeros_like(gain_rows)

    def middle_grads(r):
        rows, arrived = middle[r], grad_normed[r]
        inverse = lax.rsqrt(jnp.mean(rows * rows, axis=-1, keepdims=True) + norm_eps)
        gain_rows[1:2, :] += fold(arrived * rows * inverse)
        weighted = arrived * gains[1:2, :]
        inner = jnp.mean(weighted * rows, axis=-1, keepdims=True)
        value = grads[r].astype(f32) + inverse * weighted - rows * (inverse * inverse * inverse * inner)
        grad_branch[r] = value.astype(bf16)

    by_rows(length, middle_grads)
    load_o.wait()

    def context_step(i, carry):
        tile = tile_at(i, 512)
        grad_context[:, tile] = dot_t(grad_branch[...], weight[tile, :]).astype(bf16)
        return carry

    lax.fori_loop(0, D // 512, context_step, 0)
    steps = D // 512

    def out(i, slot):
        return pltpu.make_async_copy(stage.at[slot], grad_o.at[tile_at(i, 512)], out_sem.at[slot])

    def step(i, carry):
        slot = i % 2

        @pl.when(i >= 2)
        def _():
            out(i - 2, slot).wait()

        stage[slot] = dot_tn(context[:, tile_at(i, 512)], grad_branch[...]).astype(bf16)
        out(i, slot).start()
        return carry

    load_context.wait()
    lax.fori_loop(0, steps, step, 0)
    load_layer.wait()
    for way in range(2):
        last[way].wait()

        def add_last(r):
            there = pl.ds(pl.multiple_of(r.start + way * half, 16), r.size)
            layer_out[there] = (middle[there] + layer[there].astype(f32) + arrived_layer[way, r].astype(f32)).astype(bf16)

        by_rows(half, add_last)
    out(steps - 2, 0).wait()
    out(steps - 1, 1).wait()


def branch(grads, grad_normed, middle, gains, context, weights, layer, onward):
    length = middle.shape[0]
    dma = pltpu.SemaphoreType.DMA
    vmem, hbm = pl.BlockSpec(memory_space=pltpu.VMEM), pl.BlockSpec(memory_space=pl.ANY)
    rows = jax.ShapeDtypeStruct((length, D), bf16)
    return pl.pallas_call(
        branch_kernel,
        out_shape=(rows, rows, rows, jax.ShapeDtypeStruct((D, D), bf16), jax.ShapeDtypeStruct((8, D), f32)),
        in_specs=[vmem] * 4 + [hbm] * 4,
        out_specs=(vmem, vmem, vmem, hbm, vmem),
        scratch_shapes=[
            pltpu.VMEM((D, D), bf16), pltpu.VMEM((2, 512, D), bf16), pltpu.VMEM((2, length // 2, D), bf16),
            pltpu.VMEM((length, D), bf16), pltpu.VMEM((length, D), bf16), dma((3,)), dma((2,)), dma((2,)), dma((2,)),
        ],
        compiler_params=pltpu.CompilerParams(
            collective_id=4, has_side_effects=True, vmem_limit_bytes=feed_vmem_limit
        ),
        cost_estimate=cost(22),
        name="branch",
    )(grads, grad_normed, middle, gains, context, weights, layer, onward)


def backward_kernel(lines, x_hbm, normed_hbm, qkv, grad_context, log_totals, gains, cosine, sine, seg_col, seg_row, gain_two,
                    grad_o, branch_hbm, weights, input_grad, out_o, out_q, weight, grad_proj, grad_one, gain_rows,
                    gain_columns, staged, x, normed_one, *refs):
    groups = [refs[i * 2 : i * 2 + 2] for i in range(6)] + [(out_o, out_q)]
    scatter_sems, (load_sem, weight_sem) = refs[12:20], refs[20:]
    scatter = Scatter(lines, groups, scatter_sems)
    z, c, f = place()
    length, width = x.shape[0], D + 2 * KW
    order = scatter.order
    rows = scatter.rows

    def load(d):
        return pltpu.make_async_copy(grad_o.at[d, c], scatter.sums[0].at[d], load_sem.at[d])

    def load_weight(i):
        tile = pl.ds(i * 512, 512)
        return pltpu.make_async_copy(weights.at[tile, pl.ds(0, width)], weight.at[i % 2], weight_sem.at[i % 2])

    for d in order:
        scatter.to_core(0, d, grad_o.at[d, 1 - c]).start()
        load(d).start()
    load_branch = pltpu.make_async_copy(branch_hbm, input_grad, load_sem.at[lines])
    load_branch.start()
    load_x = pltpu.make_async_copy(x_hbm, x, load_sem.at[lines + 1])
    load_normed = pltpu.make_async_copy(normed_hbm, normed_one, load_sem.at[lines + 2])
    load_x.start()
    load_normed.start()
    load_weight(0).start()
    load_weight(1).start()
    gain_rows[...] = gain_two[...]

    def between(group):
        if group == 0:
            for d in order:
                load(d).wait()
                scatter.over_core(0, d)
        elif group == 1:
            scatter.over_first(0, order[0])
            scatter.over_first(0, order[1])
        elif group == 2:
            for d in order[2:]:
                scatter.over_first(0, d)
        else:
            scatter.over_second(0, order[0])
            scatter.over_second(0, order[1])

    allowed = mask_keys_rows(seg_col[...], seg_row[...], length)
    attend_heads_grad(
        qkv, grad_context, log_totals, grad_proj, allowed, cosine[...], sine[...], between if lines > 1 else None
    )
    for i in range(D // 512):
        load_weight(i).wait()
        grad_one[:, i * 512 : (i + 1) * 512] = dot_t(grad_proj[...], weight[i % 2])
        if i + 2 < D // 512:
            load_weight(i + 2).start()
    for d in order[2:]:
        scatter.over_second(0, d)
    load_branch.wait()
    load_x.wait()
    load_normed.wait()

    def input_grads(r):
        values, arrived = x[r].astype(f32), grad_one[r]
        inverse = lax.rsqrt(jnp.mean(values * values, axis=-1, keepdims=True) + norm_eps)
        gain_rows[0:1, :] += fold(arrived * values * inverse)
        weighted = arrived * gains[0:1, :]
        inner = jnp.mean(weighted * values, axis=-1, keepdims=True)
        value = inverse * weighted - values * (inverse * inverse * inverse * inner)
        input_grad[r] = (input_grad[r].astype(f32) + value).astype(bf16)

    by_rows(length, input_grads)
    for i in range(D // 128):
        lanes = pl.ds(i * 128, 128)
        square = jnp.concatenate([gain_rows[:, lanes], jnp.zeros((120, 128), f32)], axis=0)
        gain_columns[lanes, :] = square.T.astype(bf16)

    def blocks(d, core):
        start = pl.multiple_of((2 * d + core) * (4 * rows), 128)
        tile = pl.ds(start, 4 * rows)
        value = dot_tn(normed_one[:, tile], grad_proj[...]).astype(bf16)
        return value.reshape(4, rows, width), gain_columns[tile, :].reshape(4, rows, 128)

    def put(target, value):
        target[:, :, 0:width] = value[0]
        target[:, :, width:] = value[1]

    def staged_copy(j):
        return scatter.to_core(1, order[j], staged.at[j % 2])

    for j, d in enumerate(order):
        if j >= 2:
            staged_copy(j - 2).wait_send()
        put(staged.at[j % 2], blocks(d, 1 - c))
        staged_copy(j).start()
        put(scatter.sums[1].at[d], blocks(d, c))
        if j:
            scatter.over_core(1, order[j - 1])
        if j < len(order) - 1:
            scatter.over_line(0, d)
    scatter.over_core(1, order[-1])
    for j in range(len(order) + 2):
        if j < len(order):
            scatter.over_first(1, order[j])
        if 0 <= j - 1 < len(order):
            scatter.over_second(1, order[j - 1])
        if 0 <= j - 2 < len(order) - 1:
            scatter.over_line(1, order[j - 2])
    for d in order:
        scatter.to_core(0, d, grad_o.at[d, 1 - c]).wait_send()
    for j in range(max(0, len(order) - 2), len(order)):
        staged_copy(j).wait_send()
    scatter.finish()


def backward(x, normed_one, qkv, grad_context, log_totals, gains, cosine, sine, seg_col, seg_row, gain_two, grad_o,
             grad_branch, weights, n_dp, n_tp):
    length = x.shape[0]
    lines, rows = n_dp // 2, D // (n_dp * n_tp)
    width = D + 2 * KW
    dma = pltpu.SemaphoreType.DMA
    vmem, hbm = pl.BlockSpec(memory_space=pltpu.VMEM), pl.BlockSpec(memory_space=pl.ANY)
    buffers, sems = scatter_scratch(lines, n_tp, rows, (D, width + 128))
    return pl.pallas_call(
        functools.partial(backward_kernel, lines),
        out_shape=(
            jax.ShapeDtypeStruct((length, D), bf16),
            jax.ShapeDtypeStruct((rows, D), f32),
            jax.ShapeDtypeStruct((rows, width + 128), f32),
        ),
        in_specs=[hbm] * 2 + [vmem] * 9 + [hbm] * 3,
        out_specs=(vmem,) * 3,
        scratch_shapes=[
            pltpu.VMEM((2, 512, width), bf16), pltpu.VMEM((length, width), bf16), pltpu.VMEM((length, D), f32),
            pltpu.VMEM((8, D), f32), pltpu.VMEM((D, 128), bf16), pltpu.VMEM((2, n_tp, rows, width + 128), bf16),
            pltpu.VMEM((length, D), bf16), pltpu.VMEM((length, D), bf16),
        ]
        + buffers + sems + [dma((lines + 3,)), dma((2,))],
        compiler_params=pltpu.CompilerParams(
            collective_id=7, has_side_effects=True, vmem_limit_bytes=feed_vmem_limit
        ),
        cost_estimate=cost(105),
        name="backward",
    )(x, normed_one, qkv, grad_context, log_totals, gains, cosine, sine, seg_col, seg_row, gain_two,
      grad_o.reshape(lines, 2, n_tp, rows, D), grad_branch, weights)


def norm_kernel(n_dp, n_tp, parts, qkv, out, down, mlp, total, got, held, got_dp, got_tp, send, recv, total_send,
                total_recv, here_sem):
    z, c, f = place()
    dp = z * 2 + c
    columns = [(f + k) % n_tp for k in range(1, n_tp)]
    lines = [(dp + k) % n_dp for k in range(1, n_dp)]
    greet([device(z, c, to) for to in columns] + [{"dp": to, "fsdp": f} for to in lines], [])
    unit = mlp.shape[1] // (2 * n_dp * n_tp)
    half = n_dp * unit

    def away(k):
        to = columns[k - 1]
        return pltpu.make_async_remote_copy(
            parts.at[to], got.at[f], send.at[k], recv.at[k], device_id=device(z, c, to), device_id_type=MESH
        )

    for k in range(1, n_tp):
        away(k).start()
    here = pltpu.make_async_copy(parts.at[f], got.at[f], here_sem)
    here.start()
    held[...] = jnp.zeros_like(held)

    def add_squares(ref):
        def step(r):
            part = ref[r, :].astype(f32)
            part = part * part
            lanes = [part[:, i : i + 128] for i in range(0, part.shape[1], 128)]
            held[...] += functools.reduce(jnp.add, lanes)

        by_rows(ref.shape[0], step)

    add_squares(qkv)
    add_squares(out)
    add_squares(down)
    here.wait()
    for k in range(1, n_tp):
        away(k).wait()
    for frm in range(n_tp):
        add_squares(got.at[frm])

    def spread(buffer, own, value, partners, base):
        buffer[own] = value
        copies = [
            pltpu.make_async_remote_copy(
                buffer.at[own], buffer.at[own], total_send.at[base + k], total_recv.at[base + k],
                device_id=partner, device_id_type=MESH,
            )
            for k, partner in enumerate(partners)
        ]
        for copy in copies:
            copy.start()
        return copies

    def summed(buffer, copies):
        for copy in copies:
            copy.wait()
        return functools.reduce(jnp.add, [buffer[i] for i in range(buffer.shape[0])])

    own_total = jnp.sum(jnp.sum(held[...], axis=0, keepdims=True), axis=1, keepdims=True)
    copies = spread(
        got_dp, dp, jnp.broadcast_to(own_total, (8, 128)), [{"dp": to, "fsdp": f} for to in lines], 0
    )
    for side in range(2):
        pieces = [
            got[frm, :, side * half + j * unit : side * half + (j + 1) * unit].astype(f32)
            for j in range(n_dp)
            for frm in range(n_tp)
        ]
        mlp[:, side * n_tp * half : (side + 1) * n_tp * half] = jnp.concatenate(pieces, axis=1)
    line_total = summed(got_dp, copies)
    copies = spread(got_tp, f, line_total, [device(z, c, to) for to in columns], n_dp)
    total[...] = summed(got_tp, copies)


def norm_parts(parts, qkv, out, down, n_dp, n_tp):
    _, rows, width = parts.shape
    dma = pltpu.SemaphoreType.DMA
    vmem, hbm = pl.BlockSpec(memory_space=pltpu.VMEM), pl.BlockSpec(memory_space=pl.ANY)
    return pl.pallas_call(
        functools.partial(norm_kernel, n_dp, n_tp),
        out_shape=(jax.ShapeDtypeStruct((rows, width * n_tp), f32), jax.ShapeDtypeStruct((8, 128), f32)),
        in_specs=[hbm, vmem, vmem, vmem],
        scratch_shapes=[
            pltpu.VMEM(parts.shape, bf16), pltpu.VMEM((16, 128), f32), pltpu.VMEM((n_dp, 8, 128), f32),
            pltpu.VMEM((n_tp, 8, 128), f32), dma((n_tp,)), dma((n_tp,)), dma((n_dp + n_tp,)), dma((n_dp + n_tp,)),
            dma(()),
        ],
        compiler_params=pltpu.CompilerParams(
            collective_id=8, has_side_effects=True, vmem_limit_bytes=feed_vmem_limit
        ),
        cost_estimate=cost(35),
        name="norm_parts",
    )(parts, qkv, out, down)


def adam_kernel(total, gain_block, *refs):
    scale = clip_norm / jnp.maximum(jnp.sqrt(total[0:1, 0:1]), clip_norm)
    grads, refs = refs[:4], refs[4:]
    states, news = refs[:15], refs[15:]

    def update(i, gradient, rate, decay):
        new = adam_update(
            states[3 * i][...], gradient * scale, states[3 * i + 1][...], states[3 * i + 2][...], rate, decay
        )
        for k in range(3):
            news[3 * i + k][...] = new[k]

    for i in range(4):
        update(i, grads[i][...].astype(f32), matrix_rate, weight_decay)

    @pl.when(pl.program_id(0) == 0)
    def _():
        rows = gain_block.shape[0]
        square = jnp.concatenate([gain_block[...], jnp.zeros((128 - rows, 128), f32)], axis=0)
        update(4, square.T[0:2, 0:rows], gain_rate, 0.0)


def adam_all(total, grads, states):
    shapes = [state[0].shape for state in states[:4]]

    def block(shape, steps):
        rows, columns = shape
        if rows % (8 * steps) == 0:
            return pl.BlockSpec((rows // steps, columns), lambda i: (i, 0))
        if columns % (128 * steps) == 0:
            return pl.BlockSpec((rows, columns // steps), lambda i: (0, i))
        return None

    steps = 4
    specs = [block(shape, steps) for shape in shapes]
    flat = [array for state in states for array in state]
    gains = pl.BlockSpec(states[4][0].shape, lambda i: (0, 0))
    state_specs = [spec for spec in specs + [gains] for _ in range(3)]
    last = grads[0].shape[1] // 128 - 1
    gain_block = pl.BlockSpec((grads[0].shape[0], 128), lambda i: (0, last))
    return pl.pallas_call(
        adam_kernel,
        grid=(steps,),
        out_shape=[jax.ShapeDtypeStruct(array.shape, f32) for array in flat],
        in_specs=[pl.BlockSpec((8, 128), lambda i: (0, 0)), gain_block] + specs + state_specs,
        out_specs=state_specs,
        compiler_params=pltpu.CompilerParams(vmem_limit_bytes=feed_vmem_limit),
        cost_estimate=cost(14),
        name="adam",
    )(total, grads[0], *grads, *flat)


def feed_front_kernel(n_hbm, g_hbm, wm_hbm, wd_hbm, gh_hbm, grad_down, layer_sum, onward, n, g, wm, wd, act, gh, stage,
                      parts, ones, *sems):
    sum_sems, (load_sem, weight_sem, out_sem, far_send, far_recv) = sems[:2], sems[2:]
    z, c, f = place()
    x_dev, y_dev = device(z, c, flipped(f, 1)), device(z, c, flipped(f, 2))
    tokens = n.shape[0]
    length = tokens // 4
    ff = wd.shape[0]
    half = length // 2
    order = (1, 2, 3, 0)

    def rows_of(k):
        return pl.ds(k * length, length)

    load_n = [pltpu.make_async_copy(n_hbm.at[rows_of(k)], n.at[rows_of(k)], load_sem.at[0, k]) for k in range(4)]
    load_g = [pltpu.make_async_copy(g_hbm.at[rows_of(k)], g.at[rows_of(k)], load_sem.at[1, k]) for k in range(3)]
    tiles = [(start, min(256, ff - start)) for start in range(0, ff, 256)]
    load_w = []
    for t, (start, size) in enumerate(tiles):
        gate, up = pl.ds(start, size), pl.ds(ff + start, size)
        load_w.append(
            [
                pltpu.make_async_copy(wm_hbm.at[:, gate], wm.at[:, gate], weight_sem.at[0, t]),
                pltpu.make_async_copy(wm_hbm.at[:, up], wm.at[:, up], weight_sem.at[1, t]),
                pltpu.make_async_copy(wd_hbm.at[gate], wd.at[gate], weight_sem.at[2, t]),
            ]
        )
    load_n[order[0]].start()
    load_g[order[0]].start()
    for copies in load_w:
        for copy in copies:
            copy.start()
    for k in order[1:]:
        load_n[k].start()
        if k < 3:
            load_g[k].start()
    greet([x_dev, y_dev], [])
    far_grads = [
        pltpu.make_async_remote_copy(
            g_hbm.at[pl.ds(start, half)], g.at[pl.ds(to, half)], far_send.at[i], far_recv.at[i], device_id=dev,
            device_id_type=MESH,
        )
        for i, (start, to, dev) in enumerate(
            ((2 * length, 3 * length, x_dev), (length + half, 3 * length + half, y_dev))
        )
    ]
    for copy in far_grads:
        copy.start()
    summed = PlaneSum(parts, ones, None, (*sum_sems, None, None), x_dev, y_dev)

    def hidden(k, slot, lanes, up_lanes):
        rows = rows_of(k)
        gate = dot_n(n[rows, :], wm[:, lanes])
        up = dot_n(n[rows, :], wm[:, up_lanes])
        grad = dot_t(g[rows, :], wd[lanes, :])
        sigmoid = jax.nn.sigmoid(gate)
        silu = gate * sigmoid
        act[rows, lanes] = (silu * up).astype(bf16)
        gh[slot, :, lanes] = (grad * up * sigmoid * (1.0 + gate * (1.0 - sigmoid))).astype(bf16)
        gh[slot, :, up_lanes] = (grad * silu).astype(bf16)

    def hidden_out(i):
        return pltpu.make_async_copy(gh.at[i % 2], gh_hbm.at[rows_of(order[i])], out_sem.at[1, i % 2])

    for i, k in enumerate(order):
        load_n[k].wait()
        for copy in load_g[k : k + 1] or far_grads:
            copy.wait()
        if i >= 2:
            hidden_out(i - 2).wait()
        if i == 0:
            for copies, (start, size) in zip(load_w, tiles):
                for copy in copies:
                    copy.wait()
                hidden(k, 0, pl.ds(start, size), pl.ds(ff + start, size))
        else:

            def hidden_step(t, carry):
                hidden(k, i % 2, tile_at(t, 256), tile_at(t, 256, ff))
                return carry

            lax.fori_loop(0, ff // 256, hidden_step, 0)
            if ff % 256:
                start, size = tiles[-1]
                hidden(k, i % 2, pl.ds(start, size), pl.ds(ff + start, size))
        hidden_out(i).start()

        def layer_step(t, carry):
            value = dot_n(act[rows_of(k), :], wd[:, tile_at(t, 512)]).astype(bf16)
            if k:
                parts[k - 1, :, tile_at(t, 512)] = value
            else:
                layer_sum[:, tile_at(t, 512)] = value
            return carry

        lax.fori_loop(0, D // 512, layer_step, 0)
        if k == 3:
            for copy in summed.far:
                copy.start()
        elif k:
            summed.near[k - 1].start()
    wide = ff // 256

    def down_out(i, slot, width=256):
        rows = pl.ds(pl.multiple_of((i // 2) * 256, 128), width)
        lanes = tile_at(i % 2, D // 2)
        return pltpu.make_async_copy(stage.at[slot, pl.ds(0, width)], grad_down.at[rows, lanes], out_sem.at[0, slot])

    def down_tile(i, slot, width=256):
        lanes = tile_at(i % 2, D // 2)
        value = dot_tn(act[:, pl.ds(pl.multiple_of((i // 2) * 256, 128), width)], g[:, lanes])
        stage[slot, 0:width] = value.astype(bf16)
        down_out(i, slot, width).start()

    def down_step(i, carry):
        slot = i % 2

        @pl.when(i >= 2)
        def _():
            down_out(i - 2, slot).wait()

        down_tile(i, slot)
        return carry

    lax.fori_loop(0, 2 * wide, down_step, 0)
    for slot in range(2):
        down_out(2 * wide - 2 + slot, slot).wait()
        if ff % 256:
            down_tile(2 * wide + slot, slot, ff % 256)
    for slot in range(2):
        if ff % 256:
            down_out(2 * wide + slot, slot, ff % 256).wait()
        hidden_out(2 + slot).wait()

    for way in range(2):
        summed.far[way].wait()

        def add_far(r):
            mine = parts[1 - way, summed.there(r, way)].astype(f32)
            onward[way, r] = (mine + ones[way, 1, r].astype(f32)).astype(bf16)

        by_rows(summed.half, add_far)
    for way in range(2):
        summed.near[way].wait()

        def add_near(r):
            there = summed.there(r, way)
            layer_sum[there] = (layer_sum[there].astype(f32) + ones[way, 0, r].astype(f32)).astype(bf16)

        by_rows(summed.half, add_near)


def feed_back_kernel(gh_hbm, wm_hbm, n_hbm, grad_normed, grad_mlp, gh, wm, n, stage, parts, ones, twos, *sems):
    sum_sems, (load_sem, out_sem) = sems[:4], sems[4:]
    z, c, f = place()
    x_dev, y_dev = device(z, c, flipped(f, 1)), device(z, c, flipped(f, 2))
    tokens = n.shape[0]
    length = tokens // 4
    ff = gh.shape[1] // 2
    order = (3, 1, 2, 0)
    rows_of = [pl.ds(k * length, length) for k in range(4)]
    load_gh = [pltpu.make_async_copy(gh_hbm.at[rows_of[k]], gh.at[rows_of[k]], load_sem.at[0, k]) for k in range(4)]
    wide_tiles = [pl.ds(start, 1024) for start in range(0, D, 1024)]
    load_w = [
        pltpu.make_async_copy(wm_hbm.at[tile], wm.at[tile], load_sem.at[1, t]) for t, tile in enumerate(wide_tiles)
    ]
    load_n = pltpu.make_async_copy(n_hbm, n, load_sem.at[1, 3])
    for copy in [load_gh[order[0]]] + load_w + [load_gh[k] for k in order[1:]] + [load_n]:
        copy.start()
    greet([x_dev, y_dev], [])
    summed = PlaneSum(parts, ones, twos, sum_sems, x_dev, y_dev)
    for k in order:
        load_gh[k].wait()
        for t, tile in enumerate(wide_tiles):
            if k == order[0]:
                load_w[t].wait()
            value = dot_t(gh[rows_of[k], :], wm[tile, :])
            if k:
                parts[k - 1, :, tile] = value.astype(bf16)
            else:
                grad_normed[:, tile] = value
        if k == 3:
            for copy in summed.far:
                copy.start()
        elif k:
            summed.near[k - 1].start()
    summed.pass_on()
    load_n.wait()
    steps = 2 * D // 512

    def mlp_out(i, slot):
        rows = pl.ds(pl.multiple_of((i // 2) * 512, 512), 512)
        return pltpu.make_async_copy(stage.at[slot], grad_mlp.at[rows, tile_at(i % 2, ff)], out_sem.at[slot])

    def mlp_step(i, carry):
        slot = i % 2

        @pl.when(i >= 2)
        def _():
            mlp_out(i - 2, slot).wait()

        stage[slot] = dot_tn(n[:, tile_at(i // 2, 512)], gh[:, tile_at(i % 2, ff)]).astype(bf16)
        mlp_out(i, slot).start()
        return carry

    lax.fori_loop(0, steps, mlp_step, 0)

    def add_normed(r, value):
        grad_normed[r] += value

    summed.finish(add_normed)
    mlp_out(steps - 2, 0).wait()
    mlp_out(steps - 1, 1).wait()


def feed(normed_all, grads_all, mlp_cols, down_cols):
    tokens, ff = 4 * normed_all.shape[1], down_cols.shape[0]
    length = tokens // 4
    dma = pltpu.SemaphoreType.DMA
    vmem, hbm = pl.BlockSpec(memory_space=pltpu.VMEM), pl.BlockSpec(memory_space=pl.ANY)
    sum_buffers, sum_sems = plane_sum_scratch(length, D)
    normed_all = normed_all.reshape(tokens, D)

    def buffers(*shapes):
        return [pltpu.VMEM(shape, bf16) for shape in shapes]

    grad_hidden, grad_down, layer_sum, onward = pl.pallas_call(
        feed_front_kernel,
        out_shape=(
            jax.ShapeDtypeStruct((tokens, 2 * ff), bf16),
            jax.ShapeDtypeStruct((ff, D), bf16),
            jax.ShapeDtypeStruct((length, D), bf16),
            jax.ShapeDtypeStruct((2, length // 2, D), bf16),
        ),
        in_specs=[hbm] * 4,
        out_specs=(hbm, hbm, vmem, vmem),
        scratch_shapes=buffers(
            (tokens, D), (tokens, D), (D, 2 * ff), (ff, D), (tokens, ff), (2, length, 2 * ff), (2, 256, D // 2)
        )
        + sum_buffers[:2] + sum_sems[:2]
        + [dma((2, 4)), dma((3, -(-ff // 256))), dma((2, 2)), dma((2,)), dma((2,))],
        compiler_params=pltpu.CompilerParams(
            collective_id=6, has_side_effects=True, vmem_limit_bytes=feed_vmem_limit
        ),
        cost_estimate=cost(65),
        name="feed_front",
    )(normed_all, grads_all.reshape(-1, D), mlp_cols, down_cols)
    grad_normed, grad_mlp = pl.pallas_call(
        feed_back_kernel,
        out_shape=(jax.ShapeDtypeStruct((length, D), f32), jax.ShapeDtypeStruct((D, 2 * ff), bf16)),
        in_specs=[hbm] * 3,
        out_specs=(vmem, hbm),
        scratch_shapes=buffers((tokens, 2 * ff), (D, 2 * ff), (tokens, D), (2, 512, ff))
        + sum_buffers + sum_sems + [dma((2, 4)), dma((2,))],
        compiler_params=pltpu.CompilerParams(
            collective_id=9, has_side_effects=True, vmem_limit_bytes=feed_vmem_limit
        ),
        cost_estimate=cost(60),
        name="feed_back",
    )(grad_hidden, mlp_cols, normed_all)
    return grad_normed, grad_down, grad_mlp, layer_sum, onward


def local(
    n_dp,
    n_tp,
    inputs,
    cotangent,
    segments,
    qkv_weight,
    out_weight,
    mlp_weight,
    down_weight,
    norm_gains,
    qkv_first,
    out_first,
    mlp_first,
    down_first,
    gains_first,
    qkv_second,
    out_second,
    mlp_second,
    down_second,
    gains_second,
):
    length = inputs.shape[0]
    lines = n_dp // 2
    rows = mlp_weight.shape[0]
    down_rows = down_weight.shape[0]
    ff = n_dp * down_rows
    cosine, sine = tables(segments[0])
    seg_row = segments
    seg_col = segments.reshape(length, 1)

    shard = jnp.concatenate(
        [qkv_weight, out_weight, jnp.pad(norm_gains.T, ((0, 0), (0, 126)))], axis=1
    ).astype(bf16)
    attn_full, mlp_parts, down_cols = gather_all(shard, mlp_weight, down_weight.astype(bf16), n_dp, n_tp)
    qkv_full = attn_full[:, : D + 2 * KW]
    out_full = attn_full[:, D + 2 * KW : 2 * D + 2 * KW]
    gains_full = attn_full[:, 2 * D + 2 * KW :].astype(f32).T
    mlp_cols = lax.all_gather(mlp_parts.reshape(n_tp * rows, 2 * ff), "dp", axis=0, tiled=True)
    tokens_f = inputs.astype(f32)
    gain_one, gain_two = gains_full[0], gains_full[1]
    inverse_one = lax.rsqrt(jnp.mean(tokens_f * tokens_f, axis=-1, keepdims=True) + norm_eps)
    if n_tp == 4:
        qkv, attended, log_totals, middle, normed_one, normed_all, grads_all = forward(
            inputs, cotangent, gains_full, cosine, sine, seg_col, seg_row, attn_full
        )
    else:
        normed_one = (tokens_f * inverse_one * gain_one).astype(bf16)
        projected = matmul(normed_one, qkv_full)
        qkv, attended, log_totals = attend(projected, cosine, sine, seg_col, seg_row)
        middle = tokens_f + matmul(attended, out_full)
    inverse_two = lax.rsqrt(jnp.mean(middle * middle, axis=-1, keepdims=True) + norm_eps)
    if n_tp == 4:
        grad_normed_two, grad_down, grad_mlp, layer_sum, onward = feed(normed_all, grads_all, mlp_cols, down_cols)
    else:
        normed_two = (middle * inverse_two * gain_two).astype(bf16)
        normed_all = plane_gather(normed_two, n_tp)
        grads_all = plane_gather(cotangent, n_tp)
        hidden = matmul(normed_all, mlp_cols)
        gate, up_part = hidden[:, :ff], hidden[:, ff:]
        sigmoid_gate = jax.nn.sigmoid(gate)
        silu_gate = gate * sigmoid_gate
        activated = (silu_gate * up_part).astype(bf16)
        grad_act = matmul_t(grads_all, down_cols)
        grad_gate = grad_act * up_part * sigmoid_gate * (1.0 + gate * (1.0 - sigmoid_gate))
        grad_up = grad_act * silu_gate
        grad_hidden = jnp.concatenate([grad_gate, grad_up], axis=1).astype(bf16)
        grad_normed = matmul_t(grad_hidden, mlp_cols).reshape(n_tp, length, D)
        grad_normed_two = grad_normed[0]
        for k in range(1, n_tp):
            swapped = plane_swap(grad_normed[k].astype(bf16), k, n_tp)
            grad_normed_two = grad_normed_two + swapped.astype(f32)
        grad_down = matmul_tn(activated, grads_all).astype(bf16)
        grad_mlp = matmul_tn(normed_all, grad_hidden).astype(bf16)
        layer_parts = matmul(activated, down_cols).astype(bf16).reshape(n_tp, length, D)
    down_sum = lax.psum_scatter(grad_down, "dp", scatter_dimension=0, tiled=True)
    mlp_sum = lax.psum_scatter(grad_mlp, "dp", scatter_dimension=0, tiled=True).reshape(n_tp, rows, 2 * ff)

    if n_tp == 4:
        layer_out, grad_branch, grad_context, grad_out, gain_two_rows = branch(
            cotangent, grad_normed_two, middle, gains_full, attended, attn_full, layer_sum, onward
        )
        input_grad, out_sum, qkv_sum = backward(
            inputs, normed_one, qkv, grad_context, log_totals, gains_full, cosine, sine, seg_col, seg_row,
            gain_two_rows, grad_out, grad_branch, attn_full, n_dp, n_tp,
        )
        mlp_sum, total = norm_parts(mlp_sum, qkv_sum, out_sum, down_sum, n_dp, n_tp)
    else:
        layer_out = middle + layer_parts[0].astype(f32)
        for k in range(1, n_tp):
            layer_out = layer_out + plane_swap(layer_parts[k], k, n_tp).astype(f32)
        layer_out = layer_out.astype(bf16)
        gain_grad_two = jnp.sum(grad_normed_two * middle * inverse_two, axis=0)
        weighted_two = grad_normed_two * gain_two
        grad_middle = (
            cotangent.astype(f32)
            + inverse_two * weighted_two
            - middle * inverse_two**3 * jnp.mean(weighted_two * middle, axis=-1, keepdims=True)
        )
        grad_branch = grad_middle.astype(bf16)
        grad_context = matmul_t(grad_branch, out_full).astype(bf16)
        grad_projected = attend_grad(qkv, grad_context, log_totals, cosine, sine, seg_col, seg_row)
        grad_out = matmul_tn(attended, grad_branch).astype(bf16)
        grad_qkv = matmul_tn(normed_one, grad_projected)
        grad_normed_one = matmul_t(grad_projected, qkv_full)
        gain_grad_one = jnp.sum(grad_normed_one * tokens_f * inverse_one, axis=0)
        weighted_one = grad_normed_one * gain_one
        grad_inputs = (
            grad_middle
            + inverse_one * weighted_one
            - tokens_f * inverse_one**3 * jnp.mean(weighted_one * tokens_f, axis=-1, keepdims=True)
        )
        input_grad = grad_inputs.astype(bf16)
        gain_grads = jnp.pad(jnp.stack([gain_grad_one, gain_grad_two], axis=1), ((0, 0), (0, 126)))
        grad_qkv = jnp.concatenate([grad_qkv.astype(bf16), gain_grads.astype(bf16)], axis=1)
        out_sum, qkv_sum = scatter_all([grad_out, grad_qkv], n_dp, n_tp)
        mlp_sum = columns_back(mlp_sum, n_dp, n_tp)
        squares = jnp.sum(qkv_sum * qkv_sum) + jnp.sum(out_sum * out_sum) + jnp.sum(mlp_sum * mlp_sum)
        squares = squares + jnp.sum(jnp.square(down_sum.astype(f32)))
        total = total_over_devices(squares, n_dp, n_tp)
    grad_norm = jnp.sqrt(total[0, 0])
    states = (
        (qkv_weight, qkv_first, qkv_second),
        (out_weight, out_first, out_second),
        (mlp_weight, mlp_first, mlp_second),
        (down_weight, down_first, down_second),
        (norm_gains, gains_first, gains_second),
    )
    stepped = adam_all(total, (qkv_sum, out_sum, mlp_sum, down_sum), states)
    news = [stepped[i::3] for i in range(3)]
    return (layer_out, input_grad, grad_norm, *news[0], *news[1], *news[2])


def solution(mesh):
    split_rows = P(("dp", "fsdp"), None)
    split_columns = P(None, ("dp", "fsdp"))
    weights = (split_rows,) * 4 + (split_columns,)
    return jax.shard_map(
        functools.partial(local, mesh.shape["dp"], mesh.shape["fsdp"]),
        mesh=mesh,
        in_specs=(split_rows,) * 3 + weights * 3,
        out_specs=(split_rows, split_rows, P()) + weights * 3,
        check_vma=False,
    )
```
